32 devices in a mesh: pts: 8 (over y, x, core), cen: 4 (over z).
Axes of the slice: x: 2, y: 2, z: 4, core: 2. Of those that a mesh axis runs over, the one named last changes fastest.
Arguments:
- points: bfloat16 [32768, 1024], P('pts'), may hold values from -60 to 60
- fine_assign: int32 [2, 32768], P(None, 'pts'), may hold values from 0 to 2047
- fine_start: float32 [2048, 1024], P('cen'), may hold values from -3 to 3
- coarse_start: float32 [64, 1024], replicated, may hold values from -3 to 3
- coarse_assign: int32 [2048], P('cen'), may hold values from 0 to 63
Outputs:
- fine_centroids: float32 [2048, 1024], P('cen')
- coarse_centroids: float32 [64, 1024], replicated
- gaps: float32 [2, 32768], P(None, 'pts')
The draws below stay inside these ranges and needn't reach their ends.
All inputs are finite; a program needn't handle non-finite values.
Results may differ from the reference program's by a relative error of at most 0.0028.
Values sent between devices are 32-bit elements; how exact they have to be, the bound alone decides.
No kernel may reach another device: no remote copies, remote signals or barrier semaphores. Data moves between devices by JAX's collectives and lax.ppermute only.
A program may use at most 64 MiB of HBM per device.

```python
import math
import jax
import jax.numpy as jnp
from jax import lax

D = 1024
NF = 2048
NC = 64
PASSES = 2
NPTS = 32768


def draw_points(key, part):
    first, second = jax.random.split(jax.random.fold_in(key, 11), 2)
    positions = jnp.arange(NPTS, dtype=jnp.float32) / NPTS
    base = jax.random.truncated_normal(first, -6.0, 6.0, (NPTS, D), jnp.float32)
    rising = jnp.exp(math.log(3.0) * positions)
    scales = jnp.exp(jax.random.uniform(second, (NPTS,), jnp.float32, math.log(0.3), math.log(3.0))) * rising
    return (base * scales[:, None]).astype(jnp.bfloat16)


def with_ends(result, own_key, smallest, top_value):
    longest = result.shape.index(max(result.shape))
    spots = []
    for shift in (0, 1):
        where = [jax.random.randint(jax.random.fold_in(own_key, axis), (), 0, length) for axis, length in enumerate(result.shape)]
        where[longest] = (where[longest] + shift) % result.shape[longest]
        spots.append(tuple(where))
    return result.at[spots[0]].set(smallest).at[spots[1]].set(top_value)


def level_of(own_key, dims, cuts, smallest, largest):
    def one(axis_at, parts):
        heights = jax.random.uniform(jax.random.fold_in(jax.random.fold_in(own_key, 6), axis_at), (parts,), jnp.float32, smallest / len(cuts), largest / len(cuts))
        return jnp.repeat(jnp.exp(heights), dims[axis_at] // parts).reshape((-1,) + (1,) * (len(dims) - axis_at - 1))

    loudness = one(*cuts[0])
    for cut in cuts[1:]:
        loudness = loudness * one(*cut)
    return loudness


def scatter_about(rng, extent, scale, bound, pieces=(), kind=jnp.bfloat16):
    factor_of = level_of(rng, extent, pieces, -0.22, 0.18) if pieces else 1.0
    drawn = jax.random.normal(rng, extent, jnp.float32) * scale * factor_of
    return jnp.minimum(jnp.maximum(drawn, -bound), bound).astype(kind)


def setup_inputs(seed: int = 0) -> dict:
    streams_of = jax.random.split(jax.random.key(seed), 6)
    return {
        "points": draw_points(jax.random.fold_in(streams_of[5], 71), 0),
        "fine_assign": with_ends(jax.random.randint(streams_of[1], (PASSES, NPTS), 0, NF), jax.random.fold_in(streams_of[1], 1), 0, NF - 1).astype(jnp.int32),
        "fine_start": scatter_about(streams_of[2], (NF, D), 0.5, 3.0, ((0, 4),), jnp.float32),
        "coarse_start": scatter_about(streams_of[3], (NC, D), 0.5, 3.0, (), jnp.float32),
        "coarse_assign": with_ends(jax.random.randint(streams_of[4], (NF,), 0, NC), jax.random.fold_in(streams_of[4], 1), 0, NC - 1).astype(jnp.int32),
    }


prior_weight = 4.0

def reference(points, fine_assign, fine_start, coarse_start, coarse_assign):
    block = math.gcd(NPTS, 512)
    blocks = NPTS // block
    point_values = points.astype(jnp.float32)
    squares = lax.optimization_barrier(jnp.sum(point_values * point_values, axis=1))
    fine = fine_start
    coarse = coarse_start
    gap_rows = []
    for pass_index in range(PASSES):
        assign = fine_assign[pass_index]
        fine_low = fine.astype(jnp.bfloat16).astype(jnp.float32)
        norms = lax.optimization_barrier(jnp.sum(fine * fine, axis=1))

        def block_terms(items):
            rows_in, ids_in = items
            products = jnp.dot(rows_in.astype(jnp.float32), fine_low.T, precision=lax.Precision.HIGHEST)
            energy = norms[None, :] - 2.0 * products
            picked_one = jnp.take_along_axis(energy, ids_in[:, None].astype(jnp.int32), axis=1)[:, 0]
            return (picked_one, lax.optimization_barrier(jnp.min(energy, axis=1)))
        picked, nearest = lax.map(block_terms, (points.reshape(blocks, block, D), assign.reshape(blocks, block)))
        picked = picked.reshape(NPTS)
        nearest = nearest.reshape(NPTS)
        gap_rows.append((picked - nearest) / math.sqrt(D))
        weights = 1.0 / (1.0 + (squares + picked) / D)
        scaled = (point_values * weights[:, None]).astype(jnp.bfloat16)
        totals = jax.ops.segment_sum(scaled.astype(jnp.float32), assign, NF)
        counts = jax.ops.segment_sum(weights, assign, NF)
        lookup = coarse[coarse_assign]
        fine = (totals + prior_weight * lookup) / (counts + prior_weight)[:, None]
        coarse_sum = jax.ops.segment_sum(counts[:, None] * fine, coarse_assign, NC)
        coarse_count = jax.ops.segment_sum(counts, coarse_assign, NC)
        coarse = (coarse_sum + prior_weight * coarse) / (coarse_count + prior_weight)[:, None]
    return (fine, coarse, jnp.stack(gap_rows))
```

```python
import functools
import math

import jax
import jax.numpy as jnp
from jax import lax
from jax.experimental import pallas as pl
from jax.experimental.pallas import tpu as pltpu
from jax.sharding import PartitionSpec as P

NC = 64
PASSES = 2
FAR = 3.0e38

prior_weight = 4.0
HIGHEST = lax.Precision.HIGHEST


def refine(totals, counts, coarse_cols, coarse_table):
    lookup = jnp.dot(coarse_table, coarse_cols, precision=HIGHEST)
    fine_next = (totals + prior_weight * lookup) / (counts + prior_weight)[:, None]
    coarse_part = lax.dot_general(
        coarse_table,
        counts[:, None] * fine_next,
        (((0,), (0,)), ((), ())),
        precision=HIGHEST,
    )
    coarse_weight = jnp.sum(coarse_table * counts[:, None], axis=0)
    return (fine_next, coarse_part, coarse_weight)


def on_device_any(points, fine_assign, fine_start, coarse_start, coarse_assign):
    width = points.shape[1]
    local_count = fine_start.shape[0]
    offset = lax.axis_index("cen") * local_count
    columns = jnp.arange(local_count, dtype=jnp.int32)
    coarse_table = (coarse_assign[:, None] == jnp.arange(NC, dtype=jnp.int32)[None, :]).astype(
        jnp.float32
    )
    point_values = points.astype(jnp.float32)
    squares = jnp.sum(point_values * point_values, axis=1)
    fine_now = fine_start
    coarse_now = coarse_start
    gap_rows = []
    for pass_index in range(PASSES):
        member = (fine_assign[pass_index] - offset)[:, None] == columns[None, :]
        products = jnp.dot(
            points, fine_now.astype(jnp.bfloat16).T, preferred_element_type=jnp.float32
        )
        energy = jnp.sum(fine_now * fine_now, axis=1)[None, :] - 2.0 * products
        picked_local = jnp.sum(jnp.where(member, energy, 0.0), axis=1)
        nearest_local = jnp.min(energy, axis=1)
        picked = lax.psum(picked_local, "cen")
        nearest = lax.pmin(nearest_local, "cen")
        gap_rows.append((picked - nearest) / math.sqrt(width))
        weights = 1.0 / (1.0 + (squares + picked) / width)
        scaled = (point_values * weights[:, None]).astype(jnp.bfloat16)
        partial_sums = lax.dot_general(
            member.astype(jnp.bfloat16),
            scaled,
            (((0,), (0,)), ((), ())),
            preferred_element_type=jnp.float32,
        )
        partial_weights = jnp.sum(jnp.where(member, weights[:, None], 0.0), axis=0)
        share_width = width // lax.axis_size("pts")
        start = lax.axis_index("pts") * share_width
        shares = lax.psum_scatter(partial_sums, "pts", scatter_dimension=1, tiled=True)
        counts = lax.psum(partial_weights, "pts")
        coarse_cols = lax.dynamic_slice_in_dim(coarse_now, start, share_width, 1)
        fine_share, coarse_part, coarse_weight = refine(shares, counts, coarse_cols, coarse_table)
        coarse_sum, coarse_count = lax.psum((coarse_part, coarse_weight), "cen")
        coarse_share = (coarse_sum + prior_weight * coarse_cols) / (coarse_count + prior_weight)[
            :, None
        ]
        fine_now, coarse_now = (
            lax.all_gather(fine_share, "pts", axis=1, tiled=True),
            lax.all_gather(coarse_share, "pts", axis=1, tiled=True),
        )
    return (fine_now, coarse_now, jnp.stack(gap_rows))


CORE, ACROSS_X, ACROSS_Y = 1, 2, 4
SLOTS = 4
TAIL = 8


def swap(value, bit, axis="pts"):
    size = lax.axis_size(axis)
    return lax.ppermute(value, axis, [(i, i ^ bit) for i in range(size)])


def pass_body(info, points, assign, *refs, pass_index, pieces, first, chained, sub):
    refs = list(refs)
    fine_refs = [refs.pop(0) for _ in pieces] if pieces else [refs.pop(0)]
    squares_in = None if first else refs.pop(0)
    seen_in = refs.pop(0) if chained else None
    payload, seen = refs.pop(0), refs.pop(0)
    squares_out = refs.pop(0) if first else None
    low, norms, sums, tallies = refs
    step = pl.program_id(0)
    rows, width = low.shape
    block_width = width // SLOTS
    here, base = info[0], info[2]

    @pl.when(step == 0)
    def _():
        if pieces:
            total = jnp.zeros((rows, 1), jnp.float32)
            parts = {}
            for (slot, top, height), ref in zip(pieces, fine_refs):
                block = ref[...]
                column = pl.multiple_of((here ^ slot) * block_width, block_width)
                low[top : top + height, pl.ds(column, block_width)] = (-2.0 * block).astype(
                    jnp.bfloat16
                )
                parts.setdefault(slot, []).append(jnp.sum(block * block, axis=1, keepdims=True))
            for column_parts in parts.values():
                total = total + (
                    column_parts[0] if len(column_parts) == 1 else jnp.concatenate(column_parts, 0)
                )
            norms[...] = jnp.broadcast_to(total, norms.shape)
        else:
            block = fine_refs[0][...]
            low[...] = (-2.0 * block).astype(jnp.bfloat16)
            norms[...] = jnp.broadcast_to(
                jnp.sum(block * block, axis=1, keepdims=True), norms.shape
            )
        sums[...] = jnp.zeros_like(sums)
        tallies[...] = jnp.zeros_like(tallies)

    norm = norms[:, :1]
    for at in range(0, points.shape[0], sub):
        span = slice(at, at + sub)
        tile = points[span, :]
        energy = norm + lax.dot_general(
            low[...], tile, (((1,), (1,)), ((), ())), preferred_element_type=jnp.float32
        )
        chosen = assign[pass_index : pass_index + 1, span] - base
        member = lax.broadcasted_iota(jnp.int32, energy.shape, 0) == chosen
        picked = jnp.sum(jnp.where(member, energy, 0.0), axis=0, keepdims=True)
        nearest = jnp.min(energy, axis=0, keepdims=True)
        inside = (chosen >= 0) & (chosen < rows)
        picked_seen = jnp.where(inside, picked, FAR)
        if chained:
            picked_seen = jnp.minimum(picked_seen, seen_in[0:1, span])
            nearest = jnp.minimum(nearest, seen_in[1:2, span])
        seen[0:1, span] = picked_seen
        seen[1:2, span] = nearest
        if first:
            folded = jnp.zeros((sub, 128), jnp.float32)
            for lane in range(0, width, 128):
                values = tile[:, lane : lane + 128].astype(jnp.float32)
                folded = folded + values * values
            squares = lax.dot_general(
                jnp.ones((8, 128), jnp.float32),
                folded,
                (((1,), (1,)), ((), ())),
                precision=HIGHEST,
                preferred_element_type=jnp.float32,
            )[:1]
            squares_out[0:1, span] = squares
        else:
            squares = squares_in[0:1, span]
        weights = 1.0 / (1.0 + (squares + picked) / width)
        held = jnp.where(member, weights, 0.0)
        tally = tallies[...]
        for lane in range(0, sub, 128):
            tally = tally + held[:, lane : lane + 128]
        tallies[...] = tally
        sums[...] += jnp.dot(
            held.astype(jnp.bfloat16), tile, preferred_element_type=jnp.float32
        )

    @pl.when(step == pl.num_programs(0) - 1)
    def _():
        for slot in range(SLOTS):
            column = pl.multiple_of((here ^ slot) * block_width, block_width)
            payload[slot * rows : (slot + 1) * rows, :] = sums[:, pl.ds(column, block_width)]
        counts = jnp.sum(tallies[...].T, axis=0, keepdims=True)
        payload[SLOTS * rows :, :] = jnp.broadcast_to(counts, (TAIL, rows))


def run_pass(info, points, fine_assign, fine, squares, seen, *, pass_index, pieces, rows):
    count, width = points.shape
    block_width = width // SLOTS
    tile = min(count, 1024)
    first = squares is None
    chained = seen is not None
    whole = lambda i, info: (0, 0)
    along = lambda i, info: (0, i)
    in_specs = [
        pl.BlockSpec((tile, width), lambda i, info: (i, 0)),
        pl.BlockSpec((PASSES, tile), along),
    ]
    args = [points, fine_assign]
    if pieces:
        for (slot, top, height), piece in zip(pieces, fine):
            in_specs.append(pl.BlockSpec((height, block_width), whole))
            args.append(piece)
    else:
        in_specs.append(pl.BlockSpec((rows, width), lambda i, info: (info[1], 0)))
        args.append(fine)
    if not first:
        in_specs.append(pl.BlockSpec((1, tile), along))
        args.append(squares)
    if chained:
        in_specs.append(pl.BlockSpec((2, tile), along))
        args.append(seen)
    out_shape = [
        jax.ShapeDtypeStruct((SLOTS * rows + TAIL, block_width), jnp.float32),
        jax.ShapeDtypeStruct((2, count), jnp.float32),
    ]
    out_specs = [
        pl.BlockSpec((SLOTS * rows + TAIL, block_width), whole),
        pl.BlockSpec((2, tile), along),
    ]
    if first:
        out_shape.append(jax.ShapeDtypeStruct((1, count), jnp.float32))
        out_specs.append(pl.BlockSpec((1, tile), along))
    body = functools.partial(
        pass_body,
        pass_index=pass_index,
        pieces=pieces,
        first=first,
        chained=chained,
        sub=min(tile, 512),
    )
    return pl.pallas_call(
        body,
        out_shape=out_shape,
        grid_spec=pltpu.PrefetchScalarGridSpec(
            num_scalar_prefetch=1,
            grid=(count // tile,),
            in_specs=in_specs,
            out_specs=out_specs,
            scratch_shapes=[
                pltpu.VMEM((rows, width), jnp.bfloat16),
                pltpu.VMEM((rows, 128), jnp.float32),
                pltpu.VMEM((rows, width), jnp.float32),
                pltpu.VMEM((rows, 128), jnp.float32),
            ],
        ),
        compiler_params=pltpu.CompilerParams(vmem_limit_bytes=40 * 2**20),
        cost_estimate=pl.CostEstimate(
            flops=4 * rows * count * width, bytes_accessed=2 * count * width, transcendentals=0
        ),
        name=f"energies_and_sums_{pass_index}{int(chained)}",
    )(info, *args)


def refine_body(own, sibling, over_x, over_y, tail, owner, coarse, fine, coarse_part):
    rows = own.shape[0]
    totals = own[...] + sibling[...] + over_x[...] + over_y[:rows, :]
    counts_row = tail[...] + over_y[rows:, :]
    counts = jnp.broadcast_to(counts_row[:1], (128, rows)).T[:, :1]
    table = (
        lax.broadcasted_iota(jnp.int32, (NC, rows), 0) == owner[...]
    ).astype(jnp.float32)
    lookup = lax.dot_general(
        table,
        coarse[...],
        (((0,), (0,)), ((), ())),
        precision=HIGHEST,
        preferred_element_type=jnp.float32,
    )
    new = (totals + prior_weight * lookup) / (counts + prior_weight)
    fine[...] = new
    coarse_part[:NC, : new.shape[1]] = jnp.dot(
        table, counts * new, precision=HIGHEST, preferred_element_type=jnp.float32
    )
    weight = jnp.sum(table * counts_row[:1], axis=1, keepdims=True)
    coarse_part[:NC, new.shape[1] :] = jnp.broadcast_to(weight, (NC, 128))


def refine_half(own, sibling, over_x, over_y, tail, owner, coarse):
    rows, block_width = over_x.shape
    full = lambda shape: pl.BlockSpec(shape, lambda i: (0, 0))
    return pl.pallas_call(
        refine_body,
        grid=(1,),
        out_shape=[
            jax.ShapeDtypeStruct((rows, block_width), jnp.float32),
            jax.ShapeDtypeStruct((NC, block_width + 128), jnp.float32),
        ],
        in_specs=[
            full((rows, block_width)),
            full((rows, block_width)),
            full((rows, block_width)),
            full((rows + TAIL, block_width)),
            full((TAIL, block_width)),
            full((1, rows)),
            full((NC, block_width)),
        ],
        out_specs=[full((rows, block_width)), full((NC, block_width + 128))],
        compiler_params=pltpu.CompilerParams(vmem_limit_bytes=16 * 2**20),
        name="refine_half",
    )(own, sibling, over_x, over_y, tail, owner, coarse)


def scatter_sums(own, sibling, rows):
    mid = rows // 2
    slot = lambda s: slice(s * rows, (s + 1) * rows)
    end = slice(SLOTS * rows, SLOTS * rows + TAIL)
    tail = own[end] + sibling[end]
    corner = own[slot(3)] + sibling[slot(3)]
    first_x = swap(jnp.concatenate([corner[:mid], tail], 0), ACROSS_X)
    first_y = swap(corner[mid:], ACROSS_Y)
    two = own[slot(2)] + sibling[slot(2)]
    one = own[slot(1)] + sibling[slot(1)]
    tail = tail + first_x[mid:]
    two = jnp.concatenate([two[:mid] + first_x[:mid], two[mid:], tail], 0)
    one = jnp.concatenate([one[:mid], one[mid:] + first_y], 0)
    over_y = swap(two, ACROSS_Y)
    over_x = swap(one, ACROSS_X)
    return over_x, over_y, tail


def gather_half(fine, rows):
    mid = rows // 2
    over_x = swap(fine, ACROSS_X)
    over_y = swap(fine, ACROSS_Y)
    top = swap(over_y[:mid], ACROSS_X)
    bottom = swap(over_x[mid:], ACROSS_Y)
    return [fine, over_x, over_y, top, bottom]


def add_everywhere(value):
    value = value + swap(value, CORE)
    bit = 1
    while bit < lax.axis_size("cen"):
        value = value + swap(value, bit, "cen")
        bit *= 2
    return value


def place_body(info, *refs, pieces):
    own = refs[:5]
    other = refs[5:10]
    coarse = refs[10:14]
    fine_out, coarse_out, sems = refs[14:]
    rows, block_width = own[0].shape
    here, half = info[0], info[1]
    copies = []
    for at, refs_of in ((half, own), (1 - half, other)):
        for (slot, top, height), ref in zip(pieces, refs_of):
            row = pl.multiple_of(at * rows + top, 8)
            column = pl.multiple_of((here ^ slot) * block_width, block_width)
            copies.append((ref, fine_out.at[pl.ds(row, height), pl.ds(column, block_width)]))
    for slot, ref in enumerate(coarse):
        column = pl.multiple_of((here ^ slot) * block_width, block_width)
        copies.append((ref, coarse_out.at[:, pl.ds(column, block_width)]))
    started = [
        pltpu.make_async_copy(source, target, sems.at[i])
        for i, (source, target) in enumerate(copies)
    ]
    for copy in started:
        copy.start()
    for copy in started:
        copy.wait()


def place(info, own, other, coarse, pieces):
    rows, block_width = own[0].shape
    anywhere = pl.BlockSpec(memory_space=pl.ANY)
    return pl.pallas_call(
        functools.partial(place_body, pieces=pieces),
        out_shape=[
            jax.ShapeDtypeStruct((2 * rows, SLOTS * block_width), jnp.float32),
            jax.ShapeDtypeStruct((NC, SLOTS * block_width), jnp.float32),
        ],
        grid_spec=pltpu.PrefetchScalarGridSpec(
            num_scalar_prefetch=1,
            grid=(1,),
            in_specs=[anywhere] * 14,
            out_specs=[anywhere] * 2,
            scratch_shapes=[pltpu.SemaphoreType.DMA((14,))],
        ),
        name="place_blocks",
    )(info, *own, *other, *coarse)


def on_device_paired(points, fine_assign, fine_start, coarse_start, coarse_assign):
    width = points.shape[1]
    local_count = fine_start.shape[0]
    rows = local_count // 2
    block_width = width // SLOTS
    offset = lax.axis_index("cen") * local_count
    me = lax.axis_index("pts")
    core, here = me & 1, me >> 1
    pieces = (
        (0, 0, rows),
        (1, 0, rows),
        (2, 0, rows),
        (3, 0, rows // 2),
        (3, rows // 2, rows // 2),
    )
    owners = coarse_assign.reshape(2, 1, rows)
    info_of = lambda half: jnp.stack([here, half, offset + half * rows]).astype(jnp.int32)
    coarse = lax.dynamic_slice_in_dim(coarse_start, here * block_width, block_width, 1)

    seen_rows = []
    squares = None
    own = other = None
    for pass_index in range(PASSES):
        keep = core if pass_index % 2 == 0 else 1 - core
        away = 1 - keep
        call = functools.partial(run_pass, pass_index=pass_index, rows=rows)
        if pass_index == 0:
            sent, seen, squares = call(
                info_of(away), points, fine_assign, fine_start, None, None, pieces=None
            )
        else:
            sent, seen = call(
                info_of(away), points, fine_assign, own, squares, None, pieces=pieces
            )
        sibling = swap(sent, CORE)
        held, seen = call(
            info_of(keep),
            points,
            fine_assign,
            fine_start if pass_index == 0 else other,
            squares,
            seen,
            pieces=None if pass_index == 0 else pieces,
        )
        seen_rows.append(seen)
        over_x, over_y, tail = scatter_sums(held, sibling, rows)
        owner = lax.dynamic_index_in_dim(owners, keep, 0, keepdims=False)
        fine, coarse_part = refine_half(held, sibling, over_x, over_y, tail, owner, coarse)
        own = gather_half(fine, rows)
        other = [swap(piece, CORE) for piece in own]
        coarse_sum = add_everywhere(coarse_part)
        coarse = (coarse_sum[:, :block_width] + prior_weight * coarse) / (
            coarse_sum[:, block_width : block_width + 1] + prior_weight
        )

    coarse_x = swap(coarse, ACROSS_X)
    coarse_y = swap(coarse, ACROSS_Y)
    corner = swap(coarse_y, ACROSS_X)
    fine_now, coarse_now = place(
        info_of(keep), own, other, [coarse, coarse_x, coarse_y, corner], pieces
    )

    seen = jnp.concatenate(seen_rows, 0)
    others = [swap(seen, bit, "cen") for bit in range(1, lax.axis_size("cen"))]
    for value in others:
        seen = jnp.minimum(seen, value)
    gaps = (seen[0::2] - seen[1::2]) / math.sqrt(width)
    return (fine_now, coarse_now, gaps)


def solution(mesh):
    placed = (P("pts", None), P(None, "pts"), P("cen", None), P(), P("cen"))

    def on_device(points, fine_assign, fine_start, coarse_start, coarse_assign):
        count, width = points.shape
        local_count = fine_start.shape[0]
        centres = mesh.shape["cen"]
        fits = (
            mesh.shape["pts"] == 2 * SLOTS
            and centres & (centres - 1) == 0
            and width // SLOTS == local_count // 2
            and (width // SLOTS) % 128 == 0
            and count % 1024 == 0
        )
        plan = on_device_paired if fits else on_device_any
        return plan(points, fine_assign, fine_start, coarse_start, coarse_assign)

    return jax.shard_map(
        on_device,
        mesh=mesh,
        in_specs=placed,
        out_specs=(P("cen", None), P(), P(None, "pts")),
        check_vma=False,
    )
```

```python
import functools
import math

import jax
import jax.numpy as jnp
from jax import lax
from jax.experimental import pallas as pl
from jax.experimental.pallas import tpu as pltpu
from jax.sharding import PartitionSpec as P

NC = 64
PASSES = 2
FAR = 3.0e38

prior_weight = 4.0
HIGHEST = lax.Precision.HIGHEST


def refine(totals, counts, coarse_cols, coarse_table):
    lookup = jnp.dot(coarse_table, coarse_cols, precision=HIGHEST)
    fine_next = (totals + prior_weight * lookup) / (counts + prior_weight)[:, None]
    coarse_part = lax.dot_general(
        coarse_table,
        counts[:, None] * fine_next,
        (((0,), (0,)), ((), ())),
        precision=HIGHEST,
    )
    coarse_weight = jnp.sum(coarse_table * counts[:, None], axis=0)
    return (fine_next, coarse_part, coarse_weight)


def on_device_any(points, fine_assign, fine_start, coarse_start, coarse_assign):
    width = points.shape[1]
    local_count = fine_start.shape[0]
    offset = lax.axis_index("cen") * local_count
    columns = jnp.arange(local_count, dtype=jnp.int32)
    coarse_table = (coarse_assign[:, None] == jnp.arange(NC, dtype=jnp.int32)[None, :]).astype(
        jnp.float32
    )
    point_values = points.astype(jnp.float32)
    squares = jnp.sum(point_values * point_values, axis=1)
    fine_now = fine_start
    coarse_now = coarse_start
    gap_rows = []
    for pass_index in range(PASSES):
        member = (fine_assign[pass_index] - offset)[:, None] == columns[None, :]
        products = jnp.dot(
            points, fine_now.astype(jnp.bfloat16).T, preferred_element_type=jnp.float32
        )
        energy = jnp.sum(fine_now * fine_now, axis=1)[None, :] - 2.0 * products
        picked_local = jnp.sum(jnp.where(member, energy, 0.0), axis=1)
        nearest_local = jnp.min(energy, axis=1)
        picked = lax.psum(picked_local, "cen")
        nearest = lax.pmin(nearest_local, "cen")
        gap_rows.append((picked - nearest) / math.sqrt(width))
        weights = 1.0 / (1.0 + (squares + picked) / width)
        scaled = (point_values * weights[:, None]).astype(jnp.bfloat16)
        partial_sums = lax.dot_general(
            member.astype(jnp.bfloat16),
            scaled,
            (((0,), (0,)), ((), ())),
            preferred_element_type=jnp.float32,
        )
        partial_weights = jnp.sum(jnp.where(member, weights[:, None], 0.0), axis=0)
        share_width = width // lax.axis_size("pts")
        start = lax.axis_index("pts") * share_width
        shares = lax.psum_scatter(partial_sums, "pts", scatter_dimension=1, tiled=True)
        counts = lax.psum(partial_weights, "pts")
        coarse_cols = lax.dynamic_slice_in_dim(coarse_now, start, share_width, 1)
        fine_share, coarse_part, coarse_weight = refine(shares, counts, coarse_cols, coarse_table)
        coarse_sum, coarse_count = lax.psum((coarse_part, coarse_weight), "cen")
        coarse_share = (coarse_sum + prior_weight * coarse_cols) / (coarse_count + prior_weight)[
            :, None
        ]
        fine_now, coarse_now = (
            lax.all_gather(fine_share, "pts", axis=1, tiled=True),
            lax.all_gather(coarse_share, "pts", axis=1, tiled=True),
        )
    return (fine_now, coarse_now, jnp.stack(gap_rows))


CORE, ACROSS_X, ACROSS_Y = 1, 2, 4
SLOTS = 4
TAIL = 8


def swap(value, bit, axis="pts"):
    size = lax.axis_size(axis)
    return lax.ppermute(value, axis, [(i, i ^ bit) for i in range(size)])


def pass_body(info, points, assign, *refs, pass_index, pieces, first, chained, tile):
    refs = list(refs)
    fine_refs = [refs.pop(0) for _ in pieces] if pieces else [refs.pop(0)]
    squares_in = None if first else refs.pop(0)
    seen_in = refs.pop(0) if chained else None
    payload, seen = refs.pop(0), refs.pop(0)
    squares_out = refs.pop(0) if first else None
    kept, arrived, low, sums, tallies, products, held = refs
    rows, width = low.shape
    block_width = width // SLOTS
    here, base = info[0], info[2]
    tiles = points.shape[0] // tile

    def span(i):
        return slice(i * tile, (i + 1) * tile)

    loads = [
        pltpu.make_async_copy(points.at[span(i)], kept.at[span(i)], arrived.at[i])
        for i in range(tiles)
    ]
    for load in loads:
        load.start()

    norm = jnp.zeros((rows, 1), jnp.float32)
    for slot, ref in zip(pieces, fine_refs) if pieces else [(None, fine_refs[0])]:
        block = ref[...]
        norm = norm + jnp.sum(block * block, axis=1, keepdims=True)
        block = (-2.0 * block).astype(jnp.bfloat16)
        if pieces:
            column = pl.multiple_of((here ^ slot) * block_width, block_width)
            low[:, pl.ds(column, block_width)] = block
        else:
            low[...] = block
    sums[...] = jnp.zeros_like(sums)
    tallies[...] = jnp.zeros_like(tallies)

    def multiply(i):
        loads[i].wait()
        products[i % 2] = lax.dot_general(
            low[...], kept[span(i), :], (((1,), (1,)), ((), ())), preferred_element_type=jnp.float32
        )

    def weigh(i):
        energy = norm + products[i % 2]
        chosen = assign[pass_index : pass_index + 1, span(i)] - base
        member = lax.broadcasted_iota(jnp.int32, energy.shape, 0) == chosen
        picked = jnp.sum(jnp.where(member, energy, 0.0), axis=0, keepdims=True)
        nearest = jnp.min(energy, axis=0, keepdims=True)
        inside = (chosen >= 0) & (chosen < rows)
        picked_seen = jnp.where(inside, picked, FAR)
        if chained:
            picked_seen = jnp.minimum(picked_seen, seen_in[0:1, span(i)])
            nearest = jnp.minimum(nearest, seen_in[1:2, span(i)])
        seen[0:1, span(i)] = picked_seen
        seen[1:2, span(i)] = nearest
        if first:
            folded = jnp.zeros((tile, 128), jnp.float32)
            for lane in range(0, width, 128):
                values = kept[span(i), lane : lane + 128].astype(jnp.float32)
                folded = folded + values * values
            squares = lax.dot_general(
                jnp.ones((8, 128), jnp.float32),
                folded,
                (((1,), (1,)), ((), ())),
                precision=HIGHEST,
                preferred_element_type=jnp.float32,
            )[:1]
            squares_out[0:1, span(i)] = squares
        else:
            squares = squares_in[0:1, span(i)]
        weights = 1.0 / (1.0 + (squares + picked) / width)
        weighted = jnp.where(member, weights, 0.0)
        tally = tallies[...]
        for lane in range(0, tile, 128):
            tally = tally + weighted[:, lane : lane + 128]
        tallies[...] = tally
        held[i % 2] = weighted.astype(jnp.bfloat16)

    def collect(i):
        sums[...] += jnp.dot(held[i % 2], kept[span(i), :], preferred_element_type=jnp.float32)

    multiply(0)
    for i in range(tiles):
        if i + 1 < tiles:
            multiply(i + 1)
        if i > 0:
            collect(i - 1)
        weigh(i)
    collect(tiles - 1)

    counts = jnp.broadcast_to(jnp.sum(tallies[...].T, axis=0, keepdims=True), (TAIL, rows))
    for slot in range(SLOTS):
        column = pl.multiple_of((here ^ slot) * block_width, block_width)
        top = slot * (rows + TAIL)
        payload[top : top + rows, :] = sums[:, pl.ds(column, block_width)]
        payload[top + rows : top + rows + TAIL, :] = counts


def run_pass(info, points, fine_assign, fine, squares, seen, *, pass_index, pieces, rows):
    count, width = points.shape
    block_width = width // SLOTS
    tile = 512
    first = squares is None
    chained = seen is not None
    full = lambda *shape: pl.BlockSpec(shape, lambda i, info: (0, 0))
    in_specs = [pl.BlockSpec(memory_space=pl.ANY), full(PASSES, count)]
    args = [points, fine_assign]
    if pieces:
        in_specs += [full(rows, block_width)] * len(pieces)
        args += fine
    else:
        in_specs.append(pl.BlockSpec((rows, width), lambda i, info: (info[1], 0)))
        args.append(fine)
    if not first:
        in_specs.append(full(1, count))
        args.append(squares)
    if chained:
        in_specs.append(full(2, count))
        args.append(seen)
    shapes = [(SLOTS * (rows + TAIL), block_width), (2, count)]
    if first:
        shapes.append((1, count))
    body = functools.partial(
        pass_body,
        pass_index=pass_index,
        pieces=pieces,
        first=first,
        chained=chained,
        tile=tile,
    )
    return pl.pallas_call(
        body,
        out_shape=[jax.ShapeDtypeStruct(shape, jnp.float32) for shape in shapes],
        grid_spec=pltpu.PrefetchScalarGridSpec(
            num_scalar_prefetch=1,
            grid=(1,),
            in_specs=in_specs,
            out_specs=[full(*shape) for shape in shapes],
            scratch_shapes=[
                pltpu.VMEM((count, width), jnp.bfloat16),
                pltpu.SemaphoreType.DMA((count // tile,)),
                pltpu.VMEM((rows, width), jnp.bfloat16),
                pltpu.VMEM((rows, width), jnp.float32),
                pltpu.VMEM((rows, 128), jnp.float32),
                pltpu.VMEM((2, rows, tile), jnp.float32),
                pltpu.VMEM((2, rows, tile), jnp.bfloat16),
            ],
        ),
        compiler_params=pltpu.CompilerParams(vmem_limit_bytes=56 * 2**20),
        cost_estimate=pl.CostEstimate(
            flops=4 * rows * count * width, bytes_accessed=2 * count * width, transcendentals=0
        ),
        name=f"energies_and_sums_{pass_index}{int(chained)}",
    )(info, *args)


def refine_body(own, sibling, over_x, over_y, over_xy, owner, coarse, fine, coarse_part):
    rows = fine.shape[0]
    received = own[...] + sibling[...] + over_x[...] + over_y[...] + over_xy[...]
    totals, counts_row = received[:rows], received[rows:]
    counts = jnp.broadcast_to(counts_row[:1], (128, rows)).T[:, :1]
    table = (
        lax.broadcasted_iota(jnp.int32, (NC, rows), 0) == owner[...]
    ).astype(jnp.float32)
    lookup = lax.dot_general(
        table,
        coarse[...],
        (((0,), (0,)), ((), ())),
        precision=HIGHEST,
        preferred_element_type=jnp.float32,
    )
    new = (totals + prior_weight * lookup) / (counts + prior_weight)
    fine[...] = new
    coarse_part[:NC, :] = jnp.dot(
        table, counts * new, precision=HIGHEST, preferred_element_type=jnp.float32
    )
    coarse_part[NC:, :] = jnp.zeros((TAIL, coarse_part.shape[1]), jnp.float32)
    coarse_part[NC:, :NC] = lax.dot_general(
        counts_row,
        table,
        (((1,), (1,)), ((), ())),
        precision=HIGHEST,
        preferred_element_type=jnp.float32,
    )


def refine_half(own, sibling, over_x, over_y, over_xy, owner, coarse):
    block_width = coarse.shape[1]
    rows = owner.shape[1]
    full = lambda *shape: pl.BlockSpec(shape, lambda i: (0, 0))
    return pl.pallas_call(
        refine_body,
        grid=(1,),
        out_shape=[
            jax.ShapeDtypeStruct((rows, block_width), jnp.float32),
            jax.ShapeDtypeStruct((NC + TAIL, block_width), jnp.float32),
        ],
        in_specs=[full(rows + TAIL, block_width)] * 5
        + [full(1, rows), full(NC, block_width)],
        out_specs=[full(rows, block_width), full(NC + TAIL, block_width)],
        compiler_params=pltpu.CompilerParams(vmem_limit_bytes=16 * 2**20),
        name="refine_half",
    )(own, sibling, over_x, over_y, over_xy, owner, coarse)


def spread(value):
    corner = swap(value, ACROSS_X | ACROSS_Y)
    return [value, swap(value, ACROSS_X), swap(value, ACROSS_Y), corner]


def add_over_cen(value):
    others = [swap(value, bit, "cen") for bit in range(1, lax.axis_size("cen"))]
    return functools.reduce(jnp.add, others, value)


def place_body(info, *refs):
    own, other, coarse = refs[:SLOTS], refs[SLOTS : 2 * SLOTS], refs[2 * SLOTS : 3 * SLOTS]
    fine_out, coarse_out = refs[3 * SLOTS :]
    block_width = own[0].shape[1]
    here = info[0]

    def put(pieces, target):
        for slot, piece in enumerate(pieces):
            column = pl.multiple_of((here ^ slot) * block_width, block_width)
            target[:, pl.ds(column, block_width)] = piece[...]

    @pl.when(pl.program_id(0) == 0)
    def _():
        put(own, fine_out)
        put(coarse, coarse_out)

    @pl.when(pl.program_id(0) == 1)
    def _():
        put(other, fine_out)


def place(info, own, other, coarse):
    rows, block_width = own[0].shape
    width = SLOTS * block_width
    full = lambda *shape: pl.BlockSpec(shape, lambda i, info: (0, 0))
    return pl.pallas_call(
        place_body,
        out_shape=[
            jax.ShapeDtypeStruct((2 * rows, width), jnp.float32),
            jax.ShapeDtypeStruct((NC, width), jnp.float32),
        ],
        grid_spec=pltpu.PrefetchScalarGridSpec(
            num_scalar_prefetch=1,
            grid=(2,),
            in_specs=[full(rows, block_width)] * (2 * SLOTS) + [full(NC, block_width)] * SLOTS,
            out_specs=[
                pl.BlockSpec((rows, width), lambda i, info: (info[1] ^ i, 0)),
                full(NC, width),
            ],
        ),
        compiler_params=pltpu.CompilerParams(vmem_limit_bytes=24 * 2**20),
        name="place_blocks",
    )(info, *own, *other, *coarse)


def on_device_paired(points, fine_assign, fine_start, coarse_start, coarse_assign):
    width = points.shape[1]
    local_count = fine_start.shape[0]
    rows = local_count // 2
    block_width = width // SLOTS
    offset = lax.axis_index("cen") * local_count
    me = lax.axis_index("pts")
    core, here = me & 1, me >> 1
    owners = coarse_assign.reshape(2, 1, rows)
    info_of = lambda half: jnp.stack([here, half, offset + half * rows]).astype(jnp.int32)
    coarse = lax.dynamic_slice_in_dim(coarse_start, here * block_width, block_width, 1)
    slot_rows = lambda array, slot: array[slot * (rows + TAIL) : (slot + 1) * (rows + TAIL)]

    def renew(coarse, coarse_sum):
        return (coarse_sum[:NC] + prior_weight * coarse) / (
            coarse_sum[NC, :NC] + prior_weight
        )[:, None]

    first_pass = functools.partial(run_pass, pass_index=0, pieces=None, rows=rows)
    sent, seen, squares = first_pass(
        info_of(1 - core), points, fine_assign, fine_start, None, None
    )
    sibling = swap(sent, CORE)
    held, seen_first = first_pass(
        info_of(core), points, fine_assign, fine_start, squares, seen
    )

    def exchange(held, sibling):
        outgoing = [slot_rows(held, s) + slot_rows(sibling, s) for s in range(1, SLOTS)]
        over_xy = swap(outgoing[2], ACROSS_X | ACROSS_Y)
        return swap(outgoing[0], ACROSS_X), swap(outgoing[1], ACROSS_Y), over_xy

    incoming = exchange(held, sibling)
    owner = lax.dynamic_index_in_dim(owners, core, 0, keepdims=False)
    fine, coarse_part = refine_half(held, sibling, *incoming, owner, coarse)
    own = spread(fine)
    coarse_part = coarse_part + swap(coarse_part, CORE)
    other = [swap(piece, CORE) for piece in own]

    second_pass = functools.partial(
        run_pass, pass_index=1, pieces=tuple(range(SLOTS)), rows=rows
    )
    own[0], coarse_part = lax.optimization_barrier((own[0], coarse_part))
    sent, seen = second_pass(info_of(core), points, fine_assign, own, squares, None)
    sibling = swap(sent, CORE)
    held, seen_second = second_pass(
        info_of(1 - core), points, fine_assign, other, squares, seen
    )
    incoming = exchange(held, sibling)
    coarse = renew(coarse, add_over_cen(coarse_part))

    seen = jnp.concatenate([seen_first, seen_second], 0)
    others = [swap(seen, bit, "cen") for bit in range(1, lax.axis_size("cen"))]
    seen = functools.reduce(jnp.minimum, others, seen)
    gaps = (seen[0::2] - seen[1::2]) / math.sqrt(width)

    owner = lax.dynamic_index_in_dim(owners, 1 - core, 0, keepdims=False)
    owner, gaps = lax.optimization_barrier((owner, gaps))
    fine, coarse_part = refine_half(held, sibling, *incoming, owner, coarse)
    own = spread(fine)
    coarse_part = coarse_part + swap(coarse_part, CORE)
    coarse = renew(coarse, add_over_cen(coarse_part))
    other = [swap(piece, CORE) for piece in own]
    fine_now, coarse_now = place(info_of(1 - core), own, other, spread(coarse))
    return (fine_now, coarse_now, gaps)


def solution(mesh):
    placed = (P("pts", None), P(None, "pts"), P("cen", None), P(), P("cen"))

    def on_device(points, fine_assign, fine_start, coarse_start, coarse_assign):
        count, width = points.shape
        local_count = fine_start.shape[0]
        centres = mesh.shape["cen"]
        fits = (
            mesh.shape["pts"] == 2 * SLOTS
            and centres & (centres - 1) == 0
            and width // SLOTS == local_count // 2
            and (width // SLOTS) % 128 == 0
            and count % 1024 == 0
        )
        plan = on_device_paired if fits else on_device_any
        return plan(points, fine_assign, fine_start, coarse_start, coarse_assign)

    return jax.shard_map(
        on_device,
        mesh=mesh,
        in_specs=placed,
        out_specs=(P("cen", None), P(), P(None, "pts")),
        check_vma=False,
    )
```

```python
import functools
import math

import jax
import jax.numpy as jnp
from jax import lax
from jax.experimental import pallas as pl
from jax.experimental.pallas import tpu as pltpu
from jax.sharding import PartitionSpec as P

NC = 64
PASSES = 2
FAR = 3.0e38

prior_weight = 4.0
HIGHEST = lax.Precision.HIGHEST


def refine(totals, counts, coarse_cols, coarse_table):
    lookup = jnp.dot(coarse_table, coarse_cols, precision=HIGHEST)
    fine_next = (totals + prior_weight * lookup) / (counts + prior_weight)[:, None]
    coarse_part = lax.dot_general(
        coarse_table,
        counts[:, None] * fine_next,
        (((0,), (0,)), ((), ())),
        precision=HIGHEST,
    )
    coarse_weight = jnp.sum(coarse_table * counts[:, None], axis=0)
    return (fine_next, coarse_part, coarse_weight)


def on_device_any(points, fine_assign, fine_start, coarse_start, coarse_assign):
    width = points.shape[1]
    local_count = fine_start.shape[0]
    offset = lax.axis_index("cen") * local_count
    columns = jnp.arange(local_count, dtype=jnp.int32)
    coarse_table = (coarse_assign[:, None] == jnp.arange(NC, dtype=jnp.int32)[None, :]).astype(
        jnp.float32
    )
    point_values = points.astype(jnp.float32)
    squares = jnp.sum(point_values * point_values, axis=1)
    fine_now = fine_start
    coarse_now = coarse_start
    gap_rows = []
    for pass_index in range(PASSES):
        member = (fine_assign[pass_index] - offset)[:, None] == columns[None, :]
        products = jnp.dot(
            points, fine_now.astype(jnp.bfloat16).T, preferred_element_type=jnp.float32
        )
        energy = jnp.sum(fine_now * fine_now, axis=1)[None, :] - 2.0 * products
        picked_local = jnp.sum(jnp.where(member, energy, 0.0), axis=1)
        nearest_local = jnp.min(energy, axis=1)
        picked = lax.psum(picked_local, "cen")
        nearest = lax.pmin(nearest_local, "cen")
        gap_rows.append((picked - nearest) / math.sqrt(width))
        weights = 1.0 / (1.0 + (squares + picked) / width)
        scaled = (point_values * weights[:, None]).astype(jnp.bfloat16)
        partial_sums = lax.dot_general(
            member.astype(jnp.bfloat16),
            scaled,
            (((0,), (0,)), ((), ())),
            preferred_element_type=jnp.float32,
        )
        partial_weights = jnp.sum(jnp.where(member, weights[:, None], 0.0), axis=0)
        share_width = width // lax.axis_size("pts")
        start = lax.axis_index("pts") * share_width
        shares = lax.psum_scatter(partial_sums, "pts", scatter_dimension=1, tiled=True)
        counts = lax.psum(partial_weights, "pts")
        coarse_cols = lax.dynamic_slice_in_dim(coarse_now, start, share_width, 1)
        fine_share, coarse_part, coarse_weight = refine(shares, counts, coarse_cols, coarse_table)
        coarse_sum, coarse_count = lax.psum((coarse_part, coarse_weight), "cen")
        coarse_share = (coarse_sum + prior_weight * coarse_cols) / (coarse_count + prior_weight)[
            :, None
        ]
        fine_now, coarse_now = (
            lax.all_gather(fine_share, "pts", axis=1, tiled=True),
            lax.all_gather(coarse_share, "pts", axis=1, tiled=True),
        )
    return (fine_now, coarse_now, jnp.stack(gap_rows))


CORE, ACROSS_X, ACROSS_Y = 1, 2, 4
SLOTS = 4
TAIL = 8


def swap(value, bit, axis="pts"):
    size = lax.axis_size(axis)
    return lax.ppermute(value, axis, [(i, i ^ bit) for i in range(size)])


def pass_body(info, points, assign, *refs, pass_index, pieces, first, chained, tile):
    refs = list(refs)
    fine_refs = [refs.pop(0) for _ in range(SLOTS if pieces else 1)]
    squares_in = None if first else refs.pop(0)
    seen_in = refs.pop(0) if chained else None
    payload, seen = refs.pop(0), refs.pop(0)
    squares_out = refs.pop(0) if first else None
    kept, arrived, low, sums, tallies, even, odd = refs
    rows, width = low.shape
    block_width = width // SLOTS
    base = info[2]
    tiles = points.shape[0] // tile

    def span(i):
        return pl.ds(pl.multiple_of(i * tile, tile), tile)

    def load(i):
        return pltpu.make_async_copy(points.at[span(i)], kept.at[span(i)], arrived.at[i])

    @pl.loop(0, tiles)
    def _(i):
        load(i).start()

    norm = jnp.zeros((rows, 1), jnp.float32)
    for slot, ref in enumerate(fine_refs):
        block = ref[...]
        norm = norm + jnp.sum(block * block, axis=1, keepdims=True)
        wide = block.shape[1]
        low[:, slot * wide : (slot + 1) * wide] = (-2.0 * block).astype(jnp.bfloat16)
    sums[...] = jnp.zeros_like(sums)
    tallies[...] = jnp.zeros_like(tallies)

    def multiply(i, target):
        target[...] = lax.dot_general(
            low[...], kept[span(i), :], (((1,), (1,)), ((), ())), preferred_element_type=jnp.float32
        )

    def collect(i, products):
        energy = norm + products[...]
        chosen = assign[pass_index : pass_index + 1, span(i)] - base
        member = lax.broadcasted_iota(jnp.int32, energy.shape, 0) == chosen
        picked = jnp.sum(jnp.where(member, energy, 0.0), axis=0, keepdims=True)
        nearest = jnp.min(energy, axis=0, keepdims=True)
        inside = (chosen >= 0) & (chosen < rows)
        picked_seen = jnp.where(inside, picked, FAR)
        if chained:
            picked_seen = jnp.minimum(picked_seen, seen_in[0:1, span(i)])
            nearest = jnp.minimum(nearest, seen_in[1:2, span(i)])
        seen[0:1, span(i)] = picked_seen
        seen[1:2, span(i)] = nearest
        if first:
            folded = jnp.zeros((tile, 128), jnp.float32)
            for lane in range(0, width, 128):
                values = kept[span(i), lane : lane + 128].astype(jnp.float32)
                folded = folded + values * values
            squares = lax.dot_general(
                jnp.ones((8, 128), jnp.float32),
                folded,
                (((1,), (1,)), ((), ())),
                precision=HIGHEST,
                preferred_element_type=jnp.float32,
            )[:1]
            squares_out[0:1, span(i)] = squares
        else:
            squares = squares_in[0:1, span(i)]
        weights = 1.0 / (1.0 + (squares + picked) / width)
        weighted = jnp.where(member, weights, 0.0)
        tally = tallies[...]
        for lane in range(0, tile, 128):
            tally = tally + weighted[:, lane : lane + 128]
        tallies[...] = tally
        sums[...] += jnp.dot(
            weighted.astype(jnp.bfloat16), kept[span(i), :], preferred_element_type=jnp.float32
        )

    load(0).wait()
    multiply(0, even)

    @pl.loop(0, tiles // 2)
    def _(pair):
        i = 2 * pair
        load(i + 1).wait()

        @pl.when(i + 2 < tiles)
        def _():
            load(i + 2).wait()

        multiply(i + 1, odd)
        collect(i, even)
        multiply(jnp.minimum(i + 2, tiles - 1), even)
        collect(i + 1, odd)

    counts = jnp.broadcast_to(jnp.sum(tallies[...].T, axis=0, keepdims=True), (TAIL, rows))
    for slot in range(SLOTS):
        payload[slot, :rows, :] = sums[:, slot * block_width : (slot + 1) * block_width]
        payload[slot, rows:, :] = counts


def run_pass(info, points, fine_assign, fine, squares, seen, *, pass_index, pieces, rows):
    count, width = points.shape
    block_width = width // SLOTS
    tile = 512
    first = squares is None
    chained = seen is not None
    full = lambda *shape: pl.BlockSpec(shape, lambda i, info: (0,) * len(shape))
    in_specs = [pl.BlockSpec(memory_space=pl.ANY), full(PASSES, count)]
    args = [points, fine_assign]
    if pieces:
        for slot in range(SLOTS):
            in_specs.append(
                pl.BlockSpec((None, rows, block_width), lambda i, info, slot=slot: (slot, 0, 0))
            )
            args.append(fine)
    else:
        in_specs.append(pl.BlockSpec((rows, width), lambda i, info: (info[1], 0)))
        args.append(fine)
    if not first:
        in_specs.append(full(1, count))
        args.append(squares)
    if chained:
        in_specs.append(full(2, count))
        args.append(seen)
    shapes = [(SLOTS, rows + TAIL, block_width), (2, count)]
    if first:
        shapes.append((1, count))
    body = functools.partial(
        pass_body,
        pass_index=pass_index,
        pieces=pieces,
        first=first,
        chained=chained,
        tile=tile,
    )
    return pl.pallas_call(
        body,
        out_shape=[jax.ShapeDtypeStruct(shape, jnp.float32) for shape in shapes],
        grid_spec=pltpu.PrefetchScalarGridSpec(
            num_scalar_prefetch=1,
            grid=(1,),
            in_specs=in_specs,
            out_specs=[full(*shape) for shape in shapes],
            scratch_shapes=[
                pltpu.VMEM((count, width), jnp.bfloat16),
                pltpu.SemaphoreType.DMA((count // tile,)),
                pltpu.VMEM((rows, width), jnp.bfloat16),
                pltpu.VMEM((rows, width), jnp.float32),
                pltpu.VMEM((rows, 128), jnp.float32),
                pltpu.VMEM((rows, tile), jnp.float32),
                pltpu.VMEM((rows, tile), jnp.float32),
            ],
        ),
        compiler_params=pltpu.CompilerParams(vmem_limit_bytes=56 * 2**20),
        cost_estimate=pl.CostEstimate(
            flops=4 * rows * count * width, bytes_accessed=2 * count * width, transcendentals=0
        ),
        name=f"energies_and_sums_{pass_index}{int(chained)}",
    )(info, *args)


def refine_body(received, owner, coarse, fine, coarse_part):
    rows = owner.shape[1]
    total = (received[0] + received[1]) + (received[2] + received[3])
    totals, counts_row = total[:rows], total[rows:]
    counts = jnp.broadcast_to(counts_row[:1], (128, rows)).T[:, :1]
    table = (
        lax.broadcasted_iota(jnp.int32, (NC, rows), 0) == owner[...]
    ).astype(jnp.float32)
    lookup = lax.dot_general(
        table,
        coarse[...],
        (((0,), (0,)), ((), ())),
        precision=HIGHEST,
        preferred_element_type=jnp.float32,
    )
    new = (totals + prior_weight * lookup) / (counts + prior_weight)
    for slot in range(SLOTS):
        fine[slot] = new
    coarse_part[:NC, :] = jnp.dot(
        table, counts * new, precision=HIGHEST, preferred_element_type=jnp.float32
    )
    coarse_part[NC:, :] = jnp.zeros((TAIL, coarse_part.shape[1]), jnp.float32)
    coarse_part[NC:, :NC] = lax.dot_general(
        counts_row,
        table,
        (((1,), (1,)), ((), ())),
        precision=HIGHEST,
        preferred_element_type=jnp.float32,
    )


def refine_half(received, owner, coarse):
    block_width = coarse.shape[1]
    rows = owner.shape[1]
    full = lambda *shape: pl.BlockSpec(shape, lambda i: (0,) * len(shape))
    return pl.pallas_call(
        refine_body,
        grid=(1,),
        out_shape=[
            jax.ShapeDtypeStruct((SLOTS, rows, block_width), jnp.float32),
            jax.ShapeDtypeStruct((NC + TAIL, block_width), jnp.float32),
        ],
        in_specs=[full(*received.shape), full(1, rows), full(NC, block_width)],
        out_specs=[full(SLOTS, rows, block_width), full(NC + TAIL, block_width)],
        compiler_params=pltpu.CompilerParams(vmem_limit_bytes=16 * 2**20),
        name="refine_half",
    )(received, owner, coarse)


def trade(value):
    size = lax.axis_size("pts")
    groups = [list(range(core, size, 2)) for core in range(2)]
    return lax.all_to_all(value, "pts", 0, 0, axis_index_groups=groups)


def add_over_cen(value):
    others = [swap(value, bit, "cen") for bit in range(1, lax.axis_size("cen"))]
    return functools.reduce(jnp.add, others, value)


def place_body(info, own, other, coarse, fine_out, coarse_out):
    block_width = own.shape[2]

    def put(pieces, target):
        for slot in range(SLOTS):
            target[:, slot * block_width : (slot + 1) * block_width] = pieces[slot]

    @pl.when(pl.program_id(0) == 0)
    def _():
        put(own, fine_out)
        put(coarse, coarse_out)

    @pl.when(pl.program_id(0) == 1)
    def _():
        put(other, fine_out)


def place(info, own, other, coarse):
    _, rows, block_width = own.shape
    width = SLOTS * block_width
    full = lambda *shape: pl.BlockSpec(shape, lambda i, info: (0,) * len(shape))
    return pl.pallas_call(
        place_body,
        out_shape=[
            jax.ShapeDtypeStruct((2 * rows, width), jnp.float32),
            jax.ShapeDtypeStruct((NC, width), jnp.float32),
        ],
        grid_spec=pltpu.PrefetchScalarGridSpec(
            num_scalar_prefetch=1,
            grid=(2,),
            in_specs=[full(*own.shape), full(*other.shape), full(*coarse.shape)],
            out_specs=[
                pl.BlockSpec((rows, width), lambda i, info: (info[1] ^ i, 0)),
                full(NC, width),
            ],
        ),
        compiler_params=pltpu.CompilerParams(vmem_limit_bytes=24 * 2**20),
        name="place_blocks",
    )(info, own, other, coarse)


def on_device_paired(points, fine_assign, fine_start, coarse_start, coarse_assign):
    width = points.shape[1]
    local_count = fine_start.shape[0]
    rows = local_count // 2
    block_width = width // SLOTS
    offset = lax.axis_index("cen") * local_count
    me = lax.axis_index("pts")
    core, here = me & 1, me >> 1
    owners = coarse_assign.reshape(2, 1, rows)
    info_of = lambda half: jnp.stack([here, half, offset + half * rows]).astype(jnp.int32)
    coarse = lax.dynamic_slice_in_dim(coarse_start, here * block_width, block_width, 1)

    def renew(coarse, coarse_sum):
        return (coarse_sum[:NC] + prior_weight * coarse) / (
            coarse_sum[NC, :NC] + prior_weight
        )[:, None]

    first_pass = functools.partial(run_pass, pass_index=0, pieces=None, rows=rows)
    sent, seen, squares = first_pass(
        info_of(1 - core), points, fine_assign, fine_start, None, None
    )
    sibling = swap(sent, CORE)
    held, seen_first = first_pass(
        info_of(core), points, fine_assign, fine_start, squares, seen
    )

    received = trade(held + sibling)
    owner = lax.dynamic_index_in_dim(owners, core, 0, keepdims=False)
    fine, coarse_part = refine_half(received, owner, coarse)
    own = trade(fine)
    coarse_part = coarse_part + swap(coarse_part, CORE)
    other = swap(own, CORE)

    second_pass = functools.partial(run_pass, pass_index=1, pieces=True, rows=rows)
    own, coarse_part = lax.optimization_barrier((own, coarse_part))
    sent, seen = second_pass(info_of(core), points, fine_assign, own, squares, None)
    sibling = swap(sent, CORE)
    held, seen_second = second_pass(
        info_of(1 - core), points, fine_assign, other, squares, seen
    )
    received = trade(held + sibling)
    coarse = renew(coarse, add_over_cen(coarse_part))

    owner = lax.dynamic_index_in_dim(owners, 1 - core, 0, keepdims=False)
    fine, coarse_part = refine_half(received, owner, coarse)
    own = trade(fine)
    coarse_part = coarse_part + swap(coarse_part, CORE)
    coarse = renew(coarse, add_over_cen(coarse_part))
    other = swap(own, CORE)
    coarse = trade(jnp.broadcast_to(coarse, (SLOTS,) + coarse.shape))
    fine_now, coarse_now = place(info_of(1 - core), own, other, coarse)

    seen = jnp.concatenate([seen_first, seen_second], 0)
    others = [swap(seen, bit, "cen") for bit in range(1, lax.axis_size("cen"))]
    seen = functools.reduce(jnp.minimum, others, seen)
    gaps = (seen[0::2] - seen[1::2]) / math.sqrt(width)
    return (fine_now, coarse_now, gaps)


def solution(mesh):
    placed = (P("pts", None), P(None, "pts"), P("cen", None), P(), P("cen"))

    def on_device(points, fine_assign, fine_start, coarse_start, coarse_assign):
        count, width = points.shape
        local_count = fine_start.shape[0]
        centres = mesh.shape["cen"]
        fits = (
            mesh.shape["pts"] == 2 * SLOTS
            and centres & (centres - 1) == 0
            and width // SLOTS == local_count // 2
            and (width // SLOTS) % 128 == 0
            and count % 1024 == 0
        )
        plan = on_device_paired if fits else on_device_any
        return plan(points, fine_assign, fine_start, coarse_start, coarse_assign)

    return jax.shard_map(
        on_device,
        mesh=mesh,
        in_specs=placed,
        out_specs=(P("cen", None), P(), P(None, "pts")),
        check_vma=False,
    )
```

```python
import functools
import math

import jax
import jax.numpy as jnp
from jax import lax
from jax.experimental import pallas as pl
from jax.experimental.pallas import tpu as pltpu
from jax.sharding import PartitionSpec as P

NC = 64
PASSES = 2
FAR = 3.0e38

prior_weight = 4.0
HIGHEST = lax.Precision.HIGHEST


def refine(totals, counts, coarse_cols, coarse_table):
    lookup = jnp.dot(coarse_table, coarse_cols, precision=HIGHEST)
    fine_next = (totals + prior_weight * lookup) / (counts + prior_weight)[:, None]
    coarse_part = lax.dot_general(
        coarse_table,
        counts[:, None] * fine_next,
        (((0,), (0,)), ((), ())),
        precision=HIGHEST,
    )
    coarse_weight = jnp.sum(coarse_table * counts[:, None], axis=0)
    return (fine_next, coarse_part, coarse_weight)


def on_device_any(points, fine_assign, fine_start, coarse_start, coarse_assign):
    width = points.shape[1]
    local_count = fine_start.shape[0]
    offset = lax.axis_index("cen") * local_count
    columns = jnp.arange(local_count, dtype=jnp.int32)
    coarse_table = (coarse_assign[:, None] == jnp.arange(NC, dtype=jnp.int32)[None, :]).astype(
        jnp.float32
    )
    point_values = points.astype(jnp.float32)
    squares = jnp.sum(point_values * point_values, axis=1)
    fine_now = fine_start
    coarse_now = coarse_start
    gap_rows = []
    for pass_index in range(PASSES):
        member = (fine_assign[pass_index] - offset)[:, None] == columns[None, :]
        products = jnp.dot(
            points, fine_now.astype(jnp.bfloat16).T, preferred_element_type=jnp.float32
        )
        energy = jnp.sum(fine_now * fine_now, axis=1)[None, :] - 2.0 * products
        picked_local = jnp.sum(jnp.where(member, energy, 0.0), axis=1)
        nearest_local = jnp.min(energy, axis=1)
        picked = lax.psum(picked_local, "cen")
        nearest = lax.pmin(nearest_local, "cen")
        gap_rows.append((picked - nearest) / math.sqrt(width))
        weights = 1.0 / (1.0 + (squares + picked) / width)
        scaled = (point_values * weights[:, None]).astype(jnp.bfloat16)
        partial_sums = lax.dot_general(
            member.astype(jnp.bfloat16),
            scaled,
            (((0,), (0,)), ((), ())),
            preferred_element_type=jnp.float32,
        )
        partial_weights = jnp.sum(jnp.where(member, weights[:, None], 0.0), axis=0)
        share_width = width // lax.axis_size("pts")
        start = lax.axis_index("pts") * share_width
        shares = lax.psum_scatter(partial_sums, "pts", scatter_dimension=1, tiled=True)
        counts = lax.psum(partial_weights, "pts")
        coarse_cols = lax.dynamic_slice_in_dim(coarse_now, start, share_width, 1)
        fine_share, coarse_part, coarse_weight = refine(shares, counts, coarse_cols, coarse_table)
        coarse_sum, coarse_count = lax.psum((coarse_part, coarse_weight), "cen")
        coarse_share = (coarse_sum + prior_weight * coarse_cols) / (coarse_count + prior_weight)[
            :, None
        ]
        fine_now, coarse_now = (
            lax.all_gather(fine_share, "pts", axis=1, tiled=True),
            lax.all_gather(coarse_share, "pts", axis=1, tiled=True),
        )
    return (fine_now, coarse_now, jnp.stack(gap_rows))


CORE, ACROSS_X, ACROSS_Y = 1, 2, 4
SLOTS = 4
TAIL = 8


def swap(value, bit, axis="pts"):
    size = lax.axis_size(axis)
    return lax.ppermute(value, axis, [(i, i ^ bit) for i in range(size)])


def full(*shape):
    return pl.BlockSpec(shape, lambda i, info: (0,) * len(shape))


def as_column(row, rows):
    return jnp.broadcast_to(row, (128, rows)).T


def pass_body(info, points, assign, fine, *refs, pass_index, slots, first, chained, tile):
    refs = list(refs)
    squares_in = None if first else refs.pop(0)
    seen_in = refs.pop(0) if chained else None
    payload, seen = refs.pop(0), refs.pop(0)
    squares_out, kept = (refs.pop(0), refs.pop(0)) if first else (None, points)
    low, sums, tallies, even, odd, scaled = refs[:6]
    rows, width = low.shape
    block_width = width // SLOTS
    here, base = info[0], info[2]
    tiles = points.shape[0] // tile

    def span(i):
        return pl.ds(pl.multiple_of(i * tile, tile), tile)

    def column_of(slot):
        return pl.ds(pl.multiple_of((here ^ slot) * block_width, block_width), block_width)

    def load(i):
        return pltpu.make_async_copy(points.at[span(i)], kept.at[span(i)], refs[6].at[i])

    if first:

        @pl.loop(0, tiles)
        def _(i):
            load(i).start()

    if slots:
        norm = jnp.zeros((rows, 1), jnp.float32)
        for slot in range(SLOTS):
            block = fine[slot]
            norm = norm + jnp.sum(block * block, axis=1, keepdims=True)
            low[:, column_of(slot)] = (-2.0 * block).astype(jnp.bfloat16)
    else:
        block = fine[...]
        norm = jnp.sum(block * block, axis=1, keepdims=True)
        low[...] = (-2.0 * block).astype(jnp.bfloat16)
    sums[...] = jnp.zeros_like(sums)
    tallies[...] = jnp.zeros_like(tallies)

    def multiply(i, target):
        target[...] = lax.dot_general(
            low[...], kept[span(i), :], (((1,), (1,)), ((), ())), preferred_element_type=jnp.float32
        )

    def collect(i, products):
        energy = norm + products[...]
        chosen = assign[pass_index : pass_index + 1, span(i)] - base
        member = lax.broadcasted_iota(jnp.int32, energy.shape, 0) == chosen
        picked = jnp.sum(jnp.where(member, energy, 0.0), axis=0, keepdims=True)
        nearest = jnp.min(energy, axis=0, keepdims=True)
        inside = (chosen >= 0) & (chosen < rows)
        picked_seen = jnp.where(inside, picked, FAR)
        if chained:
            picked_seen = jnp.minimum(picked_seen, seen_in[0:1, span(i)])
            nearest = jnp.minimum(nearest, seen_in[1:2, span(i)])
        seen[0:1, span(i)] = picked_seen
        seen[1:2, span(i)] = nearest
        if first:
            folded = jnp.zeros((tile, 128), jnp.float32)
            for lane in range(0, width, 128):
                values = kept[span(i), lane : lane + 128].astype(jnp.float32)
                folded = folded + values * values
            squares = jnp.sum(folded.T, axis=0, keepdims=True)
            squares_out[0:1, span(i)] = squares
        else:
            squares = squares_in[0:1, span(i)]
        weights = 1.0 / (1.0 + (squares + picked) / width)
        weighted = jnp.where(member, weights, 0.0)
        tally = tallies[...]
        for lane in range(0, tile, 128):
            tally = tally + weighted[:, lane : lane + 128]
        tallies[...] = tally
        factor = as_column(weights, tile)
        for lane in range(0, width, 128):
            values = kept[span(i), lane : lane + 128].astype(jnp.float32)
            scaled[:, lane : lane + 128] = (values * factor).astype(jnp.bfloat16)
        sums[...] += jnp.dot(
            member.astype(jnp.float32).astype(jnp.bfloat16),
            scaled[...],
            preferred_element_type=jnp.float32,
        )

    if first:
        load(0).wait()
    multiply(0, even)

    @pl.loop(0, tiles // 2)
    def _(pair):
        i = 2 * pair
        if first:
            load(i + 1).wait()

            @pl.when(i + 2 < tiles)
            def _():
                load(i + 2).wait()

        multiply(i + 1, odd)
        collect(i, even)
        multiply(jnp.minimum(i + 2, tiles - 1), even)
        collect(i + 1, odd)

    counts = jnp.broadcast_to(jnp.sum(tallies[...].T, axis=0, keepdims=True), (TAIL, rows))
    for slot in range(SLOTS):
        payload[slot, :rows, :] = sums[:, column_of(slot)]
        payload[slot, rows:, :] = counts


def run_pass(info, points, fine_assign, fine, squares, seen, *, pass_index, slots, rows):
    count, width = points.shape
    block_width = width // SLOTS
    tile = 512
    first = squares is None
    chained = seen is not None
    whole = pl.BlockSpec(memory_space=pltpu.VMEM)
    in_specs = [pl.BlockSpec(memory_space=pl.ANY) if first else whole, full(PASSES, count)]
    args = [
        pltpu.with_memory_space_constraint(points, pltpu.HBM if first else pltpu.VMEM),
        fine_assign,
    ]
    if slots:
        in_specs.append(full(SLOTS, rows, block_width))
    else:
        in_specs.append(pl.BlockSpec((rows, width), lambda i, info: (info[1], 0)))
    args.append(fine)
    if not first:
        in_specs.append(full(1, count))
        args.append(squares)
    if chained:
        in_specs.append(full(2, count))
        args.append(seen)
    shapes = [(SLOTS, rows + TAIL, block_width), (2, count)] + ([(1, count)] if first else [])
    out_shape = [jax.ShapeDtypeStruct(shape, jnp.float32) for shape in shapes]
    out_specs = [full(*shape) for shape in shapes]
    scratch = [
        pltpu.VMEM((rows, width), jnp.bfloat16),
        pltpu.VMEM((rows, width), jnp.float32),
        pltpu.VMEM((rows, 128), jnp.float32),
        pltpu.VMEM((rows, tile), jnp.float32),
        pltpu.VMEM((rows, tile), jnp.float32),
        pltpu.VMEM((tile, width), jnp.bfloat16),
    ]
    if first:
        out_shape.append(pltpu.VMEM(points.shape, points.dtype))
        out_specs.append(whole)
        scratch.append(pltpu.SemaphoreType.DMA((count // tile,)))
    body = functools.partial(
        pass_body,
        pass_index=pass_index,
        slots=slots,
        first=first,
        chained=chained,
        tile=tile,
    )
    return pl.pallas_call(
        body,
        out_shape=out_shape,
        grid_spec=pltpu.PrefetchScalarGridSpec(
            num_scalar_prefetch=1,
            grid=(1,),
            in_specs=in_specs,
            out_specs=out_specs,
            scratch_shapes=scratch,
        ),
        compiler_params=pltpu.CompilerParams(vmem_limit_bytes=24 * 2**20),
        cost_estimate=pl.CostEstimate(
            flops=4 * rows * count * width, bytes_accessed=2 * count * width, transcendentals=0
        ),
        name=f"energies_and_sums_{pass_index}{int(chained)}",
    )(info, *args)


def refine_body(info, own, sibling, over_x, over_y, over_xy, owner, coarse, fine, part):
    rows = owner.shape[1]
    received = own[...] + sibling[...] + over_x[...] + over_y[...] + over_xy[...]
    totals, counts_row = received[:rows], received[rows:]
    counts = as_column(counts_row[:1], rows)[:, :1]
    table = (
        lax.broadcasted_iota(jnp.int32, (NC, rows), 0) == owner[...]
    ).astype(jnp.float32)
    lookup = lax.dot_general(
        table,
        coarse[...],
        (((0,), (0,)), ((), ())),
        precision=HIGHEST,
        preferred_element_type=jnp.float32,
    )
    new = (totals + prior_weight * lookup) / (counts + prior_weight)
    fine[...] = new
    prior = jnp.where(info[0] == 0, prior_weight, 0.0)
    part[:NC, :] = prior * coarse[...] + jnp.dot(
        table, counts * new, precision=HIGHEST, preferred_element_type=jnp.float32
    )
    part[NC:, :] = jnp.zeros((TAIL, part.shape[1]), jnp.float32)
    part[NC:, :NC] = prior + lax.dot_general(
        counts_row,
        table,
        (((1,), (1,)), ((), ())),
        precision=HIGHEST,
        preferred_element_type=jnp.float32,
    )


def refine_half(info, own, sibling, over_x, over_y, over_xy, owner, coarse):
    block_width = coarse.shape[1]
    rows = owner.shape[1]
    slot = pl.BlockSpec((None, rows + TAIL, block_width), lambda i, info: (0, 0, 0))
    return pl.pallas_call(
        refine_body,
        out_shape=[
            jax.ShapeDtypeStruct((rows, block_width), jnp.float32),
            jax.ShapeDtypeStruct((NC + TAIL, block_width), jnp.float32),
        ],
        grid_spec=pltpu.PrefetchScalarGridSpec(
            num_scalar_prefetch=1,
            grid=(1,),
            in_specs=[slot] * 2
            + [full(rows + TAIL, block_width)] * 3
            + [full(1, rows), full(NC, block_width)],
            out_specs=[full(rows, block_width), full(NC + TAIL, block_width)],
        ),
        compiler_params=pltpu.CompilerParams(vmem_limit_bytes=16 * 2**20),
        name="refine_half",
    )(info, own, sibling, over_x, over_y, over_xy, owner, coarse)


def spread(value):
    corner = swap(value, ACROSS_X | ACROSS_Y)
    return [value, swap(value, ACROSS_X), swap(value, ACROSS_Y), corner]


def over_cen(value, combine):
    others = [swap(value, bit, "cen") for bit in range(1, lax.axis_size("cen"))]
    return functools.reduce(combine, others, value)


def place_body(info, own, other, fine_out, coarse_out):
    block_width = own.shape[2]
    rows = fine_out.shape[0]
    here = info[0]

    def put(pieces):
        for slot in range(SLOTS):
            column = pl.multiple_of((here ^ slot) * block_width, block_width)
            fine_out[:, pl.ds(column, block_width)] = pieces[slot, :rows, :]

    @pl.when(pl.program_id(0) == 0)
    def _():
        put(own)
        weight = own[0, rows + NC : rows + NC + 1, :128] + other[0, rows + NC : rows + NC + 1, :128]
        weight = as_column(weight, 128)[:NC, :1]
        for slot in range(SLOTS):
            column = pl.multiple_of((here ^ slot) * block_width, block_width)
            total = own[slot, rows : rows + NC, :] + other[slot, rows : rows + NC, :]
            coarse_out[:, pl.ds(column, block_width)] = total / weight

    @pl.when(pl.program_id(0) == 1)
    def _():
        put(other)


def place(info, own, other, rows):
    _, _, block_width = own.shape
    width = SLOTS * block_width
    return pl.pallas_call(
        place_body,
        out_shape=[
            jax.ShapeDtypeStruct((2 * rows, width), jnp.float32),
            jax.ShapeDtypeStruct((NC, width), jnp.float32),
        ],
        grid_spec=pltpu.PrefetchScalarGridSpec(
            num_scalar_prefetch=1,
            grid=(2,),
            in_specs=[full(*own.shape), full(*other.shape)],
            out_specs=[
                pl.BlockSpec((rows, width), lambda i, info: (info[1] ^ i, 0)),
                full(NC, width),
            ],
        ),
        compiler_params=pltpu.CompilerParams(vmem_limit_bytes=24 * 2**20),
        name="place_blocks",
    )(info, own, other)


def on_device_paired(points, fine_assign, fine_start, coarse_start, coarse_assign):
    width = points.shape[1]
    local_count = fine_start.shape[0]
    rows = local_count // 2
    block_width = width // SLOTS
    cen = lax.axis_index("cen")
    offset = cen * local_count
    me = lax.axis_index("pts")
    core, here = me & 1, me >> 1
    owners = coarse_assign.reshape(2, 1, rows)
    owner_of = lambda half: lax.dynamic_index_in_dim(owners, half, 0, keepdims=False)
    info_of = lambda half: jnp.stack([here, half, offset + half * rows]).astype(jnp.int32)
    group_place = jnp.stack([cen * 2 + core]).astype(jnp.int32)
    coarse = lax.dynamic_slice_in_dim(coarse_start, here * block_width, block_width, 1)

    def exchange(held, sibling):
        outgoing = [held[s] + sibling[s] for s in range(1, SLOTS)]
        over_xy = swap(outgoing[2], ACROSS_X | ACROSS_Y)
        return swap(outgoing[0], ACROSS_X), swap(outgoing[1], ACROSS_Y), over_xy

    first_pass = functools.partial(run_pass, pass_index=0, slots=False, rows=rows)
    sent, seen, squares, kept = first_pass(
        info_of(1 - core), points, fine_assign, fine_start, None, None
    )
    sibling = swap(sent, CORE)
    held, seen_first = first_pass(
        info_of(core), kept, fine_assign, fine_start, squares, seen
    )
    incoming = exchange(held, sibling)
    fine, part = refine_half(group_place, held, sibling, *incoming, owner_of(core), coarse)
    own = jnp.stack(spread(fine))
    part = part + swap(part, CORE)

    second_pass = functools.partial(run_pass, pass_index=1, slots=True, rows=rows)
    own, part = lax.optimization_barrier((own, part))
    other = swap(own, CORE)
    sent, seen = second_pass(info_of(core), kept, fine_assign, own, squares, None)
    sibling = swap(sent, CORE)
    held, seen_second = second_pass(info_of(1 - core), kept, fine_assign, other, squares, seen)
    incoming = exchange(held, sibling)

    seen = jnp.concatenate([seen_first, seen_second], 0)
    cen_size = lax.axis_size("cen")
    folded = jnp.concatenate([part, seen.reshape(-1, block_width)], 0)
    gathered = [folded] + [swap(folded, bit, "cen") for bit in range(1, cen_size)]
    part = functools.reduce(jnp.add, [each[: NC + TAIL] for each in gathered])
    seen = functools.reduce(jnp.minimum, [each[NC + TAIL :] for each in gathered])
    seen = seen.reshape(2, 2, -1)
    gaps = (seen[:, 0] - seen[:, 1]) / math.sqrt(width)
    coarse = part[:NC] / part[NC, :NC][:, None]

    fine, part = refine_half(
        group_place, held, sibling, *incoming, owner_of(1 - core), coarse
    )
    own = spread(fine)
    parts = spread(over_cen(part, jnp.add))
    own = jnp.stack([jnp.concatenate(pair, 0) for pair in zip(own, parts)])
    other = swap(own, CORE)
    fine_now, coarse_now = place(info_of(1 - core), own, other, rows)
    return (fine_now, coarse_now, gaps)


def solution(mesh):
    placed = (P("pts", None), P(None, "pts"), P("cen", None), P(), P("cen"))

    def on_device(points, fine_assign, fine_start, coarse_start, coarse_assign):
        count, width = points.shape
        local_count = fine_start.shape[0]
        centres = mesh.shape["cen"]
        fits = (
            mesh.shape["pts"] == 2 * SLOTS
            and centres & (centres - 1) == 0
            and width // SLOTS == local_count // 2
            and (width // SLOTS) % 128 == 0
            and count % 1024 == 0
        )
        plan = on_device_paired if fits else on_device_any
        return plan(points, fine_assign, fine_start, coarse_start, coarse_assign)

    return jax.shard_map(
        on_device,
        mesh=mesh,
        in_specs=placed,
        out_specs=(P("cen", None), P(), P(None, "pts")),
        check_vma=False,
    )
```

```python
import functools
import math

import jax
import jax.numpy as jnp
from jax import lax
from jax.experimental import pallas as pl
from jax.experimental.pallas import tpu as pltpu
from jax.sharding import PartitionSpec as P

NC = 64
PASSES = 2
FAR = 3.0e38

prior_weight = 4.0
HIGHEST = lax.Precision.HIGHEST


def refine(totals, counts, coarse_cols, coarse_table):
    lookup = jnp.dot(coarse_table, coarse_cols, precision=HIGHEST)
    fine_next = (totals + prior_weight * lookup) / (counts + prior_weight)[:, None]
    coarse_part = lax.dot_general(
        coarse_table,
        counts[:, None] * fine_next,
        (((0,), (0,)), ((), ())),
        precision=HIGHEST,
    )
    coarse_weight = jnp.sum(coarse_table * counts[:, None], axis=0)
    return (fine_next, coarse_part, coarse_weight)


def on_device_any(points, fine_assign, fine_start, coarse_start, coarse_assign):
    width = points.shape[1]
    local_count = fine_start.shape[0]
    offset = lax.axis_index("cen") * local_count
    columns = jnp.arange(local_count, dtype=jnp.int32)
    coarse_table = (coarse_assign[:, None] == jnp.arange(NC, dtype=jnp.int32)[None, :]).astype(
        jnp.float32
    )
    point_values = points.astype(jnp.float32)
    squares = jnp.sum(point_values * point_values, axis=1)
    fine_now = fine_start
    coarse_now = coarse_start
    gap_rows = []
    for pass_index in range(PASSES):
        member = (fine_assign[pass_index] - offset)[:, None] == columns[None, :]
        products = jnp.dot(
            points, fine_now.astype(jnp.bfloat16).T, preferred_element_type=jnp.float32
        )
        energy = jnp.sum(fine_now * fine_now, axis=1)[None, :] - 2.0 * products
        picked_local = jnp.sum(jnp.where(member, energy, 0.0), axis=1)
        nearest_local = jnp.min(energy, axis=1)
        picked = lax.psum(picked_local, "cen")
        nearest = lax.pmin(nearest_local, "cen")
        gap_rows.append((picked - nearest) / math.sqrt(width))
        weights = 1.0 / (1.0 + (squares + picked) / width)
        scaled = (point_values * weights[:, None]).astype(jnp.bfloat16)
        partial_sums = lax.dot_general(
            member.astype(jnp.bfloat16),
            scaled,
            (((0,), (0,)), ((), ())),
            preferred_element_type=jnp.float32,
        )
        partial_weights = jnp.sum(jnp.where(member, weights[:, None], 0.0), axis=0)
        share_width = width // lax.axis_size("pts")
        start = lax.axis_index("pts") * share_width
        shares = lax.psum_scatter(partial_sums, "pts", scatter_dimension=1, tiled=True)
        counts = lax.psum(partial_weights, "pts")
        coarse_cols = lax.dynamic_slice_in_dim(coarse_now, start, share_width, 1)
        fine_share, coarse_part, coarse_weight = refine(shares, counts, coarse_cols, coarse_table)
        coarse_sum, coarse_count = lax.psum((coarse_part, coarse_weight), "cen")
        coarse_share = (coarse_sum + prior_weight * coarse_cols) / (coarse_count + prior_weight)[
            :, None
        ]
        fine_now, coarse_now = (
            lax.all_gather(fine_share, "pts", axis=1, tiled=True),
            lax.all_gather(coarse_share, "pts", axis=1, tiled=True),
        )
    return (fine_now, coarse_now, jnp.stack(gap_rows))


CORE, ACROSS_X, ACROSS_Y = 1, 2, 4
SLOTS = 4
TAIL = 8


def swap(value, bit, axis="pts"):
    size = lax.axis_size(axis)
    return lax.ppermute(value, axis, [(i, i ^ bit) for i in range(size)])


def full(*shape):
    return pl.BlockSpec(shape, lambda i, info: (0,) * len(shape))


def as_column(row, rows):
    return jnp.broadcast_to(row, (128, rows)).T


def pass_body(info, points, assign, fine, *refs, pass_index, flip, stream, chained, tile):
    refs = list(refs)
    initial = pass_index == 0
    first = initial and stream
    squares_in = None if first else refs.pop(0)
    seen_in = refs.pop(0) if chained else None
    payload, seen = refs.pop(0), refs.pop(0)
    squares_out = refs.pop(0) if first else None
    kept = refs.pop(0) if stream else points
    low, tallies, even, odd, scaled, table, chosen_in, small_sems = refs[:8]
    start = refs[8] if initial else None
    point_sems = refs[-1] if stream else None
    rows, width = low.shape
    block_width = width // SLOTS
    here = info[0]
    half = info[1] ^ flip
    base = info[2] + half * rows
    tiles = points.shape[0] // tile

    def span(i):
        return pl.ds(pl.multiple_of(i * tile, tile), tile)

    def column_of(slot):
        return pl.ds(pl.multiple_of((here ^ slot) * block_width, block_width), block_width)

    def load(i):
        return pltpu.make_async_copy(points.at[span(i)], kept.at[span(i)], point_sems.at[i])

    load_assign = pltpu.make_async_copy(assign, chosen_in, small_sems.at[0])
    if initial:
        load_start = pltpu.make_async_copy(
            fine.at[pl.ds(pl.multiple_of(half * rows, rows), rows)], start, small_sems.at[1]
        )
        load_start.start()
    if stream:
        load(0).start()
    load_assign.start()
    if stream:

        @pl.loop(1, tiles)
        def _(i):
            load(i).start()

    if initial:
        load_start.wait()
        block = start[...]
        norm = jnp.sum(block * block, axis=1, keepdims=True)
        low[...] = (-2.0 * block).astype(jnp.bfloat16)
    else:
        norm = jnp.zeros((rows, 1), jnp.float32)
        for slot in range(SLOTS):
            block = fine[slot]
            norm = norm + jnp.sum(block * block, axis=1, keepdims=True)
            low[:, column_of(slot)] = (-2.0 * block).astype(jnp.bfloat16)
    tallies[...] = jnp.zeros_like(tallies)

    def multiply(i, target):
        target[...] = lax.dot_general(
            low[...], kept[span(i), :], (((1,), (1,)), ((), ())), preferred_element_type=jnp.float32
        )

    def weigh(i, products):
        energy = norm + products[...]
        chosen = chosen_in[pass_index : pass_index + 1, span(i)] - base
        member = lax.broadcasted_iota(jnp.int32, energy.shape, 0) == chosen
        picked = jnp.sum(jnp.where(member, energy, 0.0), axis=0, keepdims=True)
        nearest = jnp.min(energy, axis=0, keepdims=True)
        inside = (chosen >= 0) & (chosen < rows)
        picked_seen = jnp.where(inside, picked, FAR)
        if chained:
            picked_seen = jnp.minimum(picked_seen, seen_in[0:1, span(i)])
            nearest = jnp.minimum(nearest, seen_in[1:2, span(i)])
        seen[0:1, span(i)] = picked_seen
        seen[1:2, span(i)] = nearest
        if first:
            folded = jnp.zeros((tile, 128), jnp.float32)
            for lane in range(0, width, 128):
                values = kept[span(i), lane : lane + 128].astype(jnp.float32)
                folded = folded + values * values
            squares = jnp.sum(folded.T, axis=0, keepdims=True)
            squares_out[0:1, span(i)] = squares
        else:
            squares = squares_in[0:1, span(i)]
        weights = 1.0 / (1.0 + (squares + picked) / width)
        weighted = jnp.where(member, weights, 0.0)
        tally = tallies[...]
        for lane in range(0, tile, 128):
            tally = tally + weighted[:, lane : lane + 128]
        tallies[...] = tally
        factor = as_column(weights, tile)
        for lane in range(0, width, 128):
            values = kept[span(i), lane : lane + 128].astype(jnp.float32)
            scaled[span(i), lane : lane + 128] = (values * factor).astype(jnp.bfloat16)
        table[:, span(i)] = member.astype(jnp.float32).astype(jnp.bfloat16)

    load_assign.wait()
    if stream:
        load(0).wait()
    multiply(0, even)

    @pl.loop(0, tiles // 2 - 1)
    def _(pair):
        i = 2 * pair
        if stream:
            load(i + 1).wait()
            load(i + 2).wait()
        multiply(i + 1, odd)
        weigh(i, even)
        multiply(i + 2, even)
        weigh(i + 1, odd)

    if stream:
        load(tiles - 1).wait()
    multiply(tiles - 1, odd)
    weigh(tiles - 2, even)
    weigh(tiles - 1, odd)

    counts = jnp.broadcast_to(jnp.sum(tallies[...].T, axis=0, keepdims=True), (TAIL, rows))

    for slot in range(SLOTS):
        payload[slot, :rows, :] = jnp.zeros((rows, block_width), jnp.float32)
        payload[slot, rows:, :] = counts

    @pl.loop(0, tiles // 2)
    def _(i):
        part = pl.ds(pl.multiple_of(2 * i * tile, 2 * tile), 2 * tile)
        for slot in range(SLOTS):
            payload[slot, :rows, :] += jnp.dot(
                table[:, part], scaled[part, column_of(slot)], preferred_element_type=jnp.float32
            )


def run_pass(info, points, fine_assign, fine, squares, seen, *, pass_index, flip, rows):
    count, width = points.shape
    block_width = width // SLOTS
    tile = 512
    initial = pass_index == 0
    chained = seen is not None
    stream = not chained
    whole = pl.BlockSpec(memory_space=pltpu.VMEM)
    anywhere = pl.BlockSpec(memory_space=pl.ANY)
    in_hbm = lambda value: pltpu.with_memory_space_constraint(value, pltpu.HBM)
    in_specs = [
        anywhere if stream else whole,
        anywhere,
        anywhere if initial else full(SLOTS, rows, block_width),
    ]
    args = [
        in_hbm(points) if stream else pltpu.with_memory_space_constraint(points, pltpu.VMEM),
        in_hbm(fine_assign),
        in_hbm(fine) if initial else fine,
    ]
    if squares is not None:
        in_specs.append(full(1, count))
        args.append(squares)
    if chained:
        in_specs.append(full(2, count))
        args.append(seen)
    shapes = [(SLOTS, rows + TAIL, block_width), (2, count)]
    if squares is None:
        shapes.append((1, count))
    out_shape = [jax.ShapeDtypeStruct(shape, jnp.float32) for shape in shapes]
    out_specs = [full(*shape) for shape in shapes]
    scratch = [
        pltpu.VMEM((rows, width), jnp.bfloat16),
        pltpu.VMEM((rows, 128), jnp.float32),
        pltpu.VMEM((rows, tile), jnp.float32),
        pltpu.VMEM((rows, tile), jnp.float32),
        pltpu.VMEM((count, width), jnp.bfloat16),
        pltpu.VMEM((rows, count), jnp.bfloat16),
        pltpu.VMEM((PASSES, count), jnp.int32),
        pltpu.SemaphoreType.DMA((2,)),
    ]
    if initial:
        scratch.append(pltpu.VMEM((rows, width), jnp.float32))
    if stream:
        out_shape.append(pltpu.VMEM(points.shape, points.dtype))
        out_specs.append(whole)
        scratch.append(pltpu.SemaphoreType.DMA((count // tile,)))
    body = functools.partial(
        pass_body,
        pass_index=pass_index,
        flip=flip,
        stream=stream,
        chained=chained,
        tile=tile,
    )
    return pl.pallas_call(
        body,
        out_shape=out_shape,
        grid_spec=pltpu.PrefetchScalarGridSpec(
            num_scalar_prefetch=1,
            grid=(1,),
            in_specs=in_specs,
            out_specs=out_specs,
            scratch_shapes=scratch,
        ),
        compiler_params=pltpu.CompilerParams(vmem_limit_bytes=28 * 2**20),
        cost_estimate=pl.CostEstimate(
            flops=4 * rows * count * width, bytes_accessed=2 * count * width, transcendentals=0
        ),
        name=f"energies_and_sums_{pass_index}{int(chained)}",
    )(info, *args)


def refine_body(info, own, sibling, x_top, x_low, y_top, y_low, tail, owner, coarse, *outs):
    top, low, part = outs
    rows = owner.shape[1]
    mid = rows // 2
    counts_row = tail[...] + y_top[mid:, :]
    counts = as_column(counts_row[:1], rows)[:, :1]
    table = (
        lax.broadcasted_iota(jnp.int32, (NC, rows), 0) == owner[...]
    ).astype(jnp.float32)
    lookup = lax.dot_general(
        table,
        coarse[...],
        (((0,), (0,)), ((), ())),
        precision=HIGHEST,
        preferred_element_type=jnp.float32,
    )
    totals = own[:rows, :] + sibling[:rows, :] + jnp.concatenate(
        [x_top[...] + y_top[:mid, :], x_low[...] + y_low[...]], 0
    )
    new = (totals + prior_weight * lookup) / (counts + prior_weight)
    top[...] = new[:mid]
    low[...] = new[mid:]
    prior = jnp.where(info[3] == 0, prior_weight, 0.0)
    part[:NC, :] = prior * coarse[...] + jnp.dot(
        table, counts * new, precision=HIGHEST, preferred_element_type=jnp.float32
    )
    part[NC:, :] = jnp.zeros((TAIL, part.shape[1]), jnp.float32)
    part[NC:, :NC] = prior + lax.dot_general(
        counts_row,
        table,
        (((1,), (1,)), ((), ())),
        precision=HIGHEST,
        preferred_element_type=jnp.float32,
    )


def refine_half(info, own, sibling, incoming, owners, coarse, *, flip):
    _, rows, block_width = own.shape
    rows -= TAIL
    mid = rows // 2
    slot = pl.BlockSpec((None, rows + TAIL, block_width), lambda i, info: (0, 0, 0))
    wide = coarse.shape[1] != block_width
    return pl.pallas_call(
        refine_body,
        out_shape=[
            jax.ShapeDtypeStruct((mid, block_width), jnp.float32),
            jax.ShapeDtypeStruct((mid, block_width), jnp.float32),
            jax.ShapeDtypeStruct((NC + TAIL, block_width), jnp.float32),
        ],
        grid_spec=pltpu.PrefetchScalarGridSpec(
            num_scalar_prefetch=1,
            grid=(1,),
            in_specs=[slot] * 2
            + [full(*value.shape) for value in incoming]
            + [
                pl.BlockSpec((None, 1, rows), lambda i, info: (info[1] ^ flip, 0, 0)),
                pl.BlockSpec((NC, block_width), lambda i, info: (0, info[0] if wide else 0)),
            ],
            out_specs=[
                full(mid, block_width),
                full(mid, block_width),
                full(NC + TAIL, block_width),
            ],
        ),
        compiler_params=pltpu.CompilerParams(vmem_limit_bytes=16 * 2**20),
        name="refine_half",
    )(info, own, sibling, *incoming, owners, coarse)


def exchange(held, sibling):
    rows = held.shape[1] - TAIL
    mid = rows // 2
    top, low, tail = slice(0, mid), slice(mid, rows), slice(rows, rows + TAIL)
    both = lambda slot, part: held[slot, part] + sibling[slot, part]
    counts = both(0, tail)
    corner_top = swap(jnp.concatenate([both(3, top), counts], 0), ACROSS_X)
    corner_low = swap(both(3, low), ACROSS_Y)
    x_top = swap(both(1, top), ACROSS_X)
    y_low = swap(both(2, low), ACROSS_Y)
    counts = counts + corner_top[mid:]
    y_top = swap(jnp.concatenate([both(2, top) + corner_top[:mid], counts], 0), ACROSS_Y)
    x_low = swap(both(1, low) + corner_low, ACROSS_X)
    return x_top, x_low, y_top, y_low, counts


def gather_half(top, low):
    x_low = swap(low, ACROSS_X)
    y_top = swap(top, ACROSS_Y)
    x_top = swap(top, ACROSS_X)
    y_low = swap(low, ACROSS_Y)
    corner_top = swap(y_top, ACROSS_X)
    corner_low = swap(x_low, ACROSS_Y)
    blocks = [(top, low), (x_top, x_low), (y_top, y_low), (corner_top, corner_low)]
    return [jnp.concatenate(block, 0) for block in blocks]


def spread(value):
    corner = swap(value, ACROSS_X | ACROSS_Y)
    return [value, swap(value, ACROSS_X), swap(value, ACROSS_Y), corner]


def over_cen(value, combine):
    others = [swap(value, bit, "cen") for bit in range(1, lax.axis_size("cen"))]
    return functools.reduce(combine, others, value)


def place_body(info, *refs):
    own, other = refs[:2], refs[2:4]
    parts, others_parts, fine_out, coarse_out = refs[4:]
    block_width = parts.shape[2]
    here = info[0]

    def column_of(slot):
        return pl.ds(pl.multiple_of((here ^ slot) * block_width, block_width), block_width)

    def put(pieces):
        for slot in range(SLOTS):
            fine_out[:, column_of(slot)] = pieces[slot // 2][slot % 2]

    @pl.when(pl.program_id(0) == 0)
    def _():
        put(own)
        weight = parts[0, NC : NC + 1, :128] + others_parts[0, NC : NC + 1, :128]
        weight = as_column(weight, 128)[:NC, :1]
        for slot in range(SLOTS):
            total = parts[slot, :NC, :] + others_parts[slot, :NC, :]
            coarse_out[:, column_of(slot)] = total / weight

    @pl.when(pl.program_id(0) == 1)
    def _():
        put(other)


def place(info, own, other, parts, others_parts, *, flip):
    _, rows, block_width = own[0].shape
    width = SLOTS * block_width
    args = [*own, *other, parts, others_parts]
    return pl.pallas_call(
        place_body,
        out_shape=[
            jax.ShapeDtypeStruct((2 * rows, width), jnp.float32),
            jax.ShapeDtypeStruct((NC, width), jnp.float32),
        ],
        grid_spec=pltpu.PrefetchScalarGridSpec(
            num_scalar_prefetch=1,
            grid=(2,),
            in_specs=[full(*value.shape) for value in args],
            out_specs=[
                pl.BlockSpec((rows, width), lambda i, info: (info[1] ^ flip ^ i, 0)),
                full(NC, width),
            ],
        ),
        compiler_params=pltpu.CompilerParams(vmem_limit_bytes=24 * 2**20),
        name="place_blocks",
    )(info, *args)


def on_device_paired(points, fine_assign, fine_start, coarse_start, coarse_assign):
    width = points.shape[1]
    local_count = fine_start.shape[0]
    rows = local_count // 2
    block_width = width // SLOTS
    cen, me = lax.axis_index("cen"), lax.axis_index("pts")
    core = me & 1
    info = jnp.stack([me >> 1, core, cen * local_count, cen * 2 + core]).astype(jnp.int32)
    owners = coarse_assign.reshape(2, 1, rows)

    call = functools.partial(run_pass, info, pass_index=0, rows=rows)
    sent, seen, squares, kept = call(points, fine_assign, fine_start, None, None, flip=1)
    sibling = swap(sent, CORE)
    held, seen_first = call(kept, fine_assign, fine_start, squares, seen, flip=0)
    incoming = exchange(held, sibling)
    top, low, part = refine_half(info, held, sibling, incoming, owners, coarse_start, flip=0)
    own = jnp.stack(gather_half(top, low))
    part = part + swap(part, CORE)
    own, part = lax.optimization_barrier((own, part))
    other = swap(own, CORE)

    call = functools.partial(run_pass, info, pass_index=1, rows=rows)
    sent, seen, kept = call(points, fine_assign, own, squares, None, flip=0)
    sibling = swap(sent, CORE)
    held, seen_second = call(kept, fine_assign, other, squares, seen, flip=1)
    incoming = exchange(held, sibling)

    seen = jnp.concatenate([seen_first, seen_second], 0)
    folded = jnp.concatenate([part, seen.reshape(-1, block_width)], 0)
    gathered = [folded] + [swap(folded, bit, "cen") for bit in range(1, lax.axis_size("cen"))]
    part = functools.reduce(jnp.add, [each[: NC + TAIL] for each in gathered])
    seen = functools.reduce(jnp.minimum, [each[NC + TAIL :] for each in gathered])
    seen = seen.reshape(2, 2, -1)
    gaps = (seen[:, 0] - seen[:, 1]) / math.sqrt(width)
    coarse = part[:NC] / part[NC, :NC][:, None]

    top, low, part = refine_half(info, held, sibling, incoming, owners, coarse, flip=1)
    own = gather_half(top, low)
    own = [jnp.stack(own[:2]), jnp.stack(own[2:])]
    parts = jnp.stack(spread(over_cen(part, jnp.add)))
    other = [swap(pair, CORE) for pair in own]
    fine_now, coarse_now = place(info, own, other, parts, swap(parts, CORE), flip=1)
    return (fine_now, coarse_now, gaps)


def solution(mesh):
    placed = (P("pts", None), P(None, "pts"), P("cen", None), P(), P("cen"))

    def on_device(points, fine_assign, fine_start, coarse_start, coarse_assign):
        count, width = points.shape
        local_count = fine_start.shape[0]
        centres = mesh.shape["cen"]
        fits = (
            mesh.shape["pts"] == 2 * SLOTS
            and centres & (centres - 1) == 0
            and width // SLOTS == local_count // 2
            and (width // SLOTS) % 128 == 0
            and count % 1024 == 0
        )
        plan = on_device_paired if fits else on_device_any
        return plan(points, fine_assign, fine_start, coarse_start, coarse_assign)

    return jax.shard_map(
        on_device,
        mesh=mesh,
        in_specs=placed,
        out_specs=(P("cen", None), P(), P(None, "pts")),
        check_vma=False,
    )
```

```python
import functools
import math

import jax
import jax.numpy as jnp
from jax import lax
from jax.experimental import pallas as pl
from jax.experimental.pallas import tpu as pltpu
from jax.sharding import PartitionSpec as P

NC = 64
PASSES = 2
FAR = 3.0e38

prior_weight = 4.0
HIGHEST = lax.Precision.HIGHEST


def refine(totals, counts, coarse_cols, coarse_table):
    lookup = jnp.dot(coarse_table, coarse_cols, precision=HIGHEST)
    fine_next = (totals + prior_weight * lookup) / (counts + prior_weight)[:, None]
    coarse_part = lax.dot_general(
        coarse_table,
        counts[:, None] * fine_next,
        (((0,), (0,)), ((), ())),
        precision=HIGHEST,
    )
    coarse_weight = jnp.sum(coarse_table * counts[:, None], axis=0)
    return (fine_next, coarse_part, coarse_weight)


def on_device_any(points, fine_assign, fine_start, coarse_start, coarse_assign):
    width = points.shape[1]
    local_count = fine_start.shape[0]
    offset = lax.axis_index("cen") * local_count
    columns = jnp.arange(local_count, dtype=jnp.int32)
    coarse_table = (coarse_assign[:, None] == jnp.arange(NC, dtype=jnp.int32)[None, :]).astype(
        jnp.float32
    )
    point_values = points.astype(jnp.float32)
    squares = jnp.sum(point_values * point_values, axis=1)
    fine_now = fine_start
    coarse_now = coarse_start
    gap_rows = []
    for pass_index in range(PASSES):
        member = (fine_assign[pass_index] - offset)[:, None] == columns[None, :]
        products = jnp.dot(
            points, fine_now.astype(jnp.bfloat16).T, preferred_element_type=jnp.float32
        )
        energy = jnp.sum(fine_now * fine_now, axis=1)[None, :] - 2.0 * products
        picked_local = jnp.sum(jnp.where(member, energy, 0.0), axis=1)
        nearest_local = jnp.min(energy, axis=1)
        picked = lax.psum(picked_local, "cen")
        nearest = lax.pmin(nearest_local, "cen")
        gap_rows.append((picked - nearest) / math.sqrt(width))
        weights = 1.0 / (1.0 + (squares + picked) / width)
        scaled = (point_values * weights[:, None]).astype(jnp.bfloat16)
        partial_sums = lax.dot_general(
            member.astype(jnp.bfloat16),
            scaled,
            (((0,), (0,)), ((), ())),
            preferred_element_type=jnp.float32,
        )
        partial_weights = jnp.sum(jnp.where(member, weights[:, None], 0.0), axis=0)
        share_width = width // lax.axis_size("pts")
        start = lax.axis_index("pts") * share_width
        shares = lax.psum_scatter(partial_sums, "pts", scatter_dimension=1, tiled=True)
        counts = lax.psum(partial_weights, "pts")
        coarse_cols = lax.dynamic_slice_in_dim(coarse_now, start, share_width, 1)
        fine_share, coarse_part, coarse_weight = refine(shares, counts, coarse_cols, coarse_table)
        coarse_sum, coarse_count = lax.psum((coarse_part, coarse_weight), "cen")
        coarse_share = (coarse_sum + prior_weight * coarse_cols) / (coarse_count + prior_weight)[
            :, None
        ]
        fine_now, coarse_now = (
            lax.all_gather(fine_share, "pts", axis=1, tiled=True),
            lax.all_gather(coarse_share, "pts", axis=1, tiled=True),
        )
    return (fine_now, coarse_now, jnp.stack(gap_rows))


CORE, ACROSS_X, ACROSS_Y = 1, 2, 4
SLOTS = 4
TAIL = 8


def swap(value, bit, axis="pts"):
    size = lax.axis_size(axis)
    return lax.ppermute(value, axis, [(i, i ^ bit) for i in range(size)])


def full(*shape):
    return pl.BlockSpec(shape, lambda i, info: (0,) * len(shape))


def as_column(row, rows):
    return jnp.broadcast_to(row, (128, rows)).T


def pass_body(info, points, assign, fine, *refs, pass_index, flip, stream, chained, tile):
    refs = list(refs)
    initial = pass_index == 0
    first = initial and stream
    squares_in = None if first else refs.pop(0)
    seen_in = refs.pop(0) if chained else None
    payload, seen = refs.pop(0), refs.pop(0)
    squares_out = refs.pop(0) if first else None
    kept = refs.pop(0) if stream else points
    low, norms, tallies, sums, chosen_in, small_sems = refs[:6]
    products, factors, tables, scaleds = refs[6:8], refs[8:10], refs[10:12], refs[12:14]
    start = refs[14] if initial else None
    point_sems = refs[-1] if stream else None
    rows, width = low.shape
    block_width = width // SLOTS
    here = info[0]
    half = info[1] ^ flip
    base = info[2] + half * rows
    tiles = points.shape[0] // tile

    def span(i):
        return pl.ds(pl.multiple_of(i * tile, tile), tile)

    def column_of(slot):
        return pl.ds(pl.multiple_of((here ^ slot) * block_width, block_width), block_width)

    def load(i):
        return pltpu.make_async_copy(points.at[span(i)], kept.at[span(i)], point_sems.at[i])

    load_assign = pltpu.make_async_copy(assign, chosen_in, small_sems.at[0])
    if initial:
        load_start = pltpu.make_async_copy(
            fine.at[pl.ds(pl.multiple_of(half * rows, rows), rows)], start, small_sems.at[1]
        )
        load_start.start()
    if stream:
        load(0).start()
    load_assign.start()
    if stream:

        @pl.loop(1, tiles)
        def _(i):
            load(i).start()

    if initial:
        load_start.wait()
        block = start[...]
        norm = jnp.sum(block * block, axis=1, keepdims=True)
        low[...] = (-2.0 * block).astype(jnp.bfloat16)
    else:
        norm = jnp.zeros((rows, 1), jnp.float32)
        for slot in range(SLOTS):
            block = fine[slot]
            norm = norm + jnp.sum(block * block, axis=1, keepdims=True)
            low[:, column_of(slot)] = (-2.0 * block).astype(jnp.bfloat16)
    norms[...] = jnp.broadcast_to(norm, norms.shape)
    tallies[...] = jnp.zeros_like(tallies)
    sums[...] = jnp.zeros_like(sums)

    def multiply(i, odd):
        products[odd][...] = lax.dot_general(
            low[...], kept[span(i), :], (((1,), (1,)), ((), ())), preferred_element_type=jnp.float32
        )

    def weigh(i, odd):
        energy = products[odd][...] + jnp.concatenate([norms[...]] * (tile // 128), axis=1)
        chosen = chosen_in[pass_index : pass_index + 1, span(i)] - base
        member = lax.broadcasted_iota(jnp.int32, energy.shape, 0) == chosen
        picked = jnp.sum(jnp.where(member, energy, 0.0), axis=0, keepdims=True)
        nearest = jnp.min(energy, axis=0, keepdims=True)
        inside = (chosen >= 0) & (chosen < rows)
        picked_seen = jnp.where(inside, picked, FAR)
        if chained:
            picked_seen = jnp.minimum(picked_seen, seen_in[0:1, span(i)])
            nearest = jnp.minimum(nearest, seen_in[1:2, span(i)])
        seen[0:1, span(i)] = picked_seen
        seen[1:2, span(i)] = nearest
        if first:
            folded = jnp.zeros((tile, 128), jnp.float32)
            for lane in range(0, width, 128):
                values = kept[span(i), lane : lane + 128].astype(jnp.float32)
                folded = folded + values * values
            squares = jnp.sum(folded.T, axis=0, keepdims=True)
            squares_out[0:1, span(i)] = squares
        else:
            squares = squares_in[0:1, span(i)]
        weights = 1.0 / (1.0 + (squares + picked) / width)
        weighted = jnp.where(member, weights, 0.0)
        tally = tallies[...]
        for lane in range(0, tile, 128):
            tally = tally + weighted[:, lane : lane + 128]
        tallies[...] = tally
        factors[odd][...] = as_column(weights, tile)
        tables[odd][...] = member.astype(jnp.float32).astype(jnp.bfloat16)

    def collect(i, odd):
        factor = factors[odd][...]
        for lane in range(0, width, 128):
            values = kept[span(i), lane : lane + 128].astype(jnp.float32)
            scaleds[odd][:, lane : lane + 128] = (values * factor).astype(jnp.bfloat16)
        sums[...] += jnp.dot(
            tables[odd][...], scaleds[odd][...], preferred_element_type=jnp.float32
        )

    load_assign.wait()
    if stream:
        load(0).wait()
        load(1).wait()
    multiply(0, 0)
    multiply(1, 1)
    weigh(0, 0)

    @pl.loop(0, tiles // 2 - 1)
    def _(pair):
        i = 2 * pair + 1
        if stream:
            load(i + 1).wait()
            load(i + 2).wait()
        multiply(i + 1, 0)
        collect(i - 1, 0)
        weigh(i, 1)
        multiply(i + 2, 1)
        collect(i, 1)
        weigh(i + 1, 0)

    collect(tiles - 2, 0)
    weigh(tiles - 1, 1)
    collect(tiles - 1, 1)

    counts = jnp.broadcast_to(jnp.sum(tallies[...].T, axis=0, keepdims=True), (TAIL, rows))
    for slot in range(SLOTS):
        payload[slot, :rows, :] = sums[:, column_of(slot)]
        payload[slot, rows:, :] = counts


def run_pass(info, points, fine_assign, fine, squares, seen, *, pass_index, flip, rows):
    count, width = points.shape
    block_width = width // SLOTS
    tile = 512
    initial = pass_index == 0
    chained = seen is not None
    stream = not chained
    whole = pl.BlockSpec(memory_space=pltpu.VMEM)
    anywhere = pl.BlockSpec(memory_space=pl.ANY)
    in_hbm = lambda value: pltpu.with_memory_space_constraint(value, pltpu.HBM)
    in_specs = [
        anywhere if stream else whole,
        anywhere,
        anywhere if initial else full(SLOTS, rows, block_width),
    ]
    args = [
        in_hbm(points) if stream else pltpu.with_memory_space_constraint(points, pltpu.VMEM),
        in_hbm(fine_assign),
        in_hbm(fine) if initial else fine,
    ]
    if squares is not None:
        in_specs.append(full(1, count))
        args.append(squares)
    if chained:
        in_specs.append(full(2, count))
        args.append(seen)
    shapes = [(SLOTS, rows + TAIL, block_width), (2, count)]
    if squares is None:
        shapes.append((1, count))
    out_shape = [jax.ShapeDtypeStruct(shape, jnp.float32) for shape in shapes]
    out_specs = [full(*shape) for shape in shapes]
    scratch = [
        pltpu.VMEM((rows, width), jnp.bfloat16),
        pltpu.VMEM((rows, 128), jnp.float32),
        pltpu.VMEM((rows, 128), jnp.float32),
        pltpu.VMEM((rows, width), jnp.float32),
        pltpu.VMEM((PASSES, count), jnp.int32),
        pltpu.SemaphoreType.DMA((2,)),
    ]
    for shape, kind in (
        ((rows, tile), jnp.float32),
        ((tile, 128), jnp.float32),
        ((rows, tile), jnp.bfloat16),
        ((tile, width), jnp.bfloat16),
    ):
        scratch += [pltpu.VMEM(shape, kind)] * 2
    if initial:
        scratch.append(pltpu.VMEM((rows, width), jnp.float32))
    if stream:
        out_shape.append(pltpu.VMEM(points.shape, points.dtype))
        out_specs.append(whole)
        scratch.append(pltpu.SemaphoreType.DMA((count // tile,)))
    body = functools.partial(
        pass_body,
        pass_index=pass_index,
        flip=flip,
        stream=stream,
        chained=chained,
        tile=tile,
    )
    return pl.pallas_call(
        body,
        out_shape=out_shape,
        grid_spec=pltpu.PrefetchScalarGridSpec(
            num_scalar_prefetch=1,
            grid=(1,),
            in_specs=in_specs,
            out_specs=out_specs,
            scratch_shapes=scratch,
        ),
        compiler_params=pltpu.CompilerParams(vmem_limit_bytes=28 * 2**20),
        cost_estimate=pl.CostEstimate(
            flops=4 * rows * count * width, bytes_accessed=2 * count * width, transcendentals=0
        ),
        name=f"energies_and_sums_{pass_index}{int(chained)}",
    )(info, *args)


def refine_body(info, own, sibling, over_x, over_y, tail, owner, coarse, *outs):
    top, low, part = outs
    rows = owner.shape[1]
    mid = rows // 2
    counts_row = tail[...] + over_y[rows:, :]
    counts = as_column(counts_row[:1], rows)[:, :1]
    table = (
        lax.broadcasted_iota(jnp.int32, (NC, rows), 0) == owner[...]
    ).astype(jnp.float32)
    lookup = lax.dot_general(
        table,
        coarse[...],
        (((0,), (0,)), ((), ())),
        precision=HIGHEST,
        preferred_element_type=jnp.float32,
    )
    totals = (own[:rows, :] + sibling[:rows, :]) + (over_x[...] + over_y[:rows, :])
    new = (totals + prior_weight * lookup) / (counts + prior_weight)
    top[...] = new[:mid]
    low[...] = new[mid:]
    prior = jnp.where(info[3] == 0, prior_weight, 0.0)
    part[:NC, :] = prior * coarse[...] + jnp.dot(
        table, counts * new, precision=HIGHEST, preferred_element_type=jnp.float32
    )
    part[NC:, :] = jnp.zeros((TAIL, part.shape[1]), jnp.float32)
    part[NC:, :NC] = prior + lax.dot_general(
        counts_row,
        table,
        (((1,), (1,)), ((), ())),
        precision=HIGHEST,
        preferred_element_type=jnp.float32,
    )


def refine_half(info, own, sibling, incoming, owners, coarse, *, flip):
    _, rows, block_width = own.shape
    rows -= TAIL
    mid = rows // 2
    slot = pl.BlockSpec((None, rows + TAIL, block_width), lambda i, info: (0, 0, 0))
    wide = coarse.shape[1] != block_width
    return pl.pallas_call(
        refine_body,
        out_shape=[
            jax.ShapeDtypeStruct((mid, block_width), jnp.float32),
            jax.ShapeDtypeStruct((mid, block_width), jnp.float32),
            jax.ShapeDtypeStruct((NC + TAIL, block_width), jnp.float32),
        ],
        grid_spec=pltpu.PrefetchScalarGridSpec(
            num_scalar_prefetch=1,
            grid=(1,),
            in_specs=[slot] * 2
            + [full(*value.shape) for value in incoming]
            + [
                pl.BlockSpec((None, 1, rows), lambda i, info: (info[1] ^ flip, 0, 0)),
                pl.BlockSpec((NC, block_width), lambda i, info: (0, info[0] if wide else 0)),
            ],
            out_specs=[
                full(mid, block_width),
                full(mid, block_width),
                full(NC + TAIL, block_width),
            ],
        ),
        compiler_params=pltpu.CompilerParams(vmem_limit_bytes=16 * 2**20),
        name="refine_half",
    )(info, own, sibling, *incoming, owners, coarse)


def exchange(held, sibling):
    rows = held.shape[1] - TAIL
    mid = rows // 2
    top, low, tail = slice(0, mid), slice(mid, rows), slice(rows, rows + TAIL)
    both = lambda slot, part: held[slot, part] + sibling[slot, part]
    counts = both(0, tail)
    corner_top = swap(jnp.concatenate([both(3, top), counts], 0), ACROSS_X)
    corner_low = swap(both(3, low), ACROSS_Y)
    counts = counts + corner_top[mid:]
    over_y = swap(
        jnp.concatenate([both(2, top) + corner_top[:mid], both(2, low), counts], 0), ACROSS_Y
    )
    over_x = swap(jnp.concatenate([both(1, top), both(1, low) + corner_low], 0), ACROSS_X)
    return over_x, over_y, counts


def gather_half(top, low):
    x_low = swap(low, ACROSS_X)
    y_top = swap(top, ACROSS_Y)
    x_top = swap(top, ACROSS_X)
    y_low = swap(low, ACROSS_Y)
    corner_top = swap(y_top, ACROSS_X)
    corner_low = swap(x_low, ACROSS_Y)
    blocks = [(top, low), (x_top, x_low), (y_top, y_low), (corner_top, corner_low)]
    return [jnp.concatenate(block, 0) for block in blocks]


def spread(value):
    corner = swap(value, ACROSS_X | ACROSS_Y)
    return [value, swap(value, ACROSS_X), swap(value, ACROSS_Y), corner]


def over_cen(value, combine):
    others = [swap(value, bit, "cen") for bit in range(1, lax.axis_size("cen"))]
    return functools.reduce(combine, others, value)


def place_body(info, *refs):
    own, other = refs[:2], refs[2:4]
    parts, others_parts, fine_out, coarse_out = refs[4:]
    block_width = parts.shape[2]
    here = info[0]

    def column_of(slot):
        return pl.ds(pl.multiple_of((here ^ slot) * block_width, block_width), block_width)

    def put(pieces):
        for slot in range(SLOTS):
            fine_out[:, column_of(slot)] = pieces[slot // 2][slot % 2]

    @pl.when(pl.program_id(0) == 0)
    def _():
        put(own)
        weight = parts[0, NC : NC + 1, :128] + others_parts[0, NC : NC + 1, :128]
        weight = as_column(weight, 128)[:NC, :1]
        for slot in range(SLOTS):
            total = parts[slot, :NC, :] + others_parts[slot, :NC, :]
            coarse_out[:, column_of(slot)] = total / weight

    @pl.when(pl.program_id(0) == 1)
    def _():
        put(other)


def place(info, own, other, parts, others_parts, *, flip):
    _, rows, block_width = own[0].shape
    width = SLOTS * block_width
    args = [*own, *other, parts, others_parts]
    return pl.pallas_call(
        place_body,
        out_shape=[
            jax.ShapeDtypeStruct((2 * rows, width), jnp.float32),
            jax.ShapeDtypeStruct((NC, width), jnp.float32),
        ],
        grid_spec=pltpu.PrefetchScalarGridSpec(
            num_scalar_prefetch=1,
            grid=(2,),
            in_specs=[full(*value.shape) for value in args],
            out_specs=[
                pl.BlockSpec((rows, width), lambda i, info: (info[1] ^ flip ^ i, 0)),
                full(NC, width),
            ],
        ),
        compiler_params=pltpu.CompilerParams(vmem_limit_bytes=24 * 2**20),
        name="place_blocks",
    )(info, *args)


def on_device_paired(points, fine_assign, fine_start, coarse_start, coarse_assign):
    width = points.shape[1]
    local_count = fine_start.shape[0]
    rows = local_count // 2
    block_width = width // SLOTS
    cen, me = lax.axis_index("cen"), lax.axis_index("pts")
    core = me & 1
    info = jnp.stack([me >> 1, core, cen * local_count, cen * 2 + core]).astype(jnp.int32)
    owners = coarse_assign.reshape(2, 1, rows)

    call = functools.partial(run_pass, info, pass_index=0, rows=rows)
    sent, seen, squares, kept = call(points, fine_assign, fine_start, None, None, flip=1)
    sibling = swap(sent, CORE)
    held, seen_first = call(kept, fine_assign, fine_start, squares, seen, flip=0)
    incoming = exchange(held, sibling)
    top, low, part = refine_half(info, held, sibling, incoming, owners, coarse_start, flip=0)
    own = jnp.stack(gather_half(top, low))
    part = part + swap(part, CORE)
    own, part = lax.optimization_barrier((own, part))
    other = swap(own, CORE)

    call = functools.partial(run_pass, info, pass_index=1, rows=rows)
    sent, seen, kept = call(points, fine_assign, own, squares, None, flip=0)
    sibling = swap(sent, CORE)
    held, seen_second = call(kept, fine_assign, other, squares, seen, flip=1)
    incoming = exchange(held, sibling)

    folded = jnp.concatenate([part, seen_first.reshape(-1, block_width)], 0)
    gathered = [folded] + [swap(folded, bit, "cen") for bit in range(1, lax.axis_size("cen"))]
    part = functools.reduce(jnp.add, [each[: NC + TAIL] for each in gathered])
    seen_first = functools.reduce(jnp.minimum, [each[NC + TAIL :] for each in gathered])
    coarse = part[:NC] / part[NC, :NC][:, None]

    top, low, part = refine_half(info, held, sibling, incoming, owners, coarse, flip=1)
    own = gather_half(top, low)
    own = [jnp.stack(own[:2]), jnp.stack(own[2:])]
    parts = jnp.stack(spread(over_cen(part, jnp.add)))
    other = [swap(pair, CORE) for pair in own]
    fine_now, coarse_now = place(info, own, other, parts, swap(parts, CORE), flip=1)

    seen_first = seen_first.reshape(2, -1)
    seen_second = over_cen(seen_second, jnp.minimum)
    gaps = [(seen[0] - seen[1]) / math.sqrt(width) for seen in (seen_first, seen_second)]
    gaps = jnp.stack(gaps)
    return (fine_now, coarse_now, gaps)


def solution(mesh):
    placed = (P("pts", None), P(None, "pts"), P("cen", None), P(), P("cen"))

    def on_device(points, fine_assign, fine_start, coarse_start, coarse_assign):
        count, width = points.shape
        local_count = fine_start.shape[0]
        centres = mesh.shape["cen"]
        fits = (
            mesh.shape["pts"] == 2 * SLOTS
            and centres & (centres - 1) == 0
            and width // SLOTS == local_count // 2
            and (width // SLOTS) % 128 == 0
            and count % 1024 == 0
        )
        plan = on_device_paired if fits else on_device_any
        return plan(points, fine_assign, fine_start, coarse_start, coarse_assign)

    return jax.shard_map(
        on_device,
        mesh=mesh,
        in_specs=placed,
        out_specs=(P("cen", None), P(), P(None, "pts")),
        check_vma=False,
    )
```

```python
import functools
import math

import jax
import jax.numpy as jnp
from jax import lax
from jax.experimental import pallas as pl
from jax.experimental.pallas import tpu as pltpu
from jax.sharding import PartitionSpec as P

NC = 64
PASSES = 2
FAR = 3.0e38

prior_weight = 4.0
HIGHEST = lax.Precision.HIGHEST


def refine(totals, counts, coarse_cols, coarse_table):
    lookup = jnp.dot(coarse_table, coarse_cols, precision=HIGHEST)
    fine_next = (totals + prior_weight * lookup) / (counts + prior_weight)[:, None]
    coarse_part = lax.dot_general(
        coarse_table,
        counts[:, None] * fine_next,
        (((0,), (0,)), ((), ())),
        precision=HIGHEST,
    )
    coarse_weight = jnp.sum(coarse_table * counts[:, None], axis=0)
    return (fine_next, coarse_part, coarse_weight)


def on_device_any(points, fine_assign, fine_start, coarse_start, coarse_assign):
    width = points.shape[1]
    local_count = fine_start.shape[0]
    offset = lax.axis_index("cen") * local_count
    columns = jnp.arange(local_count, dtype=jnp.int32)
    coarse_table = (coarse_assign[:, None] == jnp.arange(NC, dtype=jnp.int32)[None, :]).astype(
        jnp.float32
    )
    point_values = points.astype(jnp.float32)
    squares = jnp.sum(point_values * point_values, axis=1)
    fine_now = fine_start
    coarse_now = coarse_start
    gap_rows = []
    for pass_index in range(PASSES):
        member = (fine_assign[pass_index] - offset)[:, None] == columns[None, :]
        products = jnp.dot(
            points, fine_now.astype(jnp.bfloat16).T, preferred_element_type=jnp.float32
        )
        energy = jnp.sum(fine_now * fine_now, axis=1)[None, :] - 2.0 * products
        picked_local = jnp.sum(jnp.where(member, energy, 0.0), axis=1)
        nearest_local = jnp.min(energy, axis=1)
        picked = lax.psum(picked_local, "cen")
        nearest = lax.pmin(nearest_local, "cen")
        gap_rows.append((picked - nearest) / math.sqrt(width))
        weights = 1.0 / (1.0 + (squares + picked) / width)
        scaled = (point_values * weights[:, None]).astype(jnp.bfloat16)
        partial_sums = lax.dot_general(
            member.astype(jnp.bfloat16),
            scaled,
            (((0,), (0,)), ((), ())),
            preferred_element_type=jnp.float32,
        )
        partial_weights = jnp.sum(jnp.where(member, weights[:, None], 0.0), axis=0)
        share_width = width // lax.axis_size("pts")
        start = lax.axis_index("pts") * share_width
        shares = lax.psum_scatter(partial_sums, "pts", scatter_dimension=1, tiled=True)
        counts = lax.psum(partial_weights, "pts")
        coarse_cols = lax.dynamic_slice_in_dim(coarse_now, start, share_width, 1)
        fine_share, coarse_part, coarse_weight = refine(shares, counts, coarse_cols, coarse_table)
        coarse_sum, coarse_count = lax.psum((coarse_part, coarse_weight), "cen")
        coarse_share = (coarse_sum + prior_weight * coarse_cols) / (coarse_count + prior_weight)[
            :, None
        ]
        fine_now, coarse_now = (
            lax.all_gather(fine_share, "pts", axis=1, tiled=True),
            lax.all_gather(coarse_share, "pts", axis=1, tiled=True),
        )
    return (fine_now, coarse_now, jnp.stack(gap_rows))


CORE, ACROSS_X, ACROSS_Y = 1, 2, 4
SLOTS = 4
TAIL = 8


def swap(value, bit, axis="pts"):
    size = lax.axis_size(axis)
    return lax.ppermute(value, axis, [(i, i ^ bit) for i in range(size)])


def full(*shape):
    return pl.BlockSpec(shape, lambda i, info: (0,) * len(shape))


def as_column(row, rows):
    return jnp.broadcast_to(row, (128, rows)).T


def pass_body(info, points, assign, fine, *refs, pass_index, flip, stream, chained, tile):
    refs = list(refs)
    initial = pass_index == 0
    first = initial and stream
    squares_in = None if first else refs.pop(0)
    seen_in = refs.pop(0) if chained else None
    payload, seen = refs.pop(0), refs.pop(0)
    squares_out = refs.pop(0) if first else None
    kept = refs.pop(0) if stream else points
    low, norms, tallies, sums, places, even, odd, tables = refs[:8]
    chosen_in = refs[8] if stream else assign
    small_sems, point_sems = refs[9:11] if stream else (None, None)
    start = refs[11] if first else fine
    rows, width = low.shape
    block_width = width // SLOTS
    here = info[0]
    half = info[1] ^ flip
    base = info[2] + half * rows
    tiles = points.shape[0] // tile

    def span(i):
        return pl.ds(pl.multiple_of(i * tile, tile), tile)

    def column_of(slot):
        return pl.ds(pl.multiple_of((here ^ slot) * block_width, block_width), block_width)

    def load(i):
        return pltpu.make_async_copy(points.at[span(i)], kept.at[span(i)], point_sems.at[i])

    if first:
        load_start = pltpu.make_async_copy(
            fine.at[pl.ds(pl.multiple_of(half * rows, rows), rows)], start, small_sems.at[1]
        )
        load_start.start()
    if stream:
        load(0).start()
        load_assign = pltpu.make_async_copy(assign, chosen_in, small_sems.at[0])
        load_assign.start()

        @pl.loop(1, tiles)
        def _(i):
            load(i).start()

    if initial:
        if first:
            load_start.wait()
        block = start[...]
        norm = jnp.sum(block * block, axis=1, keepdims=True)
        low[...] = (-2.0 * block).astype(jnp.bfloat16)
    else:
        norm = jnp.zeros((rows, 1), jnp.float32)
        for slot in range(SLOTS):
            block = fine[slot]
            norm = norm + jnp.sum(block * block, axis=1, keepdims=True)
            low[:, column_of(slot)] = (-2.0 * block).astype(jnp.bfloat16)
    norms[...] = jnp.broadcast_to(norm, norms.shape)
    tallies[...] = jnp.zeros_like(tallies)
    sums[...] = jnp.zeros_like(sums)
    places[...] = lax.broadcasted_iota(jnp.int32, places.shape, 0).astype(jnp.int16)

    def multiply(i, target):
        target[...] = lax.dot_general(
            low[...], kept[span(i), :], (((1,), (1,)), ((), ())), preferred_element_type=jnp.float32
        )

    def collect(i, products):
        energy = products[...] + jnp.concatenate([norms[...]] * (tile // 128), axis=1)
        chosen = chosen_in[pass_index : pass_index + 1, span(i)] - base
        member = lax.broadcasted_iota(jnp.int32, energy.shape, 0) == chosen
        picked = jnp.sum(jnp.where(member, energy, 0.0), axis=0, keepdims=True)
        nearest = jnp.min(energy, axis=0, keepdims=True)
        inside = (chosen >= 0) & (chosen < rows)
        picked_seen = jnp.where(inside, picked, FAR)
        if chained:
            picked_seen = jnp.minimum(picked_seen, seen_in[0:1, span(i)])
            nearest = jnp.minimum(nearest, seen_in[1:2, span(i)])
        seen[0:1, span(i)] = picked_seen
        seen[1:2, span(i)] = nearest
        if first:
            folded = jnp.zeros((tile, 128), jnp.float32)
            for lane in range(0, width, 128):
                values = kept[span(i), lane : lane + 128].astype(jnp.float32)
                folded = folded + values * values
            squares = jnp.sum(folded.T, axis=0, keepdims=True)
            squares_out[0:1, span(i)] = squares
        else:
            squares = squares_in[0:1, span(i)]
        weights = 1.0 / (1.0 + (squares + picked) / width)
        weighted = jnp.where(member, weights, 0.0)
        tally = tallies[...]
        for lane in range(0, tile, 128):
            tally = tally + weighted[:, lane : lane + 128]
        tallies[...] = tally
        high = weights.astype(jnp.bfloat16)
        rest = (weights - high.astype(jnp.float32)).astype(jnp.bfloat16)
        narrow = jnp.where(inside, chosen, -1).astype(jnp.int16)
        member = places[...] == narrow
        nothing = jnp.zeros((rows, tile), jnp.bfloat16)
        tables[:rows, :] = jnp.where(member, jnp.broadcast_to(high, nothing.shape), nothing)
        tables[rows:, :] = jnp.where(member, jnp.broadcast_to(rest, nothing.shape), nothing)
        both = jnp.dot(tables[...], kept[span(i), :], preferred_element_type=jnp.float32)
        sums[...] += both[:rows] + both[rows:]

    if stream:
        load_assign.wait()
        load(0).wait()
    multiply(0, even)

    @pl.loop(0, tiles // 2 - 1)
    def _(pair):
        i = 2 * pair
        if stream:
            load(i + 1).wait()
            load(i + 2).wait()
        multiply(i + 1, odd)
        collect(i, even)
        multiply(i + 2, even)
        collect(i + 1, odd)

    if stream:
        load(tiles - 1).wait()
    multiply(tiles - 1, odd)
    collect(tiles - 2, even)
    collect(tiles - 1, odd)

    counts = jnp.broadcast_to(jnp.sum(tallies[...].T, axis=0, keepdims=True), (TAIL, rows))
    for slot in range(SLOTS):
        payload[slot, :rows, :] = sums[:, column_of(slot)]
        payload[slot, rows:, :] = counts


def run_pass(info, points, fine_assign, fine, squares, seen, *, pass_index, flip, rows):
    count, width = points.shape
    block_width = width // SLOTS
    tile = 512
    initial = pass_index == 0
    chained = seen is not None
    stream = not chained
    whole = pl.BlockSpec(memory_space=pltpu.VMEM)
    anywhere = pl.BlockSpec(memory_space=pl.ANY)
    in_hbm = lambda value: pltpu.with_memory_space_constraint(value, pltpu.HBM)
    if stream:
        in_specs = [anywhere, anywhere]
        args = [in_hbm(points), in_hbm(fine_assign)]
    else:
        in_specs = [whole, full(PASSES, count)]
        args = [pltpu.with_memory_space_constraint(points, pltpu.VMEM), fine_assign]
    if not initial:
        in_specs.append(full(SLOTS, rows, block_width))
    elif stream:
        in_specs.append(anywhere)
        fine = in_hbm(fine)
    else:
        in_specs.append(pl.BlockSpec((rows, width), lambda i, info: (info[1] ^ flip, 0)))
    args.append(fine)
    if squares is not None:
        in_specs.append(full(1, count))
        args.append(squares)
    if chained:
        in_specs.append(full(2, count))
        args.append(seen)
    shapes = [(SLOTS, rows + TAIL, block_width), (2, count)]
    if squares is None:
        shapes.append((1, count))
    out_shape = [jax.ShapeDtypeStruct(shape, jnp.float32) for shape in shapes]
    out_specs = [full(*shape) for shape in shapes]
    scratch = [
        pltpu.VMEM((rows, width), jnp.bfloat16),
        pltpu.VMEM((rows, 128), jnp.float32),
        pltpu.VMEM((rows, 128), jnp.float32),
        pltpu.VMEM((rows, width), jnp.float32),
        pltpu.VMEM((rows, tile), jnp.int16),
        pltpu.VMEM((rows, tile), jnp.float32),
        pltpu.VMEM((rows, tile), jnp.float32),
        pltpu.VMEM((2 * rows, tile), jnp.bfloat16),
    ]
    if stream:
        scratch += [
            pltpu.VMEM((PASSES, count), jnp.int32),
            pltpu.SemaphoreType.DMA((2,)),
            pltpu.SemaphoreType.DMA((count // tile,)),
        ]
        if initial:
            scratch.append(pltpu.VMEM((rows, width), jnp.float32))
        out_shape.append(pltpu.VMEM(points.shape, points.dtype))
        out_specs.append(whole)
    body = functools.partial(
        pass_body,
        pass_index=pass_index,
        flip=flip,
        stream=stream,
        chained=chained,
        tile=tile,
    )
    return pl.pallas_call(
        body,
        out_shape=out_shape,
        grid_spec=pltpu.PrefetchScalarGridSpec(
            num_scalar_prefetch=1,
            grid=(1,),
            in_specs=in_specs,
            out_specs=out_specs,
            scratch_shapes=scratch,
        ),
        compiler_params=pltpu.CompilerParams(vmem_limit_bytes=28 * 2**20),
        cost_estimate=pl.CostEstimate(
            flops=4 * rows * count * width, bytes_accessed=2 * count * width, transcendentals=0
        ),
        name=f"energies_and_sums_{pass_index}{int(chained)}",
    )(info, *args)


def refine_body(info, own, sibling, over_x, over_y, tail, owner, coarse, *outs):
    top, low, part = outs
    rows = owner.shape[1]
    mid = rows // 2
    counts_row = tail[...] + over_y[rows:, :]
    counts = as_column(counts_row[:1], rows)[:, :1]
    table = (
        lax.broadcasted_iota(jnp.int32, (NC, rows), 0) == owner[...]
    ).astype(jnp.float32)
    lookup = lax.dot_general(
        table,
        coarse[...],
        (((0,), (0,)), ((), ())),
        precision=HIGHEST,
        preferred_element_type=jnp.float32,
    )
    totals = (own[:rows, :] + sibling[:rows, :]) + (over_x[...] + over_y[:rows, :])
    new = (totals + prior_weight * lookup) / (counts + prior_weight)
    top[...] = new[:mid]
    low[...] = new[mid:]
    prior = jnp.where(info[3] == 0, prior_weight, 0.0)
    part[:NC, :] = prior * coarse[...] + jnp.dot(
        table, counts * new, precision=HIGHEST, preferred_element_type=jnp.float32
    )
    part[NC:, :] = jnp.zeros((TAIL, part.shape[1]), jnp.float32)
    part[NC:, :NC] = prior + lax.dot_general(
        counts_row,
        table,
        (((1,), (1,)), ((), ())),
        precision=HIGHEST,
        preferred_element_type=jnp.float32,
    )


def refine_half(info, own, sibling, incoming, owners, coarse, *, flip):
    _, rows, block_width = own.shape
    rows -= TAIL
    mid = rows // 2
    slot = pl.BlockSpec((None, rows + TAIL, block_width), lambda i, info: (0, 0, 0))
    wide = coarse.shape[1] != block_width
    return pl.pallas_call(
        refine_body,
        out_shape=[
            jax.ShapeDtypeStruct((mid, block_width), jnp.float32),
            jax.ShapeDtypeStruct((mid, block_width), jnp.float32),
            jax.ShapeDtypeStruct((NC + TAIL, block_width), jnp.float32),
        ],
        grid_spec=pltpu.PrefetchScalarGridSpec(
            num_scalar_prefetch=1,
            grid=(1,),
            in_specs=[slot] * 2
            + [full(*value.shape) for value in incoming]
            + [
                pl.BlockSpec((None, 1, rows), lambda i, info: (info[1] ^ flip, 0, 0)),
                pl.BlockSpec((NC, block_width), lambda i, info: (0, info[0] if wide else 0)),
            ],
            out_specs=[
                full(mid, block_width),
                full(mid, block_width),
                full(NC + TAIL, block_width),
            ],
        ),
        compiler_params=pltpu.CompilerParams(vmem_limit_bytes=16 * 2**20),
        name="refine_half",
    )(info, own, sibling, *incoming, owners, coarse)


def exchange(held, sibling):
    rows = held.shape[1] - TAIL
    mid = rows // 2
    top, low, tail = slice(0, mid), slice(mid, rows), slice(rows, rows + TAIL)
    both = lambda slot, part: held[slot, part] + sibling[slot, part]
    counts = both(0, tail)
    corner_top = swap(jnp.concatenate([both(3, top), counts], 0), ACROSS_X)
    corner_low = swap(both(3, low), ACROSS_Y)
    counts = counts + corner_top[mid:]
    over_y = swap(
        jnp.concatenate([both(2, top) + corner_top[:mid], both(2, low), counts], 0), ACROSS_Y
    )
    over_x = swap(jnp.concatenate([both(1, top), both(1, low) + corner_low], 0), ACROSS_X)
    return over_x, over_y, counts


def gather_half(top, low):
    x_low = swap(low, ACROSS_X)
    y_top = swap(top, ACROSS_Y)
    x_top = swap(top, ACROSS_X)
    y_low = swap(low, ACROSS_Y)
    corner_top = swap(y_top, ACROSS_X)
    corner_low = swap(x_low, ACROSS_Y)
    blocks = [(top, low), (x_top, x_low), (y_top, y_low), (corner_top, corner_low)]
    return [jnp.concatenate(block, 0) for block in blocks]


def spread(value):
    corner = swap(value, ACROSS_X | ACROSS_Y)
    return [value, swap(value, ACROSS_X), swap(value, ACROSS_Y), corner]


def over_cen(value, combine):
    others = [swap(value, bit, "cen") for bit in range(1, lax.axis_size("cen"))]
    return functools.reduce(combine, others, value)


def place_body(info, *refs):
    own, other = refs[:2], refs[2:4]
    parts, others_parts, fine_out, coarse_out = refs[4:]
    block_width = parts.shape[2]
    here = info[0]

    def column_of(slot):
        return pl.ds(pl.multiple_of((here ^ slot) * block_width, block_width), block_width)

    def put(pieces):
        for slot in range(SLOTS):
            fine_out[:, column_of(slot)] = pieces[slot // 2][slot % 2]

    @pl.when(pl.program_id(0) == 0)
    def _():
        put(own)
        weight = parts[0, NC : NC + 1, :128] + others_parts[0, NC : NC + 1, :128]
        weight = as_column(weight, 128)[:NC, :1]
        for slot in range(SLOTS):
            total = parts[slot, :NC, :] + others_parts[slot, :NC, :]
            coarse_out[:, column_of(slot)] = total / weight

    @pl.when(pl.program_id(0) == 1)
    def _():
        put(other)


def place(info, own, other, parts, others_parts, *, flip):
    _, rows, block_width = own[0].shape
    width = SLOTS * block_width
    args = [*own, *other, parts, others_parts]
    return pl.pallas_call(
        place_body,
        out_shape=[
            jax.ShapeDtypeStruct((2 * rows, width), jnp.float32),
            jax.ShapeDtypeStruct((NC, width), jnp.float32),
        ],
        grid_spec=pltpu.PrefetchScalarGridSpec(
            num_scalar_prefetch=1,
            grid=(2,),
            in_specs=[full(*value.shape) for value in args],
            out_specs=[
                pl.BlockSpec((rows, width), lambda i, info: (info[1] ^ flip ^ i, 0)),
                full(NC, width),
            ],
        ),
        compiler_params=pltpu.CompilerParams(vmem_limit_bytes=24 * 2**20),
        name="place_blocks",
    )(info, *args)


def on_device_paired(points, fine_assign, fine_start, coarse_start, coarse_assign):
    width = points.shape[1]
    local_count = fine_start.shape[0]
    rows = local_count // 2
    block_width = width // SLOTS
    cen, me = lax.axis_index("cen"), lax.axis_index("pts")
    core = me & 1
    info = jnp.stack([me >> 1, core, cen * local_count, cen * 2 + core]).astype(jnp.int32)
    owners = coarse_assign.reshape(2, 1, rows)

    call = functools.partial(run_pass, info, pass_index=0, rows=rows)
    sent, seen, squares, kept = call(points, fine_assign, fine_start, None, None, flip=1)
    sibling = swap(sent, CORE)
    held, seen_first = call(kept, fine_assign, fine_start, squares, seen, flip=0)
    incoming = exchange(held, sibling)
    top, low, part = refine_half(info, held, sibling, incoming, owners, coarse_start, flip=0)
    own = jnp.stack(gather_half(top, low))
    part = part + swap(part, CORE)
    own, part = lax.optimization_barrier((own, part))
    other = swap(own, CORE)

    call = functools.partial(run_pass, info, pass_index=1, rows=rows)
    sent, seen, kept = call(points, fine_assign, own, squares, None, flip=0)
    sibling = swap(sent, CORE)
    held, seen_second = call(kept, fine_assign, other, squares, seen, flip=1)
    incoming = exchange(held, sibling)

    seen = [each.reshape(-1, block_width) for each in (seen_first, seen_second)]
    gathered = lax.all_gather(jnp.concatenate([part, *seen], 0), "cen")
    part = jnp.sum(gathered[:, : NC + TAIL], axis=0)
    seen = jnp.min(gathered[:, NC + TAIL :], axis=0).reshape(2, 2, -1)
    gaps = (seen[:, 0] - seen[:, 1]) / math.sqrt(width)
    coarse = part[:NC] / part[NC, :NC][:, None]

    top, low, part = refine_half(info, held, sibling, incoming, owners, coarse, flip=1)
    own = gather_half(top, low)
    own = [jnp.stack(own[:2]), jnp.stack(own[2:])]
    parts = jnp.stack(spread(over_cen(part, jnp.add)))
    other = [swap(pair, CORE) for pair in own]
    fine_now, coarse_now = place(info, own, other, parts, swap(parts, CORE), flip=1)
    return (fine_now, coarse_now, gaps)


def solution(mesh):
    placed = (P("pts", None), P(None, "pts"), P("cen", None), P(), P("cen"))

    def on_device(points, fine_assign, fine_start, coarse_start, coarse_assign):
        count, width = points.shape
        local_count = fine_start.shape[0]
        centres = mesh.shape["cen"]
        fits = (
            mesh.shape["pts"] == 2 * SLOTS
            and centres & (centres - 1) == 0
            and width // SLOTS == local_count // 2
            and (width // SLOTS) % 128 == 0
            and count % 1024 == 0
        )
        plan = on_device_paired if fits else on_device_any
        return plan(points, fine_assign, fine_start, coarse_start, coarse_assign)

    return jax.shard_map(
        on_device,
        mesh=mesh,
        in_specs=placed,
        out_specs=(P("cen", None), P(), P(None, "pts")),
        check_vma=False,
    )
```

```python
import functools
import math

import jax
import jax.numpy as jnp
from jax import lax
from jax.experimental import pallas as pl
from jax.experimental.pallas import tpu as pltpu
from jax.sharding import PartitionSpec as P

NC = 64
PASSES = 2
FAR = 3.0e38

prior_weight = 4.0
HIGHEST = lax.Precision.HIGHEST


def refine(totals, counts, coarse_cols, coarse_table):
    lookup = jnp.dot(coarse_table, coarse_cols, precision=HIGHEST)
    fine_next = (totals + prior_weight * lookup) / (counts + prior_weight)[:, None]
    coarse_part = lax.dot_general(
        coarse_table,
        counts[:, None] * fine_next,
        (((0,), (0,)), ((), ())),
        precision=HIGHEST,
    )
    coarse_weight = jnp.sum(coarse_table * counts[:, None], axis=0)
    return (fine_next, coarse_part, coarse_weight)


def on_device_any(points, fine_assign, fine_start, coarse_start, coarse_assign):
    width = points.shape[1]
    local_count = fine_start.shape[0]
    offset = lax.axis_index("cen") * local_count
    columns = jnp.arange(local_count, dtype=jnp.int32)
    coarse_table = (coarse_assign[:, None] == jnp.arange(NC, dtype=jnp.int32)[None, :]).astype(
        jnp.float32
    )
    point_values = points.astype(jnp.float32)
    squares = jnp.sum(point_values * point_values, axis=1)
    fine_now = fine_start
    coarse_now = coarse_start
    gap_rows = []
    for pass_index in range(PASSES):
        member = (fine_assign[pass_index] - offset)[:, None] == columns[None, :]
        products = jnp.dot(
            points, fine_now.astype(jnp.bfloat16).T, preferred_element_type=jnp.float32
        )
        energy = jnp.sum(fine_now * fine_now, axis=1)[None, :] - 2.0 * products
        picked_local = jnp.sum(jnp.where(member, energy, 0.0), axis=1)
        nearest_local = jnp.min(energy, axis=1)
        picked = lax.psum(picked_local, "cen")
        nearest = lax.pmin(nearest_local, "cen")
        gap_rows.append((picked - nearest) / math.sqrt(width))
        weights = 1.0 / (1.0 + (squares + picked) / width)
        scaled = (point_values * weights[:, None]).astype(jnp.bfloat16)
        partial_sums = lax.dot_general(
            member.astype(jnp.bfloat16),
            scaled,
            (((0,), (0,)), ((), ())),
            preferred_element_type=jnp.float32,
        )
        partial_weights = jnp.sum(jnp.where(member, weights[:, None], 0.0), axis=0)
        share_width = width // lax.axis_size("pts")
        start = lax.axis_index("pts") * share_width
        shares = lax.psum_scatter(partial_sums, "pts", scatter_dimension=1, tiled=True)
        counts = lax.psum(partial_weights, "pts")
        coarse_cols = lax.dynamic_slice_in_dim(coarse_now, start, share_width, 1)
        fine_share, coarse_part, coarse_weight = refine(shares, counts, coarse_cols, coarse_table)
        coarse_sum, coarse_count = lax.psum((coarse_part, coarse_weight), "cen")
        coarse_share = (coarse_sum + prior_weight * coarse_cols) / (coarse_count + prior_weight)[
            :, None
        ]
        fine_now, coarse_now = (
            lax.all_gather(fine_share, "pts", axis=1, tiled=True),
            lax.all_gather(coarse_share, "pts", axis=1, tiled=True),
        )
    return (fine_now, coarse_now, jnp.stack(gap_rows))


CORE, ACROSS_X, ACROSS_Y = 1, 2, 4
SLOTS = 4
TAIL = 8


def swap(value, bit, axis="pts"):
    size = lax.axis_size(axis)
    return lax.ppermute(value, axis, [(i, i ^ bit) for i in range(size)])


def full(*shape):
    return pl.BlockSpec(shape, lambda i, info: (0,) * len(shape))


def as_column(row, rows):
    return jnp.broadcast_to(row, (128, rows)).T


def pass_body(info, points, assign, fine, *refs, pass_index, flip, stream, chained, tile):
    refs = list(refs)
    initial = pass_index == 0
    first = initial and stream
    squares_in = None if first else refs.pop(0)
    seen_in = refs.pop(0) if chained else None
    payload, seen = refs.pop(0), refs.pop(0)
    squares_out = refs.pop(0) if first else None
    kept = refs.pop(0) if stream else points
    low, norms, tallies, sums, even, odd, scaled = refs[:7]
    chosen_in = refs[7] if stream else assign
    small_sems, point_sems = refs[8:10] if stream else (None, None)
    start = refs[10] if first else fine
    width, rows = low.shape
    block_width = width // SLOTS
    here = info[0]
    half = info[1] ^ flip
    base = info[2] + half * rows
    tiles = points.shape[0] // tile

    def span(i):
        return pl.ds(pl.multiple_of(i * tile, tile), tile)

    def column_of(slot):
        return pl.ds(pl.multiple_of((here ^ slot) * block_width, block_width), block_width)

    def load(i):
        return pltpu.make_async_copy(points.at[span(i)], kept.at[span(i)], point_sems.at[i])

    if first:
        load_start = pltpu.make_async_copy(
            fine.at[pl.ds(pl.multiple_of(half * rows, rows), rows)], start, small_sems.at[1]
        )
        load_start.start()
    if stream:
        load(0).start()
        load_assign = pltpu.make_async_copy(assign, chosen_in, small_sems.at[0])
        load_assign.start()

        @pl.loop(1, tiles)
        def _(i):
            load(i).start()

    if initial:
        if first:
            load_start.wait()
        block = start[...]
        norm = jnp.sum(block * block, axis=1, keepdims=True)
        low[...] = (-2.0 * block).T.astype(jnp.bfloat16)
    else:
        norm = jnp.zeros((rows, 1), jnp.float32)
        for slot in range(SLOTS):
            block = fine[slot]
            norm = norm + jnp.sum(block * block, axis=1, keepdims=True)
            low[column_of(slot), :] = (-2.0 * block).T.astype(jnp.bfloat16)
    norms[...] = jnp.broadcast_to(norm, norms.shape)
    tallies[...] = jnp.zeros_like(tallies)
    sums[...] = jnp.zeros_like(sums)

    def multiply(i, target):
        target[...] = jnp.dot(
            kept[span(i), :], low[...], preferred_element_type=jnp.float32
        ).T

    def collect(i, products):
        energy = products[...] + jnp.concatenate([norms[...]] * (tile // 128), axis=1)
        chosen = chosen_in[pass_index : pass_index + 1, span(i)] - base
        member = lax.broadcasted_iota(jnp.int32, energy.shape, 0) == chosen
        picked = jnp.sum(jnp.where(member, energy, 0.0), axis=0, keepdims=True)
        nearest = jnp.min(energy, axis=0, keepdims=True)
        inside = (chosen >= 0) & (chosen < rows)
        picked_seen = jnp.where(inside, picked, FAR)
        if chained:
            picked_seen = jnp.minimum(picked_seen, seen_in[0:1, span(i)])
            nearest = jnp.minimum(nearest, seen_in[1:2, span(i)])
        seen[0:1, span(i)] = picked_seen
        seen[1:2, span(i)] = nearest
        if first:
            folded = jnp.zeros((tile, 128), jnp.float32)
            for lane in range(0, width, 128):
                values = kept[span(i), lane : lane + 128].astype(jnp.float32)
                folded = folded + values * values
            squares = jnp.sum(folded.T, axis=0, keepdims=True)
            squares_out[0:1, span(i)] = squares
        else:
            squares = squares_in[0:1, span(i)]
        weights = 1.0 / (1.0 + (squares + picked) / width)
        weighted = jnp.where(member, weights, 0.0)
        tally = tallies[...]
        for lane in range(0, tile, 128):
            tally = tally + weighted[:, lane : lane + 128]
        tallies[...] = tally
        factor = as_column(weights, tile)
        for lane in range(0, width, 128):
            values = kept[span(i), lane : lane + 128].astype(jnp.float32)
            scaled[:, lane : lane + 128] = (values * factor).astype(jnp.bfloat16)
        sums[...] += jnp.dot(
            member.astype(jnp.float32).astype(jnp.bfloat16),
            scaled[...],
            preferred_element_type=jnp.float32,
        )

    if stream:
        load_assign.wait()
        load(0).wait()
    multiply(0, even)

    @pl.loop(0, tiles // 2 - 1)
    def _(pair):
        i = 2 * pair
        if stream:
            load(i + 1).wait()
            load(i + 2).wait()
        multiply(i + 1, odd)
        collect(i, even)
        multiply(i + 2, even)
        collect(i + 1, odd)

    if stream:
        load(tiles - 1).wait()
    multiply(tiles - 1, odd)
    collect(tiles - 2, even)
    collect(tiles - 1, odd)

    counts = jnp.broadcast_to(jnp.sum(tallies[...].T, axis=0, keepdims=True), (TAIL, rows))
    for slot in range(SLOTS):
        payload[slot, :rows, :] = sums[:, column_of(slot)]
        payload[slot, rows:, :] = counts


def run_pass(info, points, fine_assign, fine, squares, seen, *, pass_index, flip, rows):
    count, width = points.shape
    block_width = width // SLOTS
    tile = 512
    initial = pass_index == 0
    chained = seen is not None
    stream = not chained
    whole = pl.BlockSpec(memory_space=pltpu.VMEM)
    anywhere = pl.BlockSpec(memory_space=pl.ANY)
    in_hbm = lambda value: pltpu.with_memory_space_constraint(value, pltpu.HBM)
    if stream:
        in_specs = [anywhere, anywhere]
        args = [in_hbm(points), in_hbm(fine_assign)]
    else:
        in_specs = [whole, full(PASSES, count)]
        args = [pltpu.with_memory_space_constraint(points, pltpu.VMEM), fine_assign]
    if not initial:
        in_specs.append(full(SLOTS, rows, block_width))
    elif stream:
        in_specs.append(anywhere)
        fine = in_hbm(fine)
    else:
        in_specs.append(pl.BlockSpec((rows, width), lambda i, info: (info[1] ^ flip, 0)))
    args.append(fine)
    if squares is not None:
        in_specs.append(full(1, count))
        args.append(squares)
    if chained:
        in_specs.append(full(2, count))
        args.append(seen)
    shapes = [(SLOTS, rows + TAIL, block_width), (2, count)]
    if squares is None:
        shapes.append((1, count))
    out_shape = [jax.ShapeDtypeStruct(shape, jnp.float32) for shape in shapes]
    out_specs = [full(*shape) for shape in shapes]
    scratch = [
        pltpu.VMEM((width, rows), jnp.bfloat16),
        pltpu.VMEM((rows, 128), jnp.float32),
        pltpu.VMEM((rows, 128), jnp.float32),
        pltpu.VMEM((rows, width), jnp.float32),
        pltpu.VMEM((rows, tile), jnp.float32),
        pltpu.VMEM((rows, tile), jnp.float32),
        pltpu.VMEM((tile, width), jnp.bfloat16),
    ]
    if stream:
        scratch += [
            pltpu.VMEM((PASSES, count), jnp.int32),
            pltpu.SemaphoreType.DMA((2,)),
            pltpu.SemaphoreType.DMA((count // tile,)),
        ]
        if initial:
            scratch.append(pltpu.VMEM((rows, width), jnp.float32))
        out_shape.append(pltpu.VMEM(points.shape, points.dtype))
        out_specs.append(whole)
    body = functools.partial(
        pass_body,
        pass_index=pass_index,
        flip=flip,
        stream=stream,
        chained=chained,
        tile=tile,
    )
    return pl.pallas_call(
        body,
        out_shape=out_shape,
        grid_spec=pltpu.PrefetchScalarGridSpec(
            num_scalar_prefetch=1,
            grid=(1,),
            in_specs=in_specs,
            out_specs=out_specs,
            scratch_shapes=scratch,
        ),
        compiler_params=pltpu.CompilerParams(vmem_limit_bytes=18 * 2**20),
        cost_estimate=pl.CostEstimate(
            flops=4 * rows * count * width, bytes_accessed=2 * count * width, transcendentals=0
        ),
        name=f"energies_and_sums_{pass_index}{int(chained)}",
    )(info, *args)


def refine_body(info, own, sibling, over_x, over_y, tail, owner, coarse, *outs):
    top, low, part = outs
    rows = owner.shape[1]
    mid = rows // 2
    counts_row = tail[...] + over_y[rows:, :]
    counts = as_column(counts_row[:1], rows)[:, :1]
    table = (
        lax.broadcasted_iota(jnp.int32, (NC, rows), 0) == owner[...]
    ).astype(jnp.float32)
    lookup = lax.dot_general(
        table,
        coarse[...],
        (((0,), (0,)), ((), ())),
        precision=HIGHEST,
        preferred_element_type=jnp.float32,
    )
    totals = (own[:rows, :] + sibling[:rows, :]) + (over_x[...] + over_y[:rows, :])
    new = (totals + prior_weight * lookup) / (counts + prior_weight)
    top[...] = new[:mid]
    low[...] = new[mid:]
    prior = jnp.where(info[3] == 0, prior_weight, 0.0)
    part[:NC, :] = prior * coarse[...] + jnp.dot(
        table, counts * new, precision=HIGHEST, preferred_element_type=jnp.float32
    )
    part[NC:, :] = jnp.zeros((TAIL, part.shape[1]), jnp.float32)
    part[NC:, :NC] = prior + lax.dot_general(
        counts_row,
        table,
        (((1,), (1,)), ((), ())),
        precision=HIGHEST,
        preferred_element_type=jnp.float32,
    )


def refine_half(info, own, sibling, incoming, owners, coarse, *, flip):
    _, rows, block_width = own.shape
    rows -= TAIL
    mid = rows // 2
    slot = pl.BlockSpec((None, rows + TAIL, block_width), lambda i, info: (0, 0, 0))
    wide = coarse.shape[1] != block_width
    return pl.pallas_call(
        refine_body,
        out_shape=[
            jax.ShapeDtypeStruct((mid, block_width), jnp.float32),
            jax.ShapeDtypeStruct((mid, block_width), jnp.float32),
            jax.ShapeDtypeStruct((NC + TAIL, block_width), jnp.float32),
        ],
        grid_spec=pltpu.PrefetchScalarGridSpec(
            num_scalar_prefetch=1,
            grid=(1,),
            in_specs=[slot] * 2
            + [full(*value.shape) for value in incoming]
            + [
                pl.BlockSpec((None, 1, rows), lambda i, info: (info[1] ^ flip, 0, 0)),
                pl.BlockSpec((NC, block_width), lambda i, info: (0, info[0] if wide else 0)),
            ],
            out_specs=[
                full(mid, block_width),
                full(mid, block_width),
                full(NC + TAIL, block_width),
            ],
        ),
        compiler_params=pltpu.CompilerParams(vmem_limit_bytes=16 * 2**20),
        name="refine_half",
    )(info, own, sibling, *incoming, owners, coarse)


def exchange(held, sibling, later):
    rows = held.shape[1] - TAIL
    mid = rows // 2
    top, low, tail = slice(0, mid), slice(mid, rows), slice(rows, rows + TAIL)
    both = lambda slot, part: held[slot, part] + sibling[slot, part]
    counts = both(0, tail)
    corner_top = swap(jnp.concatenate([both(3, top), counts], 0), ACROSS_X)
    corner_low = swap(both(3, low), ACROSS_Y)
    counts = counts + corner_top[mid:]
    to_y = jnp.concatenate([both(2, top) + corner_top[:mid], both(2, low), counts], 0)
    to_x = jnp.concatenate([both(1, top), both(1, low) + corner_low], 0)
    to_y, to_x, later = lax.optimization_barrier((to_y, to_x, later))
    return (swap(to_x, ACROSS_X), swap(to_y, ACROSS_Y), counts), later


def gather_half(top, low, later):
    x_low = swap(low, ACROSS_X)
    y_top = swap(top, ACROSS_Y)
    x_top = swap(top, ACROSS_X)
    y_low = swap(low, ACROSS_Y)
    x_low, y_top, later = lax.optimization_barrier((x_low, y_top, later))
    corner_top = swap(y_top, ACROSS_X)
    corner_low = swap(x_low, ACROSS_Y)
    blocks = [(top, low), (x_top, x_low), (y_top, y_low), (corner_top, corner_low)]
    return [jnp.concatenate(block, 0) for block in blocks], later


def gather_last(top, low):
    mid = top.shape[0]
    block = jnp.concatenate([top, low], 0)
    over_x, over_y = swap(block, ACROSS_X), swap(block, ACROSS_Y)
    corner_top = swap(over_y[:mid], ACROSS_X)
    corner_low = swap(over_x[mid:], ACROSS_Y)
    return jnp.stack([block, over_x, over_y]), jnp.concatenate([corner_top, corner_low], 0)


def spread(value):
    corner = swap(value, ACROSS_X | ACROSS_Y)
    return [value, swap(value, ACROSS_X), swap(value, ACROSS_Y), corner]


def over_cen(value, combine, bits=None):
    for bit in range(lax.axis_size("cen").bit_length() - 1) if bits is None else bits:
        value = combine(value, swap(value, 1 << bit, "cen"))
    return value


def fold(first, second):
    cut = NC + TAIL
    return jnp.concatenate(
        [first[:cut] + second[:cut], jnp.minimum(first[cut:], second[cut:])], 0
    )


def place_body(info, own, other, last, last_other, fine_out, coarse_out):
    _, rows, block_width = own.shape
    here = info[0]

    def column_of(slot):
        return pl.ds(pl.multiple_of((here ^ slot) * block_width, block_width), block_width)

    def put(pieces, corner):
        for slot in range(SLOTS - 1):
            fine_out[:, column_of(slot)] = pieces[slot]
        fine_out[:, column_of(SLOTS - 1)] = corner[:rows, :]

    @pl.when(pl.program_id(0) == 0)
    def _():
        put(own, last)
        part = lambda slot, start, size: (
            last[pl.ds(rows + slot * (NC + TAIL) + start, size), :]
            + last_other[pl.ds(rows + slot * (NC + TAIL) + start, size), :]
        )
        weight = as_column(part(0, NC, TAIL)[:1, :128], 128)[:NC, :1]
        for slot in range(SLOTS):
            coarse_out[:, column_of(slot)] = part(slot, 0, NC) / weight

    @pl.when(pl.program_id(0) == 1)
    def _():
        put(other, last_other)


def place(info, own, other, last, last_other, *, flip):
    _, rows, block_width = own.shape
    width = SLOTS * block_width
    args = [own, other, last, last_other]
    return pl.pallas_call(
        place_body,
        out_shape=[
            jax.ShapeDtypeStruct((2 * rows, width), jnp.float32),
            jax.ShapeDtypeStruct((NC, width), jnp.float32),
        ],
        grid_spec=pltpu.PrefetchScalarGridSpec(
            num_scalar_prefetch=1,
            grid=(2,),
            in_specs=[full(*value.shape) for value in args],
            out_specs=[
                pl.BlockSpec((rows, width), lambda i, info: (info[1] ^ flip ^ i, 0)),
                full(NC, width),
            ],
        ),
        compiler_params=pltpu.CompilerParams(vmem_limit_bytes=24 * 2**20),
        name="place_blocks",
    )(info, *args)


def on_device_paired(points, fine_assign, fine_start, coarse_start, coarse_assign):
    width = points.shape[1]
    local_count = fine_start.shape[0]
    rows = local_count // 2
    block_width = width // SLOTS
    cen, me = lax.axis_index("cen"), lax.axis_index("pts")
    core = me & 1
    info = jnp.stack([me >> 1, core, cen * local_count, cen * 2 + core]).astype(jnp.int32)
    owners = coarse_assign.reshape(2, 1, rows)

    call = functools.partial(run_pass, info, pass_index=0, rows=rows)
    sent, seen, squares, kept = call(points, fine_assign, fine_start, None, None, flip=1)
    sibling = swap(sent, CORE)
    held, seen_first = call(kept, fine_assign, fine_start, squares, seen, flip=0)
    incoming, _ = exchange(held, sibling, ())
    top, low, part = refine_half(info, held, sibling, incoming, owners, coarse_start, flip=0)
    part = part + swap(part, CORE)
    seen_first = seen_first.reshape(-1, block_width)
    own, folded = gather_half(top, low, jnp.concatenate([part, seen_first], 0))
    bits = range(lax.axis_size("cen").bit_length() - 1)
    folded = over_cen(folded, fold, bits[:1])
    own, folded = lax.optimization_barrier((jnp.stack(own), folded))
    other = swap(own, CORE)

    call = functools.partial(run_pass, info, pass_index=1, rows=rows)
    sent, seen, kept = call(points, fine_assign, own, squares, None, flip=0)
    sibling = swap(sent, CORE)
    held, seen_second = call(kept, fine_assign, other, squares, seen, flip=1)

    folded = over_cen(folded, fold, bits[1:])
    part, seen_first = folded[: NC + TAIL], folded[NC + TAIL :]
    coarse = part[:NC] / part[NC, :NC][:, None]

    incoming, seen_second = exchange(held, sibling, seen_second)
    seen_second = over_cen(seen_second, jnp.minimum)
    seen_second, coarse = lax.optimization_barrier((seen_second, coarse))
    top, low, part = refine_half(info, held, sibling, incoming, owners, coarse, flip=1)
    own, corner = gather_last(top, low)
    parts = spread(over_cen(part, jnp.add))
    last = jnp.concatenate([corner, *parts], 0)
    fine_now, coarse_now = place(info, own, swap(own, CORE), last, swap(last, CORE), flip=1)

    gaps = [(seen[0] - seen[1]) for seen in (seen_first.reshape(2, -1), seen_second)]
    return (fine_now, coarse_now, jnp.stack(gaps) / math.sqrt(width))


def solution(mesh):
    placed = (P("pts", None), P(None, "pts"), P("cen", None), P(), P("cen"))

    def on_device(points, fine_assign, fine_start, coarse_start, coarse_assign):
        count, width = points.shape
        local_count = fine_start.shape[0]
        centres = mesh.shape["cen"]
        fits = (
            mesh.shape["pts"] == 2 * SLOTS
            and centres & (centres - 1) == 0
            and width // SLOTS == local_count // 2
            and (width // SLOTS) % 128 == 0
            and count % 1024 == 0
        )
        plan = on_device_paired if fits else on_device_any
        return plan(points, fine_assign, fine_start, coarse_start, coarse_assign)

    return jax.shard_map(
        on_device,
        mesh=mesh,
        in_specs=placed,
        out_specs=(P("cen", None), P(), P(None, "pts")),
        check_vma=False,
    )
```

```python
import functools
import math

import jax
import jax.numpy as jnp
from jax import lax
from jax.experimental import pallas as pl
from jax.experimental.pallas import tpu as pltpu
from jax.sharding import PartitionSpec as P

NC = 64
PASSES = 2
FAR = 3.0e38

prior_weight = 4.0
HIGHEST = lax.Precision.HIGHEST


def refine(totals, counts, coarse_cols, coarse_table):
    lookup = jnp.dot(coarse_table, coarse_cols, precision=HIGHEST)
    fine_next = (totals + prior_weight * lookup) / (counts + prior_weight)[:, None]
    coarse_part = lax.dot_general(
        coarse_table,
        counts[:, None] * fine_next,
        (((0,), (0,)), ((), ())),
        precision=HIGHEST,
    )
    coarse_weight = jnp.sum(coarse_table * counts[:, None], axis=0)
    return (fine_next, coarse_part, coarse_weight)


def on_device_any(points, fine_assign, fine_start, coarse_start, coarse_assign):
    width = points.shape[1]
    local_count = fine_start.shape[0]
    offset = lax.axis_index("cen") * local_count
    columns = jnp.arange(local_count, dtype=jnp.int32)
    coarse_table = (coarse_assign[:, None] == jnp.arange(NC, dtype=jnp.int32)[None, :]).astype(
        jnp.float32
    )
    point_values = points.astype(jnp.float32)
    squares = jnp.sum(point_values * point_values, axis=1)
    fine_now = fine_start
    coarse_now = coarse_start
    gap_rows = []
    for pass_index in range(PASSES):
        member = (fine_assign[pass_index] - offset)[:, None] == columns[None, :]
        products = jnp.dot(
            points, fine_now.astype(jnp.bfloat16).T, preferred_element_type=jnp.float32
        )
        energy = jnp.sum(fine_now * fine_now, axis=1)[None, :] - 2.0 * products
        picked_local = jnp.sum(jnp.where(member, energy, 0.0), axis=1)
        nearest_local = jnp.min(energy, axis=1)
        picked = lax.psum(picked_local, "cen")
        nearest = lax.pmin(nearest_local, "cen")
        gap_rows.append((picked - nearest) / math.sqrt(width))
        weights = 1.0 / (1.0 + (squares + picked) / width)
        scaled = (point_values * weights[:, None]).astype(jnp.bfloat16)
        partial_sums = lax.dot_general(
            member.astype(jnp.bfloat16),
            scaled,
            (((0,), (0,)), ((), ())),
            preferred_element_type=jnp.float32,
        )
        partial_weights = jnp.sum(jnp.where(member, weights[:, None], 0.0), axis=0)
        share_width = width // lax.axis_size("pts")
        start = lax.axis_index("pts") * share_width
        shares = lax.psum_scatter(partial_sums, "pts", scatter_dimension=1, tiled=True)
        counts = lax.psum(partial_weights, "pts")
        coarse_cols = lax.dynamic_slice_in_dim(coarse_now, start, share_width, 1)
        fine_share, coarse_part, coarse_weight = refine(shares, counts, coarse_cols, coarse_table)
        coarse_sum, coarse_count = lax.psum((coarse_part, coarse_weight), "cen")
        coarse_share = (coarse_sum + prior_weight * coarse_cols) / (coarse_count + prior_weight)[
            :, None
        ]
        fine_now, coarse_now = (
            lax.all_gather(fine_share, "pts", axis=1, tiled=True),
            lax.all_gather(coarse_share, "pts", axis=1, tiled=True),
        )
    return (fine_now, coarse_now, jnp.stack(gap_rows))


CORE, ACROSS_X, ACROSS_Y = 1, 2, 4
SLOTS = 4
TAIL = 8


def swap(value, bit, axis="pts"):
    size = lax.axis_size(axis)
    return lax.ppermute(value, axis, [(i, i ^ bit) for i in range(size)])


def swap_first(value):
    pairs = [(i, i ^ (ACROSS_Y if i & CORE else ACROSS_X)) for i in range(lax.axis_size("pts"))]
    return lax.ppermute(value, "pts", pairs)


def swap_second(value):
    pairs = [(i, i ^ (ACROSS_X if i & CORE else ACROSS_Y)) for i in range(lax.axis_size("pts"))]
    return lax.ppermute(value, "pts", pairs)


def block_of(info, slot, core):
    crossed = (slot >> 1) | ((slot & 1) << 1)
    return info[0] ^ (slot + core * (crossed - slot))


def full(*shape):
    return pl.BlockSpec(shape, lambda i, info: (0,) * len(shape))


def as_column(row, rows):
    return jnp.broadcast_to(row, (128, rows)).T


def pass_body(info, points, assign, fine, *refs, pass_index, flip, stream, chained, tile):
    refs = list(refs)
    initial = pass_index == 0
    first = initial and stream
    squares_in = None if first else refs.pop(0)
    seen_in = refs.pop(0) if chained else None
    payload, seen = refs.pop(0), refs.pop(0)
    squares_out = refs.pop(0) if first else None
    kept = refs.pop(0) if stream else points
    low, norms, tallies, sums, even, odd, scaled = refs[:7]
    chosen_in = refs[7] if stream else assign
    small_sems, point_sems = refs[8:10] if stream else (None, None)
    start = refs[10] if first else fine
    rows, width = low.shape
    block_width = width // SLOTS
    half = info[1] ^ flip
    base = info[2] + half * rows
    tiles = points.shape[0] // tile

    def span(i):
        return pl.ds(pl.multiple_of(i * tile, tile), tile)

    def column_of(slot, core):
        start = block_of(info, slot, core) * block_width
        return pl.ds(pl.multiple_of(start, block_width), block_width)

    def load(i):
        return pltpu.make_async_copy(points.at[span(i)], kept.at[span(i)], point_sems.at[i])

    if first:
        load_start = pltpu.make_async_copy(
            fine.at[pl.ds(pl.multiple_of(half * rows, rows), rows)], start, small_sems.at[1]
        )
        load_start.start()
    if stream:
        load(0).start()
        load_assign = pltpu.make_async_copy(assign, chosen_in, small_sems.at[0])
        load_assign.start()

        @pl.loop(1, tiles)
        def _(i):
            load(i).start()

    if initial:
        if first:
            load_start.wait()
        block = start[...]
        norm = jnp.sum(block * block, axis=1, keepdims=True)
        low[...] = (-2.0 * block).astype(jnp.bfloat16)
    else:
        norm = jnp.zeros((rows, 1), jnp.float32)
        for slot in range(SLOTS):
            block = fine[slot]
            norm = norm + jnp.sum(block * block, axis=1, keepdims=True)
            low[:, column_of(slot, info[1] ^ chained)] = (-2.0 * block).astype(jnp.bfloat16)
    norms[...] = jnp.broadcast_to(norm, norms.shape)
    tallies[...] = jnp.zeros_like(tallies)
    sums[...] = jnp.zeros_like(sums)

    def multiply(i, target):
        target[...] = lax.dot_general(
            low[...], kept[span(i), :], (((1,), (1,)), ((), ())), preferred_element_type=jnp.float32
        )

    def collect(i, products):
        energy = products[...] + jnp.concatenate([norms[...]] * (tile // 128), axis=1)
        chosen = chosen_in[pass_index : pass_index + 1, span(i)] - base
        member = lax.broadcasted_iota(jnp.int32, energy.shape, 0) == chosen
        picked = jnp.sum(jnp.where(member, energy, 0.0), axis=0, keepdims=True)
        nearest = jnp.min(energy, axis=0, keepdims=True)
        inside = (chosen >= 0) & (chosen < rows)
        picked_seen = jnp.where(inside, picked, FAR)
        if chained:
            picked_seen = jnp.minimum(picked_seen, seen_in[0:1, span(i)])
            nearest = jnp.minimum(nearest, seen_in[1:2, span(i)])
        seen[0:1, span(i)] = picked_seen
        seen[1:2, span(i)] = nearest
        if first:
            folded = jnp.zeros((tile, 128), jnp.float32)
            for lane in range(0, width, 128):
                values = kept[span(i), lane : lane + 128].astype(jnp.float32)
                folded = folded + values * values
            squares = jnp.sum(folded.T, axis=0, keepdims=True)
            squares_out[0:1, span(i)] = squares
        else:
            squares = squares_in[0:1, span(i)]
        weights = 1.0 / (1.0 + (squares + picked) / width)
        weighted = jnp.where(member, weights, 0.0)
        tally = tallies[...]
        for lane in range(0, tile, 128):
            tally = tally + weighted[:, lane : lane + 128]
        tallies[...] = tally
        factor = as_column(weights, tile)
        for lane in range(0, width, 128):
            values = kept[span(i), lane : lane + 128].astype(jnp.float32)
            scaled[:, lane : lane + 128] = (values * factor).astype(jnp.bfloat16)
        sums[...] += jnp.dot(
            member.astype(jnp.float32).astype(jnp.bfloat16),
            scaled[...],
            preferred_element_type=jnp.float32,
        )

    if stream:
        load_assign.wait()
        load(0).wait()
    multiply(0, even)

    @pl.loop(0, tiles // 2 - 1)
    def _(pair):
        i = 2 * pair
        if stream:
            load(i + 1).wait()
            load(i + 2).wait()
        multiply(i + 1, odd)
        collect(i, even)
        multiply(i + 2, even)
        collect(i + 1, odd)

    if stream:
        load(tiles - 1).wait()
    multiply(tiles - 1, odd)
    collect(tiles - 2, even)
    collect(tiles - 1, odd)

    counts = jnp.broadcast_to(jnp.sum(tallies[...].T, axis=0, keepdims=True), (TAIL, rows))
    for slot in range(SLOTS):
        payload[slot, :rows, :] = sums[:, column_of(slot, info[1] ^ (not chained))]
        payload[slot, rows:, :] = counts


def run_pass(info, points, fine_assign, fine, squares, seen, *, pass_index, flip, rows):
    count, width = points.shape
    block_width = width // SLOTS
    tile = 512
    initial = pass_index == 0
    chained = seen is not None
    stream = not chained
    whole = pl.BlockSpec(memory_space=pltpu.VMEM)
    anywhere = pl.BlockSpec(memory_space=pl.ANY)
    in_hbm = lambda value: pltpu.with_memory_space_constraint(value, pltpu.HBM)
    if stream:
        in_specs = [anywhere, anywhere]
        args = [in_hbm(points), in_hbm(fine_assign)]
    else:
        in_specs = [whole, full(PASSES, count)]
        args = [pltpu.with_memory_space_constraint(points, pltpu.VMEM), fine_assign]
    if not initial:
        in_specs.append(full(SLOTS, rows, block_width))
    elif stream:
        in_specs.append(anywhere)
        fine = in_hbm(fine)
    else:
        in_specs.append(pl.BlockSpec((rows, width), lambda i, info: (info[1] ^ flip, 0)))
    args.append(fine)
    if squares is not None:
        in_specs.append(full(1, count))
        args.append(squares)
    if chained:
        in_specs.append(full(2, count))
        args.append(seen)
    shapes = [(SLOTS, rows + TAIL, block_width), (2, count)]
    if squares is None:
        shapes.append((1, count))
    out_shape = [jax.ShapeDtypeStruct(shape, jnp.float32) for shape in shapes]
    out_specs = [full(*shape) for shape in shapes]
    scratch = [
        pltpu.VMEM((rows, width), jnp.bfloat16),
        pltpu.VMEM((rows, 128), jnp.float32),
        pltpu.VMEM((rows, 128), jnp.float32),
        pltpu.VMEM((rows, width), jnp.float32),
        pltpu.VMEM((rows, tile), jnp.float32),
        pltpu.VMEM((rows, tile), jnp.float32),
        pltpu.VMEM((tile, width), jnp.bfloat16),
    ]
    if stream:
        scratch += [
            pltpu.VMEM((PASSES, count), jnp.int32),
            pltpu.SemaphoreType.DMA((2,)),
            pltpu.SemaphoreType.DMA((count // tile,)),
        ]
        if initial:
            scratch.append(pltpu.VMEM((rows, width), jnp.float32))
        out_shape.append(pltpu.VMEM(points.shape, points.dtype))
        out_specs.append(whole)
    body = functools.partial(
        pass_body,
        pass_index=pass_index,
        flip=flip,
        stream=stream,
        chained=chained,
        tile=tile,
    )
    return pl.pallas_call(
        body,
        out_shape=out_shape,
        grid_spec=pltpu.PrefetchScalarGridSpec(
            num_scalar_prefetch=1,
            grid=(1,),
            in_specs=in_specs,
            out_specs=out_specs,
            scratch_shapes=scratch,
        ),
        compiler_params=pltpu.CompilerParams(vmem_limit_bytes=18 * 2**20),
        cost_estimate=pl.CostEstimate(
            flops=4 * rows * count * width, bytes_accessed=2 * count * width, transcendentals=0
        ),
        name=f"energies_and_sums_{pass_index}{int(chained)}",
    )(info, *args)


def refine_body(info, own, sibling, first, second, owner, coarse, fine, part):
    rows = owner.shape[1]
    total = (own[...] + sibling[...]) + (first[...] + second[...])
    totals, counts_row = total[:rows], total[rows:]
    counts = as_column(counts_row[:1], rows)[:, :1]
    table = (
        lax.broadcasted_iota(jnp.int32, (NC, rows), 0) == owner[...]
    ).astype(jnp.float32)
    lookup = lax.dot_general(
        table,
        coarse[...],
        (((0,), (0,)), ((), ())),
        precision=HIGHEST,
        preferred_element_type=jnp.float32,
    )
    new = (totals + prior_weight * lookup) / (counts + prior_weight)
    fine[...] = new
    prior = jnp.where(info[3] == 0, prior_weight, 0.0)
    part[:NC, :] = prior * coarse[...] + jnp.dot(
        table, counts * new, precision=HIGHEST, preferred_element_type=jnp.float32
    )
    part[NC:, :] = jnp.zeros((TAIL, part.shape[1]), jnp.float32)
    part[NC:, :NC] = prior + lax.dot_general(
        counts_row,
        table,
        (((1,), (1,)), ((), ())),
        precision=HIGHEST,
        preferred_element_type=jnp.float32,
    )


def refine_half(info, own, sibling, first, second, owners, coarse, *, flip):
    _, rows, block_width = own.shape
    rows -= TAIL
    slot = pl.BlockSpec((None, rows + TAIL, block_width), lambda i, info: (0, 0, 0))
    wide = coarse.shape[1] != block_width
    return pl.pallas_call(
        refine_body,
        out_shape=[
            jax.ShapeDtypeStruct((rows, block_width), jnp.float32),
            jax.ShapeDtypeStruct((NC + TAIL, block_width), jnp.float32),
        ],
        grid_spec=pltpu.PrefetchScalarGridSpec(
            num_scalar_prefetch=1,
            grid=(1,),
            in_specs=[
                slot,
                slot,
                slot,
                full(*second.shape),
                pl.BlockSpec((None, 1, rows), lambda i, info: (info[1] ^ flip, 0, 0)),
                pl.BlockSpec((NC, block_width), lambda i, info: (0, info[0] if wide else 0)),
            ],
            out_specs=[full(rows, block_width), full(NC + TAIL, block_width)],
        ),
        compiler_params=pltpu.CompilerParams(vmem_limit_bytes=16 * 2**20),
        name="refine_half",
    )(info, own, sibling, first, second, owners, coarse)


def exchange(held, sibling):
    first = swap_first(held[1::2] + sibling[1::2])
    second = swap_second(held[2] + sibling[2] + first[1])
    return first, second


def over_cen(value, combine, bits=None):
    for bit in range(lax.axis_size("cen").bit_length() - 1) if bits is None else bits:
        value = combine(value, swap(value, 1 << bit, "cen"))
    return value


def fold(first, second):
    cut = NC + TAIL
    return jnp.concatenate(
        [first[:cut] + second[:cut], jnp.minimum(first[cut:], second[cut:])], 0
    )


def place_body(info, own, other, last, last_other, fine_out, coarse_out):
    _, rows, block_width = own.shape

    def column_of(slot, core):
        start = block_of(info, slot, core) * block_width
        return pl.ds(pl.multiple_of(start, block_width), block_width)

    def put(near, far, core):
        for slot in range(SLOTS):
            block = far[slot // 2, :rows, :] if slot % 2 else near[slot // 2]
            fine_out[:, column_of(slot, core)] = block

    @pl.when(pl.program_id(0) == 0)
    def _():
        put(own, last, info[1])
        def part(source, slot, start, size):
            top = rows + (0 if slot % 2 else NC + TAIL) + start
            return source[slot // 2, top : top + size, :]

        weight = part(last, 0, NC, TAIL) + part(last_other, 0, NC, TAIL)
        weight = as_column(weight[:1, :128], 128)[:NC, :1]
        for slot, crossed in enumerate((0, 2, 1, 3)):
            total = part(last, slot, 0, NC) + part(last_other, crossed, 0, NC)
            coarse_out[:, column_of(slot, info[1])] = total / weight

    @pl.when(pl.program_id(0) == 1)
    def _():
        put(other, last_other, 1 - info[1])


def place(info, own, other, last, last_other, *, flip):
    _, rows, block_width = own.shape
    width = SLOTS * block_width
    args = [own, other, last, last_other]
    return pl.pallas_call(
        place_body,
        out_shape=[
            jax.ShapeDtypeStruct((2 * rows, width), jnp.float32),
            jax.ShapeDtypeStruct((NC, width), jnp.float32),
        ],
        grid_spec=pltpu.PrefetchScalarGridSpec(
            num_scalar_prefetch=1,
            grid=(2,),
            in_specs=[full(*value.shape) for value in args],
            out_specs=[
                pl.BlockSpec((rows, width), lambda i, info: (info[1] ^ flip ^ i, 0)),
                full(NC, width),
            ],
        ),
        compiler_params=pltpu.CompilerParams(vmem_limit_bytes=24 * 2**20),
        name="place_blocks",
    )(info, *args)


def on_device_paired(points, fine_assign, fine_start, coarse_start, coarse_assign):
    width = points.shape[1]
    local_count = fine_start.shape[0]
    rows = local_count // 2
    block_width = width // SLOTS
    cen, me = lax.axis_index("cen"), lax.axis_index("pts")
    core = me & 1
    info = jnp.stack([me >> 1, core, cen * local_count, cen * 2 + core]).astype(jnp.int32)
    owners = coarse_assign.reshape(2, 1, rows)

    call = functools.partial(run_pass, info, pass_index=0, rows=rows)
    sent, seen, squares, kept = call(points, fine_assign, fine_start, None, None, flip=1)
    sibling = swap(sent, CORE)
    held, seen_first = call(kept, fine_assign, fine_start, squares, seen, flip=0)
    first, second = exchange(held, sibling)
    fine, part = refine_half(
        info, held, sibling, first, second, owners, coarse_start, flip=0
    )
    part = part + swap(part, CORE)
    near = jnp.stack([fine, swap_second(fine)])
    far = swap_first(near)
    bits = range(lax.axis_size("cen").bit_length() - 1)
    folded = jnp.concatenate([part, seen_first.reshape(-1, block_width)], 0)
    folded = over_cen(folded, fold, bits[:1])
    own = jnp.stack([near[0], far[0], near[1], far[1]])
    own, folded = lax.optimization_barrier((own, folded))
    other = swap(own, CORE)

    call = functools.partial(run_pass, info, pass_index=1, rows=rows)
    sent, seen, kept = call(points, fine_assign, own, squares, None, flip=0)
    sibling = swap(sent, CORE)
    held, seen_second = call(kept, fine_assign, other, squares, seen, flip=1)
    first, second = exchange(held, sibling)

    folded = over_cen(folded, fold, bits[1:])
    part, seen_first = folded[: NC + TAIL], folded[NC + TAIL :]
    coarse = part[:NC] / part[NC, :NC][:, None]
    seen_second = over_cen(seen_second, jnp.minimum)

    fine, part = refine_half(info, held, sibling, first, second, owners, coarse, flip=1)
    near = jnp.stack([fine, swap_second(fine)])
    far = swap_first(near)
    part = over_cen(part, jnp.add)
    parts = jnp.stack([part, swap_second(part)])
    last = jnp.concatenate([far, swap_first(parts), parts], 1)
    fine_now, coarse_now = place(info, near, swap(near, CORE), last, swap(last, CORE), flip=1)

    gaps = [(seen[0] - seen[1]) for seen in (seen_first.reshape(2, -1), seen_second)]
    return (fine_now, coarse_now, jnp.stack(gaps) / math.sqrt(width))


def solution(mesh):
    placed = (P("pts", None), P(None, "pts"), P("cen", None), P(), P("cen"))

    def on_device(points, fine_assign, fine_start, coarse_start, coarse_assign):
        count, width = points.shape
        local_count = fine_start.shape[0]
        centres = mesh.shape["cen"]
        fits = (
            mesh.shape["pts"] == 2 * SLOTS
            and centres & (centres - 1) == 0
            and width // SLOTS == local_count // 2
            and (width // SLOTS) % 128 == 0
            and count % 1024 == 0
        )
        plan = on_device_paired if fits else on_device_any
        return plan(points, fine_assign, fine_start, coarse_start, coarse_assign)

    return jax.shard_map(
        on_device,
        mesh=mesh,
        in_specs=placed,
        out_specs=(P("cen", None), P(), P(None, "pts")),
        check_vma=False,
    )
```

```python
import functools
import math

import jax
import jax.numpy as jnp
from jax import lax
from jax.experimental import pallas as pl
from jax.experimental.pallas import tpu as pltpu
from jax.sharding import PartitionSpec as P

NC = 64
PASSES = 2
FAR = 3.0e38

prior_weight = 4.0
HIGHEST = lax.Precision.HIGHEST


def refine(totals, counts, coarse_cols, coarse_table):
    lookup = jnp.dot(coarse_table, coarse_cols, precision=HIGHEST)
    fine_next = (totals + prior_weight * lookup) / (counts + prior_weight)[:, None]
    coarse_part = lax.dot_general(
        coarse_table,
        counts[:, None] * fine_next,
        (((0,), (0,)), ((), ())),
        precision=HIGHEST,
    )
    coarse_weight = jnp.sum(coarse_table * counts[:, None], axis=0)
    return (fine_next, coarse_part, coarse_weight)


def on_device_any(points, fine_assign, fine_start, coarse_start, coarse_assign):
    width = points.shape[1]
    local_count = fine_start.shape[0]
    offset = lax.axis_index("cen") * local_count
    columns = jnp.arange(local_count, dtype=jnp.int32)
    coarse_table = (coarse_assign[:, None] == jnp.arange(NC, dtype=jnp.int32)[None, :]).astype(
        jnp.float32
    )
    point_values = points.astype(jnp.float32)
    squares = jnp.sum(point_values * point_values, axis=1)
    fine_now = fine_start
    coarse_now = coarse_start
    gap_rows = []
    for pass_index in range(PASSES):
        member = (fine_assign[pass_index] - offset)[:, None] == columns[None, :]
        products = jnp.dot(
            points, fine_now.astype(jnp.bfloat16).T, preferred_element_type=jnp.float32
        )
        energy = jnp.sum(fine_now * fine_now, axis=1)[None, :] - 2.0 * products
        picked_local = jnp.sum(jnp.where(member, energy, 0.0), axis=1)
        nearest_local = jnp.min(energy, axis=1)
        picked = lax.psum(picked_local, "cen")
        nearest = lax.pmin(nearest_local, "cen")
        gap_rows.append((picked - nearest) / math.sqrt(width))
        weights = 1.0 / (1.0 + (squares + picked) / width)
        scaled = (point_values * weights[:, None]).astype(jnp.bfloat16)
        partial_sums = lax.dot_general(
            member.astype(jnp.bfloat16),
            scaled,
            (((0,), (0,)), ((), ())),
            preferred_element_type=jnp.float32,
        )
        partial_weights = jnp.sum(jnp.where(member, weights[:, None], 0.0), axis=0)
        share_width = width // lax.axis_size("pts")
        start = lax.axis_index("pts") * share_width
        shares = lax.psum_scatter(partial_sums, "pts", scatter_dimension=1, tiled=True)
        counts = lax.psum(partial_weights, "pts")
        coarse_cols = lax.dynamic_slice_in_dim(coarse_now, start, share_width, 1)
        fine_share, coarse_part, coarse_weight = refine(shares, counts, coarse_cols, coarse_table)
        coarse_sum, coarse_count = lax.psum((coarse_part, coarse_weight), "cen")
        coarse_share = (coarse_sum + prior_weight * coarse_cols) / (coarse_count + prior_weight)[
            :, None
        ]
        fine_now, coarse_now = (
            lax.all_gather(fine_share, "pts", axis=1, tiled=True),
            lax.all_gather(coarse_share, "pts", axis=1, tiled=True),
        )
    return (fine_now, coarse_now, jnp.stack(gap_rows))


CORE, ACROSS_X, ACROSS_Y = 1, 2, 4
SLOTS = 4
TAIL = 8


def swap(value, bit, axis="pts"):
    size = lax.axis_size(axis)
    return lax.ppermute(value, axis, [(i, i ^ bit) for i in range(size)])


def swap_first(value):
    pairs = [(i, i ^ (ACROSS_Y if i & CORE else ACROSS_X)) for i in range(lax.axis_size("pts"))]
    return lax.ppermute(value, "pts", pairs)


def swap_second(value):
    pairs = [(i, i ^ (ACROSS_X if i & CORE else ACROSS_Y)) for i in range(lax.axis_size("pts"))]
    return lax.ppermute(value, "pts", pairs)


def block_of(info, slot, core):
    crossed = (slot >> 1) | ((slot & 1) << 1)
    return info[0] ^ (slot + core * (crossed - slot))


def full(*shape):
    return pl.BlockSpec(shape, lambda i, info: (0,) * len(shape))


def as_column(row, rows):
    return jnp.broadcast_to(row, (128, rows)).T


def pass_body(info, points, assign, fine, *refs, pass_index, flip, stream, chained, tile):
    refs = list(refs)
    initial = pass_index == 0
    first = initial and stream
    squares_in = None if first else refs.pop(0)
    seen_in = refs.pop(0) if chained else None
    payload, seen = refs.pop(0), refs.pop(0)
    squares_out = refs.pop(0) if first else None
    kept = refs.pop(0) if stream else points
    low, norms, tallies, sums, even, odd, scaled = refs[:7]
    chosen_in = refs[7] if stream else assign
    small_sems, point_sems = refs[8:10] if stream else (None, None)
    start = refs[10] if first else fine
    rows, width = low.shape
    mid = rows // 2
    block_width = width // SLOTS
    half = info[1] ^ flip
    base = info[2] + half * rows
    tiles = points.shape[0] // tile

    def span(i):
        return pl.ds(pl.multiple_of(i * tile, tile), tile)

    def column_of(slot, core):
        start = block_of(info, slot, core) * block_width
        return pl.ds(pl.multiple_of(start, block_width), block_width)

    def load(i):
        return pltpu.make_async_copy(points.at[span(i)], kept.at[span(i)], point_sems.at[i])

    if first:
        load_start = pltpu.make_async_copy(
            fine.at[pl.ds(pl.multiple_of(half * rows, rows), rows)], start, small_sems.at[1]
        )
        load_start.start()
    if stream:
        load(0).start()
        load_assign = pltpu.make_async_copy(assign, chosen_in, small_sems.at[0])
        load_assign.start()

        @pl.loop(1, tiles)
        def _(i):
            load(i).start()

    if initial:
        if first:
            load_start.wait()
        block = start[...]
        norm = jnp.sum(block * block, axis=1, keepdims=True)
        low[...] = (-2.0 * block).astype(jnp.bfloat16)
    else:
        norm = jnp.zeros((rows, 1), jnp.float32)
        for slot in range(SLOTS):
            block = fine[slot]
            norm = norm + jnp.sum(block * block, axis=1, keepdims=True)
            low[:, column_of(slot, 0)] = (-2.0 * block).astype(jnp.bfloat16)
    norms[...] = jnp.broadcast_to(norm, norms.shape)
    tallies[...] = jnp.zeros_like(tallies)
    sums[...] = jnp.zeros_like(sums)

    def multiply(i, target):
        target[...] = lax.dot_general(
            low[...], kept[span(i), :], (((1,), (1,)), ((), ())), preferred_element_type=jnp.float32
        )

    def collect(i, products):
        energy = products[...] + jnp.concatenate([norms[...]] * (tile // 128), axis=1)
        chosen = chosen_in[pass_index : pass_index + 1, span(i)] - base
        member = lax.broadcasted_iota(jnp.int32, energy.shape, 0) == chosen
        picked = jnp.sum(jnp.where(member, energy, 0.0), axis=0, keepdims=True)
        nearest = jnp.min(energy, axis=0, keepdims=True)
        inside = (chosen >= 0) & (chosen < rows)
        picked_seen = jnp.where(inside, picked, FAR)
        if chained:
            picked_seen = jnp.minimum(picked_seen, seen_in[0:1, span(i)])
            nearest = jnp.minimum(nearest, seen_in[1:2, span(i)])
        seen[0:1, span(i)] = picked_seen
        seen[1:2, span(i)] = nearest
        if first:
            folded = jnp.zeros((tile, 128), jnp.float32)
            for lane in range(0, width, 128):
                values = kept[span(i), lane : lane + 128].astype(jnp.float32)
                folded = folded + values * values
            squares = jnp.sum(folded.T, axis=0, keepdims=True)
            squares_out[0:1, span(i)] = squares
        else:
            squares = squares_in[0:1, span(i)]
        weights = 1.0 / (1.0 + (squares + picked) / width)
        weighted = jnp.where(member, weights, 0.0)
        tally = tallies[...]
        for lane in range(0, tile, 128):
            tally = tally + weighted[:, lane : lane + 128]
        tallies[...] = tally
        factor = as_column(weights, tile)
        for lane in range(0, width, 128):
            values = kept[span(i), lane : lane + 128].astype(jnp.float32)
            scaled[:, lane : lane + 128] = (values * factor).astype(jnp.bfloat16)
        sums[...] += jnp.dot(
            member.astype(jnp.float32).astype(jnp.bfloat16),
            scaled[...],
            preferred_element_type=jnp.float32,
        )

    if stream:
        load_assign.wait()
        load(0).wait()
    multiply(0, even)

    @pl.loop(0, tiles // 2 - 1)
    def _(pair):
        i = 2 * pair
        if stream:
            load(i + 1).wait()
            load(i + 2).wait()
        multiply(i + 1, odd)
        collect(i, even)
        multiply(i + 2, even)
        collect(i + 1, odd)

    if stream:
        load(tiles - 1).wait()
    multiply(tiles - 1, odd)
    collect(tiles - 2, even)
    collect(tiles - 1, odd)

    counts = jnp.broadcast_to(jnp.sum(tallies[...].T, axis=0, keepdims=True), (TAIL, rows))
    for slot in range(SLOTS):
        columns = column_of(slot, info[1] ^ (not chained))
        payload[slot, :mid, :] = sums[:mid, columns]
        payload[slot, mid : mid + TAIL, :] = counts
        payload[slot, mid + TAIL :, :] = sums[mid:, columns]


def run_pass(info, points, fine_assign, fine, squares, seen, *, pass_index, flip, rows):
    count, width = points.shape
    block_width = width // SLOTS
    tile = 512
    initial = pass_index == 0
    chained = seen is not None
    stream = not chained
    whole = pl.BlockSpec(memory_space=pltpu.VMEM)
    anywhere = pl.BlockSpec(memory_space=pl.ANY)
    in_hbm = lambda value: pltpu.with_memory_space_constraint(value, pltpu.HBM)
    if stream:
        in_specs = [anywhere, anywhere]
        args = [in_hbm(points), in_hbm(fine_assign)]
    else:
        in_specs = [whole, full(PASSES, count)]
        args = [pltpu.with_memory_space_constraint(points, pltpu.VMEM), fine_assign]
    if not initial:
        in_specs.append(full(SLOTS, rows, block_width))
    elif stream:
        in_specs.append(anywhere)
        fine = in_hbm(fine)
    else:
        in_specs.append(pl.BlockSpec((rows, width), lambda i, info: (info[1] ^ flip, 0)))
    args.append(fine)
    if squares is not None:
        in_specs.append(full(1, count))
        args.append(squares)
    if chained:
        in_specs.append(full(2, count))
        args.append(seen)
    shapes = [(SLOTS, rows + TAIL, block_width), (2, count)]
    if squares is None:
        shapes.append((1, count))
    out_shape = [jax.ShapeDtypeStruct(shape, jnp.float32) for shape in shapes]
    out_specs = [full(*shape) for shape in shapes]
    scratch = [
        pltpu.VMEM((rows, width), jnp.bfloat16),
        pltpu.VMEM((rows, 128), jnp.float32),
        pltpu.VMEM((rows, 128), jnp.float32),
        pltpu.VMEM((rows, width), jnp.float32),
        pltpu.VMEM((rows, tile), jnp.float32),
        pltpu.VMEM((rows, tile), jnp.float32),
        pltpu.VMEM((tile, width), jnp.bfloat16),
    ]
    if stream:
        scratch += [
            pltpu.VMEM((PASSES, count), jnp.int32),
            pltpu.SemaphoreType.DMA((2,)),
            pltpu.SemaphoreType.DMA((count // tile,)),
        ]
        if initial:
            scratch.append(pltpu.VMEM((rows, width), jnp.float32))
        out_shape.append(pltpu.VMEM(points.shape, points.dtype))
        out_specs.append(whole)
    body = functools.partial(
        pass_body,
        pass_index=pass_index,
        flip=flip,
        stream=stream,
        chained=chained,
        tile=tile,
    )
    return pl.pallas_call(
        body,
        out_shape=out_shape,
        grid_spec=pltpu.PrefetchScalarGridSpec(
            num_scalar_prefetch=1,
            grid=(1,),
            in_specs=in_specs,
            out_specs=out_specs,
            scratch_shapes=scratch,
        ),
        compiler_params=pltpu.CompilerParams(vmem_limit_bytes=18 * 2**20),
        cost_estimate=pl.CostEstimate(
            flops=4 * rows * count * width, bytes_accessed=2 * count * width, transcendentals=0
        ),
        name=f"energies_and_sums_{pass_index}{int(chained)}",
    )(info, *args)


def refine_body(info, own, sibling, *refs):
    first_top, first_low, second_top, second_low, owner, coarse, top, low, part = refs
    rows = owner.shape[1]
    mid = rows // 2
    total = own[...] + sibling[...]
    head = total[: mid + TAIL] + (first_top[...] + second_top[...])
    rest = total[mid + TAIL :] + (first_low[...] + second_low[...])
    totals, counts_row = jnp.concatenate([head[:mid], rest], 0), head[mid:]
    counts = as_column(counts_row[:1], rows)[:, :1]
    table = (
        lax.broadcasted_iota(jnp.int32, (NC, rows), 0) == owner[...]
    ).astype(jnp.float32)
    lookup = lax.dot_general(
        table,
        coarse[...],
        (((0,), (0,)), ((), ())),
        precision=HIGHEST,
        preferred_element_type=jnp.float32,
    )
    new = (totals + prior_weight * lookup) / (counts + prior_weight)
    top[...] = new[:mid]
    low[...] = new[mid:]
    prior = jnp.where(info[3] == 0, prior_weight, 0.0)
    part[:NC, :] = prior * coarse[...] + jnp.dot(
        table, counts * new, precision=HIGHEST, preferred_element_type=jnp.float32
    )
    part[NC:, :] = jnp.zeros((TAIL, part.shape[1]), jnp.float32)
    part[NC:, :NC] = prior + lax.dot_general(
        counts_row,
        table,
        (((1,), (1,)), ((), ())),
        precision=HIGHEST,
        preferred_element_type=jnp.float32,
    )


def refine_half(info, own, sibling, incoming, owners, coarse, *, flip):
    _, rows, block_width = own.shape
    rows -= TAIL
    mid = rows // 2
    leading = lambda size: pl.BlockSpec((None, size, block_width), lambda i, info: (0, 0, 0))
    wide = coarse.shape[1] != block_width
    return pl.pallas_call(
        refine_body,
        out_shape=[
            jax.ShapeDtypeStruct((mid, block_width), jnp.float32),
            jax.ShapeDtypeStruct((mid, block_width), jnp.float32),
            jax.ShapeDtypeStruct((NC + TAIL, block_width), jnp.float32),
        ],
        grid_spec=pltpu.PrefetchScalarGridSpec(
            num_scalar_prefetch=1,
            grid=(1,),
            in_specs=[
                leading(rows + TAIL),
                leading(rows + TAIL),
                leading(mid + TAIL),
                leading(mid),
                full(mid + TAIL, block_width),
                full(mid, block_width),
                pl.BlockSpec((None, 1, rows), lambda i, info: (info[1] ^ flip, 0, 0)),
                pl.BlockSpec((NC, block_width), lambda i, info: (0, info[0] if wide else 0)),
            ],
            out_specs=[
                full(mid, block_width),
                full(mid, block_width),
                full(NC + TAIL, block_width),
            ],
        ),
        compiler_params=pltpu.CompilerParams(vmem_limit_bytes=16 * 2**20),
        name="refine_half",
    )(info, own, sibling, *incoming, owners, coarse)


def exchange(held, sibling, later=()):
    cut = (held.shape[1] - TAIL) // 2 + TAIL
    chunks = slice(0, cut), slice(cut, None)
    first = [swap_first(held[1::2, rows] + sibling[1::2, rows]) for rows in chunks]
    first[0], later = lax.optimization_barrier((first[0], later))
    second = [
        swap_second(held[2, rows] + sibling[2, rows] + arrived[1])
        for rows, arrived in zip(chunks, first)
    ]
    return [*first, *second], later


def gather_half(top, low):
    x_low = swap(low, ACROSS_X)
    y_top = swap(top, ACROSS_Y)
    x_top = swap(top, ACROSS_X)
    y_low = swap(low, ACROSS_Y)
    corner_top = swap(y_top, ACROSS_X)
    corner_low = swap(x_low, ACROSS_Y)
    blocks = [(top, low), (x_top, x_low), (y_top, y_low), (corner_top, corner_low)]
    return [jnp.concatenate(block, 0) for block in blocks]


def over_cen(value, combine, bits=None):
    for bit in range(lax.axis_size("cen").bit_length() - 1) if bits is None else bits:
        value = combine(value, swap(value, 1 << bit, "cen"))
    return value


def fold(first, second):
    cut = NC + TAIL
    return jnp.concatenate(
        [first[:cut] + second[:cut], jnp.minimum(first[cut:], second[cut:])], 0
    )


def place_body(info, own, other, last, last_other, fine_out, coarse_out):
    _, rows, block_width = own.shape

    def column_of(slot, core):
        start = block_of(info, slot, core) * block_width
        return pl.ds(pl.multiple_of(start, block_width), block_width)

    def put(near, far, core):
        for slot in range(SLOTS):
            block = far[slot // 2, :rows, :] if slot % 2 else near[slot // 2]
            fine_out[:, column_of(slot, core)] = block

    @pl.when(pl.program_id(0) == 0)
    def _():
        put(own, last, info[1])

        def part(source, slot, start, size):
            top = rows + (slot % 2) * (NC + TAIL) + start
            return source[slot // 2, top : top + size, :]

        weight = part(last, 0, NC, TAIL) + part(last_other, 0, NC, TAIL)
        weight = as_column(weight[:1, :128], 128)[:NC, :1]
        for slot, crossed in enumerate((0, 2, 1, 3)):
            total = part(last, slot, 0, NC) + part(last_other, crossed, 0, NC)
            coarse_out[:, column_of(slot, info[1])] = total / weight

    @pl.when(pl.program_id(0) == 1)
    def _():
        put(other, last_other, 1 - info[1])


def place(info, own, other, last, last_other, *, flip):
    _, rows, block_width = own.shape
    width = SLOTS * block_width
    args = [own, other, last, last_other]
    return pl.pallas_call(
        place_body,
        out_shape=[
            jax.ShapeDtypeStruct((2 * rows, width), jnp.float32),
            jax.ShapeDtypeStruct((NC, width), jnp.float32),
        ],
        grid_spec=pltpu.PrefetchScalarGridSpec(
            num_scalar_prefetch=1,
            grid=(2,),
            in_specs=[full(*value.shape) for value in args],
            out_specs=[
                pl.BlockSpec((rows, width), lambda i, info: (info[1] ^ flip ^ i, 0)),
                full(NC, width),
            ],
        ),
        compiler_params=pltpu.CompilerParams(vmem_limit_bytes=24 * 2**20),
        name="place_blocks",
    )(info, *args)


def on_device_paired(points, fine_assign, fine_start, coarse_start, coarse_assign):
    width = points.shape[1]
    local_count = fine_start.shape[0]
    rows = local_count // 2
    block_width = width // SLOTS
    cen, me = lax.axis_index("cen"), lax.axis_index("pts")
    core = me & 1
    info = jnp.stack([me >> 1, core, cen * local_count, cen * 2 + core]).astype(jnp.int32)
    owners = coarse_assign.reshape(2, 1, rows)

    call = functools.partial(run_pass, info, pass_index=0, rows=rows)
    sent, seen, squares, kept = call(points, fine_assign, fine_start, None, None, flip=1)
    sibling = swap(sent, CORE)
    held, seen_first = call(kept, fine_assign, fine_start, squares, seen, flip=0)
    incoming, _ = exchange(held, sibling)
    top, low, part = refine_half(
        info, held, sibling, incoming, owners, coarse_start, flip=0
    )
    part = part + swap(part, CORE)
    own = jnp.stack(gather_half(top, low))
    bits = range(lax.axis_size("cen").bit_length() - 1)
    folded = jnp.concatenate([part, seen_first.reshape(-1, block_width)], 0)
    folded = over_cen(folded, fold, bits[:1])
    own, folded = lax.optimization_barrier((own, folded))
    other = swap(own, CORE)

    call = functools.partial(run_pass, info, pass_index=1, rows=rows)
    sent, seen, kept = call(points, fine_assign, own, squares, None, flip=0)
    sibling = swap(sent, CORE)
    held, seen_second = call(kept, fine_assign, other, squares, seen, flip=1)
    incoming, folded = exchange(held, sibling, folded)

    folded = over_cen(folded, fold, bits[1:])
    part, seen_first = folded[: NC + TAIL], folded[NC + TAIL :]
    coarse = part[:NC] / part[NC, :NC][:, None]

    top, low, part = refine_half(info, held, sibling, incoming, owners, coarse, flip=1)
    fine = jnp.concatenate([top, low], 0)
    folded = jnp.concatenate([part, seen_second.reshape(-1, block_width)], 0)
    folded = over_cen(folded, fold, bits[:1])
    over_second, folded = lax.optimization_barrier((swap_second(fine), folded))
    near = jnp.stack([fine, over_second])
    far = swap_first(near)
    folded = over_cen(folded, fold, bits[1:])
    part, seen_second = folded[: NC + TAIL], folded[NC + TAIL :]
    parts = jnp.stack([part, swap_second(part)])
    last = jnp.concatenate([far, parts, swap_first(parts)], 1)
    fine_now, coarse_now = place(info, near, swap(near, CORE), last, swap(last, CORE), flip=1)

    seen = [each.reshape(2, -1) for each in (seen_first, seen_second)]
    gaps = jnp.stack([each[0] - each[1] for each in seen]) / math.sqrt(width)
    return (fine_now, coarse_now, gaps)


def solution(mesh):
    placed = (P("pts", None), P(None, "pts"), P("cen", None), P(), P("cen"))

    def on_device(points, fine_assign, fine_start, coarse_start, coarse_assign):
        count, width = points.shape
        local_count = fine_start.shape[0]
        centres = mesh.shape["cen"]
        fits = (
            mesh.shape["pts"] == 2 * SLOTS
            and centres & (centres - 1) == 0
            and width // SLOTS == local_count // 2
            and (width // SLOTS) % 128 == 0
            and count % 1024 == 0
        )
        plan = on_device_paired if fits else on_device_any
        return plan(points, fine_assign, fine_start, coarse_start, coarse_assign)

    return jax.shard_map(
        on_device,
        mesh=mesh,
        in_specs=placed,
        out_specs=(P("cen", None), P(), P(None, "pts")),
        check_vma=False,
    )
```

```python
import functools
import math

import jax
import jax.numpy as jnp
from jax import lax
from jax.experimental import pallas as pl
from jax.experimental.pallas import tpu as pltpu
from jax.sharding import PartitionSpec as P

NC = 64
PASSES = 2
FAR = 3.0e38

prior_weight = 4.0
HIGHEST = lax.Precision.HIGHEST


def refine(totals, counts, coarse_cols, coarse_table):
    lookup = jnp.dot(coarse_table, coarse_cols, precision=HIGHEST)
    fine_next = (totals + prior_weight * lookup) / (counts + prior_weight)[:, None]
    coarse_part = lax.dot_general(
        coarse_table,
        counts[:, None] * fine_next,
        (((0,), (0,)), ((), ())),
        precision=HIGHEST,
    )
    coarse_weight = jnp.sum(coarse_table * counts[:, None], axis=0)
    return (fine_next, coarse_part, coarse_weight)


def on_device_any(points, fine_assign, fine_start, coarse_start, coarse_assign):
    width = points.shape[1]
    local_count = fine_start.shape[0]
    offset = lax.axis_index("cen") * local_count
    columns = jnp.arange(local_count, dtype=jnp.int32)
    coarse_table = (coarse_assign[:, None] == jnp.arange(NC, dtype=jnp.int32)[None, :]).astype(
        jnp.float32
    )
    point_values = points.astype(jnp.float32)
    squares = jnp.sum(point_values * point_values, axis=1)
    fine_now = fine_start
    coarse_now = coarse_start
    gap_rows = []
    for pass_index in range(PASSES):
        member = (fine_assign[pass_index] - offset)[:, None] == columns[None, :]
        products = jnp.dot(
            points, fine_now.astype(jnp.bfloat16).T, preferred_element_type=jnp.float32
        )
        energy = jnp.sum(fine_now * fine_now, axis=1)[None, :] - 2.0 * products
        picked_local = jnp.sum(jnp.where(member, energy, 0.0), axis=1)
        nearest_local = jnp.min(energy, axis=1)
        picked = lax.psum(picked_local, "cen")
        nearest = lax.pmin(nearest_local, "cen")
        gap_rows.append((picked - nearest) / math.sqrt(width))
        weights = 1.0 / (1.0 + (squares + picked) / width)
        scaled = (point_values * weights[:, None]).astype(jnp.bfloat16)
        partial_sums = lax.dot_general(
            member.astype(jnp.bfloat16),
            scaled,
            (((0,), (0,)), ((), ())),
            preferred_element_type=jnp.float32,
        )
        partial_weights = jnp.sum(jnp.where(member, weights[:, None], 0.0), axis=0)
        share_width = width // lax.axis_size("pts")
        start = lax.axis_index("pts") * share_width
        shares = lax.psum_scatter(partial_sums, "pts", scatter_dimension=1, tiled=True)
        counts = lax.psum(partial_weights, "pts")
        coarse_cols = lax.dynamic_slice_in_dim(coarse_now, start, share_width, 1)
        fine_share, coarse_part, coarse_weight = refine(shares, counts, coarse_cols, coarse_table)
        coarse_sum, coarse_count = lax.psum((coarse_part, coarse_weight), "cen")
        coarse_share = (coarse_sum + prior_weight * coarse_cols) / (coarse_count + prior_weight)[
            :, None
        ]
        fine_now, coarse_now = (
            lax.all_gather(fine_share, "pts", axis=1, tiled=True),
            lax.all_gather(coarse_share, "pts", axis=1, tiled=True),
        )
    return (fine_now, coarse_now, jnp.stack(gap_rows))


CORE, ACROSS_X, ACROSS_Y = 1, 2, 4
SLOTS = 4
TAIL = 8


def swap(value, bit, axis="pts"):
    size = lax.axis_size(axis)
    return lax.ppermute(value, axis, [(i, i ^ bit) for i in range(size)])


def swap_first(value):
    pairs = [(i, i ^ (ACROSS_Y if i & CORE else ACROSS_X)) for i in range(lax.axis_size("pts"))]
    return lax.ppermute(value, "pts", pairs)


def swap_second(value):
    pairs = [(i, i ^ (ACROSS_X if i & CORE else ACROSS_Y)) for i in range(lax.axis_size("pts"))]
    return lax.ppermute(value, "pts", pairs)


def block_of(info, slot, core):
    crossed = (slot >> 1) | ((slot & 1) << 1)
    return info[0] ^ (slot + core * (crossed - slot))


HERE = pl.BlockSpec(memory_space=pltpu.VMEM)
AWAY = pl.BlockSpec(memory_space=pl.ANY)
SCALARS = pl.BlockSpec(memory_space=pltpu.SMEM)


def near_by(value):
    return pltpu.with_memory_space_constraint(value, pltpu.VMEM)


def far_off(value):
    return pltpu.with_memory_space_constraint(value, pltpu.HBM)


def as_column(row, rows):
    return jnp.broadcast_to(row, (128, rows)).T


def pass_body(info, points, assign, fine, *refs, pass_index, flip, stream, chained, tile):
    refs = list(refs)
    initial = pass_index == 0
    first = initial and stream
    squares_in = None if first else refs.pop(0)
    seen_in = refs.pop(0) if chained else None
    payload, seen = refs.pop(0), refs.pop(0)
    squares_out = refs.pop(0) if first else None
    kept = refs.pop(0) if stream else points
    low, norms, tallies, sums, even, odd, scaled = refs[:7]
    chosen_in = refs[7] if stream else assign
    small_sems, point_sems = refs[8:10] if stream else (None, None)
    start = refs[10] if first else None
    rows, width = low.shape
    mid = rows // 2
    block_width = width // SLOTS
    half = info[1] ^ flip
    base = info[2] + half * rows
    tiles = points.shape[0] // tile

    def span(i):
        return pl.ds(pl.multiple_of(i * tile, tile), tile)

    def column_of(slot, core):
        start = block_of(info, slot, core) * block_width
        return pl.ds(pl.multiple_of(start, block_width), block_width)

    def load(i):
        return pltpu.make_async_copy(points.at[span(i)], kept.at[span(i)], point_sems.at[i])

    if first:
        load_start = pltpu.make_async_copy(
            fine.at[pl.ds(pl.multiple_of(half * rows, rows), rows)], start, small_sems.at[1]
        )
        load_start.start()
    if stream:
        load(0).start()
        load_assign = pltpu.make_async_copy(assign, chosen_in, small_sems.at[0])
        load_assign.start()

        @pl.loop(1, tiles)
        def _(i):
            load(i).start()

    if initial:
        if first:
            load_start.wait()
            block = start[...]
        else:
            block = fine[pl.ds(pl.multiple_of(half * rows, rows), rows), :]
        norm = jnp.sum(block * block, axis=1, keepdims=True)
        low[...] = (-2.0 * block).astype(jnp.bfloat16)
    else:
        norm = jnp.zeros((rows, 1), jnp.float32)
        for slot in range(SLOTS):
            block = fine[slot]
            norm = norm + jnp.sum(block * block, axis=1, keepdims=True)
            low[:, column_of(slot, 0)] = (-2.0 * block).astype(jnp.bfloat16)
    norms[...] = jnp.broadcast_to(norm, norms.shape)
    tallies[...] = jnp.zeros_like(tallies)
    sums[...] = jnp.zeros_like(sums)

    def multiply(i, target):
        target[...] = lax.dot_general(
            low[...], kept[span(i), :], (((1,), (1,)), ((), ())), preferred_element_type=jnp.float32
        )

    def collect(i, products):
        energy = products[...] + jnp.concatenate([norms[...]] * (tile // 128), axis=1)
        chosen = chosen_in[pass_index : pass_index + 1, span(i)] - base
        member = lax.broadcasted_iota(jnp.int32, energy.shape, 0) == chosen
        picked = jnp.sum(jnp.where(member, energy, 0.0), axis=0, keepdims=True)
        nearest = jnp.min(energy, axis=0, keepdims=True)
        inside = (chosen >= 0) & (chosen < rows)
        picked_seen = jnp.where(inside, picked, FAR)
        if chained:
            picked_seen = jnp.minimum(picked_seen, seen_in[0:1, span(i)])
            nearest = jnp.minimum(nearest, seen_in[1:2, span(i)])
        seen[0:1, span(i)] = picked_seen
        seen[1:2, span(i)] = nearest
        if first:
            folded = jnp.zeros((tile, 128), jnp.float32)
            for lane in range(0, width, 128):
                values = kept[span(i), lane : lane + 128].astype(jnp.float32)
                folded = folded + values * values
            squares = jnp.sum(folded.T, axis=0, keepdims=True)
            squares_out[0:1, span(i)] = squares
        else:
            squares = squares_in[0:1, span(i)]
        weights = 1.0 / (1.0 + (squares + picked) / width)
        weighted = jnp.where(member, weights, 0.0)
        tally = tallies[...]
        for lane in range(0, tile, 128):
            tally = tally + weighted[:, lane : lane + 128]
        tallies[...] = tally
        factor = as_column(weights, tile)
        for lane in range(0, width, 128):
            values = kept[span(i), lane : lane + 128].astype(jnp.float32)
            scaled[:, lane : lane + 128] = (values * factor).astype(jnp.bfloat16)
        sums[...] += jnp.dot(
            member.astype(jnp.float32).astype(jnp.bfloat16),
            scaled[...],
            preferred_element_type=jnp.float32,
        )

    if stream:
        load_assign.wait()
        load(0).wait()
    multiply(0, even)

    @pl.loop(0, tiles // 2 - 1)
    def _(pair):
        i = 2 * pair
        if stream:
            load(i + 1).wait()
            load(i + 2).wait()
        multiply(i + 1, odd)
        collect(i, even)
        multiply(i + 2, even)
        collect(i + 1, odd)

    if stream:
        load(tiles - 1).wait()
    multiply(tiles - 1, odd)
    collect(tiles - 2, even)
    collect(tiles - 1, odd)

    counts = jnp.broadcast_to(jnp.sum(tallies[...].T, axis=0, keepdims=True), (TAIL, rows))
    for slot in range(SLOTS):
        columns = column_of(slot, info[1] ^ (not chained))
        payload[slot, :mid, :] = sums[:mid, columns]
        payload[slot, mid : mid + TAIL, :] = counts
        payload[slot, mid + TAIL :, :] = sums[mid:, columns]


def run_pass(info, points, fine_assign, fine, squares, seen, *, pass_index, flip, rows):
    count, width = points.shape
    block_width = width // SLOTS
    tile = 512
    initial = pass_index == 0
    chained = seen is not None
    stream = not chained
    if stream:
        in_specs = [AWAY, AWAY, AWAY if initial else HERE]
        args = [far_off(points), far_off(fine_assign), far_off(fine) if initial else near_by(fine)]
    else:
        in_specs = [HERE] * 3
        args = [near_by(points), near_by(fine_assign), near_by(fine)]
    for value in (squares, seen):
        if value is not None:
            in_specs.append(HERE)
            args.append(near_by(value))
    shapes = [(SLOTS, rows + TAIL, block_width), (2, count)]
    if squares is None:
        shapes.append((1, count))
    out_shape = [pltpu.VMEM(shape, jnp.float32) for shape in shapes]
    scratch = [
        pltpu.VMEM((rows, width), jnp.bfloat16),
        pltpu.VMEM((rows, 128), jnp.float32),
        pltpu.VMEM((rows, 128), jnp.float32),
        pltpu.VMEM((rows, width), jnp.float32),
        pltpu.VMEM((rows, tile), jnp.float32),
        pltpu.VMEM((rows, tile), jnp.float32),
        pltpu.VMEM((tile, width), jnp.bfloat16),
    ]
    if stream:
        scratch += [
            pltpu.VMEM((PASSES, count), jnp.int32),
            pltpu.SemaphoreType.DMA((2,)),
            pltpu.SemaphoreType.DMA((count // tile,)),
        ]
        if initial:
            scratch.append(pltpu.VMEM((rows, width), jnp.float32))
        out_shape.append(pltpu.VMEM(points.shape, points.dtype))
    body = functools.partial(
        pass_body,
        pass_index=pass_index,
        flip=flip,
        stream=stream,
        chained=chained,
        tile=tile,
    )
    return pl.pallas_call(
        body,
        out_shape=out_shape,
        in_specs=[SCALARS, *in_specs],
        out_specs=[HERE] * len(out_shape),
        scratch_shapes=scratch,
        compiler_params=pltpu.CompilerParams(vmem_limit_bytes=16 * 2**20),
        cost_estimate=pl.CostEstimate(
            flops=4 * rows * count * width, bytes_accessed=2 * count * width, transcendentals=0
        ),
        name=f"energies_and_sums_{pass_index}{int(chained)}",
    )(info, *args)


def refine_body(info, own, sibling, *refs, flip):
    first_top, first_low, second_top, second_low, owners, coarse_in, top, low, part = refs
    rows = owners.shape[2]
    mid = rows // 2
    block_width = part.shape[1]
    owner = owners[info[1] ^ flip]
    if coarse_in.shape[1] == block_width:
        coarse = coarse_in[...]
    else:
        coarse = coarse_in[:, pl.ds(pl.multiple_of(info[0] * block_width, block_width), block_width)]
    head = own[0, : mid + TAIL, :] + sibling[0, : mid + TAIL, :]
    rest = own[0, mid + TAIL :, :] + sibling[0, mid + TAIL :, :]
    head = head + (first_top[0] + second_top[...])
    rest = rest + (first_low[0] + second_low[...])
    totals, counts_row = jnp.concatenate([head[:mid], rest], 0), head[mid:]
    counts = as_column(counts_row[:1], rows)[:, :1]
    table = (
        lax.broadcasted_iota(jnp.int32, (NC, rows), 0) == owner
    ).astype(jnp.float32)
    lookup = lax.dot_general(
        table,
        coarse,
        (((0,), (0,)), ((), ())),
        precision=HIGHEST,
        preferred_element_type=jnp.float32,
    )
    new = (totals + prior_weight * lookup) / (counts + prior_weight)
    top[...] = new[:mid]
    low[...] = new[mid:]
    prior = jnp.where(info[3] == 0, prior_weight, 0.0)
    part[:NC, :] = prior * coarse + jnp.dot(
        table, counts * new, precision=HIGHEST, preferred_element_type=jnp.float32
    )
    part[NC:, :] = jnp.zeros((TAIL, part.shape[1]), jnp.float32)
    part[NC:, :NC] = prior + lax.dot_general(
        counts_row,
        table,
        (((1,), (1,)), ((), ())),
        precision=HIGHEST,
        preferred_element_type=jnp.float32,
    )


def refine_half(info, own, sibling, incoming, owners, coarse, *, flip):
    _, rows, block_width = own.shape
    mid = (rows - TAIL) // 2
    args = [near_by(value) for value in (own, sibling, *incoming, owners, coarse)]
    shapes = [(mid, block_width), (mid, block_width), (NC + TAIL, block_width)]
    return pl.pallas_call(
        functools.partial(refine_body, flip=flip),
        out_shape=[pltpu.VMEM(shape, jnp.float32) for shape in shapes],
        in_specs=[SCALARS] + [HERE] * len(args),
        out_specs=[HERE] * len(shapes),
        compiler_params=pltpu.CompilerParams(vmem_limit_bytes=8 * 2**20),
        name="refine_half",
    )(info, *args)


def exchange(held, sibling):
    cut = (held.shape[1] - TAIL) // 2 + TAIL
    chunks = slice(0, cut), slice(cut, None)
    first = [swap_first(held[1::2, rows] + sibling[1::2, rows]) for rows in chunks]
    second = [
        swap_second(held[2, rows] + sibling[2, rows] + arrived[1])
        for rows, arrived in zip(chunks, first)
    ]
    return [*first, *second]


def gather_half(top, low):
    x_low = swap(low, ACROSS_X)
    y_top = swap(top, ACROSS_Y)
    x_top = swap(top, ACROSS_X)
    y_low = swap(low, ACROSS_Y)
    corner_top = swap(y_top, ACROSS_X)
    corner_low = swap(x_low, ACROSS_Y)
    blocks = [(top, low), (x_top, x_low), (y_top, y_low), (corner_top, corner_low)]
    return [jnp.concatenate(block, 0) for block in blocks]


def spread(value):
    corner = swap(value, ACROSS_X | ACROSS_Y)
    return [value, swap(value, ACROSS_X), swap(value, ACROSS_Y), corner]


def over_cen(value, combine, bits=None):
    for bit in range(lax.axis_size("cen").bit_length() - 1) if bits is None else bits:
        value = combine(value, swap(value, 1 << bit, "cen"))
    return value


def fold(first, second):
    cut = NC + TAIL
    return jnp.concatenate(
        [first[:cut] + second[:cut], jnp.minimum(first[cut:], second[cut:])], 0
    )


def place_body(info, *refs, flip):
    own, other = refs[:3], refs[3:6]
    fine_out, coarse_out, fine_held, coarse_held, sems = refs[6:]
    block_width = coarse_out.shape[1] // SLOTS
    rows = fine_out.shape[0] // 2
    half = info[1] ^ flip

    def column_of(slot, core):
        start = block_of(info, slot, core) * block_width
        return pl.ds(pl.multiple_of(start, block_width), block_width)

    def put(at, near, far, core):
        for slot in range(SLOTS):
            fine_held[at, :, column_of(slot, core)] = (far if slot % 2 else near)[slot // 2]

    def send(at, half):
        span = pl.ds(pl.multiple_of(half * rows, rows), rows)
        return pltpu.make_async_copy(fine_held.at[at], fine_out.at[span], sems.at[at])

    put(0, *own[:2], info[1])
    send(0, half).start()
    put(1, *other[:2], 1 - info[1])
    send(1, 1 - half).start()
    parts, others = own[2], other[2]
    weight = parts[0, NC:, :128] + others[0, NC:, :128]
    weight = as_column(weight[:1], 128)[:NC, :1]
    for slot in range(SLOTS):
        total = parts[slot, :NC, :] + others[slot, :NC, :]
        coarse_held[:, column_of(slot, 0)] = total / weight
    send_coarse = pltpu.make_async_copy(coarse_held, coarse_out, sems.at[2])
    send_coarse.start()
    send(0, half).wait()
    send(1, 1 - half).wait()
    send_coarse.wait()


def place(info, own, other, *, flip):
    _, rows, block_width = own[0].shape
    width = SLOTS * block_width
    args = [near_by(value) for value in (*own, *other)]
    return pl.pallas_call(
        functools.partial(place_body, flip=flip),
        out_shape=[
            jax.ShapeDtypeStruct((2 * rows, width), jnp.float32),
            jax.ShapeDtypeStruct((NC, width), jnp.float32),
        ],
        in_specs=[SCALARS] + [HERE] * len(args),
        out_specs=[AWAY, AWAY],
        scratch_shapes=[
            pltpu.VMEM((2, rows, width), jnp.float32),
            pltpu.VMEM((NC, width), jnp.float32),
            pltpu.SemaphoreType.DMA((3,)),
        ],
        compiler_params=pltpu.CompilerParams(vmem_limit_bytes=8 * 2**20),
        name="place_blocks",
    )(info, *args)


def on_device_paired(points, fine_assign, fine_start, coarse_start, coarse_assign):
    width = points.shape[1]
    local_count = fine_start.shape[0]
    rows = local_count // 2
    block_width = width // SLOTS
    cen, me = lax.axis_index("cen"), lax.axis_index("pts")
    core = me & 1
    info = jnp.stack([me >> 1, core, cen * local_count, cen * 2 + core]).astype(jnp.int32)
    owners = coarse_assign.reshape(2, 1, rows)

    call = functools.partial(run_pass, info, pass_index=0, rows=rows)
    sent, seen, squares, kept = call(points, fine_assign, fine_start, None, None, flip=1)
    sibling = swap(sent, CORE)
    held, seen_first = call(kept, fine_assign, fine_start, squares, seen, flip=0)
    incoming = exchange(held, sibling)
    top, low, part = refine_half(
        info, held, sibling, incoming, owners, coarse_start, flip=0
    )
    own = jnp.stack(gather_half(top, low))
    folded = jnp.concatenate([part, seen_first.reshape(-1, block_width)], 0)
    paired = swap(folded, 1, "cen")
    other = swap(own, CORE)

    call = functools.partial(run_pass, info, pass_index=1, rows=rows)
    sent, seen, kept = call(points, fine_assign, own, squares, None, flip=0)
    sent, paired = lax.optimization_barrier((sent, paired))
    sibling = swap(sent, CORE)
    folded = fold(folded, paired)
    paired = [swap(folded, bit, "cen") for bit in (2,) if bit < lax.axis_size("cen")]
    held, seen_second = call(kept, fine_assign, other, squares, seen, flip=1)
    held, paired = lax.optimization_barrier((held, paired))
    incoming = exchange(held, sibling)
    folded = functools.reduce(fold, paired, folded)
    folded = over_cen(folded, fold, range(2, lax.axis_size("cen").bit_length() - 1))
    part, seen_first = folded[: NC + TAIL], folded[NC + TAIL :]
    part = part + swap(part, CORE)
    coarse = part[:NC] / part[NC, :NC][:, None]

    top, low, part = refine_half(info, held, sibling, incoming, owners, coarse, flip=1)
    fine = jnp.concatenate([top, low], 0)
    over_first, over_second = lax.optimization_barrier((swap_first(fine), swap_second(fine)))
    near = jnp.stack([fine, over_second])
    far = jnp.stack([over_first, swap_first(over_second)])
    folded = jnp.concatenate([part, seen_second.reshape(-1, block_width)], 0)
    folded = over_cen(folded, fold)
    part, seen_second = folded[: NC + TAIL], folded[NC + TAIL :]
    parts = jnp.stack(spread(part))
    blocks = [near, far, parts]
    fine_now, coarse_now = place(info, blocks, [swap(block, CORE) for block in blocks], flip=1)

    seen = [each.reshape(2, -1) for each in (seen_first, seen_second)]
    gaps = jnp.stack([each[0] - each[1] for each in seen]) / math.sqrt(width)
    return (fine_now, coarse_now, gaps)


def solution(mesh):
    placed = (P("pts", None), P(None, "pts"), P("cen", None), P(), P("cen"))

    def on_device(points, fine_assign, fine_start, coarse_start, coarse_assign):
        count, width = points.shape
        local_count = fine_start.shape[0]
        centres = mesh.shape["cen"]
        fits = (
            mesh.shape["pts"] == 2 * SLOTS
            and centres & (centres - 1) == 0
            and width // SLOTS == local_count // 2
            and (width // SLOTS) % 128 == 0
            and count % 1024 == 0
        )
        plan = on_device_paired if fits else on_device_any
        return plan(points, fine_assign, fine_start, coarse_start, coarse_assign)

    return jax.shard_map(
        on_device,
        mesh=mesh,
        in_specs=placed,
        out_specs=(P("cen", None), P(), P(None, "pts")),
        check_vma=False,
    )
```

```python
import functools
import math

import jax
import jax.numpy as jnp
from jax import lax
from jax.experimental import pallas as pl
from jax.experimental.pallas import tpu as pltpu
from jax.sharding import PartitionSpec as P

NC = 64
PASSES = 2
FAR = 3.0e38

prior_weight = 4.0
HIGHEST = lax.Precision.HIGHEST


def refine(totals, counts, coarse_cols, coarse_table):
    lookup = jnp.dot(coarse_table, coarse_cols, precision=HIGHEST)
    fine_next = (totals + prior_weight * lookup) / (counts + prior_weight)[:, None]
    coarse_part = lax.dot_general(
        coarse_table,
        counts[:, None] * fine_next,
        (((0,), (0,)), ((), ())),
        precision=HIGHEST,
    )
    coarse_weight = jnp.sum(coarse_table * counts[:, None], axis=0)
    return (fine_next, coarse_part, coarse_weight)


def on_device_any(points, fine_assign, fine_start, coarse_start, coarse_assign):
    width = points.shape[1]
    local_count = fine_start.shape[0]
    offset = lax.axis_index("cen") * local_count
    columns = jnp.arange(local_count, dtype=jnp.int32)
    coarse_table = (coarse_assign[:, None] == jnp.arange(NC, dtype=jnp.int32)[None, :]).astype(
        jnp.float32
    )
    point_values = points.astype(jnp.float32)
    squares = jnp.sum(point_values * point_values, axis=1)
    fine_now = fine_start
    coarse_now = coarse_start
    gap_rows = []
    for pass_index in range(PASSES):
        member = (fine_assign[pass_index] - offset)[:, None] == columns[None, :]
        products = jnp.dot(
            points, fine_now.astype(jnp.bfloat16).T, preferred_element_type=jnp.float32
        )
        energy = jnp.sum(fine_now * fine_now, axis=1)[None, :] - 2.0 * products
        picked_local = jnp.sum(jnp.where(member, energy, 0.0), axis=1)
        nearest_local = jnp.min(energy, axis=1)
        picked = lax.psum(picked_local, "cen")
        nearest = lax.pmin(nearest_local, "cen")
        gap_rows.append((picked - nearest) / math.sqrt(width))
        weights = 1.0 / (1.0 + (squares + picked) / width)
        scaled = (point_values * weights[:, None]).astype(jnp.bfloat16)
        partial_sums = lax.dot_general(
            member.astype(jnp.bfloat16),
            scaled,
            (((0,), (0,)), ((), ())),
            preferred_element_type=jnp.float32,
        )
        partial_weights = jnp.sum(jnp.where(member, weights[:, None], 0.0), axis=0)
        share_width = width // lax.axis_size("pts")
        start = lax.axis_index("pts") * share_width
        shares = lax.psum_scatter(partial_sums, "pts", scatter_dimension=1, tiled=True)
        counts = lax.psum(partial_weights, "pts")
        coarse_cols = lax.dynamic_slice_in_dim(coarse_now, start, share_width, 1)
        fine_share, coarse_part, coarse_weight = refine(shares, counts, coarse_cols, coarse_table)
        coarse_sum, coarse_count = lax.psum((coarse_part, coarse_weight), "cen")
        coarse_share = (coarse_sum + prior_weight * coarse_cols) / (coarse_count + prior_weight)[
            :, None
        ]
        fine_now, coarse_now = (
            lax.all_gather(fine_share, "pts", axis=1, tiled=True),
            lax.all_gather(coarse_share, "pts", axis=1, tiled=True),
        )
    return (fine_now, coarse_now, jnp.stack(gap_rows))


CORE, ACROSS_X, ACROSS_Y = 1, 2, 4
SLOTS = 4
TAIL = 8


def swap(value, bit, axis="pts"):
    size = lax.axis_size(axis)
    return lax.ppermute(value, axis, [(i, i ^ bit) for i in range(size)])


def swap_first(value):
    pairs = [(i, i ^ (ACROSS_Y if i & CORE else ACROSS_X)) for i in range(lax.axis_size("pts"))]
    return lax.ppermute(value, "pts", pairs)


def swap_second(value):
    pairs = [(i, i ^ (ACROSS_X if i & CORE else ACROSS_Y)) for i in range(lax.axis_size("pts"))]
    return lax.ppermute(value, "pts", pairs)


def block_of(info, slot, core):
    crossed = (slot >> 1) | ((slot & 1) << 1)
    return info[0] ^ (slot + core * (crossed - slot))


HERE = pl.BlockSpec(memory_space=pltpu.VMEM)
AWAY = pl.BlockSpec(memory_space=pl.ANY)
SCALARS = pl.BlockSpec(memory_space=pltpu.SMEM)


def near_by(value):
    return pltpu.with_memory_space_constraint(value, pltpu.VMEM)


def far_off(value):
    return pltpu.with_memory_space_constraint(value, pltpu.HBM)


def as_column(row, rows):
    return jnp.broadcast_to(row, (128, rows)).T


def pass_body(info, points, assign, *refs, pass_index, first, tile):
    refs = list(refs)
    fine = [refs.pop(0) for _ in range(1 if first else 6)]
    squares_in = None if first else refs.pop(0)
    held, sent_near, sent_far, seen = refs[:4]
    refs = refs[4:]
    squares_out = refs.pop(0) if first else None
    kept, low, norms, tallies, sums, even, odd, scaled, chosen_in, small_sems, point_sems = refs[:11]
    start = refs[11] if first else None
    rows, width = low.shape
    half_rows = rows // 2
    mid = half_rows // 2
    block_width = width // SLOTS
    core = info[1]
    tiles = points.shape[0] // tile
    halves = [slice(0, half_rows), slice(half_rows, rows)]
    bases = [info[2] + half * half_rows for half in (core, 1 - core)]

    def span(i):
        return pl.ds(pl.multiple_of(i * tile, tile), tile)

    def column_of(slot, core):
        at = block_of(info, slot, core) * block_width
        return pl.ds(pl.multiple_of(at, block_width), block_width)

    def load(i):
        return pltpu.make_async_copy(points.at[span(i)], kept.at[span(i)], point_sems.at[i])

    load_starts = []
    if first:
        for at, half in enumerate((core, 1 - core)):
            rows_of = pl.ds(pl.multiple_of(half * half_rows, half_rows), half_rows)
            load_starts.append(
                pltpu.make_async_copy(fine[0].at[rows_of], start.at[halves[at]], small_sems.at[at])
            )
    for copy in load_starts:
        copy.start()
    load(0).start()
    load_assign = pltpu.make_async_copy(assign, chosen_in, small_sems.at[2])
    load_assign.start()

    @pl.loop(1, tiles)
    def _(i):
        load(i).start()

    for at, part in enumerate(halves):
        if first:
            load_starts[at].wait()
            block = start[part, :]
            norm = jnp.sum(block * block, axis=1, keepdims=True)
            low[part, :] = (-2.0 * block).astype(jnp.bfloat16)
        else:
            near, sides, corner = fine[3 * at : 3 * at + 3]
            norm = jnp.zeros((half_rows, 1), jnp.float32)
            for slot in range(SLOTS):
                block = (near, sides.at[0], sides.at[1], corner)[slot][...]
                norm = norm + jnp.sum(block * block, axis=1, keepdims=True)
                low[part, column_of(slot, 0)] = (-2.0 * block).astype(jnp.bfloat16)
        norms[part, :] = jnp.broadcast_to(norm, (half_rows, 128))
    tallies[...] = jnp.zeros_like(tallies)
    sums[...] = jnp.zeros_like(sums)

    def multiply(i, target):
        target[...] = lax.dot_general(
            low[...], kept[span(i), :], (((1,), (1,)), ((), ())), preferred_element_type=jnp.float32
        )

    def collect(i, products):
        everyone = chosen_in[pass_index : pass_index + 1, span(i)]
        members, picked, nearest, inside = [], 0.0, FAR, False
        for part, base in zip(halves, bases):
            energy = products[part, :] + jnp.concatenate([norms[part, :]] * (tile // 128), axis=1)
            chosen = everyone - base
            member = lax.broadcasted_iota(jnp.int32, energy.shape, 0) == chosen
            members.append(member)
            picked = picked + jnp.sum(jnp.where(member, energy, 0.0), axis=0, keepdims=True)
            nearest = jnp.minimum(nearest, jnp.min(energy, axis=0, keepdims=True))
            inside = inside | ((chosen >= 0) & (chosen < half_rows))
        seen[0:1, span(i)] = jnp.where(inside, picked, FAR)
        seen[1:2, span(i)] = nearest
        if first:
            folded = jnp.zeros((tile, 128), jnp.float32)
            for lane in range(0, width, 128):
                values = kept[span(i), lane : lane + 128].astype(jnp.float32)
                folded = folded + values * values
            squares = jnp.sum(folded.T, axis=0, keepdims=True)
            squares_out[0:1, span(i)] = squares
        else:
            squares = squares_in[0:1, span(i)]
        weights = 1.0 / (1.0 + (squares + picked) / width)
        for part, member in zip(halves, members):
            weighted = jnp.where(member, weights, 0.0)
            tally = tallies[part, :]
            for lane in range(0, tile, 128):
                tally = tally + weighted[:, lane : lane + 128]
            tallies[part, :] = tally
        factor = as_column(weights, tile)
        for lane in range(0, width, 128):
            values = kept[span(i), lane : lane + 128].astype(jnp.float32)
            scaled[:, lane : lane + 128] = (values * factor).astype(jnp.bfloat16)
        member = jnp.concatenate([each.astype(jnp.float32) for each in members], 0)
        sums[...] += jnp.dot(
            member.astype(jnp.bfloat16), scaled[...], preferred_element_type=jnp.float32
        )

    load_assign.wait()
    load(0).wait()
    multiply(0, even)

    @pl.loop(0, tiles // 2 - 1)
    def _(pair):
        i = 2 * pair
        load(i + 1).wait()
        load(i + 2).wait()
        multiply(i + 1, odd)
        collect(i, even)
        multiply(i + 2, even)
        collect(i + 1, odd)

    load(tiles - 1).wait()
    multiply(tiles - 1, odd)
    collect(tiles - 2, even)
    collect(tiles - 1, odd)

    for at, part in enumerate(halves):
        counts = jnp.sum(tallies[part, :].T, axis=0, keepdims=True)
        counts = jnp.broadcast_to(counts, (TAIL, half_rows))
        for slot in range(SLOTS):
            columns = column_of(slot, core ^ at)
            target = held.at[slot] if at == 0 else sent_far.at[slot - 1] if slot else sent_near
            target[:mid, :] = sums[part, columns][:mid]
            target[mid : mid + TAIL, :] = counts
            target[mid + TAIL :, :] = sums[part, columns][mid:]


def run_pass(info, points, fine_assign, fine, squares, *, pass_index, rows):
    count, width = points.shape
    half_rows = rows // 2
    block = (half_rows + TAIL, width // SLOTS)
    tile = 512
    first = squares is None
    args = [far_off(points), far_off(fine_assign)]
    in_specs = [AWAY, AWAY]
    if first:
        args.append(far_off(fine))
        in_specs.append(AWAY)
    else:
        args += [near_by(value) for value in (*fine, squares)]
        in_specs += [HERE] * (len(fine) + 1)
    shapes = [(SLOTS, *block), block, (SLOTS - 1, *block), (2, count)]
    scratch = [
        pltpu.VMEM((count, width), jnp.bfloat16),
        pltpu.VMEM((rows, width), jnp.bfloat16),
        pltpu.VMEM((rows, 128), jnp.float32),
        pltpu.VMEM((rows, 128), jnp.float32),
        pltpu.VMEM((rows, width), jnp.float32),
        pltpu.VMEM((rows, tile), jnp.float32),
        pltpu.VMEM((rows, tile), jnp.float32),
        pltpu.VMEM((tile, width), jnp.bfloat16),
        pltpu.VMEM((PASSES, count), jnp.int32),
        pltpu.SemaphoreType.DMA((3,)),
        pltpu.SemaphoreType.DMA((count // tile,)),
    ]
    if first:
        shapes.append((1, count))
        scratch.append(pltpu.VMEM((rows, width), jnp.float32))
    return pl.pallas_call(
        functools.partial(pass_body, pass_index=pass_index, first=first, tile=tile),
        out_shape=[pltpu.VMEM(shape, jnp.float32) for shape in shapes],
        in_specs=[SCALARS, *in_specs],
        out_specs=[HERE] * len(shapes),
        scratch_shapes=scratch,
        compiler_params=pltpu.CompilerParams(vmem_limit_bytes=28 * 2**20),
        cost_estimate=pl.CostEstimate(
            flops=4 * rows * count * width, bytes_accessed=2 * count * width, transcendentals=0
        ),
        name=f"energies_and_sums_{pass_index}",
    )(info, *args)


def refine_body(info, own, sibling, *refs):
    first_top, first_low, second_top, second_low, owners, coarse_in, top, low, part = refs
    rows = owners.shape[2]
    mid = rows // 2
    block_width = part.shape[1]
    owner = owners[info[1]]
    if coarse_in.shape[1] == block_width:
        coarse = coarse_in[...]
    else:
        coarse = coarse_in[:, pl.ds(pl.multiple_of(info[0] * block_width, block_width), block_width)]
    head = own[0, : mid + TAIL, :] + sibling[: mid + TAIL, :]
    rest = own[0, mid + TAIL :, :] + sibling[mid + TAIL :, :]
    head = head + (first_top[0] + second_top[...])
    rest = rest + (first_low[0] + second_low[...])
    totals, counts_row = jnp.concatenate([head[:mid], rest], 0), head[mid:]
    counts = as_column(counts_row[:1], rows)[:, :1]
    table = (
        lax.broadcasted_iota(jnp.int32, (NC, rows), 0) == owner
    ).astype(jnp.float32)
    lookup = lax.dot_general(
        table,
        coarse,
        (((0,), (0,)), ((), ())),
        precision=HIGHEST,
        preferred_element_type=jnp.float32,
    )
    new = (totals + prior_weight * lookup) / (counts + prior_weight)
    top[...] = new[:mid]
    low[...] = new[mid:]
    prior = jnp.where(info[3] == 0, prior_weight, 0.0)
    part[:NC, :] = prior * coarse + jnp.dot(
        table, counts * new, precision=HIGHEST, preferred_element_type=jnp.float32
    )
    part[NC:, :] = jnp.zeros((TAIL, part.shape[1]), jnp.float32)
    part[NC:, :NC] = prior + lax.dot_general(
        counts_row,
        table,
        (((1,), (1,)), ((), ())),
        precision=HIGHEST,
        preferred_element_type=jnp.float32,
    )


def refine_half(info, own, sibling, incoming, owners, coarse):
    _, rows, block_width = own.shape
    mid = (rows - TAIL) // 2
    args = [near_by(value) for value in (own, sibling, *incoming, owners, coarse)]
    shapes = [(mid, block_width), (mid, block_width), (NC + TAIL, block_width)]
    return pl.pallas_call(
        refine_body,
        out_shape=[pltpu.VMEM(shape, jnp.float32) for shape in shapes],
        in_specs=[SCALARS] + [HERE] * len(args),
        out_specs=[HERE] * len(shapes),
        compiler_params=pltpu.CompilerParams(vmem_limit_bytes=8 * 2**20),
        name="refine_half",
    )(info, *args)


def exchange(held, sibling):
    cut = (held.shape[1] - TAIL) // 2 + TAIL
    chunks = slice(0, cut), slice(cut, None)
    first = [swap_first(held[1::2, rows] + sibling[::2, rows]) for rows in chunks]
    second = [
        swap_second(held[2, rows] + sibling[1, rows] + arrived[1])
        for rows, arrived in zip(chunks, first)
    ]
    return [*first, *second]


def gather_half(top, low):
    x_low = swap(low, ACROSS_X)
    y_top = swap(top, ACROSS_Y)
    x_top = swap(top, ACROSS_X)
    y_low = swap(low, ACROSS_Y)
    corner_top = swap(y_top, ACROSS_X)
    corner_low = swap(x_low, ACROSS_Y)
    near = jnp.concatenate([top, low], 0)
    sides = jnp.stack([jnp.concatenate(pair, 0) for pair in ((x_top, x_low), (y_top, y_low))])
    own = [near, sides, jnp.concatenate([corner_top, corner_low], 0)]
    return [*own, *[swap(block, CORE) for block in own]]


def spread(value):
    corner = swap(value, ACROSS_X | ACROSS_Y)
    return [value, swap(value, ACROSS_X), swap(value, ACROSS_Y), corner]


def over_cen(value, combine, bits=None):
    for bit in range(lax.axis_size("cen").bit_length() - 1) if bits is None else bits:
        value = combine(value, swap(value, 1 << bit, "cen"))
    return value


def fold(first, second):
    cut = NC + TAIL
    return jnp.concatenate(
        [first[:cut] + second[:cut], jnp.minimum(first[cut:], second[cut:])], 0
    )


def place_body(info, *refs):
    own, other = refs[:3], refs[3:6]
    fine_out, coarse_out, fine_held, coarse_held, sems = refs[6:]
    block_width = coarse_out.shape[1] // SLOTS
    rows = fine_out.shape[0] // 2
    half = info[1]

    def column_of(slot, core):
        start = block_of(info, slot, core) * block_width
        return pl.ds(pl.multiple_of(start, block_width), block_width)

    def put(at, near, far, core):
        for slot in range(SLOTS):
            fine_held[at, :, column_of(slot, core)] = (far if slot % 2 else near)[slot // 2]

    def send(at, half):
        span = pl.ds(pl.multiple_of(half * rows, rows), rows)
        return pltpu.make_async_copy(fine_held.at[at], fine_out.at[span], sems.at[at])

    put(0, *own[:2], info[1])
    send(0, half).start()
    put(1, *other[:2], 1 - info[1])
    send(1, 1 - half).start()
    parts, others = own[2], other[2]
    weight = parts[0, NC:, :128] + others[0, NC:, :128]
    weight = as_column(weight[:1], 128)[:NC, :1]
    for slot in range(SLOTS):
        total = parts[slot, :NC, :] + others[slot, :NC, :]
        coarse_held[:, column_of(slot, 0)] = total / weight
    send_coarse = pltpu.make_async_copy(coarse_held, coarse_out, sems.at[2])
    send_coarse.start()
    send(0, half).wait()
    send(1, 1 - half).wait()
    send_coarse.wait()


def place(info, own, other):
    _, rows, block_width = own[0].shape
    width = SLOTS * block_width
    args = [near_by(value) for value in (*own, *other)]
    return pl.pallas_call(
        place_body,
        out_shape=[
            jax.ShapeDtypeStruct((2 * rows, width), jnp.float32),
            jax.ShapeDtypeStruct((NC, width), jnp.float32),
        ],
        in_specs=[SCALARS] + [HERE] * len(args),
        out_specs=[AWAY, AWAY],
        scratch_shapes=[
            pltpu.VMEM((2, rows, width), jnp.float32),
            pltpu.VMEM((NC, width), jnp.float32),
            pltpu.SemaphoreType.DMA((3,)),
        ],
        compiler_params=pltpu.CompilerParams(vmem_limit_bytes=8 * 2**20),
        name="place_blocks",
    )(info, *args)


def on_device_paired(points, fine_assign, fine_start, coarse_start, coarse_assign):
    width = points.shape[1]
    local_count = fine_start.shape[0]
    rows = local_count // 2
    block_width = width // SLOTS
    cen, me = lax.axis_index("cen"), lax.axis_index("pts")
    core = me & 1
    info = jnp.stack([me >> 1, core, cen * local_count, cen * 2 + core]).astype(jnp.int32)
    owners = coarse_assign.reshape(2, 1, rows)

    held, sent_near, sent_far, seen_first, squares = run_pass(
        info, points, fine_assign, fine_start, None, pass_index=0, rows=local_count
    )
    sibling_far, sibling_near = swap(sent_far, CORE), swap(sent_near, CORE)
    incoming = exchange(held, sibling_far)
    top, low, part = refine_half(info, held, sibling_near, incoming, owners, coarse_start)
    blocks = gather_half(top, low)
    folded = jnp.concatenate([part, seen_first.reshape(-1, block_width)], 0)
    paired = swap(folded, 1, "cen")

    held, sent_near, sent_far, seen_second = run_pass(
        info, points, fine_assign, blocks, squares, pass_index=1, rows=local_count
    )
    sent_far, paired = lax.optimization_barrier((sent_far, paired))
    sibling_far, sibling_near = swap(sent_far, CORE), swap(sent_near, CORE)
    incoming = exchange(held, sibling_far)
    bits = range(1, lax.axis_size("cen").bit_length() - 1)
    folded = over_cen(fold(folded, paired), fold, bits)
    part, seen_first = folded[: NC + TAIL], folded[NC + TAIL :]
    part = part + swap(part, CORE)
    coarse = part[:NC] / part[NC, :NC][:, None]

    top, low, part = refine_half(info, held, sibling_near, incoming, owners, coarse)
    fine = jnp.concatenate([top, low], 0)
    over_first, over_second = lax.optimization_barrier((swap_first(fine), swap_second(fine)))
    near = jnp.stack([fine, over_second])
    far = jnp.stack([over_first, swap_first(over_second)])
    folded = jnp.concatenate([part, seen_second.reshape(-1, block_width)], 0)
    folded = over_cen(folded, fold)
    part, seen_second = folded[: NC + TAIL], folded[NC + TAIL :]
    parts = jnp.stack(spread(part))
    blocks = [near, far, parts]
    fine_now, coarse_now = place(info, blocks, [swap(block, CORE) for block in blocks])

    seen = [each.reshape(2, -1) for each in (seen_first, seen_second)]
    gaps = jnp.stack([each[0] - each[1] for each in seen]) / math.sqrt(width)
    return (fine_now, coarse_now, gaps)


def solution(mesh):
    placed = (P("pts", None), P(None, "pts"), P("cen", None), P(), P("cen"))

    def on_device(points, fine_assign, fine_start, coarse_start, coarse_assign):
        count, width = points.shape
        local_count = fine_start.shape[0]
        centres = mesh.shape["cen"]
        fits = (
            mesh.shape["pts"] == 2 * SLOTS
            and centres & (centres - 1) == 0
            and width // SLOTS == local_count // 2
            and (width // SLOTS) % 128 == 0
            and count % 1024 == 0
        )
        plan = on_device_paired if fits else on_device_any
        return plan(points, fine_assign, fine_start, coarse_start, coarse_assign)

    return jax.shard_map(
        on_device,
        mesh=mesh,
        in_specs=placed,
        out_specs=(P("cen", None), P(), P(None, "pts")),
        check_vma=False,
    )
```

```python
import functools
import math

import jax
import jax.numpy as jnp
from jax import lax
from jax.experimental import pallas as pl
from jax.experimental.pallas import tpu as pltpu
from jax.sharding import PartitionSpec as P

NC = 64
PASSES = 2
FAR = 3.0e38

prior_weight = 4.0
HIGHEST = lax.Precision.HIGHEST


def refine(totals, counts, coarse_cols, coarse_table):
    lookup = jnp.dot(coarse_table, coarse_cols, precision=HIGHEST)
    fine_next = (totals + prior_weight * lookup) / (counts + prior_weight)[:, None]
    coarse_part = lax.dot_general(
        coarse_table,
        counts[:, None] * fine_next,
        (((0,), (0,)), ((), ())),
        precision=HIGHEST,
    )
    coarse_weight = jnp.sum(coarse_table * counts[:, None], axis=0)
    return (fine_next, coarse_part, coarse_weight)


def on_device_any(points, fine_assign, fine_start, coarse_start, coarse_assign):
    width = points.shape[1]
    local_count = fine_start.shape[0]
    offset = lax.axis_index("cen") * local_count
    columns = jnp.arange(local_count, dtype=jnp.int32)
    coarse_table = (coarse_assign[:, None] == jnp.arange(NC, dtype=jnp.int32)[None, :]).astype(
        jnp.float32
    )
    point_values = points.astype(jnp.float32)
    squares = jnp.sum(point_values * point_values, axis=1)
    fine_now = fine_start
    coarse_now = coarse_start
    gap_rows = []
    for pass_index in range(PASSES):
        member = (fine_assign[pass_index] - offset)[:, None] == columns[None, :]
        products = jnp.dot(
            points, fine_now.astype(jnp.bfloat16).T, preferred_element_type=jnp.float32
        )
        energy = jnp.sum(fine_now * fine_now, axis=1)[None, :] - 2.0 * products
        picked_local = jnp.sum(jnp.where(member, energy, 0.0), axis=1)
        nearest_local = jnp.min(energy, axis=1)
        picked = lax.psum(picked_local, "cen")
        nearest = lax.pmin(nearest_local, "cen")
        gap_rows.append((picked - nearest) / math.sqrt(width))
        weights = 1.0 / (1.0 + (squares + picked) / width)
        scaled = (point_values * weights[:, None]).astype(jnp.bfloat16)
        partial_sums = lax.dot_general(
            member.astype(jnp.bfloat16),
            scaled,
            (((0,), (0,)), ((), ())),
            preferred_element_type=jnp.float32,
        )
        partial_weights = jnp.sum(jnp.where(member, weights[:, None], 0.0), axis=0)
        share_width = width // lax.axis_size("pts")
        start = lax.axis_index("pts") * share_width
        shares = lax.psum_scatter(partial_sums, "pts", scatter_dimension=1, tiled=True)
        counts = lax.psum(partial_weights, "pts")
        coarse_cols = lax.dynamic_slice_in_dim(coarse_now, start, share_width, 1)
        fine_share, coarse_part, coarse_weight = refine(shares, counts, coarse_cols, coarse_table)
        coarse_sum, coarse_count = lax.psum((coarse_part, coarse_weight), "cen")
        coarse_share = (coarse_sum + prior_weight * coarse_cols) / (coarse_count + prior_weight)[
            :, None
        ]
        fine_now, coarse_now = (
            lax.all_gather(fine_share, "pts", axis=1, tiled=True),
            lax.all_gather(coarse_share, "pts", axis=1, tiled=True),
        )
    return (fine_now, coarse_now, jnp.stack(gap_rows))


CORE, ACROSS_X, ACROSS_Y = 1, 2, 4
SLOTS = 4
TAIL = 8


def swap(value, bit, axis="pts"):
    size = lax.axis_size(axis)
    return lax.ppermute(value, axis, [(i, i ^ bit) for i in range(size)])


def swap_first(value):
    pairs = [(i, i ^ (ACROSS_Y if i & CORE else ACROSS_X)) for i in range(lax.axis_size("pts"))]
    return lax.ppermute(value, "pts", pairs)


def swap_second(value):
    pairs = [(i, i ^ (ACROSS_X if i & CORE else ACROSS_Y)) for i in range(lax.axis_size("pts"))]
    return lax.ppermute(value, "pts", pairs)


def block_of(info, slot, core):
    crossed = (slot >> 1) | ((slot & 1) << 1)
    return info[0] ^ (slot + core * (crossed - slot))


HERE = pl.BlockSpec(memory_space=pltpu.VMEM)
AWAY = pl.BlockSpec(memory_space=pl.ANY)
SCALARS = pl.BlockSpec(memory_space=pltpu.SMEM)


def near_by(value):
    return pltpu.with_memory_space_constraint(value, pltpu.VMEM)


def far_off(value):
    return pltpu.with_memory_space_constraint(value, pltpu.HBM)


def as_column(row, rows):
    return jnp.broadcast_to(row, (128, rows)).T


def pass_body(info, points, assign, fine, *refs, pass_index, flip, stream, chained, tile):
    refs = list(refs)
    initial = pass_index == 0
    first = initial and stream
    squares_in = None if first else refs.pop(0)
    seen_in = refs.pop(0) if chained else None
    payload, seen = refs.pop(0), refs.pop(0)
    squares_out = refs.pop(0) if first else None
    kept = refs.pop(0) if stream else points
    low, norms, tallies, sums, even, odd, scaled = refs[:7]
    chosen_in = refs[7] if stream else assign
    small_sems, point_sems = refs[8:10] if stream else (None, None)
    start = refs[10] if first else None
    rows, width = low.shape
    mid = rows // 2
    block_width = width // SLOTS
    half = info[1] ^ flip
    base = info[2] + half * rows
    tiles = points.shape[0] // tile

    def span(i):
        return pl.ds(pl.multiple_of(i * tile, tile), tile)

    def column_of(slot, core):
        start = block_of(info, slot, core) * block_width
        return pl.ds(pl.multiple_of(start, block_width), block_width)

    def load(i):
        return pltpu.make_async_copy(points.at[span(i)], kept.at[span(i)], point_sems.at[i])

    if first:
        load_start = pltpu.make_async_copy(
            fine.at[pl.ds(pl.multiple_of(half * rows, rows), rows)], start, small_sems.at[1]
        )
        load_start.start()
    if stream:
        load(0).start()
        load_assign = pltpu.make_async_copy(assign, chosen_in, small_sems.at[0])
        load_assign.start()

        @pl.loop(1, tiles)
        def _(i):
            load(i).start()

    if initial:
        if first:
            load_start.wait()
            block = start[...]
        else:
            block = fine[pl.ds(pl.multiple_of(half * rows, rows), rows), :]
        norm = jnp.sum(block * block, axis=1, keepdims=True)
        low[...] = (-2.0 * block).astype(jnp.bfloat16)
    else:
        norm = jnp.zeros((rows, 1), jnp.float32)
        for slot in range(SLOTS):
            block = fine[slot]
            norm = norm + jnp.sum(block * block, axis=1, keepdims=True)
            low[:, column_of(slot, 0)] = (-2.0 * block).astype(jnp.bfloat16)
    norms[...] = jnp.broadcast_to(norm, norms.shape)
    tallies[...] = jnp.zeros_like(tallies)
    sums[...] = jnp.zeros_like(sums)

    def multiply(i, target):
        target[...] = lax.dot_general(
            low[...], kept[span(i), :], (((1,), (1,)), ((), ())), preferred_element_type=jnp.float32
        )

    def collect(i, products):
        energy = products[...] + jnp.concatenate([norms[...]] * (tile // 128), axis=1)
        chosen = chosen_in[pass_index : pass_index + 1, span(i)] - base
        member = lax.broadcasted_iota(jnp.int32, energy.shape, 0) == chosen
        picked = jnp.sum(jnp.where(member, energy, 0.0), axis=0, keepdims=True)
        nearest = jnp.min(energy, axis=0, keepdims=True)
        inside = (chosen >= 0) & (chosen < rows)
        picked_seen = jnp.where(inside, picked, FAR)
        if chained:
            picked_seen = jnp.minimum(picked_seen, seen_in[0:1, span(i)])
            nearest = jnp.minimum(nearest, seen_in[1:2, span(i)])
        seen[0:1, span(i)] = picked_seen
        seen[1:2, span(i)] = nearest
        if first:
            folded = jnp.zeros((tile, 128), jnp.float32)
            for lane in range(0, width, 128):
                values = kept[span(i), lane : lane + 128].astype(jnp.float32)
                folded = folded + values * values
            squares = jnp.sum(folded.T, axis=0, keepdims=True)
            squares_out[0:1, span(i)] = squares
        else:
            squares = squares_in[0:1, span(i)]
        weights = 1.0 / (1.0 + (squares + picked) / width)
        weighted = jnp.where(member, weights, 0.0)
        tally = tallies[...]
        for lane in range(0, tile, 128):
            tally = tally + weighted[:, lane : lane + 128]
        tallies[...] = tally
        factor = as_column(weights, tile)
        for lane in range(0, width, 128):
            values = kept[span(i), lane : lane + 128].astype(jnp.float32)
            scaled[:, lane : lane + 128] = (values * factor).astype(jnp.bfloat16)
        sums[...] += jnp.dot(
            member.astype(jnp.float32).astype(jnp.bfloat16),
            scaled[...],
            preferred_element_type=jnp.float32,
        )

    if stream:
        load_assign.wait()
        load(0).wait()
    multiply(0, even)

    @pl.loop(0, tiles // 2 - 1)
    def _(pair):
        i = 2 * pair
        if stream:
            load(i + 1).wait()
            load(i + 2).wait()
        multiply(i + 1, odd)
        collect(i, even)
        multiply(i + 2, even)
        collect(i + 1, odd)

    if stream:
        load(tiles - 1).wait()
    multiply(tiles - 1, odd)
    collect(tiles - 2, even)
    collect(tiles - 1, odd)

    counts = jnp.broadcast_to(jnp.sum(tallies[...].T, axis=0, keepdims=True), (TAIL, rows))
    for slot in range(SLOTS):
        columns = column_of(slot, info[1] ^ (not chained))
        payload[slot, :mid, :] = sums[:mid, columns]
        payload[slot, mid : mid + TAIL, :] = counts
        payload[slot, mid + TAIL :, :] = sums[mid:, columns]


def run_pass(info, points, fine_assign, fine, squares, seen, *, pass_index, flip, rows):
    count, width = points.shape
    block_width = width // SLOTS
    tile = 1024
    initial = pass_index == 0
    chained = seen is not None
    stream = not chained
    if stream:
        in_specs = [AWAY, AWAY, AWAY if initial else HERE]
        args = [far_off(points), far_off(fine_assign), far_off(fine) if initial else near_by(fine)]
    else:
        in_specs = [HERE] * 3
        args = [near_by(points), near_by(fine_assign), near_by(fine)]
    for value in (squares, seen):
        if value is not None:
            in_specs.append(HERE)
            args.append(near_by(value))
    shapes = [(SLOTS, rows + TAIL, block_width), (2, count)]
    if squares is None:
        shapes.append((1, count))
    out_shape = [pltpu.VMEM(shape, jnp.float32) for shape in shapes]
    scratch = [
        pltpu.VMEM((rows, width), jnp.bfloat16),
        pltpu.VMEM((rows, 128), jnp.float32),
        pltpu.VMEM((rows, 128), jnp.float32),
        pltpu.VMEM((rows, width), jnp.float32),
        pltpu.VMEM((rows, tile), jnp.float32),
        pltpu.VMEM((rows, tile), jnp.float32),
        pltpu.VMEM((tile, width), jnp.bfloat16),
    ]
    if stream:
        scratch += [
            pltpu.VMEM((PASSES, count), jnp.int32),
            pltpu.SemaphoreType.DMA((2,)),
            pltpu.SemaphoreType.DMA((count // tile,)),
        ]
        if initial:
            scratch.append(pltpu.VMEM((rows, width), jnp.float32))
        out_shape.append(pltpu.VMEM(points.shape, points.dtype))
    body = functools.partial(
        pass_body,
        pass_index=pass_index,
        flip=flip,
        stream=stream,
        chained=chained,
        tile=tile,
    )
    return pl.pallas_call(
        body,
        out_shape=out_shape,
        in_specs=[SCALARS, *in_specs],
        out_specs=[HERE] * len(out_shape),
        scratch_shapes=scratch,
        compiler_params=pltpu.CompilerParams(vmem_limit_bytes=20 * 2**20),
        cost_estimate=pl.CostEstimate(
            flops=4 * rows * count * width, bytes_accessed=2 * count * width, transcendentals=0
        ),
        name=f"energies_and_sums_{pass_index}{int(chained)}",
    )(info, *args)


def refine_body(info, own, sibling, *refs, flip):
    first_top, first_low, second_top, second_low, owners, coarse_in, top, low, part = refs
    rows = owners.shape[2]
    mid = rows // 2
    block_width = part.shape[1]
    owner = owners[info[1] ^ flip]
    if coarse_in.shape[1] == block_width:
        coarse = coarse_in[...]
    else:
        coarse = coarse_in[:, pl.ds(pl.multiple_of(info[0] * block_width, block_width), block_width)]
    head = own[0, : mid + TAIL, :] + sibling[0, : mid + TAIL, :]
    rest = own[0, mid + TAIL :, :] + sibling[0, mid + TAIL :, :]
    head = head + (first_top[0] + second_top[...])
    rest = rest + (first_low[0] + second_low[...])
    totals, counts_row = jnp.concatenate([head[:mid], rest], 0), head[mid:]
    counts = as_column(counts_row[:1], rows)[:, :1]
    table = (
        lax.broadcasted_iota(jnp.int32, (NC, rows), 0) == owner
    ).astype(jnp.float32)
    lookup = lax.dot_general(
        table,
        coarse,
        (((0,), (0,)), ((), ())),
        precision=HIGHEST,
        preferred_element_type=jnp.float32,
    )
    new = (totals + prior_weight * lookup) / (counts + prior_weight)
    top[...] = new[:mid]
    low[...] = new[mid:]
    prior = jnp.where(info[3] == 0, prior_weight, 0.0)
    part[:NC, :] = prior * coarse + jnp.dot(
        table, counts * new, precision=HIGHEST, preferred_element_type=jnp.float32
    )
    part[NC:, :] = jnp.zeros((TAIL, part.shape[1]), jnp.float32)
    part[NC:, :NC] = prior + lax.dot_general(
        counts_row,
        table,
        (((1,), (1,)), ((), ())),
        precision=HIGHEST,
        preferred_element_type=jnp.float32,
    )


def refine_half(info, own, sibling, incoming, owners, coarse, *, flip):
    _, rows, block_width = own.shape
    mid = (rows - TAIL) // 2
    args = [near_by(value) for value in (own, sibling, *incoming, owners, coarse)]
    shapes = [(mid, block_width), (mid, block_width), (NC + TAIL, block_width)]
    return pl.pallas_call(
        functools.partial(refine_body, flip=flip),
        out_shape=[pltpu.VMEM(shape, jnp.float32) for shape in shapes],
        in_specs=[SCALARS] + [HERE] * len(args),
        out_specs=[HERE] * len(shapes),
        compiler_params=pltpu.CompilerParams(vmem_limit_bytes=8 * 2**20),
        name="refine_half",
    )(info, *args)


def exchange(held, sibling):
    cut = (held.shape[1] - TAIL) // 2 + TAIL
    chunks = slice(0, cut), slice(cut, None)
    first = [swap_first(held[1::2, rows] + sibling[1::2, rows]) for rows in chunks]
    second = [
        swap_second(held[2, rows] + sibling[2, rows] + arrived[1])
        for rows, arrived in zip(chunks, first)
    ]
    return [*first, *second]


def gather_half(top, low, later=()):
    x_low = swap(low, ACROSS_X)
    y_top = swap(top, ACROSS_Y)
    x_low, y_top, later = lax.optimization_barrier((x_low, y_top, later))
    corner_top = swap(y_top, ACROSS_X)
    corner_low = swap(x_low, ACROSS_Y)
    x_top = swap(top, ACROSS_X)
    y_low = swap(low, ACROSS_Y)
    blocks = [(top, low), (x_top, x_low), (y_top, y_low), (corner_top, corner_low)]
    return [jnp.concatenate(block, 0) for block in blocks], later


def spread(value):
    corner = swap(value, ACROSS_X | ACROSS_Y)
    return [value, swap(value, ACROSS_X), swap(value, ACROSS_Y), corner]


def over_cen(value, combine, bits=None):
    for bit in range(lax.axis_size("cen").bit_length() - 1) if bits is None else bits:
        value = combine(value, swap(value, 1 << bit, "cen"))
    return value


def fold(first, second):
    cut = NC + TAIL
    return jnp.concatenate(
        [first[:cut] + second[:cut], jnp.minimum(first[cut:], second[cut:])], 0
    )


def place_body(info, *refs, flip):
    own, other = refs[:3], refs[3:6]
    fine_out, coarse_out, fine_held, coarse_held, sems = refs[6:]
    block_width = coarse_out.shape[1] // SLOTS
    rows = fine_out.shape[0] // 2
    half = info[1] ^ flip

    def column_of(slot, core):
        start = block_of(info, slot, core) * block_width
        return pl.ds(pl.multiple_of(start, block_width), block_width)

    def put(at, near, far):
        for slot in range(SLOTS):
            fine_held[at, :, column_of(slot, 0)] = (near, far)[slot // 2][slot % 2]

    def send(at, half):
        span = pl.ds(pl.multiple_of(half * rows, rows), rows)
        return pltpu.make_async_copy(fine_held.at[at], fine_out.at[span], sems.at[at])

    put(0, *own[:2])
    send(0, half).start()
    put(1, *other[:2])
    send(1, 1 - half).start()
    parts, others = own[2], other[2]
    weight = parts[0, NC:, :128] + others[0, NC:, :128]
    weight = as_column(weight[:1], 128)[:NC, :1]
    for slot in range(SLOTS):
        total = parts[slot, :NC, :] + others[slot, :NC, :]
        coarse_held[:, column_of(slot, 0)] = total / weight
    send_coarse = pltpu.make_async_copy(coarse_held, coarse_out, sems.at[2])
    send_coarse.start()
    send(0, half).wait()
    send(1, 1 - half).wait()
    send_coarse.wait()


def place(info, own, other, *, flip):
    _, rows, block_width = own[0].shape
    width = SLOTS * block_width
    args = [near_by(value) for value in (*own, *other)]
    return pl.pallas_call(
        functools.partial(place_body, flip=flip),
        out_shape=[
            jax.ShapeDtypeStruct((2 * rows, width), jnp.float32),
            jax.ShapeDtypeStruct((NC, width), jnp.float32),
        ],
        in_specs=[SCALARS] + [HERE] * len(args),
        out_specs=[AWAY, AWAY],
        scratch_shapes=[
            pltpu.VMEM((2, rows, width), jnp.float32),
            pltpu.VMEM((NC, width), jnp.float32),
            pltpu.SemaphoreType.DMA((3,)),
        ],
        compiler_params=pltpu.CompilerParams(vmem_limit_bytes=8 * 2**20),
        name="place_blocks",
    )(info, *args)


def on_device_paired(points, fine_assign, fine_start, coarse_start, coarse_assign):
    width = points.shape[1]
    local_count = fine_start.shape[0]
    rows = local_count // 2
    block_width = width // SLOTS
    cen, me = lax.axis_index("cen"), lax.axis_index("pts")
    core = me & 1
    info = jnp.stack([me >> 1, core, cen * local_count, cen * 2 + core]).astype(jnp.int32)
    owners = coarse_assign.reshape(2, 1, rows)

    call = functools.partial(run_pass, info, pass_index=0, rows=rows)
    sent, seen, squares, kept = call(points, fine_assign, fine_start, None, None, flip=1)
    sibling = swap(sent, CORE)
    held, seen_first = call(kept, fine_assign, fine_start, squares, seen, flip=0)
    incoming = exchange(held, sibling)
    top, low, part = refine_half(
        info, held, sibling, incoming, owners, coarse_start, flip=0
    )
    own = jnp.stack(gather_half(top, low)[0])
    folded = jnp.concatenate([part, seen_first.reshape(-1, block_width)], 0)
    paired = swap(folded, 1, "cen")
    other = swap(own, CORE)

    call = functools.partial(run_pass, info, pass_index=1, rows=rows)
    sent, seen, kept = call(points, fine_assign, own, squares, None, flip=0)
    sent, paired = lax.optimization_barrier((sent, paired))
    sibling = swap(sent, CORE)
    folded = fold(folded, paired)
    held, seen_second = call(kept, fine_assign, other, squares, seen, flip=1)
    held, folded = lax.optimization_barrier((held, folded))
    incoming = exchange(held, sibling)
    bits = range(lax.axis_size("cen").bit_length() - 1)
    folded = over_cen(folded, fold, bits[1:])
    part, seen_first = folded[: NC + TAIL], folded[NC + TAIL :]
    part = part + swap(part, CORE)
    coarse = part[:NC] / part[NC, :NC][:, None]

    top, low, part = refine_half(info, held, sibling, incoming, owners, coarse, flip=1)
    folded = jnp.concatenate([part, seen_second.reshape(-1, block_width)], 0)
    folded = over_cen(folded, fold, bits[:1])
    own, folded = gather_half(top, low, folded)
    folded = over_cen(folded, fold, bits[1:])
    part, seen_second = folded[: NC + TAIL], folded[NC + TAIL :]
    blocks = [jnp.stack(own[:2]), jnp.stack(own[2:]), jnp.stack(spread(part))]
    fine_now, coarse_now = place(info, blocks, [swap(block, CORE) for block in blocks], flip=1)

    seen = [each.reshape(2, -1) for each in (seen_first, seen_second)]
    gaps = jnp.stack([each[0] - each[1] for each in seen]) / math.sqrt(width)
    return (fine_now, coarse_now, gaps)


def solution(mesh):
    placed = (P("pts", None), P(None, "pts"), P("cen", None), P(), P("cen"))

    def on_device(points, fine_assign, fine_start, coarse_start, coarse_assign):
        count, width = points.shape
        local_count = fine_start.shape[0]
        centres = mesh.shape["cen"]
        fits = (
            mesh.shape["pts"] == 2 * SLOTS
            and centres & (centres - 1) == 0
            and width // SLOTS == local_count // 2
            and (width // SLOTS) % 128 == 0
            and count % 1024 == 0
        )
        plan = on_device_paired if fits else on_device_any
        return plan(points, fine_assign, fine_start, coarse_start, coarse_assign)

    return jax.shard_map(
        on_device,
        mesh=mesh,
        in_specs=placed,
        out_specs=(P("cen", None), P(), P(None, "pts")),
        check_vma=False,
    )
```

```python
import functools
import math

import jax
import jax.numpy as jnp
from jax import lax
from jax.experimental import pallas as pl
from jax.experimental.pallas import tpu as pltpu
from jax.sharding import PartitionSpec as P

NC = 64
PASSES = 2
FAR = 3.0e38

prior_weight = 4.0
HIGHEST = lax.Precision.HIGHEST


def refine(totals, counts, coarse_cols, coarse_table):
    lookup = jnp.dot(coarse_table, coarse_cols, precision=HIGHEST)
    fine_next = (totals + prior_weight * lookup) / (counts + prior_weight)[:, None]
    coarse_part = lax.dot_general(
        coarse_table,
        counts[:, None] * fine_next,
        (((0,), (0,)), ((), ())),
        precision=HIGHEST,
    )
    coarse_weight = jnp.sum(coarse_table * counts[:, None], axis=0)
    return (fine_next, coarse_part, coarse_weight)


def on_device_any(points, fine_assign, fine_start, coarse_start, coarse_assign):
    width = points.shape[1]
    local_count = fine_start.shape[0]
    offset = lax.axis_index("cen") * local_count
    columns = jnp.arange(local_count, dtype=jnp.int32)
    coarse_table = (coarse_assign[:, None] == jnp.arange(NC, dtype=jnp.int32)[None, :]).astype(
        jnp.float32
    )
    point_values = points.astype(jnp.float32)
    squares = jnp.sum(point_values * point_values, axis=1)
    fine_now = fine_start
    coarse_now = coarse_start
    gap_rows = []
    for pass_index in range(PASSES):
        member = (fine_assign[pass_index] - offset)[:, None] == columns[None, :]
        products = jnp.dot(
            points, fine_now.astype(jnp.bfloat16).T, preferred_element_type=jnp.float32
        )
        energy = jnp.sum(fine_now * fine_now, axis=1)[None, :] - 2.0 * products
        picked_local = jnp.sum(jnp.where(member, energy, 0.0), axis=1)
        nearest_local = jnp.min(energy, axis=1)
        picked = lax.psum(picked_local, "cen")
        nearest = lax.pmin(nearest_local, "cen")
        gap_rows.append((picked - nearest) / math.sqrt(width))
        weights = 1.0 / (1.0 + (squares + picked) / width)
        scaled = (point_values * weights[:, None]).astype(jnp.bfloat16)
        partial_sums = lax.dot_general(
            member.astype(jnp.bfloat16),
            scaled,
            (((0,), (0,)), ((), ())),
            preferred_element_type=jnp.float32,
        )
        partial_weights = jnp.sum(jnp.where(member, weights[:, None], 0.0), axis=0)
        share_width = width // lax.axis_size("pts")
        start = lax.axis_index("pts") * share_width
        shares = lax.psum_scatter(partial_sums, "pts", scatter_dimension=1, tiled=True)
        counts = lax.psum(partial_weights, "pts")
        coarse_cols = lax.dynamic_slice_in_dim(coarse_now, start, share_width, 1)
        fine_share, coarse_part, coarse_weight = refine(shares, counts, coarse_cols, coarse_table)
        coarse_sum, coarse_count = lax.psum((coarse_part, coarse_weight), "cen")
        coarse_share = (coarse_sum + prior_weight * coarse_cols) / (coarse_count + prior_weight)[
            :, None
        ]
        fine_now, coarse_now = (
            lax.all_gather(fine_share, "pts", axis=1, tiled=True),
            lax.all_gather(coarse_share, "pts", axis=1, tiled=True),
        )
    return (fine_now, coarse_now, jnp.stack(gap_rows))


CORE, ACROSS_X, ACROSS_Y = 1, 2, 4
SLOTS = 4
TAIL = 8


def swap(value, bit, axis="pts"):
    size = lax.axis_size(axis)
    return lax.ppermute(value, axis, [(i, i ^ bit) for i in range(size)])


def swap_first(value):
    pairs = [(i, i ^ (ACROSS_Y if i & CORE else ACROSS_X)) for i in range(lax.axis_size("pts"))]
    return lax.ppermute(value, "pts", pairs)


def swap_second(value):
    pairs = [(i, i ^ (ACROSS_X if i & CORE else ACROSS_Y)) for i in range(lax.axis_size("pts"))]
    return lax.ppermute(value, "pts", pairs)


def block_of(info, slot, core):
    crossed = (slot >> 1) | ((slot & 1) << 1)
    return info[0] ^ (slot + core * (crossed - slot))


HERE = pl.BlockSpec(memory_space=pltpu.VMEM)
AWAY = pl.BlockSpec(memory_space=pl.ANY)
SCALARS = pl.BlockSpec(memory_space=pltpu.SMEM)


def near_by(value):
    return pltpu.with_memory_space_constraint(value, pltpu.VMEM)


def far_off(value):
    return pltpu.with_memory_space_constraint(value, pltpu.HBM)


def as_column(row, rows):
    return jnp.broadcast_to(row, (128, rows)).T


def pass_body(info, points, assign, fine, *refs, pass_index, flip, stream, chained, tile):
    refs = list(refs)
    initial = pass_index == 0
    first = initial and stream
    squares_in = None if first else refs.pop(0)
    seen_in = refs.pop(0) if chained else None
    payload, seen = refs.pop(0), refs.pop(0)
    squares_out = refs.pop(0) if first else None
    kept = refs.pop(0) if stream else points
    low, norms, tallies, sums, even, odd, scaled = refs[:7]
    chosen_in = refs[7] if stream else assign
    small_sems, point_sems = refs[8:10] if stream else (None, None)
    start = refs[10] if first else None
    rows, width = low.shape
    mid = rows // 2
    block_width = width // SLOTS
    half = info[1] ^ flip
    base = info[2] + half * rows
    tiles = points.shape[0] // tile

    def span(i):
        return pl.ds(pl.multiple_of(i * tile, tile), tile)

    def column_of(slot, core):
        start = block_of(info, slot, core) * block_width
        return pl.ds(pl.multiple_of(start, block_width), block_width)

    def load(i):
        return pltpu.make_async_copy(points.at[span(i)], kept.at[span(i)], point_sems.at[i])

    if first:
        load_start = pltpu.make_async_copy(
            fine.at[pl.ds(pl.multiple_of(half * rows, rows), rows)], start, small_sems.at[1]
        )
        load_start.start()
    if stream:
        load(0).start()
        load_assign = pltpu.make_async_copy(assign, chosen_in, small_sems.at[0])
        load_assign.start()

    if initial:
        if first:
            load_start.wait()
            block = start[...]
        else:
            block = fine[pl.ds(pl.multiple_of(half * rows, rows), rows), :]
        norm = jnp.sum(block * block, axis=1, keepdims=True)
        low[...] = (-2.0 * block).astype(jnp.bfloat16)
    else:
        norm = [jnp.zeros((mid, 1), jnp.float32)] * 2
        for piece, (slot, is_low) in enumerate(PIECES):
            block = fine[piece]
            norm[is_low] = norm[is_low] + jnp.sum(block * block, axis=1, keepdims=True)
            part = slice(is_low * mid, (is_low + 1) * mid)
            low[part, column_of(slot, 0)] = (-2.0 * block).astype(jnp.bfloat16)
        norm = jnp.concatenate(norm, 0)
    norms[...] = jnp.broadcast_to(norm, norms.shape)
    tallies[...] = jnp.zeros_like(tallies)
    sums[...] = jnp.zeros_like(sums)

    def multiply(i, target):
        target[...] = lax.dot_general(
            low[...], kept[span(i), :], (((1,), (1,)), ((), ())), preferred_element_type=jnp.float32
        )

    def collect(i, products):
        energy = products[...] + jnp.concatenate([norms[...]] * (tile // 128), axis=1)
        chosen = chosen_in[pass_index : pass_index + 1, span(i)] - base
        member = lax.broadcasted_iota(jnp.int32, energy.shape, 0) == chosen
        picked = jnp.sum(jnp.where(member, energy, 0.0), axis=0, keepdims=True)
        nearest = jnp.min(energy, axis=0, keepdims=True)
        inside = (chosen >= 0) & (chosen < rows)
        picked_seen = jnp.where(inside, picked, FAR)
        if chained:
            picked_seen = jnp.minimum(picked_seen, seen_in[0:1, span(i)])
            nearest = jnp.minimum(nearest, seen_in[1:2, span(i)])
        seen[0:1, span(i)] = picked_seen
        seen[1:2, span(i)] = nearest
        if first:
            folded = jnp.zeros((tile, 128), jnp.float32)
            for lane in range(0, width, 128):
                values = kept[span(i), lane : lane + 128].astype(jnp.float32)
                folded = folded + values * values
            squares = jnp.sum(folded.T, axis=0, keepdims=True)
            squares_out[0:1, span(i)] = squares
        else:
            squares = squares_in[0:1, span(i)]
        weights = 1.0 / (1.0 + (squares + picked) / width)
        weighted = jnp.where(member, weights, 0.0)
        tally = tallies[...]
        for lane in range(0, tile, 128):
            tally = tally + weighted[:, lane : lane + 128]
        tallies[...] = tally
        factor = as_column(weights, tile)
        for lane in range(0, width, 128):
            values = kept[span(i), lane : lane + 128].astype(jnp.float32)
            scaled[:, lane : lane + 128] = (values * factor).astype(jnp.bfloat16)
        sums[...] += jnp.dot(
            member.astype(jnp.float32).astype(jnp.bfloat16),
            scaled[...],
            preferred_element_type=jnp.float32,
        )

    def arrive(i, more):
        if stream:
            load(i).wait()
            if more:
                load(i + 1).start()

    if stream:
        load_assign.wait()
    arrive(0, True)
    multiply(0, even)

    @pl.loop(0, tiles // 2 - 1)
    def _(pair):
        i = 2 * pair
        arrive(i + 1, True)
        multiply(i + 1, odd)
        collect(i, even)
        arrive(i + 2, True)
        multiply(i + 2, even)
        collect(i + 1, odd)

    arrive(tiles - 1, False)
    multiply(tiles - 1, odd)
    collect(tiles - 2, even)
    collect(tiles - 1, odd)

    counts = jnp.broadcast_to(jnp.sum(tallies[...].T, axis=0, keepdims=True), (TAIL, rows))
    for slot in range(SLOTS):
        columns = column_of(slot, info[1] ^ (not chained))
        payload[slot, :mid, :] = sums[:mid, columns]
        payload[slot, mid : mid + TAIL, :] = counts
        payload[slot, mid + TAIL :, :] = sums[mid:, columns]


def run_pass(info, points, fine_assign, fine, squares, seen, *, pass_index, flip, rows):
    count, width = points.shape
    block_width = width // SLOTS
    tile = 1024
    initial = pass_index == 0
    chained = seen is not None
    stream = not chained
    if stream:
        in_specs = [AWAY, AWAY, AWAY if initial else HERE]
        args = [far_off(points), far_off(fine_assign), far_off(fine) if initial else near_by(fine)]
    else:
        in_specs = [HERE] * 3
        args = [near_by(points), near_by(fine_assign), near_by(fine)]
    for value in (squares, seen):
        if value is not None:
            in_specs.append(HERE)
            args.append(near_by(value))
    shapes = [(SLOTS, rows + TAIL, block_width), (2, count)]
    if squares is None:
        shapes.append((1, count))
    out_shape = [pltpu.VMEM(shape, jnp.float32) for shape in shapes]
    scratch = [
        pltpu.VMEM((rows, width), jnp.bfloat16),
        pltpu.VMEM((rows, 128), jnp.float32),
        pltpu.VMEM((rows, 128), jnp.float32),
        pltpu.VMEM((rows, width), jnp.float32),
        pltpu.VMEM((rows, tile), jnp.float32),
        pltpu.VMEM((rows, tile), jnp.float32),
        pltpu.VMEM((tile, width), jnp.bfloat16),
    ]
    if stream:
        scratch += [
            pltpu.VMEM((PASSES, count), jnp.int32),
            pltpu.SemaphoreType.DMA((2,)),
            pltpu.SemaphoreType.DMA((count // tile,)),
        ]
        if initial:
            scratch.append(pltpu.VMEM((rows, width), jnp.float32))
        out_shape.append(pltpu.VMEM(points.shape, points.dtype))
    body = functools.partial(
        pass_body,
        pass_index=pass_index,
        flip=flip,
        stream=stream,
        chained=chained,
        tile=tile,
    )
    return pl.pallas_call(
        body,
        out_shape=out_shape,
        in_specs=[SCALARS, *in_specs],
        out_specs=[HERE] * len(out_shape),
        scratch_shapes=scratch,
        compiler_params=pltpu.CompilerParams(vmem_limit_bytes=20 * 2**20),
        cost_estimate=pl.CostEstimate(
            flops=4 * rows * count * width, bytes_accessed=2 * count * width, transcendentals=0
        ),
        name=f"energies_and_sums_{pass_index}{int(chained)}",
    )(info, *args)


def refine_body(info, own, sibling, *refs, flip):
    first_top, first_low, second_top, second_low, owners, coarse_in, top, low, part = refs
    rows = owners.shape[2]
    mid = rows // 2
    block_width = part.shape[1]
    owner = owners[info[1] ^ flip]
    if coarse_in.shape[1] == block_width:
        coarse = coarse_in[...]
    else:
        coarse = coarse_in[:, pl.ds(pl.multiple_of(info[0] * block_width, block_width), block_width)]
    head = own[0, : mid + TAIL, :] + sibling[0, : mid + TAIL, :]
    rest = own[0, mid + TAIL :, :] + sibling[0, mid + TAIL :, :]
    head = head + (first_top[0] + second_top[...])
    rest = rest + (first_low[0] + second_low[...])
    totals, counts_row = jnp.concatenate([head[:mid], rest], 0), head[mid:]
    counts = as_column(counts_row[:1], rows)[:, :1]
    table = (
        lax.broadcasted_iota(jnp.int32, (NC, rows), 0) == owner
    ).astype(jnp.float32)
    lookup = lax.dot_general(
        table,
        coarse,
        (((0,), (0,)), ((), ())),
        precision=HIGHEST,
        preferred_element_type=jnp.float32,
    )
    new = (totals + prior_weight * lookup) / (counts + prior_weight)
    top[...] = new[:mid]
    low[...] = new[mid:]
    prior = jnp.where(info[3] == 0, prior_weight, 0.0)
    part[:NC, :] = prior * coarse + jnp.dot(
        table, counts * new, precision=HIGHEST, preferred_element_type=jnp.float32
    )
    part[NC:, :] = jnp.zeros((TAIL, part.shape[1]), jnp.float32)
    part[NC:, :NC] = prior + lax.dot_general(
        counts_row,
        table,
        (((1,), (1,)), ((), ())),
        precision=HIGHEST,
        preferred_element_type=jnp.float32,
    )


def refine_half(info, own, sibling, incoming, owners, coarse, *, flip):
    _, rows, block_width = own.shape
    mid = (rows - TAIL) // 2
    args = [near_by(value) for value in (own, sibling, *incoming, owners, coarse)]
    shapes = [(mid, block_width), (mid, block_width), (NC + TAIL, block_width)]
    return pl.pallas_call(
        functools.partial(refine_body, flip=flip),
        out_shape=[pltpu.VMEM(shape, jnp.float32) for shape in shapes],
        in_specs=[SCALARS] + [HERE] * len(args),
        out_specs=[HERE] * len(shapes),
        compiler_params=pltpu.CompilerParams(vmem_limit_bytes=8 * 2**20),
        name="refine_half",
    )(info, *args)


def exchange(held, sibling, later=()):
    cut = (held.shape[1] - TAIL) // 2 + TAIL
    chunks = slice(0, cut), slice(cut, None)
    first = [held[1::2, rows] + sibling[1::2, rows] for rows in chunks]
    first, later = lax.optimization_barrier((first, later))
    first = [swap_first(chunk) for chunk in first]
    second = [
        swap_second(held[2, rows] + sibling[2, rows] + arrived[1])
        for rows, arrived in zip(chunks, first)
    ]
    return [*first, *second], later


PIECES = ((1, 1), (2, 0), (3, 0), (3, 1), (1, 0), (2, 1), (0, 0), (0, 1))


def gather_half(top, low, later=None):
    x_low = swap(low, ACROSS_X)
    y_top = swap(top, ACROSS_Y)
    again = top, low
    if later is not None:
        x_low, y_top, again, later = lax.optimization_barrier((x_low, y_top, again, later))
    x_top = swap(again[0], ACROSS_X)
    y_low = swap(again[1], ACROSS_Y)
    corner_top = swap(y_top, ACROSS_X)
    corner_low = swap(x_low, ACROSS_Y)
    return [x_low, y_top, corner_top, corner_low, x_top, y_low, top, low], later


def spread(value):
    corner = swap(value, ACROSS_X | ACROSS_Y)
    return [value, swap(value, ACROSS_X), swap(value, ACROSS_Y), corner]


def over_cen(value, combine, bits=None):
    for bit in range(lax.axis_size("cen").bit_length() - 1) if bits is None else bits:
        value = combine(value, swap(value, 1 << bit, "cen"))
    return value


def fold(first, second):
    cut = NC + TAIL
    return jnp.concatenate(
        [first[:cut] + second[:cut], jnp.minimum(first[cut:], second[cut:])], 0
    )


def place_body(info, *refs, flip):
    own, other = refs[:3], refs[3:6]
    fine_out, coarse_out, fine_held, coarse_held, sems = refs[6:]
    block_width = coarse_out.shape[1] // SLOTS
    rows = fine_out.shape[0] // 2
    mid = rows // 2
    half = info[1] ^ flip

    def column_of(slot, core):
        start = block_of(info, slot, core) * block_width
        return pl.ds(pl.multiple_of(start, block_width), block_width)

    def put(at, *groups):
        for piece, (slot, is_low) in enumerate(PIECES):
            part = slice(is_low * mid, (is_low + 1) * mid)
            fine_held[at, part, column_of(slot, 0)] = groups[piece // SLOTS][piece % SLOTS]

    def send(at, half):
        span = pl.ds(pl.multiple_of(half * rows, rows), rows)
        return pltpu.make_async_copy(fine_held.at[at], fine_out.at[span], sems.at[at])

    put(0, *own[:2])
    send(0, half).start()
    put(1, *other[:2])
    send(1, 1 - half).start()
    parts, others = own[2], other[2]
    weight = parts[0, NC:, :128] + others[0, NC:, :128]
    weight = as_column(weight[:1], 128)[:NC, :1]
    for slot in range(SLOTS):
        total = parts[slot, :NC, :] + others[slot, :NC, :]
        coarse_held[:, column_of(slot, 0)] = total / weight
    send_coarse = pltpu.make_async_copy(coarse_held, coarse_out, sems.at[2])
    send_coarse.start()
    send(0, half).wait()
    send(1, 1 - half).wait()
    send_coarse.wait()


def place(info, own, other, *, flip):
    _, mid, block_width = own[0].shape
    rows, width = 2 * mid, SLOTS * block_width
    args = [near_by(value) for value in (*own, *other)]
    return pl.pallas_call(
        functools.partial(place_body, flip=flip),
        out_shape=[
            jax.ShapeDtypeStruct((2 * rows, width), jnp.float32),
            jax.ShapeDtypeStruct((NC, width), jnp.float32),
        ],
        in_specs=[SCALARS] + [HERE] * len(args),
        out_specs=[AWAY, AWAY],
        scratch_shapes=[
            pltpu.VMEM((2, rows, width), jnp.float32),
            pltpu.VMEM((NC, width), jnp.float32),
            pltpu.SemaphoreType.DMA((3,)),
        ],
        compiler_params=pltpu.CompilerParams(vmem_limit_bytes=8 * 2**20),
        name="place_blocks",
    )(info, *args)


def on_device_paired(points, fine_assign, fine_start, coarse_start, coarse_assign):
    width = points.shape[1]
    local_count = fine_start.shape[0]
    rows = local_count // 2
    block_width = width // SLOTS
    cen, me = lax.axis_index("cen"), lax.axis_index("pts")
    core = me & 1
    info = jnp.stack([me >> 1, core, cen * local_count, cen * 2 + core]).astype(jnp.int32)
    owners = coarse_assign.reshape(2, 1, rows)

    call = functools.partial(run_pass, info, pass_index=0, rows=rows)
    sent, seen, squares, kept = call(points, fine_assign, fine_start, None, None, flip=1)
    sibling = swap(sent, CORE)
    held, seen_first = call(kept, fine_assign, fine_start, squares, seen, flip=0)
    incoming, _ = exchange(held, sibling)
    top, low, part = refine_half(
        info, held, sibling, incoming, owners, coarse_start, flip=0
    )
    own = jnp.stack(gather_half(top, low)[0])
    folded = jnp.concatenate([part, seen_first.reshape(-1, block_width)], 0)
    paired = swap(folded, 1, "cen")
    other = swap(own, CORE)

    call = functools.partial(run_pass, info, pass_index=1, rows=rows)
    sent, seen, kept = call(points, fine_assign, own, squares, None, flip=0)
    sent, paired = lax.optimization_barrier((sent, paired))
    sibling = swap(sent, CORE)
    folded = fold(folded, paired)
    part = folded[: NC + TAIL]
    others_part = swap(part, CORE)
    held, seen_second = call(kept, fine_assign, other, squares, seen, flip=1)
    held, others_part = lax.optimization_barrier((held, others_part))
    folded = jnp.concatenate([part + others_part, folded[NC + TAIL :]], 0)
    incoming, folded = exchange(held, sibling, folded)
    bits = range(lax.axis_size("cen").bit_length() - 1)
    folded = over_cen(folded, fold, bits[1:])
    part, seen_first = folded[: NC + TAIL], folded[NC + TAIL :]
    coarse = part[:NC] / part[NC, :NC][:, None]

    top, low, part = refine_half(info, held, sibling, incoming, owners, coarse, flip=1)
    folded = jnp.concatenate([part, seen_second.reshape(-1, block_width)], 0)
    top, low, folded = lax.optimization_barrier((top, low, folded))
    folded = over_cen(folded, fold, bits[:1])
    own, folded = gather_half(top, low, folded)
    folded = over_cen(folded, fold, bits[1:])
    part, seen_second = folded[: NC + TAIL], folded[NC + TAIL :]
    blocks = [jnp.stack(own[:4]), jnp.stack(own[4:]), jnp.stack(spread(part))]
    fine_now, coarse_now = place(info, blocks, [swap(block, CORE) for block in blocks], flip=1)

    seen = [each.reshape(2, -1) for each in (seen_first, seen_second)]
    gaps = jnp.stack([each[0] - each[1] for each in seen]) / math.sqrt(width)
    return (fine_now, coarse_now, gaps)


def solution(mesh):
    placed = (P("pts", None), P(None, "pts"), P("cen", None), P(), P("cen"))

    def on_device(points, fine_assign, fine_start, coarse_start, coarse_assign):
        count, width = points.shape
        local_count = fine_start.shape[0]
        centres = mesh.shape["cen"]
        fits = (
            mesh.shape["pts"] == 2 * SLOTS
            and centres & (centres - 1) == 0
            and width // SLOTS == local_count // 2
            and (width // SLOTS) % 128 == 0
            and count % 2048 == 0
        )
        plan = on_device_paired if fits else on_device_any
        return plan(points, fine_assign, fine_start, coarse_start, coarse_assign)

    return jax.shard_map(
        on_device,
        mesh=mesh,
        in_specs=placed,
        out_specs=(P("cen", None), P(), P(None, "pts")),
        check_vma=False,
    )
```

```python
import functools
import math

import jax
import jax.numpy as jnp
from jax import lax
from jax.experimental import pallas as pl
from jax.experimental.pallas import tpu as pltpu
from jax.sharding import PartitionSpec as P

NC = 64
PASSES = 2
FAR = 3.0e38

prior_weight = 4.0
HIGHEST = lax.Precision.HIGHEST


def refine(totals, counts, coarse_cols, coarse_table):
    lookup = jnp.dot(coarse_table, coarse_cols, precision=HIGHEST)
    fine_next = (totals + prior_weight * lookup) / (counts + prior_weight)[:, None]
    coarse_part = lax.dot_general(
        coarse_table,
        counts[:, None] * fine_next,
        (((0,), (0,)), ((), ())),
        precision=HIGHEST,
    )
    coarse_weight = jnp.sum(coarse_table * counts[:, None], axis=0)
    return (fine_next, coarse_part, coarse_weight)


def on_device_any(points, fine_assign, fine_start, coarse_start, coarse_assign):
    width = points.shape[1]
    local_count = fine_start.shape[0]
    offset = lax.axis_index("cen") * local_count
    columns = jnp.arange(local_count, dtype=jnp.int32)
    coarse_table = (coarse_assign[:, None] == jnp.arange(NC, dtype=jnp.int32)[None, :]).astype(
        jnp.float32
    )
    point_values = points.astype(jnp.float32)
    squares = jnp.sum(point_values * point_values, axis=1)
    fine_now = fine_start
    coarse_now = coarse_start
    gap_rows = []
    for pass_index in range(PASSES):
        member = (fine_assign[pass_index] - offset)[:, None] == columns[None, :]
        products = jnp.dot(
            points, fine_now.astype(jnp.bfloat16).T, preferred_element_type=jnp.float32
        )
        energy = jnp.sum(fine_now * fine_now, axis=1)[None, :] - 2.0 * products
        picked_local = jnp.sum(jnp.where(member, energy, 0.0), axis=1)
        nearest_local = jnp.min(energy, axis=1)
        picked = lax.psum(picked_local, "cen")
        nearest = lax.pmin(nearest_local, "cen")
        gap_rows.append((picked - nearest) / math.sqrt(width))
        weights = 1.0 / (1.0 + (squares + picked) / width)
        scaled = (point_values * weights[:, None]).astype(jnp.bfloat16)
        partial_sums = lax.dot_general(
            member.astype(jnp.bfloat16),
            scaled,
            (((0,), (0,)), ((), ())),
            preferred_element_type=jnp.float32,
        )
        partial_weights = jnp.sum(jnp.where(member, weights[:, None], 0.0), axis=0)
        share_width = width // lax.axis_size("pts")
        start = lax.axis_index("pts") * share_width
        shares = lax.psum_scatter(partial_sums, "pts", scatter_dimension=1, tiled=True)
        counts = lax.psum(partial_weights, "pts")
        coarse_cols = lax.dynamic_slice_in_dim(coarse_now, start, share_width, 1)
        fine_share, coarse_part, coarse_weight = refine(shares, counts, coarse_cols, coarse_table)
        coarse_sum, coarse_count = lax.psum((coarse_part, coarse_weight), "cen")
        coarse_share = (coarse_sum + prior_weight * coarse_cols) / (coarse_count + prior_weight)[
            :, None
        ]
        fine_now, coarse_now = (
            lax.all_gather(fine_share, "pts", axis=1, tiled=True),
            lax.all_gather(coarse_share, "pts", axis=1, tiled=True),
        )
    return (fine_now, coarse_now, jnp.stack(gap_rows))


CORE, ACROSS_X, ACROSS_Y = 1, 2, 4
SLOTS = 4
TAIL = 8


def swap(value, bit, axis="pts"):
    size = lax.axis_size(axis)
    return lax.ppermute(value, axis, [(i, i ^ bit) for i in range(size)])


def swap_first(value):
    pairs = [(i, i ^ (ACROSS_Y if i & CORE else ACROSS_X)) for i in range(lax.axis_size("pts"))]
    return lax.ppermute(value, "pts", pairs)


def swap_second(value):
    pairs = [(i, i ^ (ACROSS_X if i & CORE else ACROSS_Y)) for i in range(lax.axis_size("pts"))]
    return lax.ppermute(value, "pts", pairs)


def block_of(info, slot, core):
    crossed = (slot >> 1) | ((slot & 1) << 1)
    return info[0] ^ (slot + core * (crossed - slot))


HERE = pl.BlockSpec(memory_space=pltpu.VMEM)
AWAY = pl.BlockSpec(memory_space=pl.ANY)
SCALARS = pl.BlockSpec(memory_space=pltpu.SMEM)


def near_by(value):
    return pltpu.with_memory_space_constraint(value, pltpu.VMEM)


def far_off(value):
    return pltpu.with_memory_space_constraint(value, pltpu.HBM)


def as_column(row, rows):
    return jnp.broadcast_to(row, (128, rows)).T


def pass_body(info, points, assign, fine, *refs, pass_index, flip, stream, chained, tile):
    refs = list(refs)
    initial = pass_index == 0
    first = stream
    squares_in = None if first else refs.pop(0)
    seen_in = refs.pop(0) if chained else None
    payload, seen = refs.pop(0), refs.pop(0)
    squares_out = refs.pop(0) if first else None
    kept = refs.pop(0) if stream else points
    low, norms, tallies, sums, even, odd, scaled = refs[:7]
    chosen_in = refs[7] if stream else assign
    small_sems, point_sems = refs[8:10] if stream else (None, None)
    start = refs[10] if first else None
    rows, width = low.shape
    mid = rows // 2
    block_width = width // SLOTS
    half = info[1] ^ flip
    base = info[2] + half * rows
    tiles = points.shape[0] // tile

    def span(i):
        return pl.ds(pl.multiple_of(i * tile, tile), tile)

    def column_of(slot, core):
        start = block_of(info, slot, core) * block_width
        return pl.ds(pl.multiple_of(start, block_width), block_width)

    def load(i, half):
        part = pl.ds(pl.multiple_of(i * tile + half * (tile // 2), tile // 2), tile // 2)
        return pltpu.make_async_copy(points.at[part], kept.at[part], point_sems.at[2 * i + half])

    if first:
        load_start = pltpu.make_async_copy(
            fine.at[pl.ds(pl.multiple_of(half * rows, rows), rows)], start, small_sems.at[1]
        )
        load_start.start()
    if stream:
        load(0, 0).start()
        load(0, 1).start()
        load_assign = pltpu.make_async_copy(assign, chosen_in, small_sems.at[0])
        load_assign.start()

    if initial:
        if first:
            load_start.wait()
            block = start[...]
        else:
            block = fine[pl.ds(pl.multiple_of(half * rows, rows), rows), :]
        norm = jnp.sum(block * block, axis=1, keepdims=True)
        low[...] = (-2.0 * block).astype(jnp.bfloat16)
    else:
        norm = [jnp.zeros((mid, 1), jnp.float32)] * 2
        for piece, (slot, is_low) in enumerate(PIECES):
            block = fine[piece]
            norm[is_low] = norm[is_low] + jnp.sum(block * block, axis=1, keepdims=True)
            part = slice(is_low * mid, (is_low + 1) * mid)
            low[part, column_of(slot, 0)] = (-2.0 * block).astype(jnp.bfloat16)
        norm = jnp.concatenate(norm, 0)
    norms[...] = jnp.broadcast_to(norm, norms.shape)
    tallies[...] = jnp.zeros_like(tallies)
    sums[...] = jnp.zeros_like(sums)

    def multiply(i, target):
        target[...] = lax.dot_general(
            low[...], kept[span(i), :], (((1,), (1,)), ((), ())), preferred_element_type=jnp.float32
        )

    def collect(i, products):
        energy = products[...] + jnp.concatenate([norms[...]] * (tile // 128), axis=1)
        chosen = chosen_in[pass_index : pass_index + 1, span(i)] - base
        member = lax.broadcasted_iota(jnp.int32, energy.shape, 0) == chosen
        picked = jnp.sum(jnp.where(member, energy, 0.0), axis=0, keepdims=True)
        nearest = jnp.min(energy, axis=0, keepdims=True)
        inside = (chosen >= 0) & (chosen < rows)
        picked_seen = jnp.where(inside, picked, FAR)
        if chained:
            picked_seen = jnp.minimum(picked_seen, seen_in[0:1, span(i)])
            nearest = jnp.minimum(nearest, seen_in[1:2, span(i)])
        seen[0:1, span(i)] = picked_seen
        seen[1:2, span(i)] = nearest
        if first:
            folded = jnp.zeros((tile, 128), jnp.float32)
            for lane in range(0, width, 128):
                values = kept[span(i), lane : lane + 128].astype(jnp.float32)
                folded = folded + values * values
            squares = jnp.sum(folded.T, axis=0, keepdims=True)
            squares_out[0:1, span(i)] = squares
        else:
            squares = squares_in[0:1, span(i)]
        weights = 1.0 / (1.0 + (squares + picked) / width)
        weighted = jnp.where(member, weights, 0.0)
        tally = tallies[...]
        for lane in range(0, tile, 128):
            tally = tally + weighted[:, lane : lane + 128]
        tallies[...] = tally
        factor = as_column(weights, tile)
        for lane in range(0, width, 128):
            values = kept[span(i), lane : lane + 128].astype(jnp.float32)
            scaled[:, lane : lane + 128] = (values * factor).astype(jnp.bfloat16)
        sums[...] += jnp.dot(
            member.astype(jnp.float32).astype(jnp.bfloat16),
            scaled[...],
            preferred_element_type=jnp.float32,
        )

    def arrive(i, more):
        for half in range(2):
            if stream:
                load(i, half).wait()
                if more:
                    load(i + 1, half).start()

    if stream:
        load_assign.wait()
    arrive(0, True)
    multiply(0, even)

    @pl.loop(0, tiles // 2 - 1)
    def _(pair):
        i = 2 * pair
        arrive(i + 1, True)
        multiply(i + 1, odd)
        collect(i, even)
        arrive(i + 2, True)
        multiply(i + 2, even)
        collect(i + 1, odd)

    arrive(tiles - 1, False)
    multiply(tiles - 1, odd)
    collect(tiles - 2, even)
    collect(tiles - 1, odd)

    counts = jnp.broadcast_to(jnp.sum(tallies[...].T, axis=0, keepdims=True), (TAIL, rows))
    for slot in range(SLOTS):
        columns = column_of(slot, info[1] ^ (not chained))
        payload[slot, :mid, :] = sums[:mid, columns]
        payload[slot, mid : mid + TAIL, :] = counts
        payload[slot, mid + TAIL :, :] = sums[mid:, columns]


def fetch_body(points, *refs):
    *_, kept, sems = refs
    share = points.shape[0] // sems.shape[0]
    copies = [
        pltpu.make_async_copy(
            points.at[i * share : (i + 1) * share], kept.at[i * share : (i + 1) * share], sems.at[i]
        )
        for i in range(sems.shape[0])
    ]
    for copy in copies:
        copy.start()
    for copy in copies:
        copy.wait()


def fetch(points, after):
    return pl.pallas_call(
        fetch_body,
        out_shape=pltpu.VMEM(points.shape, points.dtype),
        in_specs=[AWAY] + [HERE] * len(after),
        out_specs=HERE,
        scratch_shapes=[pltpu.SemaphoreType.DMA((8,))],
        compiler_params=pltpu.CompilerParams(vmem_limit_bytes=2 * 2**20),
        cost_estimate=pl.CostEstimate(
            flops=0, bytes_accessed=4 * points.size, transcendentals=0
        ),
        name="fetch_points",
    )(far_off(points), *[near_by(value) for value in after])


def run_pass(info, points, fine_assign, fine, squares, seen, *, pass_index, flip, rows):
    count, width = points.shape
    block_width = width // SLOTS
    tile = 1024
    initial = pass_index == 0
    chained = seen is not None
    stream = squares is None
    if stream:
        in_specs = [AWAY] * 3
        args = [far_off(points), far_off(fine_assign), far_off(fine)]
    else:
        in_specs = [HERE] * 3
        args = [near_by(points), near_by(fine_assign), near_by(fine)]
    for value in (squares, seen):
        if value is not None:
            in_specs.append(HERE)
            args.append(near_by(value))
    shapes = [(SLOTS, rows + TAIL, block_width), (2, count)]
    if squares is None:
        shapes.append((1, count))
    out_shape = [pltpu.VMEM(shape, jnp.float32) for shape in shapes]
    scratch = [
        pltpu.VMEM((rows, width), jnp.bfloat16),
        pltpu.VMEM((rows, 128), jnp.float32),
        pltpu.VMEM((rows, 128), jnp.float32),
        pltpu.VMEM((rows, width), jnp.float32),
        pltpu.VMEM((rows, tile), jnp.float32),
        pltpu.VMEM((rows, tile), jnp.float32),
        pltpu.VMEM((tile, width), jnp.bfloat16),
    ]
    if stream:
        scratch += [
            pltpu.VMEM((PASSES, count), jnp.int32),
            pltpu.SemaphoreType.DMA((2,)),
            pltpu.SemaphoreType.DMA((2 * count // tile,)),
        ]
        if initial:
            scratch.append(pltpu.VMEM((rows, width), jnp.float32))
        out_shape.append(pltpu.VMEM(points.shape, points.dtype))
    body = functools.partial(
        pass_body,
        pass_index=pass_index,
        flip=flip,
        stream=stream,
        chained=chained,
        tile=tile,
    )
    return pl.pallas_call(
        body,
        out_shape=out_shape,
        in_specs=[SCALARS, *in_specs],
        out_specs=[HERE] * len(out_shape),
        scratch_shapes=scratch,
        compiler_params=pltpu.CompilerParams(vmem_limit_bytes=20 * 2**20),
        cost_estimate=pl.CostEstimate(
            flops=4 * rows * count * width, bytes_accessed=2 * count * width, transcendentals=0
        ),
        name=f"energies_and_sums_{pass_index}{int(chained)}",
    )(info, *args)


def refine_body(info, own, sibling, *refs, flip):
    first_top, first_low, second_top, second_low, owners, *coarse_in, top, low, part = refs
    rows = owners.shape[2]
    mid = rows // 2
    block_width = part.shape[1]
    owner = owners[info[1] ^ flip]
    if len(coarse_in) == 1:
        column = pl.multiple_of(info[0] * block_width, block_width)
        coarse = coarse_in[0][:, pl.ds(column, block_width)]
    else:
        sums = coarse_in[0][: NC + TAIL, :] + coarse_in[1][: NC + TAIL, :]
        coarse = sums[:NC] / as_column(sums[NC : NC + 1, :128], 128)[:NC, :1]
    head = own[0, : mid + TAIL, :] + sibling[0, : mid + TAIL, :]
    rest = own[0, mid + TAIL :, :] + sibling[0, mid + TAIL :, :]
    head = head + (first_top[0] + second_top[...])
    rest = rest + (first_low[0] + second_low[...])
    totals, counts_row = jnp.concatenate([head[:mid], rest], 0), head[mid:]
    counts = as_column(counts_row[:1], rows)[:, :1]
    table = (
        lax.broadcasted_iota(jnp.int32, (NC, rows), 0) == owner
    ).astype(jnp.float32)
    lookup = lax.dot_general(
        table,
        coarse,
        (((0,), (0,)), ((), ())),
        precision=HIGHEST,
        preferred_element_type=jnp.float32,
    )
    new = (totals + prior_weight * lookup) / (counts + prior_weight)
    top[...] = new[:mid]
    low[...] = new[mid:]
    prior = jnp.where(info[3] == 0, prior_weight, 0.0)
    part[:NC, :] = prior * coarse + jnp.dot(
        table, counts * new, precision=HIGHEST, preferred_element_type=jnp.float32
    )
    part[NC:, :] = jnp.zeros((TAIL, part.shape[1]), jnp.float32)
    part[NC:, :NC] = prior + lax.dot_general(
        counts_row,
        table,
        (((1,), (1,)), ((), ())),
        precision=HIGHEST,
        preferred_element_type=jnp.float32,
    )


def refine_half(info, own, sibling, incoming, owners, coarse, *, flip):
    _, rows, block_width = own.shape
    mid = (rows - TAIL) // 2
    args = [near_by(value) for value in (own, sibling, *incoming, owners, *coarse)]
    shapes = [(mid, block_width), (mid, block_width), (NC + TAIL, block_width)]
    return pl.pallas_call(
        functools.partial(refine_body, flip=flip),
        out_shape=[pltpu.VMEM(shape, jnp.float32) for shape in shapes],
        in_specs=[SCALARS] + [HERE] * len(args),
        out_specs=[HERE] * len(shapes),
        compiler_params=pltpu.CompilerParams(vmem_limit_bytes=8 * 2**20),
        name="refine_half",
    )(info, *args)


def exchange(held, sibling, folded=None):
    cut = (held.shape[1] - TAIL) // 2 + TAIL
    chunks = slice(0, cut), slice(cut, None)
    first = [held[1::2, rows] + sibling[1::2, rows] for rows in chunks]
    first, folded = lax.optimization_barrier((first, folded))
    first = [swap_first(chunk) for chunk in first]
    if folded is not None:
        folded = swap(folded, lax.axis_size("cen") // 2, "cen")
        first[1], folded = lax.optimization_barrier((first[1], folded))
    second = [
        swap_second(held[2, rows] + sibling[2, rows] + arrived[1])
        for rows, arrived in zip(chunks, first)
    ]
    return [*first, *second], folded


PIECES = ((1, 1), (2, 0), (3, 0), (3, 1), (1, 0), (2, 1), (0, 0), (0, 1))


def gather_half(top, low, later=False):
    x_low = swap(low, ACROSS_X)
    y_top = swap(top, ACROSS_Y)
    again = top, low
    if later:
        x_low, y_top, again = lax.optimization_barrier((x_low, y_top, again))
    x_top = swap(again[0], ACROSS_X)
    y_low = swap(again[1], ACROSS_Y)
    corner_top = swap(y_top, ACROSS_X)
    corner_low = swap(x_low, ACROSS_Y)
    return [x_low, y_top, corner_top, corner_low, x_top, y_low, top, low]


def spread(value):
    corner = swap(value, ACROSS_X | ACROSS_Y)
    return [value, swap(value, ACROSS_X), swap(value, ACROSS_Y), corner]


def over_cen(value, combine, bits=None):
    for bit in range(lax.axis_size("cen").bit_length() - 1) if bits is None else bits:
        value = combine(value, swap(value, 1 << bit, "cen"))
    return value


def fold(first, second):
    cut = NC + TAIL
    return jnp.concatenate(
        [first[:cut] + second[:cut], jnp.minimum(first[cut:], second[cut:])], 0
    )


def place_body(info, *refs, flip):
    fine_out, held, sems = refs[4:]
    rows = fine_out.shape[0] // 2
    mid = rows // 2
    block_width = fine_out.shape[1] // SLOTS
    sends = []
    for at in range(2):
        for piece, (slot, is_low) in enumerate(PIECES):
            block = refs[2 * at + piece // SLOTS][piece % SLOTS]
            column = pl.multiple_of(block_of(info, slot, 0) * block_width, block_width)
            held[at, is_low * mid : (is_low + 1) * mid, pl.ds(column, block_width)] = block
        half = info[1] ^ flip ^ at
        span = pl.ds(pl.multiple_of(half * rows, rows), rows)
        sends.append(pltpu.make_async_copy(held.at[at], fine_out.at[span], sems.at[at]))
        sends[at].start()
    for send in sends:
        send.wait()


def place(info, own, other, *, flip):
    _, mid, block_width = own[0].shape
    rows, width = 2 * mid, SLOTS * block_width
    args = [near_by(value) for value in (*own, *other)]
    return pl.pallas_call(
        functools.partial(place_body, flip=flip),
        out_shape=jax.ShapeDtypeStruct((2 * rows, width), jnp.float32),
        in_specs=[SCALARS] + [HERE] * len(args),
        out_specs=AWAY,
        scratch_shapes=[
            pltpu.VMEM((2, rows, width), jnp.float32),
            pltpu.SemaphoreType.DMA((2,)),
        ],
        compiler_params=pltpu.CompilerParams(vmem_limit_bytes=8 * 2**20),
        name="place_fine",
    )(info, *args)


def place_coarse_body(info, parts, others, after, coarse_out):
    block_width = parts.shape[2]
    weight = parts[0, NC:, :128] + others[0, NC:, :128]
    weight = as_column(weight[:1], 128)[:NC, :1]
    for slot in range(SLOTS):
        total = parts[slot, :NC, :] + others[slot, :NC, :]
        column = pl.multiple_of(block_of(info, slot, 0) * block_width, block_width)
        coarse_out[:, pl.ds(column, block_width)] = total / weight


def place_coarse(info, parts, others, after):
    return pl.pallas_call(
        place_coarse_body,
        out_shape=jax.ShapeDtypeStruct((NC, SLOTS * parts.shape[2]), jnp.float32),
        in_specs=[SCALARS, HERE, HERE, AWAY],
        out_specs=HERE,
        compiler_params=pltpu.CompilerParams(vmem_limit_bytes=4 * 2**20),
        name="place_coarse",
    )(info, near_by(parts), near_by(others), far_off(after))


def on_device_paired(points, fine_assign, fine_start, coarse_start, coarse_assign):
    width = points.shape[1]
    local_count = fine_start.shape[0]
    rows = local_count // 2
    block_width = width // SLOTS
    cen, me = lax.axis_index("cen"), lax.axis_index("pts")
    core = me & 1
    info = jnp.stack([me >> 1, core, cen * local_count, cen * 2 + core]).astype(jnp.int32)
    owners = coarse_assign.reshape(2, 1, rows)

    call = functools.partial(run_pass, info, pass_index=0, rows=rows)
    sent, seen, squares, kept = call(points, fine_assign, fine_start, None, None, flip=1)
    sibling = swap(sent, CORE)
    held, seen_first = call(kept, fine_assign, fine_start, squares, seen, flip=0)
    incoming, _ = exchange(held, sibling)
    top, low, part = refine_half(
        info, held, sibling, incoming, owners, [coarse_start], flip=0
    )
    own = gather_half(top, low)
    own, kept = lax.optimization_barrier((own, fetch(points, own[:2])))
    own = jnp.stack(own)
    bits = range(lax.axis_size("cen").bit_length() - 1)
    folded = jnp.concatenate([part, seen_first.reshape(-1, block_width)], 0)
    folded = over_cen(folded, fold, bits[:1])
    own, folded = lax.optimization_barrier((own, folded))
    other = swap(own, CORE)

    call = functools.partial(run_pass, info, pass_index=1, rows=rows)
    sent, seen = call(kept, fine_assign, own, squares, None, flip=0)
    sibling = swap(sent, CORE)
    part = folded[: NC + TAIL]
    others_part = swap(part, CORE)
    held, seen_second = call(kept, fine_assign, other, squares, seen, flip=1)
    held, others_part = lax.optimization_barrier((held, others_part))
    folded = jnp.concatenate([part + others_part, folded[NC + TAIL :]], 0)
    folded = over_cen(folded, fold, bits[1:-1])
    incoming, paired = exchange(held, sibling, folded)
    seen_first = jnp.minimum(folded[NC + TAIL :], paired[NC + TAIL :])

    top, low, part = refine_half(
        info, held, sibling, incoming, owners, [folded, paired], flip=1
    )
    folded = jnp.concatenate([part, seen_second.reshape(-1, block_width)], 0)
    top, low, folded = lax.optimization_barrier((top, low, folded))
    own = gather_half(top, low, True)
    folded = over_cen(folded, fold)
    part, seen_second = folded[: NC + TAIL], folded[NC + TAIL :]
    own = [jnp.stack(own[:4]), jnp.stack(own[4:])]
    fine_now = place(info, own, [swap(group, CORE) for group in own], flip=1)
    parts = jnp.stack(spread(part))
    coarse_now = place_coarse(info, parts, swap(parts, CORE), fine_now)

    seen = [each.reshape(2, -1) for each in (seen_first, seen_second)]
    gaps = jnp.stack([each[0] - each[1] for each in seen]) / math.sqrt(width)
    return (fine_now, coarse_now, gaps)


def solution(mesh):
    placed = (P("pts", None), P(None, "pts"), P("cen", None), P(), P("cen"))

    def on_device(points, fine_assign, fine_start, coarse_start, coarse_assign):
        count, width = points.shape
        local_count = fine_start.shape[0]
        centres = mesh.shape["cen"]
        fits = (
            mesh.shape["pts"] == 2 * SLOTS
            and centres & (centres - 1) == 0
            and centres >= 4
            and width // SLOTS == local_count // 2
            and (width // SLOTS) % 128 == 0
            and count % 2048 == 0
        )
        plan = on_device_paired if fits else on_device_any
        return plan(points, fine_assign, fine_start, coarse_start, coarse_assign)

    return jax.shard_map(
        on_device,
        mesh=mesh,
        in_specs=placed,
        out_specs=(P("cen", None), P(), P(None, "pts")),
        check_vma=False,
    )
```

```python
import functools
import math

import jax
import jax.numpy as jnp
from jax import lax
from jax.experimental import pallas as pl
from jax.experimental.pallas import tpu as pltpu
from jax.sharding import PartitionSpec as P

NC = 64
PASSES = 2
FAR = 3.0e38

prior_weight = 4.0
HIGHEST = lax.Precision.HIGHEST


def refine(totals, counts, coarse_cols, coarse_table):
    lookup = jnp.dot(coarse_table, coarse_cols, precision=HIGHEST)
    fine_next = (totals + prior_weight * lookup) / (counts + prior_weight)[:, None]
    coarse_part = lax.dot_general(
        coarse_table,
        counts[:, None] * fine_next,
        (((0,), (0,)), ((), ())),
        precision=HIGHEST,
    )
    coarse_weight = jnp.sum(coarse_table * counts[:, None], axis=0)
    return (fine_next, coarse_part, coarse_weight)


def on_device_any(points, fine_assign, fine_start, coarse_start, coarse_assign):
    width = points.shape[1]
    local_count = fine_start.shape[0]
    offset = lax.axis_index("cen") * local_count
    columns = jnp.arange(local_count, dtype=jnp.int32)
    coarse_table = (coarse_assign[:, None] == jnp.arange(NC, dtype=jnp.int32)[None, :]).astype(
        jnp.float32
    )
    point_values = points.astype(jnp.float32)
    squares = jnp.sum(point_values * point_values, axis=1)
    fine_now = fine_start
    coarse_now = coarse_start
    gap_rows = []
    for pass_index in range(PASSES):
        member = (fine_assign[pass_index] - offset)[:, None] == columns[None, :]
        products = jnp.dot(
            points, fine_now.astype(jnp.bfloat16).T, preferred_element_type=jnp.float32
        )
        energy = jnp.sum(fine_now * fine_now, axis=1)[None, :] - 2.0 * products
        picked_local = jnp.sum(jnp.where(member, energy, 0.0), axis=1)
        nearest_local = jnp.min(energy, axis=1)
        picked = lax.psum(picked_local, "cen")
        nearest = lax.pmin(nearest_local, "cen")
        gap_rows.append((picked - nearest) / math.sqrt(width))
        weights = 1.0 / (1.0 + (squares + picked) / width)
        scaled = (point_values * weights[:, None]).astype(jnp.bfloat16)
        partial_sums = lax.dot_general(
            member.astype(jnp.bfloat16),
            scaled,
            (((0,), (0,)), ((), ())),
            preferred_element_type=jnp.float32,
        )
        partial_weights = jnp.sum(jnp.where(member, weights[:, None], 0.0), axis=0)
        share_width = width // lax.axis_size("pts")
        start = lax.axis_index("pts") * share_width
        shares = lax.psum_scatter(partial_sums, "pts", scatter_dimension=1, tiled=True)
        counts = lax.psum(partial_weights, "pts")
        coarse_cols = lax.dynamic_slice_in_dim(coarse_now, start, share_width, 1)
        fine_share, coarse_part, coarse_weight = refine(shares, counts, coarse_cols, coarse_table)
        coarse_sum, coarse_count = lax.psum((coarse_part, coarse_weight), "cen")
        coarse_share = (coarse_sum + prior_weight * coarse_cols) / (coarse_count + prior_weight)[
            :, None
        ]
        fine_now, coarse_now = (
            lax.all_gather(fine_share, "pts", axis=1, tiled=True),
            lax.all_gather(coarse_share, "pts", axis=1, tiled=True),
        )
    return (fine_now, coarse_now, jnp.stack(gap_rows))


CORE, ACROSS_X, ACROSS_Y = 1, 2, 4
SLOTS = 4
TAIL = 8


def swap(value, bit, axis="pts"):
    size = lax.axis_size(axis)
    return lax.ppermute(value, axis, [(i, i ^ bit) for i in range(size)])


def swap_first(value):
    pairs = [(i, i ^ (ACROSS_Y if i & CORE else ACROSS_X)) for i in range(lax.axis_size("pts"))]
    return lax.ppermute(value, "pts", pairs)


def swap_second(value):
    pairs = [(i, i ^ (ACROSS_X if i & CORE else ACROSS_Y)) for i in range(lax.axis_size("pts"))]
    return lax.ppermute(value, "pts", pairs)


def block_of(info, slot, core):
    crossed = (slot >> 1) | ((slot & 1) << 1)
    return info[0] ^ (slot + core * (crossed - slot))


HERE = pl.BlockSpec(memory_space=pltpu.VMEM)
AWAY = pl.BlockSpec(memory_space=pl.ANY)
SCALARS = pl.BlockSpec(memory_space=pltpu.SMEM)


def near_by(value):
    return pltpu.with_memory_space_constraint(value, pltpu.VMEM)


def far_off(value):
    return pltpu.with_memory_space_constraint(value, pltpu.HBM)


def as_column(row, rows):
    return jnp.broadcast_to(row, (128, rows)).T


def pass_body(info, points, assign, fine, *refs, pass_index, flip, stream, chained, tile):
    refs = list(refs)
    initial = pass_index == 0
    first = stream
    squares_in = None if first else refs.pop(0)
    seen_in = refs.pop(0) if chained else None
    payload, seen = refs.pop(0), refs.pop(0)
    squares_out = refs.pop(0) if first else None
    kept = refs.pop(0) if stream else points
    low, norms, tallies, sums, even, odd, scaled = refs[:7]
    chosen_in = refs[7] if stream else assign
    small_sems, point_sems = refs[8:10] if stream else (None, None)
    start = refs[10] if first else None
    rows, width = low.shape
    mid = rows // 2
    block_width = width // SLOTS
    half = info[1] ^ flip
    base = info[2] + half * rows
    tiles = points.shape[0] // tile

    def span(i):
        return pl.ds(pl.multiple_of(i * tile, tile), tile)

    def column_of(slot, core):
        start = block_of(info, slot, core) * block_width
        return pl.ds(pl.multiple_of(start, block_width), block_width)

    def load(i, half):
        part = pl.ds(pl.multiple_of(i * tile + half * (tile // 2), tile // 2), tile // 2)
        return pltpu.make_async_copy(points.at[part], kept.at[part], point_sems.at[2 * i + half])

    if first:
        load_start = pltpu.make_async_copy(
            fine.at[pl.ds(pl.multiple_of(half * rows, rows), rows)], start, small_sems.at[1]
        )
        load_start.start()
    if stream:
        load(0, 0).start()
        load(0, 1).start()
        load_assign = pltpu.make_async_copy(assign, chosen_in, small_sems.at[0])
        load_assign.start()

    if initial:
        if first:
            load_start.wait()
            block = start[...]
        else:
            block = fine[pl.ds(pl.multiple_of(half * rows, rows), rows), :]
        norm = jnp.sum(block * block, axis=1, keepdims=True)
        low[...] = (-2.0 * block).astype(jnp.bfloat16)
    else:
        norm = [jnp.zeros((mid, 1), jnp.float32)] * 2
        for piece, (slot, is_low) in enumerate(PIECES):
            block = fine[piece]
            norm[is_low] = norm[is_low] + jnp.sum(block * block, axis=1, keepdims=True)
            part = slice(is_low * mid, (is_low + 1) * mid)
            low[part, column_of(slot, 0)] = (-2.0 * block).astype(jnp.bfloat16)
        norm = jnp.concatenate(norm, 0)
    norms[...] = jnp.broadcast_to(norm, norms.shape)
    tallies[...] = jnp.zeros_like(tallies)
    sums[...] = jnp.zeros_like(sums)

    def multiply(i, target):
        target[...] = lax.dot_general(
            low[...], kept[span(i), :], (((1,), (1,)), ((), ())), preferred_element_type=jnp.float32
        )

    def collect(i, products):
        energy = products[...] + jnp.concatenate([norms[...]] * (tile // 128), axis=1)
        chosen = chosen_in[pass_index : pass_index + 1, span(i)] - base
        member = lax.broadcasted_iota(jnp.int32, energy.shape, 0) == chosen
        picked = jnp.sum(jnp.where(member, energy, 0.0), axis=0, keepdims=True)
        nearest = jnp.min(energy, axis=0, keepdims=True)
        inside = (chosen >= 0) & (chosen < rows)
        picked_seen = jnp.where(inside, picked, FAR)
        if chained:
            picked_seen = jnp.minimum(picked_seen, seen_in[0:1, span(i)])
            nearest = jnp.minimum(nearest, seen_in[1:2, span(i)])
        seen[0:1, span(i)] = picked_seen
        seen[1:2, span(i)] = nearest
        if first:
            folded = jnp.zeros((tile, 128), jnp.float32)
            for lane in range(0, width, 128):
                values = kept[span(i), lane : lane + 128].astype(jnp.float32)
                folded = folded + values * values
            squares = jnp.sum(folded.T, axis=0, keepdims=True)
            squares_out[0:1, span(i)] = squares
        else:
            squares = squares_in[0:1, span(i)]
        weights = 1.0 / (1.0 + (squares + picked) / width)
        weighted = jnp.where(member, weights, 0.0)
        tally = tallies[...]
        for lane in range(0, tile, 128):
            tally = tally + weighted[:, lane : lane + 128]
        tallies[...] = tally
        factor = as_column(weights, tile)
        for lane in range(0, width, 128):
            values = kept[span(i), lane : lane + 128].astype(jnp.float32)
            scaled[:, lane : lane + 128] = (values * factor).astype(jnp.bfloat16)
        sums[...] += jnp.dot(
            member.astype(jnp.float32).astype(jnp.bfloat16),
            scaled[...],
            preferred_element_type=jnp.float32,
        )

    def arrive(i, more):
        for half in range(2):
            if stream:
                load(i, half).wait()
                if more:
                    load(i + 1, half).start()

    if stream:
        load_assign.wait()
    arrive(0, True)
    multiply(0, even)

    @pl.loop(0, tiles // 2 - 1)
    def _(pair):
        i = 2 * pair
        arrive(i + 1, True)
        multiply(i + 1, odd)
        collect(i, even)
        arrive(i + 2, True)
        multiply(i + 2, even)
        collect(i + 1, odd)

    arrive(tiles - 1, False)
    multiply(tiles - 1, odd)
    collect(tiles - 2, even)
    collect(tiles - 1, odd)

    counts = jnp.broadcast_to(jnp.sum(tallies[...].T, axis=0, keepdims=True), (TAIL, rows))
    for slot in range(SLOTS):
        columns = column_of(slot, info[1] ^ (not chained))
        payload[slot, :mid, :] = sums[:mid, columns]
        payload[slot, mid : mid + TAIL, :] = counts
        payload[slot, mid + TAIL :, :] = sums[mid:, columns]


def fetch_body(points, *refs):
    *_, kept, sems = refs
    share = points.shape[0] // sems.shape[0]
    copies = [
        pltpu.make_async_copy(
            points.at[i * share : (i + 1) * share], kept.at[i * share : (i + 1) * share], sems.at[i]
        )
        for i in range(sems.shape[0])
    ]
    for copy in copies:
        copy.start()
    for copy in copies:
        copy.wait()


def fetch(points, after):
    return pl.pallas_call(
        fetch_body,
        out_shape=pltpu.VMEM(points.shape, points.dtype),
        in_specs=[AWAY] + [HERE] * len(after),
        out_specs=HERE,
        scratch_shapes=[pltpu.SemaphoreType.DMA((8,))],
        compiler_params=pltpu.CompilerParams(vmem_limit_bytes=2 * 2**20),
        cost_estimate=pl.CostEstimate(
            flops=0, bytes_accessed=4 * points.size, transcendentals=0
        ),
        name="fetch_points",
    )(far_off(points), *[near_by(value) for value in after])


def run_pass(info, points, fine_assign, fine, squares, seen, *, pass_index, flip, rows):
    count, width = points.shape
    block_width = width // SLOTS
    tile = 1024
    initial = pass_index == 0
    chained = seen is not None
    stream = squares is None
    if stream:
        in_specs = [AWAY] * 3
        args = [far_off(points), far_off(fine_assign), far_off(fine)]
    else:
        in_specs = [HERE] * 3
        args = [near_by(points), near_by(fine_assign), near_by(fine)]
    for value in (squares, seen):
        if value is not None:
            in_specs.append(HERE)
            args.append(near_by(value))
    shapes = [(SLOTS, rows + TAIL, block_width), (2, count)]
    if squares is None:
        shapes.append((1, count))
    out_shape = [pltpu.VMEM(shape, jnp.float32) for shape in shapes]
    scratch = [
        pltpu.VMEM((rows, width), jnp.bfloat16),
        pltpu.VMEM((rows, 128), jnp.float32),
        pltpu.VMEM((rows, 128), jnp.float32),
        pltpu.VMEM((rows, width), jnp.float32),
        pltpu.VMEM((rows, tile), jnp.float32),
        pltpu.VMEM((rows, tile), jnp.float32),
        pltpu.VMEM((tile, width), jnp.bfloat16),
    ]
    if stream:
        scratch += [
            pltpu.VMEM((PASSES, count), jnp.int32),
            pltpu.SemaphoreType.DMA((2,)),
            pltpu.SemaphoreType.DMA((2 * count // tile,)),
        ]
        if initial:
            scratch.append(pltpu.VMEM((rows, width), jnp.float32))
        out_shape.append(pltpu.VMEM(points.shape, points.dtype))
    body = functools.partial(
        pass_body,
        pass_index=pass_index,
        flip=flip,
        stream=stream,
        chained=chained,
        tile=tile,
    )
    return pl.pallas_call(
        body,
        out_shape=out_shape,
        in_specs=[SCALARS, *in_specs],
        out_specs=[HERE] * len(out_shape),
        scratch_shapes=scratch,
        compiler_params=pltpu.CompilerParams(vmem_limit_bytes=20 * 2**20),
        cost_estimate=pl.CostEstimate(
            flops=4 * rows * count * width, bytes_accessed=2 * count * width, transcendentals=0
        ),
        name=f"energies_and_sums_{pass_index}{int(chained)}",
    )(info, *args)


def refine_body(info, own, sibling, *refs, flip):
    first_top, first_low, second_top, second_low, owners, *coarse_in, top, low, part = refs
    rows = owners.shape[2]
    mid = rows // 2
    block_width = part.shape[1]
    owner = owners[info[1] ^ flip]
    if len(coarse_in) == 1:
        column = pl.multiple_of(info[0] * block_width, block_width)
        coarse = coarse_in[0][:, pl.ds(column, block_width)]
    else:
        sums = coarse_in[0][: NC + TAIL, :] + coarse_in[1][: NC + TAIL, :]
        coarse = sums[:NC] / as_column(sums[NC : NC + 1, :128], 128)[:NC, :1]
    head = own[0, : mid + TAIL, :] + sibling[0, : mid + TAIL, :]
    rest = own[0, mid + TAIL :, :] + sibling[0, mid + TAIL :, :]
    head = head + (first_top[0] + second_top[...])
    rest = rest + (first_low[0] + second_low[...])
    totals, counts_row = jnp.concatenate([head[:mid], rest], 0), head[mid:]
    counts = as_column(counts_row[:1], rows)[:, :1]
    table = (
        lax.broadcasted_iota(jnp.int32, (NC, rows), 0) == owner
    ).astype(jnp.float32)
    lookup = lax.dot_general(
        table,
        coarse,
        (((0,), (0,)), ((), ())),
        precision=HIGHEST,
        preferred_element_type=jnp.float32,
    )
    new = (totals + prior_weight * lookup) / (counts + prior_weight)
    top[...] = new[:mid]
    low[...] = new[mid:]
    prior = jnp.where(info[3] == 0, prior_weight, 0.0)
    part[:NC, :] = prior * coarse + jnp.dot(
        table, counts * new, precision=HIGHEST, preferred_element_type=jnp.float32
    )
    part[NC:, :] = jnp.zeros((TAIL, part.shape[1]), jnp.float32)
    part[NC:, :NC] = prior + lax.dot_general(
        counts_row,
        table,
        (((1,), (1,)), ((), ())),
        precision=HIGHEST,
        preferred_element_type=jnp.float32,
    )


def refine_half(info, own, sibling, incoming, owners, coarse, *, flip):
    _, rows, block_width = own.shape
    mid = (rows - TAIL) // 2
    args = [near_by(value) for value in (own, sibling, *incoming, owners, *coarse)]
    shapes = [(mid, block_width), (mid, block_width), (NC + TAIL, block_width)]
    return pl.pallas_call(
        functools.partial(refine_body, flip=flip),
        out_shape=[pltpu.VMEM(shape, jnp.float32) for shape in shapes],
        in_specs=[SCALARS] + [HERE] * len(args),
        out_specs=[HERE] * len(shapes),
        compiler_params=pltpu.CompilerParams(vmem_limit_bytes=8 * 2**20),
        name="refine_half",
    )(info, *args)


def exchange(held, sibling, folded=None):
    cut = (held.shape[1] - TAIL) // 2 + TAIL
    chunks = slice(0, cut), slice(cut, None)
    first = [held[1::2, rows] + sibling[1::2, rows] for rows in chunks]
    first, folded = lax.optimization_barrier((first, folded))
    first = [swap_first(chunk) for chunk in first]
    if folded is not None:
        folded = swap(folded, lax.axis_size("cen") // 2, "cen")
        first[1], folded = lax.optimization_barrier((first[1], folded))
    second = [
        swap_second(held[2, rows] + sibling[2, rows] + arrived[1])
        for rows, arrived in zip(chunks, first)
    ]
    return [*first, *second], folded


PIECES = ((1, 1), (2, 0), (3, 0), (3, 1), (1, 0), (2, 1), (0, 0), (0, 1))


def gather_half(top, low, later=False):
    x_low = swap(low, ACROSS_X)
    y_top = swap(top, ACROSS_Y)
    again = top, low
    if later:
        x_low, y_top, again = lax.optimization_barrier((x_low, y_top, again))
    x_top = swap(again[0], ACROSS_X)
    y_low = swap(again[1], ACROSS_Y)
    corner_top = swap(y_top, ACROSS_X)
    corner_low = swap(x_low, ACROSS_Y)
    return [x_low, y_top, corner_top, corner_low, x_top, y_low, top, low]


def spread(value):
    corner = swap(value, ACROSS_X | ACROSS_Y)
    return [value, swap(value, ACROSS_X), swap(value, ACROSS_Y), corner]


def over_cen(value, combine, bits=None):
    for bit in range(lax.axis_size("cen").bit_length() - 1) if bits is None else bits:
        value = combine(value, swap(value, 1 << bit, "cen"))
    return value


def fold(first, second):
    cut = NC + TAIL
    return jnp.concatenate(
        [first[:cut] + second[:cut], jnp.minimum(first[cut:], second[cut:])], 0
    )


def place_body(info, *refs, flip):
    own, other = refs[:3], refs[3:6]
    fine_out, coarse_out, fine_held, coarse_held, sems = refs[6:]
    block_width = coarse_out.shape[1] // SLOTS
    rows = fine_out.shape[0] // 2
    mid = rows // 2
    half = info[1] ^ flip

    def column_of(slot, core):
        start = block_of(info, slot, core) * block_width
        return pl.ds(pl.multiple_of(start, block_width), block_width)

    def put(at, *groups):
        for piece, (slot, is_low) in enumerate(PIECES):
            part = slice(is_low * mid, (is_low + 1) * mid)
            fine_held[at, part, column_of(slot, 0)] = groups[piece // SLOTS][piece % SLOTS]

    def send(at, half):
        span = pl.ds(pl.multiple_of(half * rows, rows), rows)
        return pltpu.make_async_copy(fine_held.at[at], fine_out.at[span], sems.at[at])

    put(0, *own[:2])
    send(0, half).start()
    put(1, *other[:2])
    send(1, 1 - half).start()
    parts, others = own[2], other[2]
    weight = parts[0, NC:, :128] + others[0, NC:, :128]
    weight = as_column(weight[:1], 128)[:NC, :1]
    for slot in range(SLOTS):
        total = parts[slot, :NC, :] + others[slot, :NC, :]
        coarse_held[:, column_of(slot, 0)] = total / weight
    send_coarse = pltpu.make_async_copy(coarse_held, coarse_out, sems.at[2])
    send_coarse.start()
    send(0, half).wait()
    send(1, 1 - half).wait()
    send_coarse.wait()


def place(info, own, other, *, flip):
    _, mid, block_width = own[0].shape
    rows, width = 2 * mid, SLOTS * block_width
    args = [near_by(value) for value in (*own, *other)]
    return pl.pallas_call(
        functools.partial(place_body, flip=flip),
        out_shape=[
            jax.ShapeDtypeStruct((2 * rows, width), jnp.float32),
            jax.ShapeDtypeStruct((NC, width), jnp.float32),
        ],
        in_specs=[SCALARS] + [HERE] * len(args),
        out_specs=[AWAY, AWAY],
        scratch_shapes=[
            pltpu.VMEM((2, rows, width), jnp.float32),
            pltpu.VMEM((NC, width), jnp.float32),
            pltpu.SemaphoreType.DMA((3,)),
        ],
        compiler_params=pltpu.CompilerParams(vmem_limit_bytes=8 * 2**20),
        name="place_blocks",
    )(info, *args)


def on_device_paired(points, fine_assign, fine_start, coarse_start, coarse_assign):
    width = points.shape[1]
    local_count = fine_start.shape[0]
    rows = local_count // 2
    block_width = width // SLOTS
    cen, me = lax.axis_index("cen"), lax.axis_index("pts")
    core = me & 1
    info = jnp.stack([me >> 1, core, cen * local_count, cen * 2 + core]).astype(jnp.int32)
    owners = coarse_assign.reshape(2, 1, rows)

    call = functools.partial(run_pass, info, pass_index=0, rows=rows)
    sent, seen, squares, kept = call(points, fine_assign, fine_start, None, None, flip=1)
    sibling = swap(sent, CORE)
    held, seen_first = call(kept, fine_assign, fine_start, squares, seen, flip=0)
    incoming, _ = exchange(held, sibling)
    top, low, part = refine_half(
        info, held, sibling, incoming, owners, [coarse_start], flip=0
    )
    own = gather_half(top, low)
    own, kept = lax.optimization_barrier((own, fetch(points, own[:2])))
    own = jnp.stack(own)
    bits = range(lax.axis_size("cen").bit_length() - 1)
    folded = jnp.concatenate([part, seen_first.reshape(-1, block_width)], 0)
    paired = swap(folded, 1, "cen")
    other = swap(own, CORE)

    call = functools.partial(run_pass, info, pass_index=1, rows=rows)
    sent, seen = call(kept, fine_assign, own, squares, None, flip=0)
    sent, paired = lax.optimization_barrier((sent, paired))
    folded = fold(folded, paired)
    sibling = swap(sent, CORE)
    part = folded[: NC + TAIL]
    others_part = swap(part, CORE)
    held, seen_second = call(kept, fine_assign, other, squares, seen, flip=1)
    held, others_part = lax.optimization_barrier((held, others_part))
    folded = jnp.concatenate([part + others_part, folded[NC + TAIL :]], 0)
    folded = over_cen(folded, fold, bits[1:-1])
    incoming, paired = exchange(held, sibling, folded)
    seen_first = jnp.minimum(folded[NC + TAIL :], paired[NC + TAIL :])

    top, low, part = refine_half(
        info, held, sibling, incoming, owners, [folded, paired], flip=1
    )
    folded = jnp.concatenate([part, seen_second.reshape(-1, block_width)], 0)
    top, low, folded = lax.optimization_barrier((top, low, folded))
    own = gather_half(top, low, True)
    folded = over_cen(folded, fold)
    part, seen_second = folded[: NC + TAIL], folded[NC + TAIL :]
    blocks = [jnp.stack(own[:4]), jnp.stack(own[4:]), jnp.stack(spread(part))]
    fine_now, coarse_now = place(info, blocks, [swap(block, CORE) for block in blocks], flip=1)

    seen = [each.reshape(2, -1) for each in (seen_first, seen_second)]
    gaps = jnp.stack([each[0] - each[1] for each in seen]) / math.sqrt(width)
    return (fine_now, coarse_now, gaps)


def solution(mesh):
    placed = (P("pts", None), P(None, "pts"), P("cen", None), P(), P("cen"))

    def on_device(points, fine_assign, fine_start, coarse_start, coarse_assign):
        count, width = points.shape
        local_count = fine_start.shape[0]
        centres = mesh.shape["cen"]
        fits = (
            mesh.shape["pts"] == 2 * SLOTS
            and centres & (centres - 1) == 0
            and centres >= 4
            and width // SLOTS == local_count // 2
            and (width // SLOTS) % 128 == 0
            and count % 2048 == 0
        )
        plan = on_device_paired if fits else on_device_any
        return plan(points, fine_assign, fine_start, coarse_start, coarse_assign)

    return jax.shard_map(
        on_device,
        mesh=mesh,
        in_specs=placed,
        out_specs=(P("cen", None), P(), P(None, "pts")),
        check_vma=False,
    )
```

```python
import functools
import math

import jax
import jax.numpy as jnp
from jax import lax
from jax.experimental import pallas as pl
from jax.experimental.pallas import tpu as pltpu
from jax.sharding import PartitionSpec as P

NC = 64
PASSES = 2
FAR = 3.0e38

prior_weight = 4.0
HIGHEST = lax.Precision.HIGHEST


def refine(totals, counts, coarse_cols, coarse_table):
    lookup = jnp.dot(coarse_table, coarse_cols, precision=HIGHEST)
    fine_next = (totals + prior_weight * lookup) / (counts + prior_weight)[:, None]
    coarse_part = lax.dot_general(
        coarse_table,
        counts[:, None] * fine_next,
        (((0,), (0,)), ((), ())),
        precision=HIGHEST,
    )
    coarse_weight = jnp.sum(coarse_table * counts[:, None], axis=0)
    return (fine_next, coarse_part, coarse_weight)


def on_device_any(points, fine_assign, fine_start, coarse_start, coarse_assign):
    width = points.shape[1]
    local_count = fine_start.shape[0]
    offset = lax.axis_index("cen") * local_count
    columns = jnp.arange(local_count, dtype=jnp.int32)
    coarse_table = (coarse_assign[:, None] == jnp.arange(NC, dtype=jnp.int32)[None, :]).astype(
        jnp.float32
    )
    point_values = points.astype(jnp.float32)
    squares = jnp.sum(point_values * point_values, axis=1)
    fine_now = fine_start
    coarse_now = coarse_start
    gap_rows = []
    for pass_index in range(PASSES):
        member = (fine_assign[pass_index] - offset)[:, None] == columns[None, :]
        products = jnp.dot(
            points, fine_now.astype(jnp.bfloat16).T, preferred_element_type=jnp.float32
        )
        energy = jnp.sum(fine_now * fine_now, axis=1)[None, :] - 2.0 * products
        picked_local = jnp.sum(jnp.where(member, energy, 0.0), axis=1)
        nearest_local = jnp.min(energy, axis=1)
        picked = lax.psum(picked_local, "cen")
        nearest = lax.pmin(nearest_local, "cen")
        gap_rows.append((picked - nearest) / math.sqrt(width))
        weights = 1.0 / (1.0 + (squares + picked) / width)
        scaled = (point_values * weights[:, None]).astype(jnp.bfloat16)
        partial_sums = lax.dot_general(
            member.astype(jnp.bfloat16),
            scaled,
            (((0,), (0,)), ((), ())),
            preferred_element_type=jnp.float32,
        )
        partial_weights = jnp.sum(jnp.where(member, weights[:, None], 0.0), axis=0)
        share_width = width // lax.axis_size("pts")
        start = lax.axis_index("pts") * share_width
        shares = lax.psum_scatter(partial_sums, "pts", scatter_dimension=1, tiled=True)
        counts = lax.psum(partial_weights, "pts")
        coarse_cols = lax.dynamic_slice_in_dim(coarse_now, start, share_width, 1)
        fine_share, coarse_part, coarse_weight = refine(shares, counts, coarse_cols, coarse_table)
        coarse_sum, coarse_count = lax.psum((coarse_part, coarse_weight), "cen")
        coarse_share = (coarse_sum + prior_weight * coarse_cols) / (coarse_count + prior_weight)[
            :, None
        ]
        fine_now, coarse_now = (
            lax.all_gather(fine_share, "pts", axis=1, tiled=True),
            lax.all_gather(coarse_share, "pts", axis=1, tiled=True),
        )
    return (fine_now, coarse_now, jnp.stack(gap_rows))


CORE, ACROSS_X, ACROSS_Y = 1, 2, 4
SLOTS = 4
TAIL = 8


def swap(value, bit, axis="pts"):
    size = lax.axis_size(axis)
    return lax.ppermute(value, axis, [(i, i ^ bit) for i in range(size)])


def swap_first(value):
    pairs = [(i, i ^ (ACROSS_Y if i & CORE else ACROSS_X)) for i in range(lax.axis_size("pts"))]
    return lax.ppermute(value, "pts", pairs)


def swap_second(value):
    pairs = [(i, i ^ (ACROSS_X if i & CORE else ACROSS_Y)) for i in range(lax.axis_size("pts"))]
    return lax.ppermute(value, "pts", pairs)


def block_of(info, slot, core):
    crossed = (slot >> 1) | ((slot & 1) << 1)
    return info[0] ^ (slot + core * (crossed - slot))


HERE = pl.BlockSpec(memory_space=pltpu.VMEM)
AWAY = pl.BlockSpec(memory_space=pl.ANY)
SCALARS = pl.BlockSpec(memory_space=pltpu.SMEM)


def near_by(value):
    return pltpu.with_memory_space_constraint(value, pltpu.VMEM)


def far_off(value):
    return pltpu.with_memory_space_constraint(value, pltpu.HBM)


def as_column(row, rows):
    return jnp.broadcast_to(row, (128, rows)).T


def pass_body(info, points, assign, fine, *refs, pass_index, flip, stream, chained, tile):
    refs = list(refs)
    initial = pass_index == 0
    first = stream
    squares_in = None if first else refs.pop(0)
    seen_in = refs.pop(0) if chained else None
    payload, seen = refs.pop(0), refs.pop(0)
    squares_out = refs.pop(0) if first else None
    kept = refs.pop(0) if stream else points
    low, norms, tallies, sums, even, odd, scaled = refs[:7]
    chosen_in = refs[7] if stream else assign
    small_sems, point_sems = refs[8:10] if stream else (None, None)
    start = refs[10] if first else None
    rows, width = low.shape
    mid = rows // 2
    block_width = width // SLOTS
    half = info[1] ^ flip
    base = info[2] + half * rows
    tiles = points.shape[0] // tile

    def span(i):
        return pl.ds(pl.multiple_of(i * tile, tile), tile)

    def column_of(slot, core):
        start = block_of(info, slot, core) * block_width
        return pl.ds(pl.multiple_of(start, block_width), block_width)

    def load(i, half):
        part = pl.ds(pl.multiple_of(i * tile + half * (tile // 2), tile // 2), tile // 2)
        return pltpu.make_async_copy(points.at[part], kept.at[part], point_sems.at[2 * i + half])

    if first:
        load_start = pltpu.make_async_copy(
            fine.at[pl.ds(pl.multiple_of(half * rows, rows), rows)], start, small_sems.at[1]
        )
        load_start.start()
    if stream:
        load(0, 0).start()
        load(0, 1).start()
        load_assign = pltpu.make_async_copy(assign, chosen_in, small_sems.at[0])
        load_assign.start()

    if initial:
        if first:
            load_start.wait()
            block = start[...]
        else:
            block = fine[pl.ds(pl.multiple_of(half * rows, rows), rows), :]
        norm = jnp.sum(block * block, axis=1, keepdims=True)
        low[...] = (-2.0 * block).astype(jnp.bfloat16)
    else:
        norm = [jnp.zeros((mid, 1), jnp.float32)] * 2
        for piece, (slot, is_low) in enumerate(PIECES):
            block = fine[piece]
            norm[is_low] = norm[is_low] + jnp.sum(block * block, axis=1, keepdims=True)
            part = slice(is_low * mid, (is_low + 1) * mid)
            low[part, column_of(slot, 0)] = (-2.0 * block).astype(jnp.bfloat16)
        norm = jnp.concatenate(norm, 0)
    norms[...] = jnp.broadcast_to(norm, norms.shape)
    tallies[...] = jnp.zeros_like(tallies)
    sums[...] = jnp.zeros_like(sums)

    def multiply(i, target):
        target[...] = lax.dot_general(
            low[...], kept[span(i), :], (((1,), (1,)), ((), ())), preferred_element_type=jnp.float32
        )

    def collect(i, products):
        energy = products[...] + jnp.concatenate([norms[...]] * (tile // 128), axis=1)
        chosen = chosen_in[pass_index : pass_index + 1, span(i)] - base
        member = lax.broadcasted_iota(jnp.int32, energy.shape, 0) == chosen
        picked = jnp.sum(jnp.where(member, energy, 0.0), axis=0, keepdims=True)
        nearest = jnp.min(energy, axis=0, keepdims=True)
        inside = (chosen >= 0) & (chosen < rows)
        picked_seen = jnp.where(inside, picked, FAR)
        if chained:
            picked_seen = jnp.minimum(picked_seen, seen_in[0:1, span(i)])
            nearest = jnp.minimum(nearest, seen_in[1:2, span(i)])
        seen[0:1, span(i)] = picked_seen
        seen[1:2, span(i)] = nearest
        if first:
            folded = jnp.zeros((tile, 128), jnp.float32)
            for lane in range(0, width, 128):
                values = kept[span(i), lane : lane + 128].astype(jnp.float32)
                folded = folded + values * values
            squares = jnp.sum(folded.T, axis=0, keepdims=True)
            squares_out[0:1, span(i)] = squares
        else:
            squares = squares_in[0:1, span(i)]
        weights = 1.0 / (1.0 + (squares + picked) / width)
        weighted = jnp.where(member, weights, 0.0)
        tally = tallies[...]
        for lane in range(0, tile, 128):
            tally = tally + weighted[:, lane : lane + 128]
        tallies[...] = tally
        factor = as_column(weights, tile)
        for lane in range(0, width, 128):
            values = kept[span(i), lane : lane + 128].astype(jnp.float32)
            scaled[:, lane : lane + 128] = (values * factor).astype(jnp.bfloat16)
        sums[...] += jnp.dot(
            member.astype(jnp.float32).astype(jnp.bfloat16),
            scaled[...],
            preferred_element_type=jnp.float32,
        )

    def arrive(i, more):
        for half in range(2):
            if stream:
                load(i, half).wait()
                if more:
                    load(i + 1, half).start()

    if stream:
        load_assign.wait()
        for half in range(2):
            load(0, half).wait()
            load(1, half).start()
            part = slice(half * (tile // 2), (half + 1) * (tile // 2))
            even[:, part] = lax.dot_general(
                low[...], kept[part, :], (((1,), (1,)), ((), ())), preferred_element_type=jnp.float32
            )
    else:
        multiply(0, even)

    @pl.loop(0, tiles // 2 - 1)
    def _(pair):
        i = 2 * pair
        arrive(i + 1, True)
        multiply(i + 1, odd)
        collect(i, even)
        arrive(i + 2, True)
        multiply(i + 2, even)
        collect(i + 1, odd)

    arrive(tiles - 1, False)
    multiply(tiles - 1, odd)
    collect(tiles - 2, even)
    collect(tiles - 1, odd)

    counts = jnp.broadcast_to(jnp.sum(tallies[...].T, axis=0, keepdims=True), (TAIL, rows))
    for slot in range(SLOTS):
        columns = column_of(slot, info[1] ^ (not chained))
        payload[slot, :mid, :] = sums[:mid, columns]
        payload[slot, mid : mid + TAIL, :] = counts
        payload[slot, mid + TAIL :, :] = sums[mid:, columns]


def fetch_body(points, *refs):
    *_, kept, sems = refs
    share = points.shape[0] // sems.shape[0]
    copies = [
        pltpu.make_async_copy(
            points.at[i * share : (i + 1) * share], kept.at[i * share : (i + 1) * share], sems.at[i]
        )
        for i in range(sems.shape[0])
    ]
    for copy in copies:
        copy.start()
    for copy in copies:
        copy.wait()


def fetch(points, after):
    return pl.pallas_call(
        fetch_body,
        out_shape=pltpu.VMEM(points.shape, points.dtype),
        in_specs=[AWAY] + [HERE] * len(after),
        out_specs=HERE,
        scratch_shapes=[pltpu.SemaphoreType.DMA((8,))],
        compiler_params=pltpu.CompilerParams(vmem_limit_bytes=2 * 2**20),
        cost_estimate=pl.CostEstimate(
            flops=0, bytes_accessed=4 * points.size, transcendentals=0
        ),
        name="fetch_points",
    )(far_off(points), *[near_by(value) for value in after])


def run_pass(info, points, fine_assign, fine, squares, seen, *, pass_index, flip, rows):
    count, width = points.shape
    block_width = width // SLOTS
    initial = pass_index == 0
    chained = seen is not None
    stream = squares is None
    tile = 1024 if stream or count % 4096 else 2048
    if stream:
        in_specs = [AWAY] * 3
        args = [far_off(points), far_off(fine_assign), far_off(fine)]
    else:
        in_specs = [HERE] * 3
        args = [near_by(points), near_by(fine_assign), near_by(fine)]
    for value in (squares, seen):
        if value is not None:
            in_specs.append(HERE)
            args.append(near_by(value))
    shapes = [(SLOTS, rows + TAIL, block_width), (2, count)]
    if squares is None:
        shapes.append((1, count))
    out_shape = [pltpu.VMEM(shape, jnp.float32) for shape in shapes]
    scratch = [
        pltpu.VMEM((rows, width), jnp.bfloat16),
        pltpu.VMEM((rows, 128), jnp.float32),
        pltpu.VMEM((rows, 128), jnp.float32),
        pltpu.VMEM((rows, width), jnp.float32),
        pltpu.VMEM((rows, tile), jnp.float32),
        pltpu.VMEM((rows, tile), jnp.float32),
        pltpu.VMEM((tile, width), jnp.bfloat16),
    ]
    if stream:
        scratch += [
            pltpu.VMEM((PASSES, count), jnp.int32),
            pltpu.SemaphoreType.DMA((2,)),
            pltpu.SemaphoreType.DMA((2 * count // tile,)),
        ]
        if initial:
            scratch.append(pltpu.VMEM((rows, width), jnp.float32))
        out_shape.append(pltpu.VMEM(points.shape, points.dtype))
    body = functools.partial(
        pass_body,
        pass_index=pass_index,
        flip=flip,
        stream=stream,
        chained=chained,
        tile=tile,
    )
    return pl.pallas_call(
        body,
        out_shape=out_shape,
        in_specs=[SCALARS, *in_specs],
        out_specs=[HERE] * len(out_shape),
        scratch_shapes=scratch,
        compiler_params=pltpu.CompilerParams(vmem_limit_bytes=24 * 2**20),
        cost_estimate=pl.CostEstimate(
            flops=4 * rows * count * width, bytes_accessed=2 * count * width, transcendentals=0
        ),
        name=f"energies_and_sums_{pass_index}{int(chained)}",
    )(info, *args)


def one_hot_dot(table, value, dims):
    table = table.astype(jnp.bfloat16)
    total = 0.0
    for _ in range(3):
        term = value.astype(jnp.bfloat16)
        value = value - term.astype(jnp.float32)
        total = total + lax.dot_general(
            table, term, dims, preferred_element_type=jnp.float32
        )
    return total


def refine_body(info, own, sibling, *refs, flip):
    first_top, first_low, second_top, second_low, owners, *coarse_in, top, low, part = refs
    rows = owners.shape[2]
    mid = rows // 2
    block_width = part.shape[1]
    owner = owners[info[1] ^ flip]
    if len(coarse_in) == 1:
        column = pl.multiple_of(info[0] * block_width, block_width)
        coarse = coarse_in[0][:, pl.ds(column, block_width)]
    else:
        sums = coarse_in[0][: NC + TAIL, :] + coarse_in[1][: NC + TAIL, :]
        coarse = sums[:NC] / as_column(sums[NC : NC + 1, :128], 128)[:NC, :1]
    head = own[0, : mid + TAIL, :] + sibling[0, : mid + TAIL, :]
    rest = own[0, mid + TAIL :, :] + sibling[0, mid + TAIL :, :]
    head = head + (first_top[0] + second_top[...])
    rest = rest + (first_low[0] + second_low[...])
    totals, counts_row = jnp.concatenate([head[:mid], rest], 0), head[mid:]
    counts = as_column(counts_row[:1], rows)[:, :1]
    table = (
        lax.broadcasted_iota(jnp.int32, (NC, rows), 0) == owner
    ).astype(jnp.float32)
    lookup = one_hot_dot(table, coarse, (((0,), (0,)), ((), ())))
    new = (totals + prior_weight * lookup) / (counts + prior_weight)
    top[...] = new[:mid]
    low[...] = new[mid:]
    prior = jnp.where(info[3] == 0, prior_weight, 0.0)
    part[:NC, :] = prior * coarse + one_hot_dot(table, counts * new, (((1,), (0,)), ((), ())))
    part[NC:, :] = jnp.zeros((TAIL, part.shape[1]), jnp.float32)
    weight = jnp.sum(table * counts_row[:1], axis=1, keepdims=True)
    weight = jnp.broadcast_to(weight, (NC, 128)).T[:TAIL]
    part[NC:, :NC] = prior + weight


def refine_half(info, own, sibling, incoming, owners, coarse, *, flip):
    _, rows, block_width = own.shape
    mid = (rows - TAIL) // 2
    args = [near_by(value) for value in (own, sibling, *incoming, owners, *coarse)]
    shapes = [(mid, block_width), (mid, block_width), (NC + TAIL, block_width)]
    return pl.pallas_call(
        functools.partial(refine_body, flip=flip),
        out_shape=[pltpu.VMEM(shape, jnp.float32) for shape in shapes],
        in_specs=[SCALARS] + [HERE] * len(args),
        out_specs=[HERE] * len(shapes),
        compiler_params=pltpu.CompilerParams(vmem_limit_bytes=8 * 2**20),
        name="refine_half",
    )(info, *args)


def exchange(held, sibling, folded=None):
    cut = (held.shape[1] - TAIL) // 2 + TAIL
    chunks = slice(0, cut), slice(cut, None)
    first = [held[1::2, rows] + sibling[1::2, rows] for rows in chunks]
    first, folded = lax.optimization_barrier((first, folded))
    first = [swap_first(chunk) for chunk in first]
    if folded is not None:
        folded = swap(folded, lax.axis_size("cen") // 2, "cen")
        first[1], folded = lax.optimization_barrier((first[1], folded))
    second = [
        swap_second(held[2, rows] + sibling[2, rows] + arrived[1])
        for rows, arrived in zip(chunks, first)
    ]
    return [*first, *second], folded


PIECES = ((1, 1), (2, 0), (3, 0), (3, 1), (1, 0), (2, 1), (0, 0), (0, 1))


def gather_half(top, low, later=False):
    x_low = swap(low, ACROSS_X)
    y_top = swap(top, ACROSS_Y)
    again = top, low
    if later:
        x_low, y_top, again = lax.optimization_barrier((x_low, y_top, again))
    x_top = swap(again[0], ACROSS_X)
    y_low = swap(again[1], ACROSS_Y)
    corner_top = swap(y_top, ACROSS_X)
    corner_low = swap(x_low, ACROSS_Y)
    return [x_low, y_top, corner_top, corner_low, x_top, y_low, top, low]


def spread(value):
    corner = swap(value, ACROSS_X | ACROSS_Y)
    return [value, swap(value, ACROSS_X), swap(value, ACROSS_Y), corner]


def over_cen(value, combine, bits=None):
    for bit in range(lax.axis_size("cen").bit_length() - 1) if bits is None else bits:
        value = combine(value, swap(value, 1 << bit, "cen"))
    return value


def fold(first, second):
    cut = NC + TAIL
    return jnp.concatenate(
        [first[:cut] + second[:cut], jnp.minimum(first[cut:], second[cut:])], 0
    )


def place_body(info, *refs, flip):
    own, other = refs[:3], refs[3:6]
    fine_out, coarse_out, fine_held, coarse_held, sems = refs[6:]
    block_width = coarse_out.shape[1] // SLOTS
    rows = fine_out.shape[0] // 2
    mid = rows // 2
    half = info[1] ^ flip

    def column_of(slot, core):
        start = block_of(info, slot, core) * block_width
        return pl.ds(pl.multiple_of(start, block_width), block_width)

    def put(at, *groups):
        for piece, (slot, is_low) in enumerate(PIECES):
            part = slice(is_low * mid, (is_low + 1) * mid)
            fine_held[at, part, column_of(slot, 0)] = groups[piece // SLOTS][piece % SLOTS]

    def send(at, half):
        span = pl.ds(pl.multiple_of(half * rows, rows), rows)
        return pltpu.make_async_copy(fine_held.at[at], fine_out.at[span], sems.at[at])

    put(0, *own[:2])
    send(0, half).start()
    put(1, *other[:2])
    send(1, 1 - half).start()
    parts, others = own[2], other[2]
    weight = parts[0, NC:, :128] + others[0, NC:, :128]
    weight = as_column(weight[:1], 128)[:NC, :1]
    for slot in range(SLOTS):
        total = parts[slot, :NC, :] + others[slot, :NC, :]
        coarse_held[:, column_of(slot, 0)] = total / weight
    send_coarse = pltpu.make_async_copy(coarse_held, coarse_out, sems.at[2])
    send_coarse.start()
    send(0, half).wait()
    send(1, 1 - half).wait()
    send_coarse.wait()


def place(info, own, other, *, flip):
    _, mid, block_width = own[0].shape
    rows, width = 2 * mid, SLOTS * block_width
    args = [near_by(value) for value in (*own, *other)]
    return pl.pallas_call(
        functools.partial(place_body, flip=flip),
        out_shape=[
            jax.ShapeDtypeStruct((2 * rows, width), jnp.float32),
            jax.ShapeDtypeStruct((NC, width), jnp.float32),
        ],
        in_specs=[SCALARS] + [HERE] * len(args),
        out_specs=[AWAY, AWAY],
        scratch_shapes=[
            pltpu.VMEM((2, rows, width), jnp.float32),
            pltpu.VMEM((NC, width), jnp.float32),
            pltpu.SemaphoreType.DMA((3,)),
        ],
        compiler_params=pltpu.CompilerParams(vmem_limit_bytes=8 * 2**20),
        name="place_blocks",
    )(info, *args)


def on_device_paired(points, fine_assign, fine_start, coarse_start, coarse_assign):
    width = points.shape[1]
    local_count = fine_start.shape[0]
    rows = local_count // 2
    block_width = width // SLOTS
    cen, me = lax.axis_index("cen"), lax.axis_index("pts")
    core = me & 1
    info = jnp.stack([me >> 1, core, cen * local_count, cen * 2 + core]).astype(jnp.int32)
    owners = coarse_assign.reshape(2, 1, rows)

    call = functools.partial(run_pass, info, pass_index=0, rows=rows)
    sent, seen, squares, kept = call(points, fine_assign, fine_start, None, None, flip=1)
    sibling = swap(sent, CORE)
    held, seen_first = call(kept, fine_assign, fine_start, squares, seen, flip=0)
    incoming, _ = exchange(held, sibling)
    top, low, part = refine_half(
        info, held, sibling, incoming, owners, [coarse_start], flip=0
    )
    own = gather_half(top, low)
    own, kept = lax.optimization_barrier((own, fetch(points, own[:2])))
    own = jnp.stack(own)
    bits = range(lax.axis_size("cen").bit_length() - 1)
    folded = jnp.concatenate([part, seen_first.reshape(-1, block_width)], 0)
    paired = swap(folded, 1, "cen")
    other = swap(own, CORE)

    call = functools.partial(run_pass, info, pass_index=1, rows=rows)
    sent, seen = call(kept, fine_assign, own, squares, None, flip=0)
    sent, paired = lax.optimization_barrier((sent, paired))
    folded = fold(folded, paired)
    sibling = swap(sent, CORE)
    part = folded[: NC + TAIL]
    others_part = swap(part, CORE)
    held, seen_second = call(kept, fine_assign, other, squares, seen, flip=1)
    held, others_part = lax.optimization_barrier((held, others_part))
    folded = jnp.concatenate([part + others_part, folded[NC + TAIL :]], 0)
    folded = over_cen(folded, fold, bits[1:-1])
    incoming, paired = exchange(held, sibling, folded)
    seen_first = jnp.minimum(folded[NC + TAIL :], paired[NC + TAIL :])

    top, low, part = refine_half(
        info, held, sibling, incoming, owners, [folded, paired], flip=1
    )
    folded = jnp.concatenate([part, seen_second.reshape(-1, block_width)], 0)
    top, low, folded = lax.optimization_barrier((top, low, folded))
    own = gather_half(top, low, True)
    folded = over_cen(folded, fold)
    part, seen_second = folded[: NC + TAIL], folded[NC + TAIL :]
    blocks = [jnp.stack(own[:4]), jnp.stack(own[4:]), jnp.stack(spread(part))]
    fine_now, coarse_now = place(info, blocks, [swap(block, CORE) for block in blocks], flip=1)

    seen = [each.reshape(2, -1) for each in (seen_first, seen_second)]
    gaps = jnp.stack([each[0] - each[1] for each in seen]) / math.sqrt(width)
    return (fine_now, coarse_now, gaps)


def solution(mesh):
    placed = (P("pts", None), P(None, "pts"), P("cen", None), P(), P("cen"))

    def on_device(points, fine_assign, fine_start, coarse_start, coarse_assign):
        count, width = points.shape
        local_count = fine_start.shape[0]
        centres = mesh.shape["cen"]
        fits = (
            mesh.shape["pts"] == 2 * SLOTS
            and centres & (centres - 1) == 0
            and centres >= 4
            and width // SLOTS == local_count // 2
            and (width // SLOTS) % 128 == 0
            and count % 2048 == 0
        )
        plan = on_device_paired if fits else on_device_any
        return plan(points, fine_assign, fine_start, coarse_start, coarse_assign)

    return jax.shard_map(
        on_device,
        mesh=mesh,
        in_specs=placed,
        out_specs=(P("cen", None), P(), P(None, "pts")),
        check_vma=False,
    )
```

```python
import functools
import math

import jax
import jax.numpy as jnp
from jax import lax
from jax.experimental import pallas as pl
from jax.experimental.pallas import tpu as pltpu
from jax.sharding import PartitionSpec as P

NC = 64
PASSES = 2
FAR = 3.0e38

prior_weight = 4.0
HIGHEST = lax.Precision.HIGHEST


def refine(totals, counts, coarse_cols, coarse_table):
    lookup = jnp.dot(coarse_table, coarse_cols, precision=HIGHEST)
    fine_next = (totals + prior_weight * lookup) / (counts + prior_weight)[:, None]
    coarse_part = lax.dot_general(
        coarse_table,
        counts[:, None] * fine_next,
        (((0,), (0,)), ((), ())),
        precision=HIGHEST,
    )
    coarse_weight = jnp.sum(coarse_table * counts[:, None], axis=0)
    return (fine_next, coarse_part, coarse_weight)


def on_device_any(points, fine_assign, fine_start, coarse_start, coarse_assign):
    width = points.shape[1]
    local_count = fine_start.shape[0]
    offset = lax.axis_index("cen") * local_count
    columns = jnp.arange(local_count, dtype=jnp.int32)
    coarse_table = (coarse_assign[:, None] == jnp.arange(NC, dtype=jnp.int32)[None, :]).astype(
        jnp.float32
    )
    point_values = points.astype(jnp.float32)
    squares = jnp.sum(point_values * point_values, axis=1)
    fine_now = fine_start
    coarse_now = coarse_start
    gap_rows = []
    for pass_index in range(PASSES):
        member = (fine_assign[pass_index] - offset)[:, None] == columns[None, :]
        products = jnp.dot(
            points, fine_now.astype(jnp.bfloat16).T, preferred_element_type=jnp.float32
        )
        energy = jnp.sum(fine_now * fine_now, axis=1)[None, :] - 2.0 * products
        picked_local = jnp.sum(jnp.where(member, energy, 0.0), axis=1)
        nearest_local = jnp.min(energy, axis=1)
        picked = lax.psum(picked_local, "cen")
        nearest = lax.pmin(nearest_local, "cen")
        gap_rows.append((picked - nearest) / math.sqrt(width))
        weights = 1.0 / (1.0 + (squares + picked) / width)
        scaled = (point_values * weights[:, None]).astype(jnp.bfloat16)
        partial_sums = lax.dot_general(
            member.astype(jnp.bfloat16),
            scaled,
            (((0,), (0,)), ((), ())),
            preferred_element_type=jnp.float32,
        )
        partial_weights = jnp.sum(jnp.where(member, weights[:, None], 0.0), axis=0)
        share_width = width // lax.axis_size("pts")
        start = lax.axis_index("pts") * share_width
        shares = lax.psum_scatter(partial_sums, "pts", scatter_dimension=1, tiled=True)
        counts = lax.psum(partial_weights, "pts")
        coarse_cols = lax.dynamic_slice_in_dim(coarse_now, start, share_width, 1)
        fine_share, coarse_part, coarse_weight = refine(shares, counts, coarse_cols, coarse_table)
        coarse_sum, coarse_count = lax.psum((coarse_part, coarse_weight), "cen")
        coarse_share = (coarse_sum + prior_weight * coarse_cols) / (coarse_count + prior_weight)[
            :, None
        ]
        fine_now, coarse_now = (
            lax.all_gather(fine_share, "pts", axis=1, tiled=True),
            lax.all_gather(coarse_share, "pts", axis=1, tiled=True),
        )
    return (fine_now, coarse_now, jnp.stack(gap_rows))


CORE, ACROSS_X, ACROSS_Y = 1, 2, 4
SLOTS = 4
TAIL = 8


def swap(value, bit, axis="pts"):
    size = lax.axis_size(axis)
    return lax.ppermute(value, axis, [(i, i ^ bit) for i in range(size)])


def swap_first(value):
    pairs = [(i, i ^ (ACROSS_Y if i & CORE else ACROSS_X)) for i in range(lax.axis_size("pts"))]
    return lax.ppermute(value, "pts", pairs)


def swap_second(value):
    pairs = [(i, i ^ (ACROSS_X if i & CORE else ACROSS_Y)) for i in range(lax.axis_size("pts"))]
    return lax.ppermute(value, "pts", pairs)


def block_of(info, slot, core):
    crossed = (slot >> 1) | ((slot & 1) << 1)
    return info[0] ^ (slot + core * (crossed - slot))


HERE = pl.BlockSpec(memory_space=pltpu.VMEM)
AWAY = pl.BlockSpec(memory_space=pl.ANY)
SCALARS = pl.BlockSpec(memory_space=pltpu.SMEM)


def near_by(value):
    return pltpu.with_memory_space_constraint(value, pltpu.VMEM)


def far_off(value):
    return pltpu.with_memory_space_constraint(value, pltpu.HBM)


def as_column(row, rows):
    return jnp.broadcast_to(row, (128, rows)).T


def pass_body(info, points, assign, fine, *refs, pass_index, flip, stream, chained, tile):
    refs = list(refs)
    initial = pass_index == 0
    first = stream
    squares_in = None if first else refs.pop(0)
    seen_in = refs.pop(0) if chained else None
    payload, seen = refs.pop(0), refs.pop(0)
    squares_out = refs.pop(0) if first else None
    kept = refs.pop(0) if stream else points
    low, norms, tallies, sums, even, odd, scaled = refs[:7]
    chosen_in = refs[7] if stream else assign
    small_sems, point_sems = refs[8:10] if stream else (None, None)
    start = refs[10] if first else None
    rows, width = low.shape
    mid = rows // 2
    block_width = width // SLOTS
    half = info[1] ^ flip
    base = info[2] + half * rows
    tiles = points.shape[0] // tile

    def span(i):
        return pl.ds(pl.multiple_of(i * tile, tile), tile)

    def column_of(slot, core):
        start = block_of(info, slot, core) * block_width
        return pl.ds(pl.multiple_of(start, block_width), block_width)

    def load(i, half):
        part = pl.ds(pl.multiple_of(i * tile + half * (tile // 2), tile // 2), tile // 2)
        return pltpu.make_async_copy(points.at[part], kept.at[part], point_sems.at[2 * i + half])

    if first:
        load_start = pltpu.make_async_copy(
            fine.at[pl.ds(pl.multiple_of(half * rows, rows), rows)], start, small_sems.at[1]
        )
        load_start.start()
    if stream:
        load(0, 0).start()
        load_assign = pltpu.make_async_copy(assign, chosen_in, small_sems.at[0])
        load_assign.start()
        load(0, 1).start()

        @pl.loop(1, tiles)
        def _(i):
            load(i, 0).start()
            load(i, 1).start()

    if initial:
        if first:
            load_start.wait()
            block = start[...]
        else:
            block = fine[pl.ds(pl.multiple_of(half * rows, rows), rows), :]
        norm = jnp.sum(block * block, axis=1, keepdims=True)
        low[...] = (-2.0 * block).astype(jnp.bfloat16)
    else:
        norm = [jnp.zeros((mid, 1), jnp.float32)] * 2
        for piece, (slot, is_low) in enumerate(PIECES):
            block = fine[piece]
            norm[is_low] = norm[is_low] + jnp.sum(block * block, axis=1, keepdims=True)
            part = slice(is_low * mid, (is_low + 1) * mid)
            low[part, column_of(slot, 0)] = (-2.0 * block).astype(jnp.bfloat16)
        norm = jnp.concatenate(norm, 0)
    norms[...] = jnp.broadcast_to(norm, norms.shape)
    tallies[...] = jnp.zeros_like(tallies)
    sums[...] = jnp.zeros_like(sums)

    def multiply(i, target):
        target[...] = lax.dot_general(
            low[...], kept[span(i), :], (((1,), (1,)), ((), ())), preferred_element_type=jnp.float32
        )

    def collect(i, products):
        energy = products[...] + jnp.concatenate([norms[...]] * (tile // 128), axis=1)
        chosen = chosen_in[pass_index : pass_index + 1, span(i)] - base
        member = lax.broadcasted_iota(jnp.int32, energy.shape, 0) == chosen
        picked = jnp.sum(jnp.where(member, energy, 0.0), axis=0, keepdims=True)
        nearest = jnp.min(energy, axis=0, keepdims=True)
        inside = (chosen >= 0) & (chosen < rows)
        picked_seen = jnp.where(inside, picked, FAR)
        if chained:
            picked_seen = jnp.minimum(picked_seen, seen_in[0:1, span(i)])
            nearest = jnp.minimum(nearest, seen_in[1:2, span(i)])
        seen[0:1, span(i)] = picked_seen
        seen[1:2, span(i)] = nearest
        if first:
            folded = jnp.zeros((tile, 128), jnp.float32)
            for lane in range(0, width, 128):
                values = kept[span(i), lane : lane + 128].astype(jnp.float32)
                folded = folded + values * values
            squares = jnp.sum(folded.T, axis=0, keepdims=True)
            squares_out[0:1, span(i)] = squares
        else:
            squares = squares_in[0:1, span(i)]
        weights = 1.0 / (1.0 + (squares + picked) / width)
        weighted = jnp.where(member, weights, 0.0)
        tally = tallies[...]
        for lane in range(0, tile, 128):
            tally = tally + weighted[:, lane : lane + 128]
        tallies[...] = tally
        factor = as_column(weights, tile)
        for lane in range(0, width, 128):
            values = kept[span(i), lane : lane + 128].astype(jnp.float32)
            scaled[:, lane : lane + 128] = (values * factor).astype(jnp.bfloat16)
        sums[...] += jnp.dot(
            member.astype(jnp.float32).astype(jnp.bfloat16),
            scaled[...],
            preferred_element_type=jnp.float32,
        )

    def arrive(i):
        for half in range(2):
            if stream:
                load(i, half).wait()

    if stream:
        load_assign.wait()
    arrive(0)
    multiply(0, even)

    @pl.loop(0, tiles // 2 - 1)
    def _(pair):
        i = 2 * pair
        arrive(i + 1)
        multiply(i + 1, odd)
        collect(i, even)
        arrive(i + 2)
        multiply(i + 2, even)
        collect(i + 1, odd)

    arrive(tiles - 1)
    multiply(tiles - 1, odd)
    collect(tiles - 2, even)
    collect(tiles - 1, odd)

    counts = jnp.broadcast_to(jnp.sum(tallies[...].T, axis=0, keepdims=True), (TAIL, rows))
    for slot in range(SLOTS):
        columns = column_of(slot, info[1] ^ (not chained))
        payload[slot, :mid, :] = sums[:mid, columns]
        payload[slot, mid : mid + TAIL, :] = counts
        payload[slot, mid + TAIL :, :] = sums[mid:, columns]


def fetch_body(points, *refs):
    *_, kept, sems = refs
    share = points.shape[0] // sems.shape[0]
    copies = [
        pltpu.make_async_copy(
            points.at[i * share : (i + 1) * share], kept.at[i * share : (i + 1) * share], sems.at[i]
        )
        for i in range(sems.shape[0])
    ]
    for copy in copies:
        copy.start()
    for copy in copies:
        copy.wait()


def fetch(points, after):
    return pl.pallas_call(
        fetch_body,
        out_shape=pltpu.VMEM(points.shape, points.dtype),
        in_specs=[AWAY] + [HERE] * len(after),
        out_specs=HERE,
        scratch_shapes=[pltpu.SemaphoreType.DMA((8,))],
        compiler_params=pltpu.CompilerParams(vmem_limit_bytes=2 * 2**20),
        cost_estimate=pl.CostEstimate(
            flops=0, bytes_accessed=4 * points.size, transcendentals=0
        ),
        name="fetch_points",
    )(far_off(points), *[near_by(value) for value in after])


def run_pass(info, points, fine_assign, fine, squares, seen, *, pass_index, flip, rows):
    count, width = points.shape
    block_width = width // SLOTS
    initial = pass_index == 0
    chained = seen is not None
    stream = squares is None
    tile = 1024
    if stream:
        in_specs = [AWAY] * 3
        args = [far_off(points), far_off(fine_assign), far_off(fine)]
    else:
        in_specs = [HERE] * 3
        args = [near_by(points), near_by(fine_assign), near_by(fine)]
    for value in (squares, seen):
        if value is not None:
            in_specs.append(HERE)
            args.append(near_by(value))
    shapes = [(SLOTS, rows + TAIL, block_width), (2, count)]
    if squares is None:
        shapes.append((1, count))
    out_shape = [pltpu.VMEM(shape, jnp.float32) for shape in shapes]
    scratch = [
        pltpu.VMEM((rows, width), jnp.bfloat16),
        pltpu.VMEM((rows, 128), jnp.float32),
        pltpu.VMEM((rows, 128), jnp.float32),
        pltpu.VMEM((rows, width), jnp.float32),
        pltpu.VMEM((rows, tile), jnp.float32),
        pltpu.VMEM((rows, tile), jnp.float32),
        pltpu.VMEM((tile, width), jnp.bfloat16),
    ]
    if stream:
        scratch += [
            pltpu.VMEM((PASSES, count), jnp.int32),
            pltpu.SemaphoreType.DMA((2,)),
            pltpu.SemaphoreType.DMA((2 * count // tile,)),
        ]
        if initial:
            scratch.append(pltpu.VMEM((rows, width), jnp.float32))
        out_shape.append(pltpu.VMEM(points.shape, points.dtype))
    body = functools.partial(
        pass_body,
        pass_index=pass_index,
        flip=flip,
        stream=stream,
        chained=chained,
        tile=tile,
    )
    return pl.pallas_call(
        body,
        out_shape=out_shape,
        in_specs=[SCALARS, *in_specs],
        out_specs=[HERE] * len(out_shape),
        scratch_shapes=scratch,
        compiler_params=pltpu.CompilerParams(vmem_limit_bytes=20 * 2**20),
        cost_estimate=pl.CostEstimate(
            flops=4 * rows * count * width, bytes_accessed=2 * count * width, transcendentals=0
        ),
        name=f"energies_and_sums_{pass_index}{int(chained)}",
    )(info, *args)


def one_hot_dot(table, value, dims):
    table = table.astype(jnp.bfloat16)
    total = 0.0
    for _ in range(3):
        term = value.astype(jnp.bfloat16)
        value = value - term.astype(jnp.float32)
        total = total + lax.dot_general(
            table, term, dims, preferred_element_type=jnp.float32
        )
    return total


def refine_body(info, own, sibling, *refs, flip):
    first_top, first_low, second_top, second_low, owners, *coarse_in, top, low, part = refs
    rows = owners.shape[2]
    mid = rows // 2
    block_width = part.shape[1]
    owner = owners[info[1] ^ flip]
    if len(coarse_in) == 1:
        column = pl.multiple_of(info[0] * block_width, block_width)
        coarse = coarse_in[0][:, pl.ds(column, block_width)]
    else:
        sums = coarse_in[0][: NC + TAIL, :] + coarse_in[1][: NC + TAIL, :]
        coarse = sums[:NC] / as_column(sums[NC : NC + 1, :128], 128)[:NC, :1]
    head = own[0, : mid + TAIL, :] + sibling[0, : mid + TAIL, :]
    rest = own[0, mid + TAIL :, :] + sibling[0, mid + TAIL :, :]
    head = head + (first_top[0] + second_top[...])
    rest = rest + (first_low[0] + second_low[...])
    totals, counts_row = jnp.concatenate([head[:mid], rest], 0), head[mid:]
    counts = as_column(counts_row[:1], rows)[:, :1]
    table = (
        lax.broadcasted_iota(jnp.int32, (NC, rows), 0) == owner
    ).astype(jnp.float32)
    lookup = one_hot_dot(table, coarse, (((0,), (0,)), ((), ())))
    new = (totals + prior_weight * lookup) / (counts + prior_weight)
    top[...] = new[:mid]
    low[...] = new[mid:]
    prior = jnp.where(info[3] == 0, prior_weight, 0.0)
    part[:NC, :] = prior * coarse + one_hot_dot(table, counts * new, (((1,), (0,)), ((), ())))
    part[NC:, :] = jnp.zeros((TAIL, part.shape[1]), jnp.float32)
    weight = jnp.sum(table * counts_row[:1], axis=1, keepdims=True)
    weight = jnp.broadcast_to(weight, (NC, 128)).T[:TAIL]
    part[NC:, :NC] = prior + weight


def refine_half(info, own, sibling, incoming, owners, coarse, *, flip):
    _, rows, block_width = own.shape
    mid = (rows - TAIL) // 2
    args = [near_by(value) for value in (own, sibling, *incoming, owners, *coarse)]
    shapes = [(mid, block_width), (mid, block_width), (NC + TAIL, block_width)]
    return pl.pallas_call(
        functools.partial(refine_body, flip=flip),
        out_shape=[pltpu.VMEM(shape, jnp.float32) for shape in shapes],
        in_specs=[SCALARS] + [HERE] * len(args),
        out_specs=[HERE] * len(shapes),
        compiler_params=pltpu.CompilerParams(vmem_limit_bytes=8 * 2**20),
        name="refine_half",
    )(info, *args)


def exchange(held, sibling, folded=None):
    cut = (held.shape[1] - TAIL) // 2 + TAIL
    chunks = slice(0, cut), slice(cut, None)
    first = [held[1::2, rows] + sibling[1::2, rows] for rows in chunks]
    first, folded = lax.optimization_barrier((first, folded))
    first = [swap_first(chunk) for chunk in first]
    if folded is not None:
        folded = swap(folded, lax.axis_size("cen") // 2, "cen")
        first[1], folded = lax.optimization_barrier((first[1], folded))
    second = [
        swap_second(held[2, rows] + sibling[2, rows] + arrived[1])
        for rows, arrived in zip(chunks, first)
    ]
    return [*first, *second], folded


PIECES = ((1, 1), (2, 0), (3, 0), (3, 1), (1, 0), (2, 1), (0, 0), (0, 1))


def gather_half(top, low, later=False):
    x_low = swap(low, ACROSS_X)
    y_top = swap(top, ACROSS_Y)
    again = top, low
    if later:
        x_low, y_top, again = lax.optimization_barrier((x_low, y_top, again))
    x_top = swap(again[0], ACROSS_X)
    y_low = swap(again[1], ACROSS_Y)
    corner_top = swap(y_top, ACROSS_X)
    corner_low = swap(x_low, ACROSS_Y)
    return [x_low, y_top, corner_top, corner_low, x_top, y_low, top, low]


def spread(value):
    corner = swap(value, ACROSS_X | ACROSS_Y)
    return [value, swap(value, ACROSS_X), swap(value, ACROSS_Y), corner]


def over_cen(value, combine, bits=None):
    for bit in range(lax.axis_size("cen").bit_length() - 1) if bits is None else bits:
        value = combine(value, swap(value, 1 << bit, "cen"))
    return value


def fold(first, second):
    cut = NC + TAIL
    return jnp.concatenate(
        [first[:cut] + second[:cut], jnp.minimum(first[cut:], second[cut:])], 0
    )


def place_body(info, *refs, flip):
    own, other = refs[:3], refs[3:6]
    fine_out, coarse_out, fine_held, coarse_held, sems = refs[6:]
    block_width = coarse_out.shape[1] // SLOTS
    rows = fine_out.shape[0] // 2
    mid = rows // 2
    half = info[1] ^ flip

    def column_of(slot, core):
        start = block_of(info, slot, core) * block_width
        return pl.ds(pl.multiple_of(start, block_width), block_width)

    def put(at, *groups):
        for piece, (slot, is_low) in enumerate(PIECES):
            part = slice(is_low * mid, (is_low + 1) * mid)
            fine_held[at, part, column_of(slot, 0)] = groups[piece // SLOTS][piece % SLOTS]

    def send(at, half):
        span = pl.ds(pl.multiple_of(half * rows, rows), rows)
        return pltpu.make_async_copy(fine_held.at[at], fine_out.at[span], sems.at[at])

    put(0, *own[:2])
    send(0, half).start()
    put(1, *other[:2])
    send(1, 1 - half).start()
    parts, others = own[2], other[2]
    weight = parts[0, NC:, :128] + others[0, NC:, :128]
    weight = as_column(weight[:1], 128)[:NC, :1]
    for slot in range(SLOTS):
        total = parts[slot, :NC, :] + others[slot, :NC, :]
        coarse_held[:, column_of(slot, 0)] = total / weight
    send_coarse = pltpu.make_async_copy(coarse_held, coarse_out, sems.at[2])
    send_coarse.start()
    send(0, half).wait()
    send(1, 1 - half).wait()
    send_coarse.wait()


def place(info, own, other, *, flip):
    _, mid, block_width = own[0].shape
    rows, width = 2 * mid, SLOTS * block_width
    args = [near_by(value) for value in (*own, *other)]
    return pl.pallas_call(
        functools.partial(place_body, flip=flip),
        out_shape=[
            jax.ShapeDtypeStruct((2 * rows, width), jnp.float32),
            jax.ShapeDtypeStruct((NC, width), jnp.float32),
        ],
        in_specs=[SCALARS] + [HERE] * len(args),
        out_specs=[AWAY, AWAY],
        scratch_shapes=[
            pltpu.VMEM((2, rows, width), jnp.float32),
            pltpu.VMEM((NC, width), jnp.float32),
            pltpu.SemaphoreType.DMA((3,)),
        ],
        compiler_params=pltpu.CompilerParams(vmem_limit_bytes=8 * 2**20),
        name="place_blocks",
    )(info, *args)


def on_device_paired(points, fine_assign, fine_start, coarse_start, coarse_assign):
    width = points.shape[1]
    local_count = fine_start.shape[0]
    rows = local_count // 2
    block_width = width // SLOTS
    cen, me = lax.axis_index("cen"), lax.axis_index("pts")
    core = me & 1
    info = jnp.stack([me >> 1, core, cen * local_count, cen * 2 + core]).astype(jnp.int32)
    owners = coarse_assign.reshape(2, 1, rows)

    call = functools.partial(run_pass, info, pass_index=0, rows=rows)
    sent, seen, squares, kept = call(points, fine_assign, fine_start, None, None, flip=1)
    sibling = swap(sent, CORE)
    held, seen_first = call(kept, fine_assign, fine_start, squares, seen, flip=0)
    incoming, _ = exchange(held, sibling)
    top, low, part = refine_half(
        info, held, sibling, incoming, owners, [coarse_start], flip=0
    )
    own = gather_half(top, low)
    bits = range(lax.axis_size("cen").bit_length() - 1)
    folded = jnp.concatenate([part, seen_first.reshape(-1, block_width)], 0)
    paired = swap(folded, 1, "cen")
    kept = fetch(points, own[:2])
    own, kept, paired = lax.optimization_barrier((own, kept, paired))
    own = jnp.stack(own)
    other = swap(own, CORE)

    call = functools.partial(run_pass, info, pass_index=1, rows=rows)
    sent, seen = call(kept, fine_assign, own, squares, None, flip=0)
    sent, paired = lax.optimization_barrier((sent, paired))
    folded = fold(folded, paired)
    sibling = swap(sent, CORE)
    part = folded[: NC + TAIL]
    others_part = swap(part, CORE)
    held, seen_second = call(kept, fine_assign, other, squares, seen, flip=1)
    held, others_part = lax.optimization_barrier((held, others_part))
    folded = jnp.concatenate([part + others_part, folded[NC + TAIL :]], 0)
    folded = over_cen(folded, fold, bits[1:-1])
    incoming, paired = exchange(held, sibling, folded)
    seen_first = jnp.minimum(folded[NC + TAIL :], paired[NC + TAIL :])

    top, low, part = refine_half(
        info, held, sibling, incoming, owners, [folded, paired], flip=1
    )
    folded = jnp.concatenate([part, seen_second.reshape(-1, block_width)], 0)
    top, low, folded = lax.optimization_barrier((top, low, folded))
    own = gather_half(top, low, True)
    folded = over_cen(folded, fold)
    part, seen_second = folded[: NC + TAIL], folded[NC + TAIL :]
    blocks = [jnp.stack(own[:4]), jnp.stack(own[4:]), jnp.stack(spread(part))]
    fine_now, coarse_now = place(info, blocks, [swap(block, CORE) for block in blocks], flip=1)

    seen = [each.reshape(2, -1) for each in (seen_first, seen_second)]
    gaps = jnp.stack([each[0] - each[1] for each in seen]) / math.sqrt(width)
    return (fine_now, coarse_now, gaps)


def solution(mesh):
    placed = (P("pts", None), P(None, "pts"), P("cen", None), P(), P("cen"))

    def on_device(points, fine_assign, fine_start, coarse_start, coarse_assign):
        count, width = points.shape
        local_count = fine_start.shape[0]
        centres = mesh.shape["cen"]
        fits = (
            mesh.shape["pts"] == 2 * SLOTS
            and centres & (centres - 1) == 0
            and centres >= 4
            and width // SLOTS == local_count // 2
            and (width // SLOTS) % 128 == 0
            and count % 2048 == 0
        )
        plan = on_device_paired if fits else on_device_any
        return plan(points, fine_assign, fine_start, coarse_start, coarse_assign)

    return jax.shard_map(
        on_device,
        mesh=mesh,
        in_specs=placed,
        out_specs=(P("cen", None), P(), P(None, "pts")),
        check_vma=False,
    )
```

```python
import functools
import math

import jax
import jax.numpy as jnp
from jax import lax
from jax.experimental import pallas as pl
from jax.experimental.pallas import tpu as pltpu
from jax.sharding import PartitionSpec as P

NC = 64
PASSES = 2
FAR = 3.0e38

prior_weight = 4.0
HIGHEST = lax.Precision.HIGHEST


def refine(totals, counts, coarse_cols, coarse_table):
    lookup = jnp.dot(coarse_table, coarse_cols, precision=HIGHEST)
    fine_next = (totals + prior_weight * lookup) / (counts + prior_weight)[:, None]
    coarse_part = lax.dot_general(
        coarse_table,
        counts[:, None] * fine_next,
        (((0,), (0,)), ((), ())),
        precision=HIGHEST,
    )
    coarse_weight = jnp.sum(coarse_table * counts[:, None], axis=0)
    return (fine_next, coarse_part, coarse_weight)


def on_device_any(points, fine_assign, fine_start, coarse_start, coarse_assign):
    width = points.shape[1]
    local_count = fine_start.shape[0]
    offset = lax.axis_index("cen") * local_count
    columns = jnp.arange(local_count, dtype=jnp.int32)
    coarse_table = (coarse_assign[:, None] == jnp.arange(NC, dtype=jnp.int32)[None, :]).astype(
        jnp.float32
    )
    point_values = points.astype(jnp.float32)
    squares = jnp.sum(point_values * point_values, axis=1)
    fine_now = fine_start
    coarse_now = coarse_start
    gap_rows = []
    for pass_index in range(PASSES):
        member = (fine_assign[pass_index] - offset)[:, None] == columns[None, :]
        products = jnp.dot(
            points, fine_now.astype(jnp.bfloat16).T, preferred_element_type=jnp.float32
        )
        energy = jnp.sum(fine_now * fine_now, axis=1)[None, :] - 2.0 * products
        picked_local = jnp.sum(jnp.where(member, energy, 0.0), axis=1)
        nearest_local = jnp.min(energy, axis=1)
        picked = lax.psum(picked_local, "cen")
        nearest = lax.pmin(nearest_local, "cen")
        gap_rows.append((picked - nearest) / math.sqrt(width))
        weights = 1.0 / (1.0 + (squares + picked) / width)
        scaled = (point_values * weights[:, None]).astype(jnp.bfloat16)
        partial_sums = lax.dot_general(
            member.astype(jnp.bfloat16),
            scaled,
            (((0,), (0,)), ((), ())),
            preferred_element_type=jnp.float32,
        )
        partial_weights = jnp.sum(jnp.where(member, weights[:, None], 0.0), axis=0)
        share_width = width // lax.axis_size("pts")
        start = lax.axis_index("pts") * share_width
        shares = lax.psum_scatter(partial_sums, "pts", scatter_dimension=1, tiled=True)
        counts = lax.psum(partial_weights, "pts")
        coarse_cols = lax.dynamic_slice_in_dim(coarse_now, start, share_width, 1)
        fine_share, coarse_part, coarse_weight = refine(shares, counts, coarse_cols, coarse_table)
        coarse_sum, coarse_count = lax.psum((coarse_part, coarse_weight), "cen")
        coarse_share = (coarse_sum + prior_weight * coarse_cols) / (coarse_count + prior_weight)[
            :, None
        ]
        fine_now, coarse_now = (
            lax.all_gather(fine_share, "pts", axis=1, tiled=True),
            lax.all_gather(coarse_share, "pts", axis=1, tiled=True),
        )
    return (fine_now, coarse_now, jnp.stack(gap_rows))


CORE, ACROSS_X, ACROSS_Y = 1, 2, 4
SLOTS = 4
TAIL = 8


def swap(value, bit, axis="pts"):
    size = lax.axis_size(axis)
    return lax.ppermute(value, axis, [(i, i ^ bit) for i in range(size)])


def swap_first(value):
    pairs = [(i, i ^ (ACROSS_Y if i & CORE else ACROSS_X)) for i in range(lax.axis_size("pts"))]
    return lax.ppermute(value, "pts", pairs)


def swap_second(value):
    pairs = [(i, i ^ (ACROSS_X if i & CORE else ACROSS_Y)) for i in range(lax.axis_size("pts"))]
    return lax.ppermute(value, "pts", pairs)


def block_of(info, slot, core):
    crossed = (slot >> 1) | ((slot & 1) << 1)
    return info[0] ^ (slot + core * (crossed - slot))


HERE = pl.BlockSpec(memory_space=pltpu.VMEM)
AWAY = pl.BlockSpec(memory_space=pl.ANY)
SCALARS = pl.BlockSpec(memory_space=pltpu.SMEM)


def near_by(value):
    return pltpu.with_memory_space_constraint(value, pltpu.VMEM)


def far_off(value):
    return pltpu.with_memory_space_constraint(value, pltpu.HBM)


def as_column(row, rows):
    return jnp.broadcast_to(row, (128, rows)).T


def pass_body(info, points, assign, fine, *refs, pass_index, flip, stream, chained, tile):
    refs = list(refs)
    initial = pass_index == 0
    first = stream
    squares_in = None if first else refs.pop(0)
    seen_in = refs.pop(0) if chained else None
    payload, seen = refs.pop(0), refs.pop(0)
    squares_out = refs.pop(0) if first else None
    kept = refs.pop(0) if stream else points
    low, norms, tallies, sums, even, odd, scaled = refs[:7]
    chosen_in = refs[7] if stream else assign
    small_sems, point_sems = refs[8:10] if stream else (None, None)
    start = refs[10] if first else None
    rows, width = low.shape
    mid = rows // 2
    block_width = width // SLOTS
    half = info[1] ^ flip
    base = info[2] + half * rows
    tiles = points.shape[0] // tile

    def span(i):
        return pl.ds(pl.multiple_of(i * tile, tile), tile)

    def column_of(slot, core):
        start = block_of(info, slot, core) * block_width
        return pl.ds(pl.multiple_of(start, block_width), block_width)

    def load(i, half):
        part = pl.ds(pl.multiple_of(i * tile + half * (tile // 2), tile // 2), tile // 2)
        return pltpu.make_async_copy(points.at[part], kept.at[part], point_sems.at[2 * i + half])

    if first:
        load_start = pltpu.make_async_copy(
            fine.at[pl.ds(pl.multiple_of(half * rows, rows), rows)], start, small_sems.at[1]
        )
        load_start.start()
    if stream:
        load(0, 0).start()
        load_assign = pltpu.make_async_copy(assign, chosen_in, small_sems.at[0])
        load_assign.start()
        load(0, 1).start()

        @pl.loop(1, tiles)
        def _(i):
            load(i, 0).start()
            load(i, 1).start()

    if initial:
        if first:
            load_start.wait()
            block = start[...]
        else:
            block = fine[pl.ds(pl.multiple_of(half * rows, rows), rows), :]
        norm = jnp.sum(block * block, axis=1, keepdims=True)
        low[...] = (-2.0 * block).astype(jnp.bfloat16)
    else:
        norm = [jnp.zeros((mid, 1), jnp.float32)] * 2
        for piece, (slot, is_low) in enumerate(PIECES):
            block = fine[piece]
            norm[is_low] = norm[is_low] + jnp.sum(block * block, axis=1, keepdims=True)
            part = slice(is_low * mid, (is_low + 1) * mid)
            low[part, column_of(slot, 0)] = (-2.0 * block).astype(jnp.bfloat16)
        norm = jnp.concatenate(norm, 0)
    norms[...] = jnp.broadcast_to(norm, norms.shape)
    tallies[...] = jnp.zeros_like(tallies)
    sums[...] = jnp.zeros_like(sums)

    def multiply(i, target):
        target[...] = lax.dot_general(
            low[...], kept[span(i), :], (((1,), (1,)), ((), ())), preferred_element_type=jnp.float32
        )

    def collect(i, products):
        energy = products[...] + jnp.concatenate([norms[...]] * (tile // 128), axis=1)
        chosen = chosen_in[pass_index : pass_index + 1, span(i)] - base
        member = lax.broadcasted_iota(jnp.int32, energy.shape, 0) == chosen
        picked = jnp.sum(jnp.where(member, energy, 0.0), axis=0, keepdims=True)
        nearest = jnp.min(energy, axis=0, keepdims=True)
        inside = (chosen >= 0) & (chosen < rows)
        picked_seen = jnp.where(inside, picked, FAR)
        if chained:
            picked_seen = jnp.minimum(picked_seen, seen_in[0:1, span(i)])
            nearest = jnp.minimum(nearest, seen_in[1:2, span(i)])
        seen[0:1, span(i)] = picked_seen
        seen[1:2, span(i)] = nearest
        if first:
            folded = jnp.zeros((tile, 128), jnp.float32)
            for lane in range(0, width, 128):
                values = kept[span(i), lane : lane + 128].astype(jnp.float32)
                folded = folded + values * values
            squares = jnp.sum(folded.T, axis=0, keepdims=True)
            squares_out[0:1, span(i)] = squares
        else:
            squares = squares_in[0:1, span(i)]
        weights = 1.0 / (1.0 + (squares + picked) / width)
        weighted = jnp.where(member, weights, 0.0)
        tally = tallies[...]
        for lane in range(0, tile, 128):
            tally = tally + weighted[:, lane : lane + 128]
        tallies[...] = tally
        factor = as_column(weights, tile)
        for lane in range(0, width, 128):
            values = kept[span(i), lane : lane + 128].astype(jnp.float32)
            scaled[:, lane : lane + 128] = (values * factor).astype(jnp.bfloat16)
        sums[...] += jnp.dot(
            member.astype(jnp.float32).astype(jnp.bfloat16),
            scaled[...],
            preferred_element_type=jnp.float32,
        )

    def arrive(i):
        for half in range(2):
            if stream:
                load(i, half).wait()

    if stream:
        load_assign.wait()
    arrive(0)
    multiply(0, even)

    @pl.loop(0, tiles // 2 - 1)
    def _(pair):
        i = 2 * pair
        arrive(i + 1)
        multiply(i + 1, odd)
        collect(i, even)
        arrive(i + 2)
        multiply(i + 2, even)
        collect(i + 1, odd)

    arrive(tiles - 1)
    multiply(tiles - 1, odd)
    collect(tiles - 2, even)
    collect(tiles - 1, odd)

    counts = jnp.broadcast_to(jnp.sum(tallies[...].T, axis=0, keepdims=True), (TAIL, rows))
    for slot in range(SLOTS):
        columns = column_of(slot, info[1] ^ (not chained))
        payload[slot, :mid, :] = sums[:mid, columns]
        payload[slot, mid : mid + TAIL, :] = counts
        payload[slot, mid + TAIL :, :] = sums[mid:, columns]


def fetch_body(points, *refs):
    *_, kept, sems = refs
    share = points.shape[0] // sems.shape[0]
    copies = [
        pltpu.make_async_copy(
            points.at[i * share : (i + 1) * share], kept.at[i * share : (i + 1) * share], sems.at[i]
        )
        for i in range(sems.shape[0])
    ]
    for copy in copies:
        copy.start()
    for copy in copies:
        copy.wait()


def fetch(points, after):
    return pl.pallas_call(
        fetch_body,
        out_shape=pltpu.VMEM(points.shape, points.dtype),
        in_specs=[AWAY] + [HERE] * len(after),
        out_specs=HERE,
        scratch_shapes=[pltpu.SemaphoreType.DMA((8,))],
        compiler_params=pltpu.CompilerParams(vmem_limit_bytes=2 * 2**20),
        cost_estimate=pl.CostEstimate(
            flops=0, bytes_accessed=4 * points.size, transcendentals=0
        ),
        name="fetch_points",
    )(far_off(points), *[near_by(value) for value in after])


def run_pass(info, points, fine_assign, fine, squares, seen, *, pass_index, flip, rows):
    count, width = points.shape
    block_width = width // SLOTS
    initial = pass_index == 0
    chained = seen is not None
    stream = squares is None
    tile = 1024
    if stream:
        in_specs = [AWAY] * 3
        args = [far_off(points), far_off(fine_assign), far_off(fine)]
    else:
        in_specs = [HERE] * 3
        args = [near_by(points), near_by(fine_assign), near_by(fine)]
    for value in (squares, seen):
        if value is not None:
            in_specs.append(HERE)
            args.append(near_by(value))
    shapes = [(SLOTS, rows + TAIL, block_width), (2, count)]
    if squares is None:
        shapes.append((1, count))
    out_shape = [pltpu.VMEM(shape, jnp.float32) for shape in shapes]
    scratch = [
        pltpu.VMEM((rows, width), jnp.bfloat16),
        pltpu.VMEM((rows, 128), jnp.float32),
        pltpu.VMEM((rows, 128), jnp.float32),
        pltpu.VMEM((rows, width), jnp.float32),
        pltpu.VMEM((rows, tile), jnp.float32),
        pltpu.VMEM((rows, tile), jnp.float32),
        pltpu.VMEM((tile, width), jnp.bfloat16),
    ]
    if stream:
        scratch += [
            pltpu.VMEM((PASSES, count), jnp.int32),
            pltpu.SemaphoreType.DMA((2,)),
            pltpu.SemaphoreType.DMA((2 * count // tile,)),
        ]
        if initial:
            scratch.append(pltpu.VMEM((rows, width), jnp.float32))
        out_shape.append(pltpu.VMEM(points.shape, points.dtype))
    body = functools.partial(
        pass_body,
        pass_index=pass_index,
        flip=flip,
        stream=stream,
        chained=chained,
        tile=tile,
    )
    return pl.pallas_call(
        body,
        out_shape=out_shape,
        in_specs=[SCALARS, *in_specs],
        out_specs=[HERE] * len(out_shape),
        scratch_shapes=scratch,
        compiler_params=pltpu.CompilerParams(vmem_limit_bytes=20 * 2**20),
        cost_estimate=pl.CostEstimate(
            flops=4 * rows * count * width, bytes_accessed=2 * count * width, transcendentals=0
        ),
        name=f"energies_and_sums_{pass_index}{int(chained)}",
    )(info, *args)


def one_hot_dot(table, value, dims):
    table = table.astype(jnp.bfloat16)
    total = 0.0
    for _ in range(3):
        term = value.astype(jnp.bfloat16)
        value = value - term.astype(jnp.float32)
        total = total + lax.dot_general(
            table, term, dims, preferred_element_type=jnp.float32
        )
    return total


def refine_body(info, own, sibling, *refs, flip):
    first_top, first_low, second_top, second_low, owners, *coarse_in, top, low, part = refs
    rows = owners.shape[2]
    mid = rows // 2
    block_width = part.shape[1]
    owner = owners[info[1] ^ flip]
    if len(coarse_in) == 1:
        column = pl.multiple_of(info[0] * block_width, block_width)
        coarse = coarse_in[0][:, pl.ds(column, block_width)]
    else:
        sums = coarse_in[0][: NC + TAIL, :] + coarse_in[1][: NC + TAIL, :]
        coarse = sums[:NC] / as_column(sums[NC : NC + 1, :128], 128)[:NC, :1]
    head = own[0, : mid + TAIL, :] + sibling[0, : mid + TAIL, :]
    rest = own[0, mid + TAIL :, :] + sibling[0, mid + TAIL :, :]
    head = head + (first_top[0] + second_top[...])
    rest = rest + (first_low[0] + second_low[...])
    totals, counts_row = jnp.concatenate([head[:mid], rest], 0), head[mid:]
    counts = as_column(counts_row[:1], rows)[:, :1]
    table = (
        lax.broadcasted_iota(jnp.int32, (NC, rows), 0) == owner
    ).astype(jnp.float32)
    lookup = one_hot_dot(table, coarse, (((0,), (0,)), ((), ())))
    new = (totals + prior_weight * lookup) / (counts + prior_weight)
    top[...] = new[:mid]
    low[...] = new[mid:]
    prior = jnp.where(info[3] == 0, prior_weight, 0.0)
    part[:NC, :] = prior * coarse + one_hot_dot(table, counts * new, (((1,), (0,)), ((), ())))
    part[NC:, :] = jnp.zeros((TAIL, part.shape[1]), jnp.float32)
    weight = jnp.sum(table * counts_row[:1], axis=1, keepdims=True)
    weight = jnp.broadcast_to(weight, (NC, 128)).T[:TAIL]
    part[NC:, :NC] = prior + weight


def refine_half(info, own, sibling, incoming, owners, coarse, *, flip):
    _, rows, block_width = own.shape
    mid = (rows - TAIL) // 2
    args = [near_by(value) for value in (own, sibling, *incoming, owners, *coarse)]
    shapes = [(mid, block_width), (mid, block_width), (NC + TAIL, block_width)]
    return pl.pallas_call(
        functools.partial(refine_body, flip=flip),
        out_shape=[pltpu.VMEM(shape, jnp.float32) for shape in shapes],
        in_specs=[SCALARS] + [HERE] * len(args),
        out_specs=[HERE] * len(shapes),
        compiler_params=pltpu.CompilerParams(vmem_limit_bytes=8 * 2**20),
        name="refine_half",
    )(info, *args)


def exchange(held, sibling, folded=None):
    cut = (held.shape[1] - TAIL) // 2 + TAIL
    chunks = slice(0, cut), slice(cut, None)
    first = [held[1::2, rows] + sibling[1::2, rows] for rows in chunks]
    first, folded = lax.optimization_barrier((first, folded))
    first = [swap_first(chunk) for chunk in first]
    if folded is not None:
        folded = swap(folded, lax.axis_size("cen") // 2, "cen")
        first[1], folded = lax.optimization_barrier((first[1], folded))
    second = [
        swap_second(held[2, rows] + sibling[2, rows] + arrived[1])
        for rows, arrived in zip(chunks, first)
    ]
    return [*first, *second], folded


PIECES = ((1, 1), (2, 0), (3, 0), (3, 1), (1, 0), (2, 1), (0, 0), (0, 1))


def gather_half(top, low, later=False):
    x_low = swap(low, ACROSS_X)
    y_top = swap(top, ACROSS_Y)
    again = top, low
    if later:
        x_low, y_top, again = lax.optimization_barrier((x_low, y_top, again))
    x_top = swap(again[0], ACROSS_X)
    y_low = swap(again[1], ACROSS_Y)
    corner_top = swap(y_top, ACROSS_X)
    corner_low = swap(x_low, ACROSS_Y)
    return [x_low, y_top, corner_top, corner_low, x_top, y_low, top, low]


def spread(value):
    corner = swap(value, ACROSS_X | ACROSS_Y)
    return [value, swap(value, ACROSS_X), swap(value, ACROSS_Y), corner]


def over_cen(value, combine, bits=None):
    for bit in range(lax.axis_size("cen").bit_length() - 1) if bits is None else bits:
        value = combine(value, swap(value, 1 << bit, "cen"))
    return value


def fold(first, second):
    cut = NC + TAIL
    return jnp.concatenate(
        [first[:cut] + second[:cut], jnp.minimum(first[cut:], second[cut:])], 0
    )


def place_body(info, *refs, flip):
    own, other = refs[:3], refs[3:6]
    fine_out, coarse_out, fine_held, coarse_held, sems = refs[6:]
    block_width = coarse_out.shape[1] // SLOTS
    rows = fine_out.shape[0] // 2
    mid = rows // 2
    half = info[1] ^ flip

    def column_of(slot, core):
        start = block_of(info, slot, core) * block_width
        return pl.ds(pl.multiple_of(start, block_width), block_width)

    def put(at, *groups):
        for piece, (slot, is_low) in enumerate(PIECES):
            part = slice(is_low * mid, (is_low + 1) * mid)
            fine_held[at, part, column_of(slot, 0)] = groups[piece // SLOTS][piece % SLOTS]

    def send(at, half):
        span = pl.ds(pl.multiple_of(half * rows, rows), rows)
        return pltpu.make_async_copy(fine_held.at[at], fine_out.at[span], sems.at[at])

    put(0, *own[:2])
    send(0, half).start()
    put(1, *other[:2])
    send(1, 1 - half).start()
    parts, others = own[2], other[2]
    weight = parts[0, NC:, :128] + others[0, NC:, :128]
    weight = as_column(weight[:1], 128)[:NC, :1]
    for slot in range(SLOTS):
        total = parts[slot, :NC, :] + others[slot, :NC, :]
        coarse_held[:, column_of(slot, 0)] = total / weight
    send_coarse = pltpu.make_async_copy(coarse_held, coarse_out, sems.at[2])
    send_coarse.start()
    send(0, half).wait()
    send(1, 1 - half).wait()
    send_coarse.wait()


def place(info, own, other, *, flip):
    _, mid, block_width = own[0].shape
    rows, width = 2 * mid, SLOTS * block_width
    args = [near_by(value) for value in (*own, *other)]
    return pl.pallas_call(
        functools.partial(place_body, flip=flip),
        out_shape=[
            jax.ShapeDtypeStruct((2 * rows, width), jnp.float32),
            jax.ShapeDtypeStruct((NC, width), jnp.float32),
        ],
        in_specs=[SCALARS] + [HERE] * len(args),
        out_specs=[AWAY, AWAY],
        scratch_shapes=[
            pltpu.VMEM((2, rows, width), jnp.float32),
            pltpu.VMEM((NC, width), jnp.float32),
            pltpu.SemaphoreType.DMA((3,)),
        ],
        compiler_params=pltpu.CompilerParams(vmem_limit_bytes=8 * 2**20),
        name="place_blocks",
    )(info, *args)


def on_device_paired(points, fine_assign, fine_start, coarse_start, coarse_assign):
    width = points.shape[1]
    local_count = fine_start.shape[0]
    rows = local_count // 2
    block_width = width // SLOTS
    cen, me = lax.axis_index("cen"), lax.axis_index("pts")
    core = me & 1
    info = jnp.stack([me >> 1, core, cen * local_count, cen * 2 + core]).astype(jnp.int32)
    owners = coarse_assign.reshape(2, 1, rows)

    call = functools.partial(run_pass, info, pass_index=0, rows=rows)
    sent, seen, squares, kept = call(points, fine_assign, fine_start, None, None, flip=1)
    sibling = swap(sent, CORE)
    held, seen_first = call(kept, fine_assign, fine_start, squares, seen, flip=0)
    incoming, _ = exchange(held, sibling)
    top, low, part = refine_half(
        info, held, sibling, incoming, owners, [coarse_start], flip=0
    )
    own = gather_half(top, low)
    bits = range(lax.axis_size("cen").bit_length() - 1)
    folded = jnp.concatenate([part, seen_first.reshape(-1, block_width)], 0)
    paired = swap(folded, 1, "cen")
    kept = fetch(points, own[:2])
    own, kept, paired = lax.optimization_barrier((own, kept, paired))
    own = jnp.stack(own)
    other = swap(own, CORE)

    call = functools.partial(run_pass, info, pass_index=1, rows=rows)
    sent, seen = call(kept, fine_assign, own, squares, None, flip=0)
    sent, paired = lax.optimization_barrier((sent, paired))
    folded = fold(folded, paired)
    sibling = swap(sent, CORE)
    part = folded[: NC + TAIL]
    others_part = swap(part, CORE)
    held, seen_second = call(kept, fine_assign, other, squares, seen, flip=1)
    held, others_part = lax.optimization_barrier((held, others_part))
    folded = jnp.concatenate([part + others_part, folded[NC + TAIL :]], 0)
    folded = over_cen(folded, fold, bits[1:-1])
    incoming, paired = exchange(held, sibling, folded)
    seen_first = jnp.minimum(folded[NC + TAIL :], paired[NC + TAIL :])

    top, low, part = refine_half(
        info, held, sibling, incoming, owners, [folded, paired], flip=1
    )
    folded = jnp.concatenate([part, seen_second.reshape(-1, block_width)], 0)
    top, low, folded = lax.optimization_barrier((top, low, folded))
    own = gather_half(top, low, True)
    folded = over_cen(folded, fold)
    part, seen_second = folded[: NC + TAIL], folded[NC + TAIL :]
    parts = spread(part)
    own[2], own[3], parts[1] = lax.optimization_barrier((own[2], own[3], parts[1]))
    blocks = [jnp.stack(own[:4]), jnp.stack(own[4:]), jnp.stack(parts)]
    fine_now, coarse_now = place(info, blocks, [swap(block, CORE) for block in blocks], flip=1)

    seen = [each.reshape(2, -1) for each in (seen_first, seen_second)]
    gaps = jnp.stack([each[0] - each[1] for each in seen]) / math.sqrt(width)
    return (fine_now, coarse_now, gaps)


def solution(mesh):
    placed = (P("pts", None), P(None, "pts"), P("cen", None), P(), P("cen"))

    def on_device(points, fine_assign, fine_start, coarse_start, coarse_assign):
        count, width = points.shape
        local_count = fine_start.shape[0]
        centres = mesh.shape["cen"]
        fits = (
            mesh.shape["pts"] == 2 * SLOTS
            and centres & (centres - 1) == 0
            and centres >= 4
            and width // SLOTS == local_count // 2
            and (width // SLOTS) % 128 == 0
            and count % 2048 == 0
        )
        plan = on_device_paired if fits else on_device_any
        return plan(points, fine_assign, fine_start, coarse_start, coarse_assign)

    return jax.shard_map(
        on_device,
        mesh=mesh,
        in_specs=placed,
        out_specs=(P("cen", None), P(), P(None, "pts")),
        check_vma=False,
    )
```

```python
import functools
import math

import jax
import jax.numpy as jnp
from jax import lax
from jax.experimental import pallas as pl
from jax.experimental.pallas import tpu as pltpu
from jax.sharding import PartitionSpec as P

NC = 64
PASSES = 2
FAR = 3.0e38

prior_weight = 4.0
HIGHEST = lax.Precision.HIGHEST


def refine(totals, counts, coarse_cols, coarse_table):
    lookup = jnp.dot(coarse_table, coarse_cols, precision=HIGHEST)
    fine_next = (totals + prior_weight * lookup) / (counts + prior_weight)[:, None]
    coarse_part = lax.dot_general(
        coarse_table,
        counts[:, None] * fine_next,
        (((0,), (0,)), ((), ())),
        precision=HIGHEST,
    )
    coarse_weight = jnp.sum(coarse_table * counts[:, None], axis=0)
    return (fine_next, coarse_part, coarse_weight)


def on_device_any(points, fine_assign, fine_start, coarse_start, coarse_assign):
    width = points.shape[1]
    local_count = fine_start.shape[0]
    offset = lax.axis_index("cen") * local_count
    columns = jnp.arange(local_count, dtype=jnp.int32)
    coarse_table = (coarse_assign[:, None] == jnp.arange(NC, dtype=jnp.int32)[None, :]).astype(
        jnp.float32
    )
    point_values = points.astype(jnp.float32)
    squares = jnp.sum(point_values * point_values, axis=1)
    fine_now = fine_start
    coarse_now = coarse_start
    gap_rows = []
    for pass_index in range(PASSES):
        member = (fine_assign[pass_index] - offset)[:, None] == columns[None, :]
        products = jnp.dot(
            points, fine_now.astype(jnp.bfloat16).T, preferred_element_type=jnp.float32
        )
        energy = jnp.sum(fine_now * fine_now, axis=1)[None, :] - 2.0 * products
        picked_local = jnp.sum(jnp.where(member, energy, 0.0), axis=1)
        nearest_local = jnp.min(energy, axis=1)
        picked = lax.psum(picked_local, "cen")
        nearest = lax.pmin(nearest_local, "cen")
        gap_rows.append((picked - nearest) / math.sqrt(width))
        weights = 1.0 / (1.0 + (squares + picked) / width)
        scaled = (point_values * weights[:, None]).astype(jnp.bfloat16)
        partial_sums = lax.dot_general(
            member.astype(jnp.bfloat16),
            scaled,
            (((0,), (0,)), ((), ())),
            preferred_element_type=jnp.float32,
        )
        partial_weights = jnp.sum(jnp.where(member, weights[:, None], 0.0), axis=0)
        share_width = width // lax.axis_size("pts")
        start = lax.axis_index("pts") * share_width
        shares = lax.psum_scatter(partial_sums, "pts", scatter_dimension=1, tiled=True)
        counts = lax.psum(partial_weights, "pts")
        coarse_cols = lax.dynamic_slice_in_dim(coarse_now, start, share_width, 1)
        fine_share, coarse_part, coarse_weight = refine(shares, counts, coarse_cols, coarse_table)
        coarse_sum, coarse_count = lax.psum((coarse_part, coarse_weight), "cen")
        coarse_share = (coarse_sum + prior_weight * coarse_cols) / (coarse_count + prior_weight)[
            :, None
        ]
        fine_now, coarse_now = (
            lax.all_gather(fine_share, "pts", axis=1, tiled=True),
            lax.all_gather(coarse_share, "pts", axis=1, tiled=True),
        )
    return (fine_now, coarse_now, jnp.stack(gap_rows))


CORE, ACROSS_X, ACROSS_Y = 1, 2, 4
SLOTS = 4
TAIL = 8


def swap(value, bit, axis="pts"):
    size = lax.axis_size(axis)
    return lax.ppermute(value, axis, [(i, i ^ bit) for i in range(size)])


def swap_first(value):
    pairs = [(i, i ^ (ACROSS_Y if i & CORE else ACROSS_X)) for i in range(lax.axis_size("pts"))]
    return lax.ppermute(value, "pts", pairs)


def swap_second(value):
    pairs = [(i, i ^ (ACROSS_X if i & CORE else ACROSS_Y)) for i in range(lax.axis_size("pts"))]
    return lax.ppermute(value, "pts", pairs)


def block_of(info, slot, core):
    crossed = (slot >> 1) | ((slot & 1) << 1)
    return info[0] ^ (slot + core * (crossed - slot))


HERE = pl.BlockSpec(memory_space=pltpu.VMEM)
AWAY = pl.BlockSpec(memory_space=pl.ANY)
SCALARS = pl.BlockSpec(memory_space=pltpu.SMEM)


def near_by(value):
    return pltpu.with_memory_space_constraint(value, pltpu.VMEM)


def far_off(value):
    return pltpu.with_memory_space_constraint(value, pltpu.HBM)


def as_column(row, rows):
    return jnp.broadcast_to(row, (128, rows)).T


def pass_body(info, points, assign, fine, *refs, pass_index, flip, stream, chained, tile):
    refs = list(refs)
    initial = pass_index == 0
    first = stream
    squares_in = None if first else refs.pop(0)
    seen_in = refs.pop(0) if chained else None
    payload, seen = refs.pop(0), refs.pop(0)
    squares_out = refs.pop(0) if first else None
    kept = refs.pop(0) if stream else points
    low, norms, tallies, sums, even, odd, scaled = refs[:7]
    chosen_in = refs[7] if stream else assign
    small_sems, point_sems = refs[8:10] if stream else (None, None)
    start = refs[10] if first else None
    rows, width = low.shape
    mid = rows // 2
    block_width = width // SLOTS
    half = info[1] ^ flip
    base = info[2] + half * rows
    tiles = points.shape[0] // tile

    def span(i):
        return pl.ds(pl.multiple_of(i * tile, tile), tile)

    def column_of(slot, core):
        start = block_of(info, slot, core) * block_width
        return pl.ds(pl.multiple_of(start, block_width), block_width)

    def load(i, half):
        part = pl.ds(pl.multiple_of(i * tile + half * (tile // 2), tile // 2), tile // 2)
        return pltpu.make_async_copy(points.at[part], kept.at[part], point_sems.at[2 * i + half])

    if first:
        load_start = pltpu.make_async_copy(
            fine.at[pl.ds(pl.multiple_of(half * rows, rows), rows)], start, small_sems.at[1]
        )
        load_start.start()
    if stream:
        load(0, 0).start()
        load_assign = pltpu.make_async_copy(assign, chosen_in, small_sems.at[0])
        load_assign.start()
        load(0, 1).start()

        @pl.loop(1, tiles)
        def _(i):
            load(i, 0).start()
            load(i, 1).start()

    if initial:
        if first:
            load_start.wait()
            block = start[...]
        else:
            block = fine[pl.ds(pl.multiple_of(half * rows, rows), rows), :]
        norm = jnp.sum(block * block, axis=1, keepdims=True)
        low[...] = (-2.0 * block).astype(jnp.bfloat16)
    else:
        norm = [jnp.zeros((mid, 1), jnp.float32)] * 2
        for piece, (slot, is_low) in enumerate(PIECES):
            block = fine[piece]
            norm[is_low] = norm[is_low] + jnp.sum(block * block, axis=1, keepdims=True)
            part = slice(is_low * mid, (is_low + 1) * mid)
            low[part, column_of(slot, 0)] = (-2.0 * block).astype(jnp.bfloat16)
        norm = jnp.concatenate(norm, 0)
    norms[...] = jnp.broadcast_to(norm, norms.shape)
    tallies[...] = jnp.zeros_like(tallies)
    sums[...] = jnp.zeros_like(sums)

    def multiply(i, target):
        target[...] = lax.dot_general(
            low[...], kept[span(i), :], (((1,), (1,)), ((), ())), preferred_element_type=jnp.float32
        )

    def collect(i, products):
        energy = products[...] + jnp.concatenate([norms[...]] * (tile // 128), axis=1)
        chosen = chosen_in[pass_index : pass_index + 1, span(i)] - base
        member = lax.broadcasted_iota(jnp.int32, energy.shape, 0) == chosen
        picked = jnp.sum(jnp.where(member, energy, 0.0), axis=0, keepdims=True)
        nearest = jnp.min(energy, axis=0, keepdims=True)
        inside = (chosen >= 0) & (chosen < rows)
        picked_seen = jnp.where(inside, picked, FAR)
        if chained:
            picked_seen = jnp.minimum(picked_seen, seen_in[0:1, span(i)])
            nearest = jnp.minimum(nearest, seen_in[1:2, span(i)])
        seen[0:1, span(i)] = picked_seen
        seen[1:2, span(i)] = nearest
        if first:
            folded = jnp.zeros((tile, 128), jnp.float32)
            for lane in range(0, width, 128):
                values = kept[span(i), lane : lane + 128].astype(jnp.float32)
                folded = folded + values * values
            squares = jnp.sum(folded.T, axis=0, keepdims=True)
            squares_out[0:1, span(i)] = squares
        else:
            squares = squares_in[0:1, span(i)]
        weights = 1.0 / (1.0 + (squares + picked) / width)
        weighted = jnp.where(member, weights, 0.0)
        tally = tallies[...]
        for lane in range(0, tile, 128):
            tally = tally + weighted[:, lane : lane + 128]
        tallies[...] = tally
        factor = as_column(weights, tile)
        for lane in range(0, width, 128):
            values = kept[span(i), lane : lane + 128].astype(jnp.float32)
            scaled[:, lane : lane + 128] = (values * factor).astype(jnp.bfloat16)
        sums[...] += jnp.dot(
            member.astype(jnp.float32).astype(jnp.bfloat16),
            scaled[...],
            preferred_element_type=jnp.float32,
        )

    def arrive(i):
        for half in range(2):
            if stream:
                load(i, half).wait()

    if stream:
        load_assign.wait()
    arrive(0)
    multiply(0, even)

    @pl.loop(0, tiles // 2 - 1)
    def _(pair):
        i = 2 * pair
        arrive(i + 1)
        multiply(i + 1, odd)
        collect(i, even)
        arrive(i + 2)
        multiply(i + 2, even)
        collect(i + 1, odd)

    arrive(tiles - 1)
    multiply(tiles - 1, odd)
    collect(tiles - 2, even)
    collect(tiles - 1, odd)

    counts = jnp.broadcast_to(jnp.sum(tallies[...].T, axis=0, keepdims=True), (TAIL, rows))
    for slot in range(SLOTS):
        columns = column_of(slot, info[1] ^ (not chained))
        payload[slot, :mid, :] = sums[:mid, columns]
        payload[slot, mid : mid + TAIL, :] = counts
        payload[slot, mid + TAIL :, :] = sums[mid:, columns]


def fetch_body(points, *refs):
    *_, kept, sems = refs
    share = points.shape[0] // sems.shape[0]
    copies = [
        pltpu.make_async_copy(
            points.at[i * share : (i + 1) * share], kept.at[i * share : (i + 1) * share], sems.at[i]
        )
        for i in range(sems.shape[0])
    ]
    for copy in copies:
        copy.start()
    for copy in copies:
        copy.wait()


def fetch(points, after):
    return pl.pallas_call(
        fetch_body,
        out_shape=pltpu.VMEM(points.shape, points.dtype),
        in_specs=[AWAY] + [HERE] * len(after),
        out_specs=HERE,
        scratch_shapes=[pltpu.SemaphoreType.DMA((8,))],
        compiler_params=pltpu.CompilerParams(vmem_limit_bytes=2 * 2**20),
        cost_estimate=pl.CostEstimate(
            flops=0, bytes_accessed=4 * points.size, transcendentals=0
        ),
        name="fetch_points",
    )(far_off(points), *[near_by(value) for value in after])


def run_pass(info, points, fine_assign, fine, squares, seen, *, pass_index, flip, rows):
    count, width = points.shape
    block_width = width // SLOTS
    initial = pass_index == 0
    chained = seen is not None
    stream = squares is None
    tile = 1024
    if stream:
        in_specs = [AWAY] * 3
        args = [far_off(points), far_off(fine_assign), far_off(fine)]
    else:
        in_specs = [HERE] * 3
        args = [near_by(points), near_by(fine_assign), near_by(fine)]
    for value in (squares, seen):
        if value is not None:
            in_specs.append(HERE)
            args.append(near_by(value))
    shapes = [(SLOTS, rows + TAIL, block_width), (2, count)]
    if squares is None:
        shapes.append((1, count))
    out_shape = [pltpu.VMEM(shape, jnp.float32) for shape in shapes]
    scratch = [
        pltpu.VMEM((rows, width), jnp.bfloat16),
        pltpu.VMEM((rows, 128), jnp.float32),
        pltpu.VMEM((rows, 128), jnp.float32),
        pltpu.VMEM((rows, width), jnp.float32),
        pltpu.VMEM((rows, tile), jnp.float32),
        pltpu.VMEM((rows, tile), jnp.float32),
        pltpu.VMEM((tile, width), jnp.bfloat16),
    ]
    if stream:
        scratch += [
            pltpu.VMEM((PASSES, count), jnp.int32),
            pltpu.SemaphoreType.DMA((2,)),
            pltpu.SemaphoreType.DMA((2 * count // tile,)),
        ]
        if initial:
            scratch.append(pltpu.VMEM((rows, width), jnp.float32))
        out_shape.append(pltpu.VMEM(points.shape, points.dtype))
    body = functools.partial(
        pass_body,
        pass_index=pass_index,
        flip=flip,
        stream=stream,
        chained=chained,
        tile=tile,
    )
    return pl.pallas_call(
        body,
        out_shape=out_shape,
        in_specs=[SCALARS, *in_specs],
        out_specs=[HERE] * len(out_shape),
        scratch_shapes=scratch,
        compiler_params=pltpu.CompilerParams(vmem_limit_bytes=20 * 2**20),
        cost_estimate=pl.CostEstimate(
            flops=4 * rows * count * width, bytes_accessed=2 * count * width, transcendentals=0
        ),
        name=f"energies_and_sums_{pass_index}{int(chained)}",
    )(info, *args)


def one_hot_dot(table, value, dims):
    table = table.astype(jnp.bfloat16)
    total = 0.0
    for _ in range(3):
        term = value.astype(jnp.bfloat16)
        value = value - term.astype(jnp.float32)
        total = total + lax.dot_general(
            table, term, dims, preferred_element_type=jnp.float32
        )
    return total


def refine_body(info, own, sibling, *refs, flip):
    first_top, first_low, second_top, second_low, owners, *coarse_in, top, low, part = refs
    rows = owners.shape[2]
    mid = rows // 2
    block_width = part.shape[1]
    owner = owners[info[1] ^ flip]
    if len(coarse_in) == 1:
        column = pl.multiple_of(info[0] * block_width, block_width)
        coarse = coarse_in[0][:, pl.ds(column, block_width)]
    else:
        sums = coarse_in[0][: NC + TAIL, :] + coarse_in[1][: NC + TAIL, :]
        coarse = sums[:NC] / as_column(sums[NC : NC + 1, :128], 128)[:NC, :1]
    head = own[0, : mid + TAIL, :] + sibling[0, : mid + TAIL, :]
    rest = own[0, mid + TAIL :, :] + sibling[0, mid + TAIL :, :]
    head = head + (first_top[0] + second_top[...])
    rest = rest + (first_low[0] + second_low[...])
    totals, counts_row = jnp.concatenate([head[:mid], rest], 0), head[mid:]
    counts = as_column(counts_row[:1], rows)[:, :1]
    table = (
        lax.broadcasted_iota(jnp.int32, (NC, rows), 0) == owner
    ).astype(jnp.float32)
    lookup = one_hot_dot(table, coarse, (((0,), (0,)), ((), ())))
    new = (totals + prior_weight * lookup) / (counts + prior_weight)
    top[...] = new[:mid]
    low[...] = new[mid:]
    prior = jnp.where(info[3] == 0, prior_weight, 0.0)
    part[:NC, :] = prior * coarse + one_hot_dot(table, counts * new, (((1,), (0,)), ((), ())))
    part[NC:, :] = jnp.zeros((TAIL, part.shape[1]), jnp.float32)
    weight = jnp.sum(table * counts_row[:1], axis=1, keepdims=True)
    weight = jnp.broadcast_to(weight, (NC, 128)).T[:TAIL]
    part[NC:, :NC] = prior + weight


def refine_half(info, own, sibling, incoming, owners, coarse, *, flip):
    _, rows, block_width = own.shape
    mid = (rows - TAIL) // 2
    args = [near_by(value) for value in (own, sibling, *incoming, owners, *coarse)]
    shapes = [(mid, block_width), (mid, block_width), (NC + TAIL, block_width)]
    return pl.pallas_call(
        functools.partial(refine_body, flip=flip),
        out_shape=[pltpu.VMEM(shape, jnp.float32) for shape in shapes],
        in_specs=[SCALARS] + [HERE] * len(args),
        out_specs=[HERE] * len(shapes),
        compiler_params=pltpu.CompilerParams(vmem_limit_bytes=8 * 2**20),
        name="refine_half",
    )(info, *args)


def exchange(held, sibling, folded=None):
    cut = (held.shape[1] - TAIL) // 2 + TAIL
    chunks = slice(0, cut), slice(cut, None)
    first = [held[1::2, rows] + sibling[1::2, rows] for rows in chunks]
    first, folded = lax.optimization_barrier((first, folded))
    first = [swap_first(chunk) for chunk in first]
    if folded is not None:
        folded = swap(folded, lax.axis_size("cen") // 2, "cen")
    second = [
        held[2, rows] + sibling[2, rows] + arrived[1] for rows, arrived in zip(chunks, first)
    ]
    if folded is not None:
        second[1], folded = lax.optimization_barrier((second[1], folded))
    second = [swap_second(chunk) for chunk in second]
    return [*first, *second], folded


PIECES = ((1, 1), (2, 0), (3, 0), (3, 1), (1, 0), (2, 1), (0, 0), (0, 1))


def gather_half(top, low, later=False):
    x_low = swap(low, ACROSS_X)
    y_top = swap(top, ACROSS_Y)
    again = top, low
    if later:
        x_low, y_top, again = lax.optimization_barrier((x_low, y_top, again))
    x_top = swap(again[0], ACROSS_X)
    y_low = swap(again[1], ACROSS_Y)
    corner_top = swap(y_top, ACROSS_X)
    corner_low = swap(x_low, ACROSS_Y)
    return [x_low, y_top, corner_top, corner_low, x_top, y_low, top, low]


def spread(value):
    corner = swap(value, ACROSS_X | ACROSS_Y)
    return [value, swap(value, ACROSS_X), swap(value, ACROSS_Y), corner]


def over_cen(value, combine, bits=None):
    for bit in range(lax.axis_size("cen").bit_length() - 1) if bits is None else bits:
        value = combine(value, swap(value, 1 << bit, "cen"))
    return value


def fold(first, second):
    cut = NC + TAIL
    return jnp.concatenate(
        [first[:cut] + second[:cut], jnp.minimum(first[cut:], second[cut:])], 0
    )


def place_body(info, *refs, flip):
    own, other = refs[:3], refs[3:6]
    fine_out, coarse_out, fine_held, coarse_held, sems = refs[6:]
    block_width = coarse_out.shape[1] // SLOTS
    rows = fine_out.shape[0] // 2
    mid = rows // 2
    half = info[1] ^ flip

    def column_of(slot, core):
        start = block_of(info, slot, core) * block_width
        return pl.ds(pl.multiple_of(start, block_width), block_width)

    def put(at, *groups):
        for piece, (slot, is_low) in enumerate(PIECES):
            part = slice(is_low * mid, (is_low + 1) * mid)
            fine_held[at, part, column_of(slot, 0)] = groups[piece // SLOTS][piece % SLOTS]

    def send(at, half):
        span = pl.ds(pl.multiple_of(half * rows, rows), rows)
        return pltpu.make_async_copy(fine_held.at[at], fine_out.at[span], sems.at[at])

    put(0, *own[:2])
    send(0, half).start()
    put(1, *other[:2])
    send(1, 1 - half).start()
    parts, others = own[2], other[2]
    weight = parts[0, NC:, :128] + others[0, NC:, :128]
    weight = as_column(weight[:1], 128)[:NC, :1]
    for slot in range(SLOTS):
        total = parts[slot, :NC, :] + others[slot, :NC, :]
        coarse_held[:, column_of(slot, 0)] = total / weight
    send_coarse = pltpu.make_async_copy(coarse_held, coarse_out, sems.at[2])
    send_coarse.start()
    send(0, half).wait()
    send(1, 1 - half).wait()
    send_coarse.wait()


def place(info, own, other, *, flip):
    _, mid, block_width = own[0].shape
    rows, width = 2 * mid, SLOTS * block_width
    args = [near_by(value) for value in (*own, *other)]
    return pl.pallas_call(
        functools.partial(place_body, flip=flip),
        out_shape=[
            jax.ShapeDtypeStruct((2 * rows, width), jnp.float32),
            jax.ShapeDtypeStruct((NC, width), jnp.float32),
        ],
        in_specs=[SCALARS] + [HERE] * len(args),
        out_specs=[AWAY, AWAY],
        scratch_shapes=[
            pltpu.VMEM((2, rows, width), jnp.float32),
            pltpu.VMEM((NC, width), jnp.float32),
            pltpu.SemaphoreType.DMA((3,)),
        ],
        compiler_params=pltpu.CompilerParams(vmem_limit_bytes=8 * 2**20),
        name="place_blocks",
    )(info, *args)


def on_device_paired(points, fine_assign, fine_start, coarse_start, coarse_assign):
    width = points.shape[1]
    local_count = fine_start.shape[0]
    rows = local_count // 2
    block_width = width // SLOTS
    cen, me = lax.axis_index("cen"), lax.axis_index("pts")
    core = me & 1
    info = jnp.stack([me >> 1, core, cen * local_count, cen * 2 + core]).astype(jnp.int32)
    owners = coarse_assign.reshape(2, 1, rows)

    call = functools.partial(run_pass, info, pass_index=0, rows=rows)
    sent, seen, squares, kept = call(points, fine_assign, fine_start, None, None, flip=1)
    sibling = swap(sent, CORE)
    held, seen_first = call(kept, fine_assign, fine_start, squares, seen, flip=0)
    incoming, _ = exchange(held, sibling)
    top, low, part = refine_half(
        info, held, sibling, incoming, owners, [coarse_start], flip=0
    )
    own = gather_half(top, low)
    bits = range(lax.axis_size("cen").bit_length() - 1)
    folded = jnp.concatenate([part, seen_first.reshape(-1, block_width)], 0)
    paired = swap(folded, 1, "cen")
    kept = fetch(points, own[:2])
    own, kept, paired = lax.optimization_barrier((own, kept, paired))
    own = jnp.stack(own)
    other = swap(own, CORE)

    call = functools.partial(run_pass, info, pass_index=1, rows=rows)
    sent, seen = call(kept, fine_assign, own, squares, None, flip=0)
    sent, paired = lax.optimization_barrier((sent, paired))
    folded = fold(folded, paired)
    sibling = swap(sent, CORE)
    part = folded[: NC + TAIL]
    others_part = swap(part, CORE)
    held, seen_second = call(kept, fine_assign, other, squares, seen, flip=1)
    held, others_part = lax.optimization_barrier((held, others_part))
    folded = jnp.concatenate([part + others_part, folded[NC + TAIL :]], 0)
    folded = over_cen(folded, fold, bits[1:-1])
    incoming, paired = exchange(held, sibling, folded)
    seen_first = jnp.minimum(folded[NC + TAIL :], paired[NC + TAIL :])

    top, low, part = refine_half(
        info, held, sibling, incoming, owners, [folded, paired], flip=1
    )
    folded = jnp.concatenate([part, seen_second.reshape(-1, block_width)], 0)
    top, low, folded = lax.optimization_barrier((top, low, folded))
    own = gather_half(top, low, True)
    folded = over_cen(folded, fold)
    part, seen_second = folded[: NC + TAIL], folded[NC + TAIL :]
    parts = spread(part)
    own[2], own[3], parts[1] = lax.optimization_barrier((own[2], own[3], parts[1]))
    blocks = [jnp.stack(own[:4]), jnp.stack(own[4:]), jnp.stack(parts)]
    fine_now, coarse_now = place(info, blocks, [swap(block, CORE) for block in blocks], flip=1)

    seen = [each.reshape(2, -1) for each in (seen_first, seen_second)]
    gaps = jnp.stack([each[0] - each[1] for each in seen]) / math.sqrt(width)
    return (fine_now, coarse_now, gaps)


def solution(mesh):
    placed = (P("pts", None), P(None, "pts"), P("cen", None), P(), P("cen"))

    def on_device(points, fine_assign, fine_start, coarse_start, coarse_assign):
        count, width = points.shape
        local_count = fine_start.shape[0]
        centres = mesh.shape["cen"]
        fits = (
            mesh.shape["pts"] == 2 * SLOTS
            and centres & (centres - 1) == 0
            and centres >= 4
            and width // SLOTS == local_count // 2
            and (width // SLOTS) % 128 == 0
            and count % 2048 == 0
        )
        plan = on_device_paired if fits else on_device_any
        return plan(points, fine_assign, fine_start, coarse_start, coarse_assign)

    return jax.shard_map(
        on_device,
        mesh=mesh,
        in_specs=placed,
        out_specs=(P("cen", None), P(), P(None, "pts")),
        check_vma=False,
    )
```

```python
import functools
import math

import jax
import jax.numpy as jnp
from jax import lax
from jax.experimental import pallas as pl
from jax.experimental.pallas import tpu as pltpu
from jax.sharding import PartitionSpec as P

NC = 64
PASSES = 2
FAR = 3.0e38

prior_weight = 4.0
HIGHEST = lax.Precision.HIGHEST


def refine(totals, counts, coarse_cols, coarse_table):
    lookup = jnp.dot(coarse_table, coarse_cols, precision=HIGHEST)
    fine_next = (totals + prior_weight * lookup) / (counts + prior_weight)[:, None]
    coarse_part = lax.dot_general(
        coarse_table,
        counts[:, None] * fine_next,
        (((0,), (0,)), ((), ())),
        precision=HIGHEST,
    )
    coarse_weight = jnp.sum(coarse_table * counts[:, None], axis=0)
    return (fine_next, coarse_part, coarse_weight)


def on_device_any(points, fine_assign, fine_start, coarse_start, coarse_assign):
    width = points.shape[1]
    local_count = fine_start.shape[0]
    offset = lax.axis_index("cen") * local_count
    columns = jnp.arange(local_count, dtype=jnp.int32)
    coarse_table = (coarse_assign[:, None] == jnp.arange(NC, dtype=jnp.int32)[None, :]).astype(
        jnp.float32
    )
    point_values = points.astype(jnp.float32)
    squares = jnp.sum(point_values * point_values, axis=1)
    fine_now = fine_start
    coarse_now = coarse_start
    gap_rows = []
    for pass_index in range(PASSES):
        member = (fine_assign[pass_index] - offset)[:, None] == columns[None, :]
        products = jnp.dot(
            points, fine_now.astype(jnp.bfloat16).T, preferred_element_type=jnp.float32
        )
        energy = jnp.sum(fine_now * fine_now, axis=1)[None, :] - 2.0 * products
        picked_local = jnp.sum(jnp.where(member, energy, 0.0), axis=1)
        nearest_local = jnp.min(energy, axis=1)
        picked = lax.psum(picked_local, "cen")
        nearest = lax.pmin(nearest_local, "cen")
        gap_rows.append((picked - nearest) / math.sqrt(width))
        weights = 1.0 / (1.0 + (squares + picked) / width)
        scaled = (point_values * weights[:, None]).astype(jnp.bfloat16)
        partial_sums = lax.dot_general(
            member.astype(jnp.bfloat16),
            scaled,
            (((0,), (0,)), ((), ())),
            preferred_element_type=jnp.float32,
        )
        partial_weights = jnp.sum(jnp.where(member, weights[:, None], 0.0), axis=0)
        share_width = width // lax.axis_size("pts")
        start = lax.axis_index("pts") * share_width
        shares = lax.psum_scatter(partial_sums, "pts", scatter_dimension=1, tiled=True)
        counts = lax.psum(partial_weights, "pts")
        coarse_cols = lax.dynamic_slice_in_dim(coarse_now, start, share_width, 1)
        fine_share, coarse_part, coarse_weight = refine(shares, counts, coarse_cols, coarse_table)
        coarse_sum, coarse_count = lax.psum((coarse_part, coarse_weight), "cen")
        coarse_share = (coarse_sum + prior_weight * coarse_cols) / (coarse_count + prior_weight)[
            :, None
        ]
        fine_now, coarse_now = (
            lax.all_gather(fine_share, "pts", axis=1, tiled=True),
            lax.all_gather(coarse_share, "pts", axis=1, tiled=True),
        )
    return (fine_now, coarse_now, jnp.stack(gap_rows))


CORE, ACROSS_X, ACROSS_Y = 1, 2, 4
SLOTS = 4
TAIL = 8


def swap(value, bit, axis="pts"):
    size = lax.axis_size(axis)
    return lax.ppermute(value, axis, [(i, i ^ bit) for i in range(size)])


def swap_first(value):
    pairs = [(i, i ^ (ACROSS_Y if i & CORE else ACROSS_X)) for i in range(lax.axis_size("pts"))]
    return lax.ppermute(value, "pts", pairs)


def swap_second(value):
    pairs = [(i, i ^ (ACROSS_X if i & CORE else ACROSS_Y)) for i in range(lax.axis_size("pts"))]
    return lax.ppermute(value, "pts", pairs)


def block_of(info, slot, core):
    crossed = (slot >> 1) | ((slot & 1) << 1)
    return info[0] ^ (slot + core * (crossed - slot))


HERE = pl.BlockSpec(memory_space=pltpu.VMEM)
AWAY = pl.BlockSpec(memory_space=pl.ANY)
SCALARS = pl.BlockSpec(memory_space=pltpu.SMEM)


def near_by(value):
    return pltpu.with_memory_space_constraint(value, pltpu.VMEM)


def far_off(value):
    return pltpu.with_memory_space_constraint(value, pltpu.HBM)


def as_column(row, rows):
    return jnp.broadcast_to(row, (128, rows)).T


def pass_body(info, points, assign, fine, *refs, pass_index, flip, stream, chained, tile):
    refs = list(refs)
    initial = pass_index == 0
    first = stream
    squares_in = None if first else refs.pop(0)
    seen_in = refs.pop(0) if chained else None
    payload, seen = refs.pop(0), refs.pop(0)
    squares_out = refs.pop(0) if first else None
    kept = refs.pop(0) if stream else points
    low, norms, tallies, sums, even, odd, scaled, places = refs[:8]
    chosen_in = refs[8] if stream else assign
    small_sems, point_sems = refs[9:11] if stream else (None, None)
    start = refs[11] if first else None
    rows, width = low.shape
    mid = rows // 2
    block_width = width // SLOTS
    half = info[1] ^ flip
    base = info[2] + half * rows
    tiles = points.shape[0] // tile

    def span(i):
        return pl.ds(pl.multiple_of(i * tile, tile), tile)

    def column_of(slot, core):
        start = block_of(info, slot, core) * block_width
        return pl.ds(pl.multiple_of(start, block_width), block_width)

    def load(i, half):
        part = pl.ds(pl.multiple_of(i * tile + half * (tile // 2), tile // 2), tile // 2)
        return pltpu.make_async_copy(points.at[part], kept.at[part], point_sems.at[2 * i + half])

    if first:
        load_start = pltpu.make_async_copy(
            fine.at[pl.ds(pl.multiple_of(half * rows, rows), rows)], start, small_sems.at[1]
        )
        load_start.start()
    if stream:
        load(0, 0).start()
        load_assign = pltpu.make_async_copy(assign, chosen_in, small_sems.at[0])
        load_assign.start()
        load(0, 1).start()

        @pl.loop(1, tiles)
        def _(i):
            load(i, 0).start()
            load(i, 1).start()

    if initial:
        if first:
            load_start.wait()
            block = start[...]
        else:
            block = fine[pl.ds(pl.multiple_of(half * rows, rows), rows), :]
        norm = jnp.sum(block * block, axis=1, keepdims=True)
        low[...] = (-2.0 * block).astype(jnp.bfloat16)
    else:
        norm = [jnp.zeros((mid, 1), jnp.float32)] * 2
        for piece, (slot, is_low) in enumerate(PIECES):
            block = fine[piece]
            norm[is_low] = norm[is_low] + jnp.sum(block * block, axis=1, keepdims=True)
            part = slice(is_low * mid, (is_low + 1) * mid)
            low[part, column_of(slot, 0)] = (-2.0 * block).astype(jnp.bfloat16)
        norm = jnp.concatenate(norm, 0)
    norms[...] = jnp.broadcast_to(norm, norms.shape)
    tallies[...] = jnp.zeros_like(tallies)
    sums[...] = jnp.zeros_like(sums)
    places[...] = lax.broadcasted_iota(jnp.int32, places.shape, 0).astype(jnp.int16)

    def multiply(i, target):
        target[...] = lax.dot_general(
            low[...], kept[span(i), :], (((1,), (1,)), ((), ())), preferred_element_type=jnp.float32
        )

    def collect(i, products):
        energy = products[...] + jnp.concatenate([norms[...]] * (tile // 128), axis=1)
        chosen = chosen_in[pass_index : pass_index + 1, span(i)] - base
        member = lax.broadcasted_iota(jnp.int32, energy.shape, 0) == chosen
        picked = jnp.sum(jnp.where(member, energy, 0.0), axis=0, keepdims=True)
        nearest = jnp.min(energy, axis=0, keepdims=True)
        inside = (chosen >= 0) & (chosen < rows)
        picked_seen = jnp.where(inside, picked, FAR)
        if chained:
            picked_seen = jnp.minimum(picked_seen, seen_in[0:1, span(i)])
            nearest = jnp.minimum(nearest, seen_in[1:2, span(i)])
        seen[0:1, span(i)] = picked_seen
        seen[1:2, span(i)] = nearest
        if first:
            folded = jnp.zeros((tile, 128), jnp.float32)
            for lane in range(0, width, 128):
                values = kept[span(i), lane : lane + 128].astype(jnp.float32)
                folded = folded + values * values
            squares = jnp.sum(folded.T, axis=0, keepdims=True)
            squares_out[0:1, span(i)] = squares
        else:
            squares = squares_in[0:1, span(i)]
        weights = 1.0 / (1.0 + (squares + picked) / width)
        weighted = jnp.where(member, weights, 0.0)
        tally = tallies[...]
        for lane in range(0, tile, 128):
            tally = tally + weighted[:, lane : lane + 128]
        tallies[...] = tally
        factor = as_column(weights, tile)
        for lane in range(0, width, 128):
            values = kept[span(i), lane : lane + 128].astype(jnp.float32)
            scaled[:, lane : lane + 128] = (values * factor).astype(jnp.bfloat16)
        narrow = jnp.where(inside, chosen, -1).astype(jnp.int16)
        table = jnp.where(
            jnp.concatenate([places[...]] * (tile // 128), axis=1) == narrow,
            jnp.ones((rows, tile), jnp.bfloat16),
            jnp.zeros((rows, tile), jnp.bfloat16),
        )
        sums[...] += jnp.dot(table, scaled[...], preferred_element_type=jnp.float32)

    def arrive(i):
        for half in range(2):
            if stream:
                load(i, half).wait()

    if stream:
        load_assign.wait()
    arrive(0)
    multiply(0, even)

    @pl.loop(0, tiles // 2 - 1)
    def _(pair):
        i = 2 * pair
        arrive(i + 1)
        multiply(i + 1, odd)
        collect(i, even)
        arrive(i + 2)
        multiply(i + 2, even)
        collect(i + 1, odd)

    arrive(tiles - 1)
    multiply(tiles - 1, odd)
    collect(tiles - 2, even)
    collect(tiles - 1, odd)

    counts = jnp.broadcast_to(jnp.sum(tallies[...].T, axis=0, keepdims=True), (TAIL, rows))
    for slot in range(SLOTS):
        columns = column_of(slot, info[1] ^ (not chained))
        payload[slot, :mid, :] = sums[:mid, columns]
        payload[slot, mid : mid + TAIL, :] = counts
        payload[slot, mid + TAIL :, :] = sums[mid:, columns]


def fetch_body(points, *refs):
    *_, kept, sems = refs
    share = points.shape[0] // sems.shape[0]
    copies = [
        pltpu.make_async_copy(
            points.at[i * share : (i + 1) * share], kept.at[i * share : (i + 1) * share], sems.at[i]
        )
        for i in range(sems.shape[0])
    ]
    for copy in copies:
        copy.start()
    for copy in copies:
        copy.wait()


def fetch(points, after):
    return pl.pallas_call(
        fetch_body,
        out_shape=pltpu.VMEM(points.shape, points.dtype),
        in_specs=[AWAY] + [HERE] * len(after),
        out_specs=HERE,
        scratch_shapes=[pltpu.SemaphoreType.DMA((8,))],
        compiler_params=pltpu.CompilerParams(vmem_limit_bytes=2 * 2**20),
        cost_estimate=pl.CostEstimate(
            flops=0, bytes_accessed=4 * points.size, transcendentals=0
        ),
        name="fetch_points",
    )(far_off(points), *[near_by(value) for value in after])


def run_pass(info, points, fine_assign, fine, squares, seen, *, pass_index, flip, rows):
    count, width = points.shape
    block_width = width // SLOTS
    initial = pass_index == 0
    chained = seen is not None
    stream = squares is None
    tile = 1024
    if stream:
        in_specs = [AWAY] * 3
        args = [far_off(points), far_off(fine_assign), far_off(fine)]
    else:
        in_specs = [HERE] * 3
        args = [near_by(points), near_by(fine_assign), near_by(fine)]
    for value in (squares, seen):
        if value is not None:
            in_specs.append(HERE)
            args.append(near_by(value))
    shapes = [(SLOTS, rows + TAIL, block_width), (2, count)]
    if squares is None:
        shapes.append((1, count))
    out_shape = [pltpu.VMEM(shape, jnp.float32) for shape in shapes]
    scratch = [
        pltpu.VMEM((rows, width), jnp.bfloat16),
        pltpu.VMEM((rows, 128), jnp.float32),
        pltpu.VMEM((rows, 128), jnp.float32),
        pltpu.VMEM((rows, width), jnp.float32),
        pltpu.VMEM((rows, tile), jnp.float32),
        pltpu.VMEM((rows, tile), jnp.float32),
        pltpu.VMEM((tile, width), jnp.bfloat16),
        pltpu.VMEM((rows, 128), jnp.int16),
    ]
    if stream:
        scratch += [
            pltpu.VMEM((PASSES, count), jnp.int32),
            pltpu.SemaphoreType.DMA((2,)),
            pltpu.SemaphoreType.DMA((2 * count // tile,)),
        ]
        if initial:
            scratch.append(pltpu.VMEM((rows, width), jnp.float32))
        out_shape.append(pltpu.VMEM(points.shape, points.dtype))
    body = functools.partial(
        pass_body,
        pass_index=pass_index,
        flip=flip,
        stream=stream,
        chained=chained,
        tile=tile,
    )
    return pl.pallas_call(
        body,
        out_shape=out_shape,
        in_specs=[SCALARS, *in_specs],
        out_specs=[HERE] * len(out_shape),
        scratch_shapes=scratch,
        compiler_params=pltpu.CompilerParams(vmem_limit_bytes=20 * 2**20),
        cost_estimate=pl.CostEstimate(
            flops=4 * rows * count * width, bytes_accessed=2 * count * width, transcendentals=0
        ),
        name=f"energies_and_sums_{pass_index}{int(chained)}",
    )(info, *args)


def one_hot_dot(table, value, dims):
    table = table.astype(jnp.bfloat16)
    total = 0.0
    for _ in range(3):
        term = value.astype(jnp.bfloat16)
        value = value - term.astype(jnp.float32)
        total = total + lax.dot_general(
            table, term, dims, preferred_element_type=jnp.float32
        )
    return total


def refine_body(info, own, sibling, *refs, flip):
    first_top, first_low, second_top, second_low, owners, *coarse_in, top, low, part = refs
    rows = owners.shape[2]
    mid = rows // 2
    block_width = part.shape[1]
    owner = owners[info[1] ^ flip]
    if len(coarse_in) == 1:
        column = pl.multiple_of(info[0] * block_width, block_width)
        coarse = coarse_in[0][:, pl.ds(column, block_width)]
    else:
        sums = coarse_in[0][: NC + TAIL, :] + coarse_in[1][: NC + TAIL, :]
        coarse = sums[:NC] / as_column(sums[NC : NC + 1, :128], 128)[:NC, :1]
    head = own[0, : mid + TAIL, :] + sibling[0, : mid + TAIL, :]
    rest = own[0, mid + TAIL :, :] + sibling[0, mid + TAIL :, :]
    head = head + (first_top[0] + second_top[...])
    rest = rest + (first_low[0] + second_low[...])
    totals, counts_row = jnp.concatenate([head[:mid], rest], 0), head[mid:]
    counts = as_column(counts_row[:1], rows)[:, :1]
    table = (
        lax.broadcasted_iota(jnp.int32, (NC, rows), 0) == owner
    ).astype(jnp.float32)
    lookup = one_hot_dot(table, coarse, (((0,), (0,)), ((), ())))
    new = (totals + prior_weight * lookup) / (counts + prior_weight)
    top[...] = new[:mid]
    low[...] = new[mid:]
    prior = jnp.where(info[3] == 0, prior_weight, 0.0)
    part[:NC, :] = prior * coarse + one_hot_dot(table, counts * new, (((1,), (0,)), ((), ())))
    part[NC:, :] = jnp.zeros((TAIL, part.shape[1]), jnp.float32)
    weight = jnp.sum(table * counts_row[:1], axis=1, keepdims=True)
    weight = jnp.broadcast_to(weight, (NC, 128)).T[:TAIL]
    part[NC:, :NC] = prior + weight


def refine_half(info, own, sibling, incoming, owners, coarse, *, flip):
    _, rows, block_width = own.shape
    mid = (rows - TAIL) // 2
    args = [near_by(value) for value in (own, sibling, *incoming, owners, *coarse)]
    shapes = [(mid, block_width), (mid, block_width), (NC + TAIL, block_width)]
    return pl.pallas_call(
        functools.partial(refine_body, flip=flip),
        out_shape=[pltpu.VMEM(shape, jnp.float32) for shape in shapes],
        in_specs=[SCALARS] + [HERE] * len(args),
        out_specs=[HERE] * len(shapes),
        compiler_params=pltpu.CompilerParams(vmem_limit_bytes=8 * 2**20),
        name="refine_half",
    )(info, *args)


def exchange(held, sibling, folded=None):
    cut = (held.shape[1] - TAIL) // 2 + TAIL
    chunks = slice(0, cut), slice(cut, None)
    first = [held[1::2, rows] + sibling[1::2, rows] for rows in chunks]
    first, folded = lax.optimization_barrier((first, folded))
    first = [swap_first(chunk) for chunk in first]
    if folded is not None:
        folded = swap(folded, lax.axis_size("cen") // 2, "cen")
    second = [
        held[2, rows] + sibling[2, rows] + arrived[1] for rows, arrived in zip(chunks, first)
    ]
    if folded is not None:
        second[1], folded = lax.optimization_barrier((second[1], folded))
    second = [swap_second(chunk) for chunk in second]
    return [*first, *second], folded


PIECES = ((1, 1), (2, 0), (3, 0), (3, 1), (1, 0), (2, 1), (0, 0), (0, 1))


def gather_half(top, low, later=False):
    x_low = swap(low, ACROSS_X)
    y_top = swap(top, ACROSS_Y)
    again = top, low
    if later:
        x_low, y_top, again = lax.optimization_barrier((x_low, y_top, again))
    x_top = swap(again[0], ACROSS_X)
    y_low = swap(again[1], ACROSS_Y)
    corner_top = swap(y_top, ACROSS_X)
    corner_low = swap(x_low, ACROSS_Y)
    return [x_low, y_top, corner_top, corner_low, x_top, y_low, top, low]


def spread(value):
    corner = swap(value, ACROSS_X | ACROSS_Y)
    return [value, swap(value, ACROSS_X), swap(value, ACROSS_Y), corner]


def over_cen(value, combine, bits=None):
    for bit in range(lax.axis_size("cen").bit_length() - 1) if bits is None else bits:
        value = combine(value, swap(value, 1 << bit, "cen"))
    return value


def fold(first, second):
    cut = NC + TAIL
    return jnp.concatenate(
        [first[:cut] + second[:cut], jnp.minimum(first[cut:], second[cut:])], 0
    )


def place_body(info, *refs, flip):
    own, other = refs[:3], refs[3:6]
    fine_out, coarse_out, fine_held, coarse_held, sems = refs[6:]
    block_width = coarse_out.shape[1] // SLOTS
    rows = fine_out.shape[0] // 2
    mid = rows // 2
    half = info[1] ^ flip

    def column_of(slot, core):
        start = block_of(info, slot, core) * block_width
        return pl.ds(pl.multiple_of(start, block_width), block_width)

    def put(at, *groups):
        for piece, (slot, is_low) in enumerate(PIECES):
            part = slice(is_low * mid, (is_low + 1) * mid)
            fine_held[at, part, column_of(slot, 0)] = groups[piece // SLOTS][piece % SLOTS]

    def send(at, half):
        span = pl.ds(pl.multiple_of(half * rows, rows), rows)
        return pltpu.make_async_copy(fine_held.at[at], fine_out.at[span], sems.at[at])

    put(0, *own[:2])
    send(0, half).start()
    put(1, *other[:2])
    send(1, 1 - half).start()
    parts, others = own[2], other[2]
    weight = parts[0, NC:, :128] + others[0, NC:, :128]
    weight = as_column(weight[:1], 128)[:NC, :1]
    for slot in range(SLOTS):
        total = parts[slot, :NC, :] + others[slot, :NC, :]
        coarse_held[:, column_of(slot, 0)] = total / weight
    send_coarse = pltpu.make_async_copy(coarse_held, coarse_out, sems.at[2])
    send_coarse.start()
    send(0, half).wait()
    send(1, 1 - half).wait()
    send_coarse.wait()


def place(info, own, other, *, flip):
    _, mid, block_width = own[0].shape
    rows, width = 2 * mid, SLOTS * block_width
    args = [near_by(value) for value in (*own, *other)]
    return pl.pallas_call(
        functools.partial(place_body, flip=flip),
        out_shape=[
            jax.ShapeDtypeStruct((2 * rows, width), jnp.float32),
            jax.ShapeDtypeStruct((NC, width), jnp.float32),
        ],
        in_specs=[SCALARS] + [HERE] * len(args),
        out_specs=[AWAY, AWAY],
        scratch_shapes=[
            pltpu.VMEM((2, rows, width), jnp.float32),
            pltpu.VMEM((NC, width), jnp.float32),
            pltpu.SemaphoreType.DMA((3,)),
        ],
        compiler_params=pltpu.CompilerParams(vmem_limit_bytes=8 * 2**20),
        name="place_blocks",
    )(info, *args)


def on_device_paired(points, fine_assign, fine_start, coarse_start, coarse_assign):
    width = points.shape[1]
    local_count = fine_start.shape[0]
    rows = local_count // 2
    block_width = width // SLOTS
    cen, me = lax.axis_index("cen"), lax.axis_index("pts")
    core = me & 1
    info = jnp.stack([me >> 1, core, cen * local_count, cen * 2 + core]).astype(jnp.int32)
    owners = coarse_assign.reshape(2, 1, rows)

    call = functools.partial(run_pass, info, pass_index=0, rows=rows)
    sent, seen, squares, kept = call(points, fine_assign, fine_start, None, None, flip=1)
    sibling = swap(sent, CORE)
    held, seen_first = call(kept, fine_assign, fine_start, squares, seen, flip=0)
    incoming, _ = exchange(held, sibling)
    top, low, part = refine_half(
        info, held, sibling, incoming, owners, [coarse_start], flip=0
    )
    own = gather_half(top, low)
    bits = range(lax.axis_size("cen").bit_length() - 1)
    folded = jnp.concatenate([part, seen_first.reshape(-1, block_width)], 0)
    paired = swap(folded, 1, "cen")
    kept = fetch(points, own[:2])
    own, kept, paired = lax.optimization_barrier((own, kept, paired))
    own = jnp.stack(own)
    other = swap(own, CORE)

    call = functools.partial(run_pass, info, pass_index=1, rows=rows)
    sent, seen = call(kept, fine_assign, own, squares, None, flip=0)
    sent, paired = lax.optimization_barrier((sent, paired))
    folded = fold(folded, paired)
    sibling = swap(sent, CORE)
    part = folded[: NC + TAIL]
    others_part = swap(part, CORE)
    held, seen_second = call(kept, fine_assign, other, squares, seen, flip=1)
    held, others_part = lax.optimization_barrier((held, others_part))
    folded = jnp.concatenate([part + others_part, folded[NC + TAIL :]], 0)
    folded = over_cen(folded, fold, bits[1:-1])
    incoming, paired = exchange(held, sibling, folded)
    seen_first = jnp.minimum(folded[NC + TAIL :], paired[NC + TAIL :])

    top, low, part = refine_half(
        info, held, sibling, incoming, owners, [folded, paired], flip=1
    )
    folded = jnp.concatenate([part, seen_second.reshape(-1, block_width)], 0)
    top, low, folded = lax.optimization_barrier((top, low, folded))
    own = gather_half(top, low, True)
    folded = over_cen(folded, fold)
    part, seen_second = folded[: NC + TAIL], folded[NC + TAIL :]
    parts = spread(part)
    own[2], own[3], parts[1] = lax.optimization_barrier((own[2], own[3], parts[1]))
    blocks = [jnp.stack(own[:4]), jnp.stack(own[4:]), jnp.stack(parts)]
    fine_now, coarse_now = place(info, blocks, [swap(block, CORE) for block in blocks], flip=1)

    seen = [each.reshape(2, -1) for each in (seen_first, seen_second)]
    gaps = jnp.stack([each[0] - each[1] for each in seen]) / math.sqrt(width)
    return (fine_now, coarse_now, gaps)


def solution(mesh):
    placed = (P("pts", None), P(None, "pts"), P("cen", None), P(), P("cen"))

    def on_device(points, fine_assign, fine_start, coarse_start, coarse_assign):
        count, width = points.shape
        local_count = fine_start.shape[0]
        centres = mesh.shape["cen"]
        fits = (
            mesh.shape["pts"] == 2 * SLOTS
            and centres & (centres - 1) == 0
            and centres >= 4
            and width // SLOTS == local_count // 2
            and (width // SLOTS) % 128 == 0
            and count % 2048 == 0
        )
        plan = on_device_paired if fits else on_device_any
        return plan(points, fine_assign, fine_start, coarse_start, coarse_assign)

    return jax.shard_map(
        on_device,
        mesh=mesh,
        in_specs=placed,
        out_specs=(P("cen", None), P(), P(None, "pts")),
        check_vma=False,
    )
```

```python
import functools
import math

import jax
import jax.numpy as jnp
from jax import lax
from jax.experimental import pallas as pl
from jax.experimental.pallas import tpu as pltpu
from jax.sharding import PartitionSpec as P

NC = 64
PASSES = 2
FAR = 3.0e38

prior_weight = 4.0
HIGHEST = lax.Precision.HIGHEST


def refine(totals, counts, coarse_cols, coarse_table):
    lookup = jnp.dot(coarse_table, coarse_cols, precision=HIGHEST)
    fine_next = (totals + prior_weight * lookup) / (counts + prior_weight)[:, None]
    coarse_part = lax.dot_general(
        coarse_table,
        counts[:, None] * fine_next,
        (((0,), (0,)), ((), ())),
        precision=HIGHEST,
    )
    coarse_weight = jnp.sum(coarse_table * counts[:, None], axis=0)
    return (fine_next, coarse_part, coarse_weight)


def on_device_any(points, fine_assign, fine_start, coarse_start, coarse_assign):
    width = points.shape[1]
    local_count = fine_start.shape[0]
    offset = lax.axis_index("cen") * local_count
    columns = jnp.arange(local_count, dtype=jnp.int32)
    coarse_table = (coarse_assign[:, None] == jnp.arange(NC, dtype=jnp.int32)[None, :]).astype(
        jnp.float32
    )
    point_values = points.astype(jnp.float32)
    squares = jnp.sum(point_values * point_values, axis=1)
    fine_now = fine_start
    coarse_now = coarse_start
    gap_rows = []
    for pass_index in range(PASSES):
        member = (fine_assign[pass_index] - offset)[:, None] == columns[None, :]
        products = jnp.dot(
            points, fine_now.astype(jnp.bfloat16).T, preferred_element_type=jnp.float32
        )
        energy = jnp.sum(fine_now * fine_now, axis=1)[None, :] - 2.0 * products
        picked_local = jnp.sum(jnp.where(member, energy, 0.0), axis=1)
        nearest_local = jnp.min(energy, axis=1)
        picked = lax.psum(picked_local, "cen")
        nearest = lax.pmin(nearest_local, "cen")
        gap_rows.append((picked - nearest) / math.sqrt(width))
        weights = 1.0 / (1.0 + (squares + picked) / width)
        scaled = (point_values * weights[:, None]).astype(jnp.bfloat16)
        partial_sums = lax.dot_general(
            member.astype(jnp.bfloat16),
            scaled,
            (((0,), (0,)), ((), ())),
            preferred_element_type=jnp.float32,
        )
        partial_weights = jnp.sum(jnp.where(member, weights[:, None], 0.0), axis=0)
        share_width = width // lax.axis_size("pts")
        start = lax.axis_index("pts") * share_width
        shares = lax.psum_scatter(partial_sums, "pts", scatter_dimension=1, tiled=True)
        counts = lax.psum(partial_weights, "pts")
        coarse_cols = lax.dynamic_slice_in_dim(coarse_now, start, share_width, 1)
        fine_share, coarse_part, coarse_weight = refine(shares, counts, coarse_cols, coarse_table)
        coarse_sum, coarse_count = lax.psum((coarse_part, coarse_weight), "cen")
        coarse_share = (coarse_sum + prior_weight * coarse_cols) / (coarse_count + prior_weight)[
            :, None
        ]
        fine_now, coarse_now = (
            lax.all_gather(fine_share, "pts", axis=1, tiled=True),
            lax.all_gather(coarse_share, "pts", axis=1, tiled=True),
        )
    return (fine_now, coarse_now, jnp.stack(gap_rows))


CORE, ACROSS_X, ACROSS_Y = 1, 2, 4
SLOTS = 4
TAIL = 8


def swap(value, bit, axis="pts"):
    size = lax.axis_size(axis)
    return lax.ppermute(value, axis, [(i, i ^ bit) for i in range(size)])


def swap_first(value):
    pairs = [(i, i ^ (ACROSS_Y if i & CORE else ACROSS_X)) for i in range(lax.axis_size("pts"))]
    return lax.ppermute(value, "pts", pairs)


def swap_second(value):
    pairs = [(i, i ^ (ACROSS_X if i & CORE else ACROSS_Y)) for i in range(lax.axis_size("pts"))]
    return lax.ppermute(value, "pts", pairs)


def block_of(info, slot, core):
    crossed = (slot >> 1) | ((slot & 1) << 1)
    return info[0] ^ (slot + core * (crossed - slot))


HERE = pl.BlockSpec(memory_space=pltpu.VMEM)
AWAY = pl.BlockSpec(memory_space=pl.ANY)
SCALARS = pl.BlockSpec(memory_space=pltpu.SMEM)


def near_by(value):
    return pltpu.with_memory_space_constraint(value, pltpu.VMEM)


def far_off(value):
    return pltpu.with_memory_space_constraint(value, pltpu.HBM)


def as_column(row, rows):
    return jnp.broadcast_to(row, (128, rows)).T


def pass_body(info, points, assign, fine, *refs, pass_index, flip, stream, chained, tile):
    refs = list(refs)
    initial = pass_index == 0
    first = stream
    squares_in = None if first else refs.pop(0)
    seen_in = refs.pop(0) if chained else None
    payload, seen = refs.pop(0), refs.pop(0)
    squares_out = refs.pop(0) if first else None
    kept = refs.pop(0) if stream else points
    low, norms, tallies, sums, even, odd, scaled, places = refs[:8]
    chosen_in = refs[8] if stream else assign
    small_sems, point_sems = refs[9:11] if stream else (None, None)
    start = refs[11] if first else None
    rows, width = low.shape
    mid = rows // 2
    block_width = width // SLOTS
    half = info[1] ^ flip
    base = info[2] + half * rows
    tiles = points.shape[0] // tile

    def span(i):
        return pl.ds(pl.multiple_of(i * tile, tile), tile)

    def column_of(slot, core):
        start = block_of(info, slot, core) * block_width
        return pl.ds(pl.multiple_of(start, block_width), block_width)

    def load(i, half):
        part = pl.ds(pl.multiple_of(i * tile + half * (tile // 2), tile // 2), tile // 2)
        return pltpu.make_async_copy(points.at[part], kept.at[part], point_sems.at[2 * i + half])

    if first:
        load_start = pltpu.make_async_copy(
            fine.at[pl.ds(pl.multiple_of(half * rows, rows), rows)], start, small_sems.at[1]
        )
        load_start.start()
    if stream:
        load(0, 0).start()
        load_assign = pltpu.make_async_copy(assign, chosen_in, small_sems.at[0])
        load_assign.start()
        load(0, 1).start()

        @pl.loop(1, tiles)
        def _(i):
            load(i, 0).start()
            load(i, 1).start()

    if initial:
        if first:
            load_start.wait()
            block = start[...]
        else:
            block = fine[pl.ds(pl.multiple_of(half * rows, rows), rows), :]
        norm = jnp.sum(block * block, axis=1, keepdims=True)
        low[...] = (-2.0 * block).astype(jnp.bfloat16)
    else:
        norm = [jnp.zeros((mid, 1), jnp.float32)] * 2
        for piece, (slot, is_low) in enumerate(PIECES):
            block = fine[piece]
            norm[is_low] = norm[is_low] + jnp.sum(block * block, axis=1, keepdims=True)
            part = slice(is_low * mid, (is_low + 1) * mid)
            low[part, column_of(slot, 0)] = (-2.0 * block).astype(jnp.bfloat16)
        norm = jnp.concatenate(norm, 0)
    norms[...] = jnp.broadcast_to(norm, norms.shape)
    tallies[...] = jnp.zeros_like(tallies)
    sums[...] = jnp.zeros_like(sums)
    places[...] = lax.broadcasted_iota(jnp.int32, places.shape, 0).astype(jnp.int16)

    def multiply(i, target):
        target[...] = lax.dot_general(
            low[...], kept[span(i), :], (((1,), (1,)), ((), ())), preferred_element_type=jnp.float32
        )

    def collect(i, products):
        energy = products[...] + jnp.concatenate([norms[...]] * (tile // 128), axis=1)
        chosen = chosen_in[pass_index : pass_index + 1, span(i)] - base
        member = lax.broadcasted_iota(jnp.int32, energy.shape, 0) == chosen
        picked = jnp.sum(jnp.where(member, energy, 0.0), axis=0, keepdims=True)
        nearest = jnp.min(energy, axis=0, keepdims=True)
        inside = (chosen >= 0) & (chosen < rows)
        picked_seen = jnp.where(inside, picked, FAR)
        if chained:
            picked_seen = jnp.minimum(picked_seen, seen_in[0:1, span(i)])
            nearest = jnp.minimum(nearest, seen_in[1:2, span(i)])
        seen[0:1, span(i)] = picked_seen
        seen[1:2, span(i)] = nearest
        if first:
            folded = jnp.zeros((tile, 128), jnp.float32)
            for lane in range(0, width, 128):
                values = kept[span(i), lane : lane + 128].astype(jnp.float32)
                folded = folded + values * values
            squares = jnp.sum(folded.T, axis=0, keepdims=True)
            squares_out[0:1, span(i)] = squares
        else:
            squares = squares_in[0:1, span(i)]
        weights = 1.0 / (1.0 + (squares + picked) / width)
        weighted = jnp.where(member, weights, 0.0)
        tally = tallies[...]
        for lane in range(0, tile, 128):
            tally = tally + weighted[:, lane : lane + 128]
        tallies[...] = tally
        factor = as_column(weights, tile)
        for lane in range(0, width, 128):
            values = kept[span(i), lane : lane + 128].astype(jnp.float32)
            scaled[:, lane : lane + 128] = (values * factor).astype(jnp.bfloat16)
        narrow = jnp.where(inside, chosen, -1).astype(jnp.int16)
        table = jnp.where(
            jnp.concatenate([places[...]] * (tile // 128), axis=1) == narrow,
            jnp.ones((rows, tile), jnp.bfloat16),
            jnp.zeros((rows, tile), jnp.bfloat16),
        )
        sums[...] += jnp.dot(table, scaled[...], preferred_element_type=jnp.float32)

    def arrive(i):
        for half in range(2):
            if stream:
                load(i, half).wait()

    if stream:
        load_assign.wait()
    arrive(0)
    multiply(0, even)

    @pl.loop(0, tiles // 2 - 1)
    def _(pair):
        i = 2 * pair
        arrive(i + 1)
        multiply(i + 1, odd)
        collect(i, even)
        arrive(i + 2)
        multiply(i + 2, even)
        collect(i + 1, odd)

    arrive(tiles - 1)
    multiply(tiles - 1, odd)
    collect(tiles - 2, even)
    collect(tiles - 1, odd)

    counts = jnp.broadcast_to(jnp.sum(tallies[...].T, axis=0, keepdims=True), (TAIL, rows))
    for slot in range(SLOTS):
        columns = column_of(slot, info[1] ^ (not chained))
        payload[slot, :mid, :] = sums[:mid, columns]
        payload[slot, mid : mid + TAIL, :] = counts
        payload[slot, mid + TAIL :, :] = sums[mid:, columns]


def run_pass(info, points, fine_assign, fine, squares, seen, *, pass_index, flip, rows):
    count, width = points.shape
    block_width = width // SLOTS
    initial = pass_index == 0
    chained = seen is not None
    stream = squares is None
    tile = 1024
    if stream:
        in_specs = [AWAY] * 3
        args = [far_off(points), far_off(fine_assign), far_off(fine)]
    else:
        in_specs = [HERE] * 3
        args = [near_by(points), near_by(fine_assign), near_by(fine)]
    for value in (squares, seen):
        if value is not None:
            in_specs.append(HERE)
            args.append(near_by(value))
    shapes = [(SLOTS, rows + TAIL, block_width), (2, count)]
    if squares is None:
        shapes.append((1, count))
    out_shape = [pltpu.VMEM(shape, jnp.float32) for shape in shapes]
    scratch = [
        pltpu.VMEM((rows, width), jnp.bfloat16),
        pltpu.VMEM((rows, 128), jnp.float32),
        pltpu.VMEM((rows, 128), jnp.float32),
        pltpu.VMEM((rows, width), jnp.float32),
        pltpu.VMEM((rows, tile), jnp.float32),
        pltpu.VMEM((rows, tile), jnp.float32),
        pltpu.VMEM((tile, width), jnp.bfloat16),
        pltpu.VMEM((rows, 128), jnp.int16),
    ]
    if stream:
        scratch += [
            pltpu.VMEM((PASSES, count), jnp.int32),
            pltpu.SemaphoreType.DMA((2,)),
            pltpu.SemaphoreType.DMA((2 * count // tile,)),
        ]
        if initial:
            scratch.append(pltpu.VMEM((rows, width), jnp.float32))
        out_shape.append(pltpu.VMEM(points.shape, points.dtype))
    body = functools.partial(
        pass_body,
        pass_index=pass_index,
        flip=flip,
        stream=stream,
        chained=chained,
        tile=tile,
    )
    return pl.pallas_call(
        body,
        out_shape=out_shape,
        in_specs=[SCALARS, *in_specs],
        out_specs=[HERE] * len(out_shape),
        scratch_shapes=scratch,
        compiler_params=pltpu.CompilerParams(vmem_limit_bytes=20 * 2**20),
        cost_estimate=pl.CostEstimate(
            flops=4 * rows * count * width, bytes_accessed=2 * count * width, transcendentals=0
        ),
        name=f"energies_and_sums_{pass_index}{int(chained)}",
    )(info, *args)


def one_hot_dot(table, value, dims):
    table = table.astype(jnp.bfloat16)
    total = 0.0
    for _ in range(3):
        term = value.astype(jnp.bfloat16)
        value = value - term.astype(jnp.float32)
        total = total + lax.dot_general(
            table, term, dims, preferred_element_type=jnp.float32
        )
    return total


def refine_body(info, own, sibling, *refs, flip):
    first_top, first_low, second_top, second_low, owners, *coarse_in, top, low, part = refs
    rows = owners.shape[2]
    mid = rows // 2
    block_width = part.shape[1]
    owner = owners[info[1] ^ flip]
    if len(coarse_in) == 1:
        column = pl.multiple_of(info[0] * block_width, block_width)
        coarse = coarse_in[0][:, pl.ds(column, block_width)]
    else:
        sums = coarse_in[0][: NC + TAIL, :] + coarse_in[1][: NC + TAIL, :]
        coarse = sums[:NC] / as_column(sums[NC : NC + 1, :128], 128)[:NC, :1]
    head = own[0, : mid + TAIL, :] + sibling[0, : mid + TAIL, :]
    rest = own[0, mid + TAIL :, :] + sibling[0, mid + TAIL :, :]
    head = head + (first_top[0] + second_top[...])
    rest = rest + (first_low[0] + second_low[...])
    totals, counts_row = jnp.concatenate([head[:mid], rest], 0), head[mid:]
    counts = as_column(counts_row[:1], rows)[:, :1]
    table = (
        lax.broadcasted_iota(jnp.int32, (NC, rows), 0) == owner
    ).astype(jnp.float32)
    lookup = one_hot_dot(table, coarse, (((0,), (0,)), ((), ())))
    new = (totals + prior_weight * lookup) / (counts + prior_weight)
    top[...] = new[:mid]
    low[...] = new[mid:]
    prior = jnp.where(info[3] == 0, prior_weight, 0.0)
    part[:NC, :] = prior * coarse + one_hot_dot(table, counts * new, (((1,), (0,)), ((), ())))
    part[NC:, :] = jnp.zeros((TAIL, part.shape[1]), jnp.float32)
    weight = jnp.sum(table * counts_row[:1], axis=1, keepdims=True)
    weight = jnp.broadcast_to(weight, (NC, 128)).T[:TAIL]
    part[NC:, :NC] = prior + weight


def refine_half(info, own, sibling, incoming, owners, coarse, *, flip):
    _, rows, block_width = own.shape
    mid = (rows - TAIL) // 2
    args = [near_by(value) for value in (own, sibling, *incoming, owners, *coarse)]
    shapes = [(mid, block_width), (mid, block_width), (NC + TAIL, block_width)]
    return pl.pallas_call(
        functools.partial(refine_body, flip=flip),
        out_shape=[pltpu.VMEM(shape, jnp.float32) for shape in shapes],
        in_specs=[SCALARS] + [HERE] * len(args),
        out_specs=[HERE] * len(shapes),
        compiler_params=pltpu.CompilerParams(vmem_limit_bytes=8 * 2**20),
        name="refine_half",
    )(info, *args)


def exchange(held, sibling, folded=None):
    cut = (held.shape[1] - TAIL) // 2 + TAIL
    chunks = slice(0, cut), slice(cut, None)
    first = [held[1::2, rows] + sibling[1::2, rows] for rows in chunks]
    first, folded = lax.optimization_barrier((first, folded))
    first = [swap_first(chunk) for chunk in first]
    if folded is not None:
        folded = swap(folded, lax.axis_size("cen") // 2, "cen")
    second = [
        held[2, rows] + sibling[2, rows] + arrived[1] for rows, arrived in zip(chunks, first)
    ]
    if folded is not None:
        second[1], folded = lax.optimization_barrier((second[1], folded))
    second = [swap_second(chunk) for chunk in second]
    return [*first, *second], folded


PIECES = ((1, 1), (2, 0), (3, 0), (3, 1), (1, 0), (2, 1), (0, 0), (0, 1))


def gather_half(top, low, later=False):
    x_low = swap(low, ACROSS_X)
    y_top = swap(top, ACROSS_Y)
    again = top, low
    if later:
        x_low, y_top, again = lax.optimization_barrier((x_low, y_top, again))
    x_top = swap(again[0], ACROSS_X)
    y_low = swap(again[1], ACROSS_Y)
    corner_top = swap(y_top, ACROSS_X)
    corner_low = swap(x_low, ACROSS_Y)
    return [x_low, y_top, corner_top, corner_low, x_top, y_low, top, low]


def spread(value):
    corner = swap(value, ACROSS_X | ACROSS_Y)
    return [value, swap(value, ACROSS_X), swap(value, ACROSS_Y), corner]


def over_cen(value, combine, bits=None):
    for bit in range(lax.axis_size("cen").bit_length() - 1) if bits is None else bits:
        value = combine(value, swap(value, 1 << bit, "cen"))
    return value


def fold(first, second):
    cut = NC + TAIL
    return jnp.concatenate(
        [first[:cut] + second[:cut], jnp.minimum(first[cut:], second[cut:])], 0
    )


def place_body(info, *refs, flip):
    own, other = refs[:3], refs[3:6]
    fine_out, coarse_out, fine_held, coarse_held, sems = refs[6:]
    block_width = coarse_out.shape[1] // SLOTS
    rows = fine_out.shape[0] // 2
    mid = rows // 2
    half = info[1] ^ flip

    def column_of(slot, core):
        start = block_of(info, slot, core) * block_width
        return pl.ds(pl.multiple_of(start, block_width), block_width)

    def put(at, *groups):
        for piece, (slot, is_low) in enumerate(PIECES):
            part = slice(is_low * mid, (is_low + 1) * mid)
            fine_held[at, part, column_of(slot, 0)] = groups[piece // SLOTS][piece % SLOTS]

    def send(at, half):
        span = pl.ds(pl.multiple_of(half * rows, rows), rows)
        return pltpu.make_async_copy(fine_held.at[at], fine_out.at[span], sems.at[at])

    put(0, *own[:2])
    send(0, half).start()
    put(1, *other[:2])
    send(1, 1 - half).start()
    parts, others = own[2], other[2]
    weight = parts[0, NC:, :128] + others[0, NC:, :128]
    weight = as_column(weight[:1], 128)[:NC, :1]
    for slot in range(SLOTS):
        total = parts[slot, :NC, :] + others[slot, :NC, :]
        coarse_held[:, column_of(slot, 0)] = total / weight
    send_coarse = pltpu.make_async_copy(coarse_held, coarse_out, sems.at[2])
    send_coarse.start()
    send(0, half).wait()
    send(1, 1 - half).wait()
    send_coarse.wait()


def place(info, own, other, *, flip):
    _, mid, block_width = own[0].shape
    rows, width = 2 * mid, SLOTS * block_width
    args = [near_by(value) for value in (*own, *other)]
    return pl.pallas_call(
        functools.partial(place_body, flip=flip),
        out_shape=[
            jax.ShapeDtypeStruct((2 * rows, width), jnp.float32),
            jax.ShapeDtypeStruct((NC, width), jnp.float32),
        ],
        in_specs=[SCALARS] + [HERE] * len(args),
        out_specs=[AWAY, AWAY],
        scratch_shapes=[
            pltpu.VMEM((2, rows, width), jnp.float32),
            pltpu.VMEM((NC, width), jnp.float32),
            pltpu.SemaphoreType.DMA((3,)),
        ],
        compiler_params=pltpu.CompilerParams(vmem_limit_bytes=8 * 2**20),
        name="place_blocks",
    )(info, *args)


def on_device_paired(points, fine_assign, fine_start, coarse_start, coarse_assign):
    width = points.shape[1]
    local_count = fine_start.shape[0]
    rows = local_count // 2
    block_width = width // SLOTS
    cen, me = lax.axis_index("cen"), lax.axis_index("pts")
    core = me & 1
    info = jnp.stack([me >> 1, core, cen * local_count, cen * 2 + core]).astype(jnp.int32)
    owners = coarse_assign.reshape(2, 1, rows)

    call = functools.partial(run_pass, info, pass_index=0, rows=rows)
    sent, seen, squares, kept = call(points, fine_assign, fine_start, None, None, flip=1)
    sibling = swap(sent, CORE)
    held, seen_first = call(kept, fine_assign, fine_start, squares, seen, flip=0)
    incoming, _ = exchange(held, sibling)
    top, low, part = refine_half(
        info, held, sibling, incoming, owners, [coarse_start], flip=0
    )
    own = gather_half(top, low)
    bits = range(lax.axis_size("cen").bit_length() - 1)
    folded = jnp.concatenate([part, seen_first.reshape(-1, block_width)], 0)
    paired = swap(folded, 1, "cen")
    own, paired = lax.optimization_barrier((own, paired))
    own = jnp.stack(own)
    other = swap(own, CORE)

    call = functools.partial(run_pass, info, pass_index=1, rows=rows)
    sent, seen = call(kept, fine_assign, own, squares, None, flip=0)
    sent, paired = lax.optimization_barrier((sent, paired))
    folded = fold(folded, paired)
    sibling = swap(sent, CORE)
    part = folded[: NC + TAIL]
    others_part = swap(part, CORE)
    held, seen_second = call(kept, fine_assign, other, squares, seen, flip=1)
    held, others_part = lax.optimization_barrier((held, others_part))
    folded = jnp.concatenate([part + others_part, folded[NC + TAIL :]], 0)
    folded = over_cen(folded, fold, bits[1:-1])
    incoming, paired = exchange(held, sibling, folded)
    seen_first = jnp.minimum(folded[NC + TAIL :], paired[NC + TAIL :])

    top, low, part = refine_half(
        info, held, sibling, incoming, owners, [folded, paired], flip=1
    )
    folded = jnp.concatenate([part, seen_second.reshape(-1, block_width)], 0)
    top, low, folded = lax.optimization_barrier((top, low, folded))
    own = gather_half(top, low, True)
    folded = over_cen(folded, fold)
    part, seen_second = folded[: NC + TAIL], folded[NC + TAIL :]
    parts = spread(part)
    own[2], own[3], parts[1] = lax.optimization_barrier((own[2], own[3], parts[1]))
    blocks = [jnp.stack(own[:4]), jnp.stack(own[4:]), jnp.stack(parts)]
    fine_now, coarse_now = place(info, blocks, [swap(block, CORE) for block in blocks], flip=1)

    seen = [each.reshape(2, -1) for each in (seen_first, seen_second)]
    gaps = jnp.stack([each[0] - each[1] for each in seen]) / math.sqrt(width)
    return (fine_now, coarse_now, gaps)


def solution(mesh):
    placed = (P("pts", None), P(None, "pts"), P("cen", None), P(), P("cen"))

    def on_device(points, fine_assign, fine_start, coarse_start, coarse_assign):
        count, width = points.shape
        local_count = fine_start.shape[0]
        centres = mesh.shape["cen"]
        fits = (
            mesh.shape["pts"] == 2 * SLOTS
            and centres & (centres - 1) == 0
            and centres >= 4
            and width // SLOTS == local_count // 2
            and (width // SLOTS) % 128 == 0
            and count % 2048 == 0
        )
        plan = on_device_paired if fits else on_device_any
        return plan(points, fine_assign, fine_start, coarse_start, coarse_assign)

    return jax.shard_map(
        on_device,
        mesh=mesh,
        in_specs=placed,
        out_specs=(P("cen", None), P(), P(None, "pts")),
        check_vma=False,
    )
```

```python
import functools
import math

import jax
import jax.numpy as jnp
from jax import lax
from jax.experimental import pallas as pl
from jax.experimental.pallas import tpu as pltpu
from jax.sharding import PartitionSpec as P

NC = 64
PASSES = 2
FAR = 3.0e38

prior_weight = 4.0
HIGHEST = lax.Precision.HIGHEST


def refine(totals, counts, coarse_cols, coarse_table):
    lookup = jnp.dot(coarse_table, coarse_cols, precision=HIGHEST)
    fine_next = (totals + prior_weight * lookup) / (counts + prior_weight)[:, None]
    coarse_part = lax.dot_general(
        coarse_table,
        counts[:, None] * fine_next,
        (((0,), (0,)), ((), ())),
        precision=HIGHEST,
    )
    coarse_weight = jnp.sum(coarse_table * counts[:, None], axis=0)
    return (fine_next, coarse_part, coarse_weight)


def on_device_any(points, fine_assign, fine_start, coarse_start, coarse_assign):
    width = points.shape[1]
    local_count = fine_start.shape[0]
    offset = lax.axis_index("cen") * local_count
    columns = jnp.arange(local_count, dtype=jnp.int32)
    coarse_table = (coarse_assign[:, None] == jnp.arange(NC, dtype=jnp.int32)[None, :]).astype(
        jnp.float32
    )
    point_values = points.astype(jnp.float32)
    squares = jnp.sum(point_values * point_values, axis=1)
    fine_now = fine_start
    coarse_now = coarse_start
    gap_rows = []
    for pass_index in range(PASSES):
        member = (fine_assign[pass_index] - offset)[:, None] == columns[None, :]
        products = jnp.dot(
            points, fine_now.astype(jnp.bfloat16).T, preferred_element_type=jnp.float32
        )
        energy = jnp.sum(fine_now * fine_now, axis=1)[None, :] - 2.0 * products
        picked_local = jnp.sum(jnp.where(member, energy, 0.0), axis=1)
        nearest_local = jnp.min(energy, axis=1)
        picked = lax.psum(picked_local, "cen")
        nearest = lax.pmin(nearest_local, "cen")
        gap_rows.append((picked - nearest) / math.sqrt(width))
        weights = 1.0 / (1.0 + (squares + picked) / width)
        scaled = (point_values * weights[:, None]).astype(jnp.bfloat16)
        partial_sums = lax.dot_general(
            member.astype(jnp.bfloat16),
            scaled,
            (((0,), (0,)), ((), ())),
            preferred_element_type=jnp.float32,
        )
        partial_weights = jnp.sum(jnp.where(member, weights[:, None], 0.0), axis=0)
        share_width = width // lax.axis_size("pts")
        start = lax.axis_index("pts") * share_width
        shares = lax.psum_scatter(partial_sums, "pts", scatter_dimension=1, tiled=True)
        counts = lax.psum(partial_weights, "pts")
        coarse_cols = lax.dynamic_slice_in_dim(coarse_now, start, share_width, 1)
        fine_share, coarse_part, coarse_weight = refine(shares, counts, coarse_cols, coarse_table)
        coarse_sum, coarse_count = lax.psum((coarse_part, coarse_weight), "cen")
        coarse_share = (coarse_sum + prior_weight * coarse_cols) / (coarse_count + prior_weight)[
            :, None
        ]
        fine_now, coarse_now = (
            lax.all_gather(fine_share, "pts", axis=1, tiled=True),
            lax.all_gather(coarse_share, "pts", axis=1, tiled=True),
        )
    return (fine_now, coarse_now, jnp.stack(gap_rows))


CORE, ACROSS_X, ACROSS_Y = 1, 2, 4
SLOTS = 4
TAIL = 8


def swap(value, bit, axis="pts"):
    size = lax.axis_size(axis)
    return lax.ppermute(value, axis, [(i, i ^ bit) for i in range(size)])


def swap_first(value):
    pairs = [(i, i ^ (ACROSS_Y if i & CORE else ACROSS_X)) for i in range(lax.axis_size("pts"))]
    return lax.ppermute(value, "pts", pairs)


def swap_second(value):
    pairs = [(i, i ^ (ACROSS_X if i & CORE else ACROSS_Y)) for i in range(lax.axis_size("pts"))]
    return lax.ppermute(value, "pts", pairs)


def block_of(info, slot, core):
    crossed = (slot >> 1) | ((slot & 1) << 1)
    return info[0] ^ (slot + core * (crossed - slot))


HERE = pl.BlockSpec(memory_space=pltpu.VMEM)
AWAY = pl.BlockSpec(memory_space=pl.ANY)
SCALARS = pl.BlockSpec(memory_space=pltpu.SMEM)


def near_by(value):
    return pltpu.with_memory_space_constraint(value, pltpu.VMEM)


def far_off(value):
    return pltpu.with_memory_space_constraint(value, pltpu.HBM)


def as_column(row, rows):
    return jnp.broadcast_to(row, (128, rows)).T


def pass_body(info, points, assign, fine, *refs, pass_index, flip, stream, chained, tile):
    refs = list(refs)
    initial = pass_index == 0
    first = stream
    squares_in = None if first else refs.pop(0)
    seen_in = refs.pop(0) if chained else None
    payload, seen = refs.pop(0), refs.pop(0)
    squares_out = refs.pop(0) if first else None
    kept = refs.pop(0) if stream else points
    low, norms, tallies, sums, even, odd, scaled, places = refs[:8]
    chosen_in = refs[8] if stream else assign
    small_sems, point_sems = refs[9:11] if stream else (None, None)
    start = refs[11] if first else None
    rows, width = low.shape
    mid = rows // 2
    block_width = width // SLOTS
    half = info[1] ^ flip
    base = info[2] + half * rows
    tiles = points.shape[0] // tile

    def span(i):
        return pl.ds(pl.multiple_of(i * tile, tile), tile)

    def column_of(slot, core):
        start = block_of(info, slot, core) * block_width
        return pl.ds(pl.multiple_of(start, block_width), block_width)

    def load(i, half):
        part = pl.ds(pl.multiple_of(i * tile + half * (tile // 2), tile // 2), tile // 2)
        return pltpu.make_async_copy(points.at[part], kept.at[part], point_sems.at[2 * i + half])

    if first:
        load_start = pltpu.make_async_copy(
            fine.at[pl.ds(pl.multiple_of(half * rows, rows), rows)], start, small_sems.at[1]
        )
        load_start.start()
    if stream:
        load(0, 0).start()
        load_assign = pltpu.make_async_copy(assign, chosen_in, small_sems.at[0])
        load_assign.start()
        load(0, 1).start()

        load(1, 0).start()
        load(1, 1).start()

    if initial:
        if first:
            load_start.wait()
            block = start[...]
        else:
            block = fine[pl.ds(pl.multiple_of(half * rows, rows), rows), :]
        norm = jnp.sum(block * block, axis=1, keepdims=True)
        low[...] = (-2.0 * block).astype(jnp.bfloat16)
    else:
        norm = [jnp.zeros((mid, 1), jnp.float32)] * 2
        for piece, (slot, is_low) in enumerate(PIECES):
            block = fine[piece]
            norm[is_low] = norm[is_low] + jnp.sum(block * block, axis=1, keepdims=True)
            part = slice(is_low * mid, (is_low + 1) * mid)
            low[part, column_of(slot, 0)] = (-2.0 * block).astype(jnp.bfloat16)
        norm = jnp.concatenate(norm, 0)
    norms[...] = jnp.broadcast_to(norm, norms.shape)
    tallies[...] = jnp.zeros_like(tallies)
    sums[...] = jnp.zeros_like(sums)
    places[...] = lax.broadcasted_iota(jnp.int32, places.shape, 0).astype(jnp.int16)

    def multiply(i, target):
        target[...] = lax.dot_general(
            low[...], kept[span(i), :], (((1,), (1,)), ((), ())), preferred_element_type=jnp.float32
        )

    def collect(i, products):
        energy = products[...] + jnp.concatenate([norms[...]] * (tile // 128), axis=1)
        chosen = chosen_in[pass_index : pass_index + 1, span(i)] - base
        member = lax.broadcasted_iota(jnp.int32, energy.shape, 0) == chosen
        picked = jnp.sum(jnp.where(member, energy, 0.0), axis=0, keepdims=True)
        nearest = jnp.min(energy, axis=0, keepdims=True)
        inside = (chosen >= 0) & (chosen < rows)
        picked_seen = jnp.where(inside, picked, FAR)
        if chained:
            picked_seen = jnp.minimum(picked_seen, seen_in[0:1, span(i)])
            nearest = jnp.minimum(nearest, seen_in[1:2, span(i)])
        seen[0:1, span(i)] = picked_seen
        seen[1:2, span(i)] = nearest
        if first:
            folded = jnp.zeros((tile, 128), jnp.float32)
            for lane in range(0, width, 128):
                values = kept[span(i), lane : lane + 128].astype(jnp.float32)
                folded = folded + values * values
            squares = jnp.sum(folded.T, axis=0, keepdims=True)
            squares_out[0:1, span(i)] = squares
        else:
            squares = squares_in[0:1, span(i)]
        weights = 1.0 / (1.0 + (squares + picked) / width)
        weighted = jnp.where(member, weights, 0.0)
        tally = tallies[...]
        for lane in range(0, tile, 128):
            tally = tally + weighted[:, lane : lane + 128]
        tallies[...] = tally
        factor = as_column(weights, tile)
        for lane in range(0, width, 128):
            values = kept[span(i), lane : lane + 128].astype(jnp.float32)
            scaled[:, lane : lane + 128] = (values * factor).astype(jnp.bfloat16)
        narrow = jnp.where(inside, chosen, -1).astype(jnp.int16)
        table = jnp.where(
            jnp.concatenate([places[...]] * (tile // 128), axis=1) == narrow,
            jnp.ones((rows, tile), jnp.bfloat16),
            jnp.zeros((rows, tile), jnp.bfloat16),
        )
        sums[...] += jnp.dot(table, scaled[...], preferred_element_type=jnp.float32)

    def arrive(i):
        for half in range(2):
            if stream:
                load(i, half).wait()
                if i + 2 < tiles:
                    load(i + 2, half).start()

    if stream:
        load_assign.wait()
    arrive(0)
    multiply(0, even)

    for i in range(0, tiles - 2, 2):
        arrive(i + 1)
        multiply(i + 1, odd)
        collect(i, even)
        arrive(i + 2)
        multiply(i + 2, even)
        collect(i + 1, odd)

    arrive(tiles - 1)
    multiply(tiles - 1, odd)
    collect(tiles - 2, even)
    collect(tiles - 1, odd)

    counts = jnp.broadcast_to(jnp.sum(tallies[...].T, axis=0, keepdims=True), (TAIL, rows))
    for slot in range(SLOTS):
        columns = column_of(slot, info[1] ^ (not chained))
        payload[slot, :mid, :] = sums[:mid, columns]
        payload[slot, mid : mid + TAIL, :] = counts
        payload[slot, mid + TAIL :, :] = sums[mid:, columns]


def fetch_body(points, *refs):
    *_, kept, sems = refs
    share = points.shape[0] // sems.shape[0]
    copies = [
        pltpu.make_async_copy(
            points.at[i * share : (i + 1) * share], kept.at[i * share : (i + 1) * share], sems.at[i]
        )
        for i in range(sems.shape[0])
    ]
    for copy in copies:
        copy.start()
    for copy in copies:
        copy.wait()


def fetch(points, after):
    return pl.pallas_call(
        fetch_body,
        out_shape=pltpu.VMEM(points.shape, points.dtype),
        in_specs=[AWAY] + [HERE] * len(after),
        out_specs=HERE,
        scratch_shapes=[pltpu.SemaphoreType.DMA((8,))],
        compiler_params=pltpu.CompilerParams(vmem_limit_bytes=2 * 2**20),
        cost_estimate=pl.CostEstimate(
            flops=0, bytes_accessed=4 * points.size, transcendentals=0
        ),
        name="fetch_points",
    )(far_off(points), *[near_by(value) for value in after])


def run_pass(info, points, fine_assign, fine, squares, seen, *, pass_index, flip, rows):
    count, width = points.shape
    block_width = width // SLOTS
    initial = pass_index == 0
    chained = seen is not None
    stream = squares is None
    tile = 1024
    if stream:
        in_specs = [AWAY] * 3
        args = [far_off(points), far_off(fine_assign), far_off(fine)]
    else:
        in_specs = [HERE] * 3
        args = [near_by(points), near_by(fine_assign), near_by(fine)]
    for value in (squares, seen):
        if value is not None:
            in_specs.append(HERE)
            args.append(near_by(value))
    shapes = [(SLOTS, rows + TAIL, block_width), (2, count)]
    if squares is None:
        shapes.append((1, count))
    out_shape = [pltpu.VMEM(shape, jnp.float32) for shape in shapes]
    scratch = [
        pltpu.VMEM((rows, width), jnp.bfloat16),
        pltpu.VMEM((rows, 128), jnp.float32),
        pltpu.VMEM((rows, 128), jnp.float32),
        pltpu.VMEM((rows, width), jnp.float32),
        pltpu.VMEM((rows, tile), jnp.float32),
        pltpu.VMEM((rows, tile), jnp.float32),
        pltpu.VMEM((tile, width), jnp.bfloat16),
        pltpu.VMEM((rows, 128), jnp.int16),
    ]
    if stream:
        scratch += [
            pltpu.VMEM((PASSES, count), jnp.int32),
            pltpu.SemaphoreType.DMA((2,)),
            pltpu.SemaphoreType.DMA((2 * count // tile,)),
        ]
        if initial:
            scratch.append(pltpu.VMEM((rows, width), jnp.float32))
        out_shape.append(pltpu.VMEM(points.shape, points.dtype))
    body = functools.partial(
        pass_body,
        pass_index=pass_index,
        flip=flip,
        stream=stream,
        chained=chained,
        tile=tile,
    )
    return pl.pallas_call(
        body,
        out_shape=out_shape,
        in_specs=[SCALARS, *in_specs],
        out_specs=[HERE] * len(out_shape),
        scratch_shapes=scratch,
        compiler_params=pltpu.CompilerParams(vmem_limit_bytes=20 * 2**20),
        cost_estimate=pl.CostEstimate(
            flops=4 * rows * count * width, bytes_accessed=2 * count * width, transcendentals=0
        ),
        name=f"energies_and_sums_{pass_index}{int(chained)}",
    )(info, *args)


def one_hot_dot(table, value, dims):
    table = table.astype(jnp.bfloat16)
    total = 0.0
    for _ in range(3):
        term = value.astype(jnp.bfloat16)
        value = value - term.astype(jnp.float32)
        total = total + lax.dot_general(
            table, term, dims, preferred_element_type=jnp.float32
        )
    return total


def refine_body(info, own, sibling, *refs, flip):
    first_top, first_low, second_top, second_low, owners, *coarse_in, top, low, part = refs
    rows = owners.shape[2]
    mid = rows // 2
    block_width = part.shape[1]
    owner = owners[info[1] ^ flip]
    if len(coarse_in) == 1:
        column = pl.multiple_of(info[0] * block_width, block_width)
        coarse = coarse_in[0][:, pl.ds(column, block_width)]
    else:
        sums = coarse_in[0][: NC + TAIL, :] + coarse_in[1][: NC + TAIL, :]
        coarse = sums[:NC] / as_column(sums[NC : NC + 1, :128], 128)[:NC, :1]
    head = own[0, : mid + TAIL, :] + sibling[0, : mid + TAIL, :]
    rest = own[0, mid + TAIL :, :] + sibling[0, mid + TAIL :, :]
    head = head + (first_top[0] + second_top[...])
    rest = rest + (first_low[0] + second_low[...])
    totals, counts_row = jnp.concatenate([head[:mid], rest], 0), head[mid:]
    counts = as_column(counts_row[:1], rows)[:, :1]
    table = (
        lax.broadcasted_iota(jnp.int32, (NC, rows), 0) == owner
    ).astype(jnp.float32)
    lookup = one_hot_dot(table, coarse, (((0,), (0,)), ((), ())))
    new = (totals + prior_weight * lookup) / (counts + prior_weight)
    top[...] = new[:mid]
    low[...] = new[mid:]
    prior = jnp.where(info[3] == 0, prior_weight, 0.0)
    part[:NC, :] = prior * coarse + one_hot_dot(table, counts * new, (((1,), (0,)), ((), ())))
    part[NC:, :] = jnp.zeros((TAIL, part.shape[1]), jnp.float32)
    weight = jnp.sum(table * counts_row[:1], axis=1, keepdims=True)
    weight = jnp.broadcast_to(weight, (NC, 128)).T[:TAIL]
    part[NC:, :NC] = prior + weight


def refine_half(info, own, sibling, incoming, owners, coarse, *, flip):
    _, rows, block_width = own.shape
    mid = (rows - TAIL) // 2
    args = [near_by(value) for value in (own, sibling, *incoming, owners, *coarse)]
    shapes = [(mid, block_width), (mid, block_width), (NC + TAIL, block_width)]
    return pl.pallas_call(
        functools.partial(refine_body, flip=flip),
        out_shape=[pltpu.VMEM(shape, jnp.float32) for shape in shapes],
        in_specs=[SCALARS] + [HERE] * len(args),
        out_specs=[HERE] * len(shapes),
        compiler_params=pltpu.CompilerParams(vmem_limit_bytes=8 * 2**20),
        name="refine_half",
    )(info, *args)


def exchange(held, sibling, folded=None):
    cut = (held.shape[1] - TAIL) // 2 + TAIL
    chunks = slice(0, cut), slice(cut, None)
    first = [held[1::2, rows] + sibling[1::2, rows] for rows in chunks]
    first, folded = lax.optimization_barrier((first, folded))
    first = [swap_first(chunk) for chunk in first]
    if folded is not None:
        folded = swap(folded, lax.axis_size("cen") // 2, "cen")
    second = [
        held[2, rows] + sibling[2, rows] + arrived[1] for rows, arrived in zip(chunks, first)
    ]
    if folded is not None:
        second[1], folded = lax.optimization_barrier((second[1], folded))
    second = [swap_second(chunk) for chunk in second]
    return [*first, *second], folded


PIECES = ((1, 1), (2, 0), (3, 0), (3, 1), (1, 0), (2, 1), (0, 0), (0, 1))


def gather_half(top, low, later=False):
    x_low = swap(low, ACROSS_X)
    y_top = swap(top, ACROSS_Y)
    again = top, low
    if later:
        x_low, y_top, again = lax.optimization_barrier((x_low, y_top, again))
    x_top = swap(again[0], ACROSS_X)
    y_low = swap(again[1], ACROSS_Y)
    corner_top = swap(y_top, ACROSS_X)
    corner_low = swap(x_low, ACROSS_Y)
    return [x_low, y_top, corner_top, corner_low, x_top, y_low, top, low]


def spread(value):
    corner = swap(value, ACROSS_X | ACROSS_Y)
    return [value, swap(value, ACROSS_X), swap(value, ACROSS_Y), corner]


def over_cen(value, combine, bits=None):
    for bit in range(lax.axis_size("cen").bit_length() - 1) if bits is None else bits:
        value = combine(value, swap(value, 1 << bit, "cen"))
    return value


def fold(first, second):
    cut = NC + TAIL
    return jnp.concatenate(
        [first[:cut] + second[:cut], jnp.minimum(first[cut:], second[cut:])], 0
    )


def place_body(info, *refs, flip):
    own, other = refs[:3], refs[3:6]
    fine_out, coarse_out, fine_held, coarse_held, sems = refs[6:]
    block_width = coarse_out.shape[1] // SLOTS
    rows = fine_out.shape[0] // 2
    mid = rows // 2
    half = info[1] ^ flip

    def column_of(slot, core):
        start = block_of(info, slot, core) * block_width
        return pl.ds(pl.multiple_of(start, block_width), block_width)

    def put(at, *groups):
        for piece, (slot, is_low) in enumerate(PIECES):
            part = slice(is_low * mid, (is_low + 1) * mid)
            fine_held[at, part, column_of(slot, 0)] = groups[piece // SLOTS][piece % SLOTS]

    def send(at, half):
        span = pl.ds(pl.multiple_of(half * rows, rows), rows)
        return pltpu.make_async_copy(fine_held.at[at], fine_out.at[span], sems.at[at])

    put(0, *own[:2])
    send(0, half).start()
    put(1, *other[:2])
    send(1, 1 - half).start()
    parts, others = own[2], other[2]
    weight = parts[0, NC:, :128] + others[0, NC:, :128]
    weight = as_column(weight[:1], 128)[:NC, :1]
    for slot in range(SLOTS):
        total = parts[slot, :NC, :] + others[slot, :NC, :]
        coarse_held[:, column_of(slot, 0)] = total / weight
    send_coarse = pltpu.make_async_copy(coarse_held, coarse_out, sems.at[2])
    send_coarse.start()
    send(0, half).wait()
    send(1, 1 - half).wait()
    send_coarse.wait()


def place(info, own, other, *, flip):
    _, mid, block_width = own[0].shape
    rows, width = 2 * mid, SLOTS * block_width
    args = [near_by(value) for value in (*own, *other)]
    return pl.pallas_call(
        functools.partial(place_body, flip=flip),
        out_shape=[
            jax.ShapeDtypeStruct((2 * rows, width), jnp.float32),
            jax.ShapeDtypeStruct((NC, width), jnp.float32),
        ],
        in_specs=[SCALARS] + [HERE] * len(args),
        out_specs=[AWAY, AWAY],
        scratch_shapes=[
            pltpu.VMEM((2, rows, width), jnp.float32),
            pltpu.VMEM((NC, width), jnp.float32),
            pltpu.SemaphoreType.DMA((3,)),
        ],
        compiler_params=pltpu.CompilerParams(vmem_limit_bytes=8 * 2**20),
        name="place_blocks",
    )(info, *args)


def on_device_paired(points, fine_assign, fine_start, coarse_start, coarse_assign):
    width = points.shape[1]
    local_count = fine_start.shape[0]
    rows = local_count // 2
    block_width = width // SLOTS
    cen, me = lax.axis_index("cen"), lax.axis_index("pts")
    core = me & 1
    info = jnp.stack([me >> 1, core, cen * local_count, cen * 2 + core]).astype(jnp.int32)
    owners = coarse_assign.reshape(2, 1, rows)

    call = functools.partial(run_pass, info, pass_index=0, rows=rows)
    sent, seen, squares, kept = call(points, fine_assign, fine_start, None, None, flip=1)
    sibling = swap(sent, CORE)
    held, seen_first = call(kept, fine_assign, fine_start, squares, seen, flip=0)
    incoming, _ = exchange(held, sibling)
    top, low, part = refine_half(
        info, held, sibling, incoming, owners, [coarse_start], flip=0
    )
    own = gather_half(top, low)
    bits = range(lax.axis_size("cen").bit_length() - 1)
    folded = jnp.concatenate([part, seen_first.reshape(-1, block_width)], 0)
    paired = swap(folded, 1, "cen")
    kept = fetch(points, own[:2])
    own, kept, paired = lax.optimization_barrier((own, kept, paired))
    own = jnp.stack(own)
    other = swap(own, CORE)

    call = functools.partial(run_pass, info, pass_index=1, rows=rows)
    sent, seen = call(kept, fine_assign, own, squares, None, flip=0)
    sent, paired = lax.optimization_barrier((sent, paired))
    folded = fold(folded, paired)
    sibling = swap(sent, CORE)
    part = folded[: NC + TAIL]
    others_part = swap(part, CORE)
    held, seen_second = call(kept, fine_assign, other, squares, seen, flip=1)
    held, others_part = lax.optimization_barrier((held, others_part))
    folded = jnp.concatenate([part + others_part, folded[NC + TAIL :]], 0)
    folded = over_cen(folded, fold, bits[1:-1])
    incoming, paired = exchange(held, sibling, folded)
    seen_first = jnp.minimum(folded[NC + TAIL :], paired[NC + TAIL :])

    top, low, part = refine_half(
        info, held, sibling, incoming, owners, [folded, paired], flip=1
    )
    folded = jnp.concatenate([part, seen_second.reshape(-1, block_width)], 0)
    top, low, folded = lax.optimization_barrier((top, low, folded))
    own = gather_half(top, low, True)
    folded = over_cen(folded, fold)
    part, seen_second = folded[: NC + TAIL], folded[NC + TAIL :]
    parts = spread(part)
    own[2], own[3], parts[1] = lax.optimization_barrier((own[2], own[3], parts[1]))
    blocks = [jnp.stack(own[:4]), jnp.stack(own[4:]), jnp.stack(parts)]
    fine_now, coarse_now = place(info, blocks, [swap(block, CORE) for block in blocks], flip=1)

    seen = [each.reshape(2, -1) for each in (seen_first, seen_second)]
    gaps = jnp.stack([each[0] - each[1] for each in seen]) / math.sqrt(width)
    return (fine_now, coarse_now, gaps)


def solution(mesh):
    placed = (P("pts", None), P(None, "pts"), P("cen", None), P(), P("cen"))

    def on_device(points, fine_assign, fine_start, coarse_start, coarse_assign):
        count, width = points.shape
        local_count = fine_start.shape[0]
        centres = mesh.shape["cen"]
        fits = (
            mesh.shape["pts"] == 2 * SLOTS
            and centres & (centres - 1) == 0
            and centres >= 4
            and width // SLOTS == local_count // 2
            and (width // SLOTS) % 128 == 0
            and count % 2048 == 0
        )
        plan = on_device_paired if fits else on_device_any
        return plan(points, fine_assign, fine_start, coarse_start, coarse_assign)

    return jax.shard_map(
        on_device,
        mesh=mesh,
        in_specs=placed,
        out_specs=(P("cen", None), P(), P(None, "pts")),
        check_vma=False,
    )
```
